128 devices in a mesh: shard: 16 (over y_hi, z, core), rep: 8 (over y_lo, x).
Axes of the slice: x: 4, y: 4 (y_hi: 2, y_lo: 2; y = y_hi * 2 + y_lo), z: 4, core: 2. Of those that a mesh axis runs over, the one named last changes fastest.
Arguments:
- tokens: bfloat16 [32, 1024, 1024], P('shard', 'rep'), may hold values from -6 to 6
- cotangent: bfloat16 [32, 1024, 1024], P('shard', 'rep'), may hold values from -6 to 6
- routes: int32 [32, 1024, 8], P('shard', 'rep'), may hold values from 0 to 15, all different within a row; in each aligned block of 128 rows (0 to 127, 128 to 255, ..., all dimensions but the last counted through in order) at most 96 rows name the same one
- picture_starts: int32 [32, 2], P('shard'), may hold values from 0 to 768, as said below
- attn_gain: bfloat16 [1024], P('shard'), may hold values from 0.25 to 1.75
- query_weight: bfloat16 [1024, 1024], P('shard'), may hold values from -0.1875 to 0.1875
- key_weight: bfloat16 [1024, 512], P('shard'), may hold values from -0.1875 to 0.1875
- value_weight: bfloat16 [1024, 512], P('shard'), may hold values from -0.1875 to 0.1875
- query_gain: bfloat16 [1024], P('shard'), may hold values from 0.25 to 1.75
- key_gain: bfloat16 [512], P('shard'), may hold values from 0.25 to 1.75
- output_weight: bfloat16 [1024, 1024], P('shard'), may hold values from -2 to 2
- ffn_gain: bfloat16 [1024], P('shard'), may hold values from 0.25 to 1.75
- router_weight: bfloat16 [1024, 16], P('shard'), may hold values from -0.09375 to 0.09375
- expert_in: bfloat16 [16, 1024, 1024], P('shard'), may hold values from -0.1875 to 0.1875
- expert_down: bfloat16 [16, 512, 1024], P('shard'), may hold values from -1 to 1
Outputs:
- block_out: bfloat16 [32, 1024, 1024], P('shard', 'rep')
- tokens_grad: bfloat16 [32, 1024, 1024], P('shard', 'rep')
- attn_gain_grad: float32 [1024], P('shard')
- query_weight_grad: float32 [1024, 1024], P('shard')
- key_weight_grad: float32 [1024, 512], P('shard')
- value_weight_grad: float32 [1024, 512], P('shard')
- query_gain_grad: float32 [1024], P('shard')
- key_gain_grad: float32 [512], P('shard')
- output_weight_grad: float32 [1024, 1024], P('shard')
- ffn_gain_grad: float32 [1024], P('shard')
- router_weight_grad: float32 [1024, 16], P('shard')
- expert_in_grad: float32 [16, 1024, 1024], P('shard')
- expert_down_grad: float32 [16, 512, 1024], P('shard')
The draws below stay inside these ranges and needn't reach their ends.
Inputs may be any that keep to these rules, and one draw needn't show every extreme that they name: `routes`: each token names 8 different experts. In each aligned block of 128 positions of a sequence (the rows of one device), no expert is named by more than 96 tokens; in some block one expert is named by exactly 96. `picture_starts`: each row holds 2 different multiples of 256 in rising order.
All inputs are finite; a program needn't handle non-finite values.
Results may differ from the reference program's by a relative error of at most 0.03.
Values may be sent and summed in bfloat16 or wider, within the bound.
A program may use at most 192 MiB of HBM per device.

```python
import math
import jax
import jax.numpy as jnp
import numpy as np
from jax import lax

D = 1024
HEADS = 16
KV_HEADS = 8
HEAD_DIM = 64
FF = 512
TOPK = 8
EXPERTS = 16
PIC = 256
NPIC = 2
QD = 1024
KVD = 512
SEQ_DEV = 128
LENGTH = 1024
SEQS = 32
CAP = 96


def draw_picture_starts(key, part):
    key = jax.random.fold_in(key, 7)
    slot_count = LENGTH // PIC
    row_keys = jax.random.split(key, SEQS)

    def one_row(row_key):
        return jax.random.permutation(row_key, slot_count)
    orders = jax.vmap(one_row)(row_keys)
    chosen = jnp.sort(orders[:, :NPIC], axis=1)
    special = jax.random.randint(jax.random.fold_in(key, 1), (), 0, SEQS)
    middle_slots = 1 + jax.random.permutation(jax.random.fold_in(key, 2), slot_count - 2)[:NPIC - 2]
    forced = jnp.sort(jnp.concatenate([jnp.array([0], dtype=jnp.int32), middle_slots.astype(jnp.int32), jnp.array([slot_count - 1], dtype=jnp.int32)]))
    chosen = jnp.where((jnp.arange(SEQS) == special)[:, None], forced[None, :], chosen.astype(jnp.int32))
    return (chosen * PIC).astype(jnp.int32)


def level_of(own_key, dims, cuts, least, high):
    def one(position, parts):
        steps = jax.random.uniform(jax.random.fold_in(jax.random.fold_in(own_key, 6), position), (parts,), jnp.float32, least / len(cuts), high / len(cuts))
        return jnp.repeat(jnp.exp(steps), dims[position] // parts).reshape((-1,) + (1,) * (len(dims) - position - 1))

    factor_of = one(*cuts[0])
    for cut in cuts[1:]:
        factor_of = factor_of * one(*cut)
    return factor_of


def shared_out(stream_key, own, number, rows, amount, top, most, slope):
    order = jax.random.permutation(stream_key, amount)
    packed, usual = load_shares(amount, rows * top, most, slope, True), load_shares(amount, rows * top, most, slope, False)
    places = jnp.arange(amount)

    def named(tallies, offset_by):
        used = int((tallies > 0).sum())
        fixed = max(1, used // 4)
        moved = fixed + (places - fixed + offset_by * (used - fixed)) % max(1, amount - fixed)
        return jnp.zeros((amount,), jnp.int32).at[order[jnp.where(places < fixed, places, moved)]].set(jnp.asarray(tallies, jnp.int32))

    tallies = jnp.where(number % 4 == 0, named(packed, number // 4), named(usual, number - number // 4 - 1))
    mixed = jax.random.permutation(jax.random.fold_in(own, 3), amount)
    source_of, taker = mixed[0:amount // 2 * 2:2], mixed[1:amount // 2 * 2:2]
    slack = jnp.minimum(tallies[source_of] - 1, most - tallies[taker]) // 2
    slack = jnp.where((source_of == order[0]) | (taker == order[0]) | (tallies[taker] == 0), 0, jnp.maximum(slack, 0))
    moved = jax.random.randint(jax.random.fold_in(own, 4), (amount // 2,), 0, 1 << 20) % (slack + 1)
    tallies = tallies.at[source_of].add(-moved).at[taker].add(moved)
    items = jnp.searchsorted(jnp.cumsum(tallies), jnp.arange(rows * top), side="right").astype(jnp.int32)
    table = items.reshape(top, rows).T
    table = table[jax.random.permutation(jax.random.fold_in(own, 1), rows)]
    offset_by = jax.random.randint(jax.random.fold_in(own, 2), (rows, 1), 0, top)
    return jnp.take_along_axis(table, (jnp.arange(top)[None, :] + offset_by) % top, axis=1)


def load_shares(count, total, limit, lean, full):
    portions = [(1 << 20) // math.isqrt(rank ** lean) + 1 for rank in range(1, count + 1)]
    largest = limit if full else min(limit, max(-(-total // count), total * portions[0] // sum(portions)))
    least = 1 if total - largest >= count - 1 else 0
    given, surplus = [largest] + [least] * (count - 1), total - largest - least * (count - 1)
    while surplus > 0:
        free = [i for i in range(1, count) if given[i] < largest] or [i for i in range(1, count) if given[i] < limit]
        whole, remaining = sum([portions[i] for i in free]), surplus
        for i in free:
            addition = min(limit - given[i], max(1, remaining * portions[i] // whole), surplus)
            given[i] = given[i] + addition
            surplus = surplus - addition
    return np.array(given)


def noise(stream_key, shape, scale, most, shards=(), held_as=jnp.bfloat16):
    drawn = scale * jax.random.normal(stream_key, shape, jnp.float32)
    if shards:
        drawn = drawn * level_of(stream_key, shape, shards, -0.22, 0.18)
    return jnp.clip(drawn, -most, most).astype(held_as)


def setup_inputs(seed: int = 0) -> dict:
    keys = jax.random.split(jax.random.key(seed), 16)
    tokens = noise(keys[0], (SEQS, LENGTH, D), 1.0, 6.0, ((0, 16), (1, 8)))
    cotangent = noise(keys[1], (SEQS, LENGTH, D), 1.0, 6.0, ((0, 16), (1, 8)))
    routes_keys = jax.random.split(jax.random.fold_in(keys[2], 1), SEQS * LENGTH // SEQ_DEV)
    routes_turns = jax.random.permutation(jax.random.fold_in(keys[2], 3), SEQS * LENGTH // SEQ_DEV)
    routes = jax.vmap(lambda own, number: shared_out(jax.random.fold_in(keys[2], 2), own, number, SEQ_DEV, EXPERTS, TOPK, CAP, 1))(routes_keys, routes_turns).reshape((SEQS, LENGTH, TOPK))
    picture_starts = draw_picture_starts(jax.random.fold_in(keys[15], 71), 0)
    attn_gain = jnp.clip(1.0 + 0.15 * jax.random.normal(keys[4], (D,), jnp.float32), 0.25, 1.75).astype(jnp.bfloat16)
    query_weight = noise(keys[5], (D, QD), D ** -0.5, 0.1875, ((0, 16),))
    key_weight = noise(keys[6], (D, KVD), D ** -0.5, 0.1875, ((0, 16),))
    value_weight = noise(keys[7], (D, KVD), D ** -0.5, 0.1875, ((0, 16),))
    query_gain = jnp.clip(1.0 + 0.15 * jax.random.normal(keys[8], (QD,), jnp.float32), 0.25, 1.75).astype(jnp.bfloat16)
    key_gain = jnp.clip(1.0 + 0.15 * jax.random.normal(keys[9], (KVD,), jnp.float32), 0.25, 1.75).astype(jnp.bfloat16)
    output_weight = noise(keys[10], (QD, D), (max(D // 128, 4)) ** -0.5, 2.0, ((0, 16),))
    ffn_gain = jnp.clip(1.0 + 0.15 * jax.random.normal(keys[11], (D,), jnp.float32), 0.25, 1.75).astype(jnp.bfloat16)
    router_weight = noise(keys[12], (D, EXPERTS), (4 * D) ** -0.5, 0.09375, ((0, 16),))
    expert_in = noise(keys[13], (EXPERTS, D, 2 * FF), D ** -0.5, 0.1875, ((0, 16),))
    expert_down = noise(keys[14], (EXPERTS, FF, D), (max(FF // 16, 2)) ** -0.5, 1.0, ((0, 16),))
    return {"tokens": tokens, "cotangent": cotangent, "routes": routes, "picture_starts": picture_starts, "attn_gain": attn_gain, "query_weight": query_weight, "key_weight": key_weight, "value_weight": value_weight, "query_gain": query_gain, "key_gain": key_gain, "output_weight": output_weight, "ffn_gain": ffn_gain, "router_weight": router_weight, "expert_in": expert_in, "expert_down": expert_down}


@jax.custom_vjp
def low(v):
    return lax.optimization_barrier(v.astype(jnp.bfloat16)).astype(jnp.float32)

@jax.custom_vjp
def low_back(v):
    return v

def low_keep(v):
    return (low(v), None)

def low_pass(kept, grad):
    return (grad,)

def back_keep(v):
    return (v, None)

def back_low(kept, grad):
    return (low(grad),)
low.defvjp(low_keep, low_pass)
low_back.defvjp(back_keep, back_low)
norm_eps = 1e-06
rope_base = 10000.0
masked_score = -1e+30
highest = lax.Precision.HIGHEST

def product(left_operand, right_operand):
    return jnp.dot(left_operand, right_operand, preferred_element_type=jnp.float32, precision=highest)

def rms_scale(values, gain):
    return values * lax.rsqrt(lax.optimization_barrier(jnp.mean(values * values, axis=-1, keepdims=True)) + norm_eps) * gain

def rotary_tables(positions, head_size):
    half_size = head_size // 2
    exponent = jnp.arange(half_size, dtype=jnp.float32) * (2.0 / head_size)
    frequency = rope_base ** (-exponent)
    angles = positions.astype(jnp.float32)[:, None] * frequency[None, :]
    cosine_table = jnp.concatenate([jnp.cos(angles), jnp.cos(angles)], axis=-1)
    sine_table = jnp.concatenate([jnp.sin(angles), jnp.sin(angles)], axis=-1)
    return (cosine_table, sine_table)

def rotate(values, cosine_table, sine_table):
    half_size = values.shape[-1] // 2
    turned = jnp.concatenate([-values[..., half_size:], values[..., :half_size]], axis=-1)
    return values * cosine_table[:, None, :] + turned * sine_table[:, None, :]

def piece_index(positions, starts):
    inside = (positions[:, None] >= starts[None, :]) & (positions[:, None] < starts[None, :] + PIC)
    labels = jnp.arange(1, starts.shape[0] + 1, dtype=jnp.int32)
    return lax.optimization_barrier(jnp.sum(jnp.where(inside, labels[None, :], 0), axis=1)) - 1

def allowed_mask(query_pos, key_pos, starts):
    query_piece = piece_index(query_pos, starts)
    key_piece = piece_index(key_pos, starts)
    causal = key_pos[None, :] <= query_pos[:, None]
    shared = (query_piece[:, None] == key_piece[None, :]) & (query_piece[:, None] >= 0)
    return causal | shared

def query_key(query_raw, key_raw, query_gain, key_gain, cosine_table, sine_table):
    row_count = query_raw.shape[0]
    query_rot = rotate(rms_scale(query_raw, query_gain).reshape(row_count, HEADS, HEAD_DIM), cosine_table, sine_table)
    key_rot = rotate(rms_scale(key_raw, key_gain).reshape(row_count, KV_HEADS, HEAD_DIM), cosine_table, sine_table)
    return (query_rot, key_rot)

def layer(inputs, attn_gain, query_weight, key_weight, value_weight, query_gain, key_gain, output_weight, ffn_gain, router_weight, expert_in, expert_down, route_ids, starts):
    length = inputs.shape[0]
    group_size = HEADS // KV_HEADS
    positions = jnp.arange(length, dtype=jnp.int32)
    cosine_table, sine_table = rotary_tables(positions, HEAD_DIM)
    attn_in = low(rms_scale(inputs, attn_gain))
    query_raw = low_back(product(attn_in, query_weight))
    key_raw = low_back(product(attn_in, key_weight))
    value_low = low_back(low(product(attn_in, value_weight)))
    query_rot, key_rot = query_key(query_raw, key_raw, query_gain, key_gain, cosine_table, sine_table)
    query_low = low_back(low(query_rot)).reshape(length, KV_HEADS, group_size, HEAD_DIM)
    key_low = low_back(low(key_rot))
    allowed = allowed_mask(positions, positions, starts)
    scores = jnp.einsum('qkgd,skd->kgqs', query_low, key_low, precision=highest) * HEAD_DIM ** (-0.5)
    scores = low_back(jnp.where(allowed[None, None], scores, masked_score))
    row_top = lax.optimization_barrier(jnp.max(scores, axis=-1, keepdims=True))
    exponent = jnp.exp(scores - row_top)
    soft_probs = low(exponent / lax.optimization_barrier(jnp.sum(exponent, axis=-1, keepdims=True)))
    mixed_heads = jnp.einsum('kgqs,skd->qkgd', soft_probs, value_low.reshape(length, KV_HEADS, HEAD_DIM), precision=highest)
    mixed_heads = low_back(low(mixed_heads.reshape(length, HEADS * HEAD_DIM)))
    middle = inputs + low_back(product(mixed_heads, output_weight))
    ffn_in = low(rms_scale(middle, ffn_gain))
    logits = low_back(product(ffn_in, router_weight))
    gate_probs = jax.nn.softmax(jnp.take_along_axis(logits, route_ids, axis=1), axis=-1)
    expert_picks = (route_ids[:, :, None] == jnp.arange(EXPERTS, dtype=jnp.int32)[None, None, :]).astype(jnp.float32)
    weight_full = lax.optimization_barrier(jnp.sum(gate_probs[:, :, None] * expert_picks, axis=1))
    expert_rows = low_back(jnp.broadcast_to(ffn_in[None], (EXPERTS,) + ffn_in.shape))
    gate_up = low_back(jnp.einsum('etd,edf->etf', expert_rows, expert_in, precision=highest))
    hidden = low(jax.nn.silu(gate_up[..., :FF]) * gate_up[..., FF:])
    expert_out = low_back(low(jnp.einsum('etf,efd->etd', hidden, expert_down, precision=highest)))
    return middle + jnp.einsum('te,etd->td', weight_full, expert_out, precision=highest)

def reference(tokens, cotangent, routes, picture_starts, attn_gain, query_weight, key_weight, value_weight, query_gain, key_gain, output_weight, ffn_gain, router_weight, expert_in, expert_down):
    weights = tuple((weight.astype(jnp.float32) for weight in (attn_gain, query_weight, key_weight, value_weight, query_gain, key_gain, output_weight, ffn_gain, router_weight, expert_in, expert_down)))

    def one_sequence(totals, sequence_item):
        inputs, seed_grad, route_ids, starts = sequence_item

        def forward(values, *params):
            return layer(values, *params, route_ids, starts)
        result, pullback = jax.vjp(forward, inputs.astype(jnp.float32), *weights)
        gradients = pullback(seed_grad.astype(jnp.float32))
        totals = tuple((running + gradient for running, gradient in zip(totals, gradients[1:])))
        return (totals, (result.astype(jnp.bfloat16), gradients[0].astype(jnp.bfloat16)))
    initial = tuple((jnp.zeros(weight.shape, jnp.float32) for weight in weights))
    totals, outputs = lax.scan(one_sequence, initial, (tokens, cotangent, routes, picture_starts))
    return (outputs[0], outputs[1], totals[0], totals[1], totals[2], totals[3], totals[4], totals[5], totals[6], totals[7], totals[8], totals[9], totals[10])
```

```python
import functools

import jax
import jax.numpy as jnp
from jax import lax
from jax.experimental import pallas as pl
from jax.experimental.pallas import tpu as pltpu
from jax.sharding import PartitionSpec as P

HEADS = 16
KV_HEADS = 8
HEAD_DIM = 64
PIC = 256
RING = 4
GROUP = 16
REPS = 8
VMEM_LIMIT = 56 << 20

norm_eps = 1e-06
rope_base = 10000.0
masked_score = -1e30

bf16 = jnp.bfloat16
f32 = jnp.float32


class Place:
    def __init__(self):
        shard = lax.axis_index("shard")
        rep = lax.axis_index("rep")
        self.shard, self.rep = shard, rep
        core = lax.rem(shard, 2)
        ring_z = lax.rem(lax.div(shard, 2), RING)
        y_hi = lax.div(shard, 8)
        ring_x = lax.rem(rep, RING)
        y_lo = lax.div(rep, RING)
        self.core = core

        def shard_of(hi, z, c):
            return (hi * RING + z) * 2 + c

        def rep_of(lo, x):
            return lo * RING + x

        def up(v):
            return lax.rem(v + 1, RING)

        def down(v):
            return lax.rem(v + RING - 1, RING)

        self.twin = (shard_of(y_hi, ring_z, 1 - core), rep)
        self.tokens = Axes(
            y_hi,
            ring_z,
            (shard_of(y_hi, up(ring_z), core), rep),
            (shard_of(y_hi, down(ring_z), core), rep),
            (shard_of(1 - y_hi, ring_z, core), rep_of(1 - y_lo, ring_x)),
        )
        self.copies = Axes(
            y_lo,
            ring_x,
            (shard, rep_of(y_lo, up(ring_x))),
            (shard, rep_of(y_lo, down(ring_x))),
            (shard, rep_of(1 - y_lo, ring_x)),
        )


class Axes:
    def __init__(self, side, spot, ahead, behind, across):
        self.side, self.spot = side, spot
        self.ahead, self.behind, self.across = ahead, behind, across

    def at(self, flip, step):
        return (1 - self.side) if flip else self.side, lax.rem(self.spot + RING + step, RING)

    def neighbours(self):
        return [self.ahead, self.behind, self.across]


def greet(devices):
    barrier = pltpu.get_barrier_semaphore()
    for device in devices:
        pl.semaphore_signal(barrier, inc=1, device_id=device, device_id_type=pl.DeviceIdType.MESH)
    pl.semaphore_wait(barrier, len(devices))


class Line:
    def __init__(self, send_sem, recv_sem):
        self.send_sem, self.recv_sem = send_sem, recv_sem
        self.sent = []

    def send(self, index, source, target, device):
        copy = pltpu.make_async_remote_copy(
            src_ref=source,
            dst_ref=target,
            send_sem=self.send_sem.at[index],
            recv_sem=self.recv_sem.at[index],
            device_id=device,
            device_id_type=pl.DeviceIdType.MESH,
        )
        copy.start()
        self.sent.append(copy)

    def take(self, index, target, device):
        pltpu.make_async_remote_copy(
            src_ref=target,
            dst_ref=target,
            send_sem=self.send_sem.at[index],
            recv_sem=self.recv_sem.at[index],
            device_id=device,
            device_id_type=pl.DeviceIdType.MESH,
        ).wait_recv()

    def finish(self):
        for copy in self.sent:
            copy.wait_send()


def abreast(*parts):
    running = list(parts)
    while running:
        for part in list(running):
            try:
                next(part)
            except StopIteration:
                running.remove(part)


GATHER_SEMS = 20


def gather_parts(axes, line, own, block, rows, local_sem, twin=None):
    half, quarter = rows // 2, rows // 4
    mine, back, front, far = axes.at(0, 0), axes.at(0, -1), axes.at(0, 1), axes.at(0, 2)
    pair, pair_back, pair_front, pair_far = (axes.at(1, n) for n in (0, -1, 1, 2))
    ahead, behind, across = axes.ahead, axes.behind, axes.across

    def full(which):
        return block(which, 0, rows)

    def share(index, which):
        if twin is not None:
            line.send(12 + index, full(which), full(which), twin)

    keep = pltpu.make_async_copy(own, full(mine), local_sem)
    keep.start()
    line.send(0, own, full(mine), ahead)
    line.send(1, own, full(mine), behind)
    line.send(2, own, full(mine), across)
    if twin is not None:
        line.send(12, own, full(mine), twin)
    yield
    line.take(0, full(back), ahead)
    line.send(3, block(back, 0, half), block(back, 0, half), ahead)
    line.send(4, block(back, half, half), block(back, half, half), across)
    share(1, back)
    line.take(1, full(front), behind)
    line.send(5, block(front, half, half), block(front, half, half), behind)
    line.send(6, block(front, half, half), block(front, half, half), across)
    share(2, front)
    line.take(2, full(pair), across)
    line.send(7, block(pair, 0, half), block(pair, 0, half), ahead)
    line.send(8, block(pair, 0, half), block(pair, 0, half), behind)
    share(3, pair)
    yield
    line.take(3, block(far, 0, half), ahead)
    line.take(5, block(far, half, half), behind)
    line.send(9, block(far, half, half), block(far, half, half), across)
    share(4, far)
    line.take(7, block(pair_back, 0, half), ahead)
    line.send(10, block(pair_back, 0, quarter), block(pair_back, 0, quarter), ahead)
    line.take(8, block(pair_front, 0, half), behind)
    line.send(
        11, block(pair_front, quarter, quarter), block(pair_front, quarter, quarter), behind
    )
    line.take(4, block(pair_back, half, half), across)
    share(5, pair_back)
    line.take(6, block(pair_front, half, half), across)
    share(6, pair_front)
    yield
    line.take(10, block(pair_far, 0, quarter), ahead)
    line.take(11, block(pair_far, quarter, quarter), behind)
    line.take(9, block(pair_far, half, half), across)
    share(7, pair_far)
    keep.wait()
    if twin is not None:
        for index, which in enumerate(
            (mine, back, front, pair, far, pair_back, pair_front, pair_far)
        ):
            line.take(12 + index, block(which, 0, rows, True), twin)
    line.finish()


SUM_SEMS = 20


def add_rows(target, source, rows):
    step = 16
    count = rows // step

    def body(index, carry):
        at = pl.ds(pl.multiple_of(index * step, step), step)
        target[at] = (target[at].astype(f32) + source[at].astype(f32)).astype(bf16)
        return carry

    lax.fori_loop(0, count, body, 0)


def stage_rows(rows):
    return 7 * rows


def sum_parts(axes, line, part, stage, rows, result, twin=None):
    half, quarter = rows // 2, rows // 4
    mine, back, front, far = axes.at(0, 0), axes.at(0, -1), axes.at(0, 1), axes.at(0, 2)
    pair, pair_back, pair_front, pair_far = (axes.at(1, n) for n in (0, -1, 1, 2))
    ahead, behind, across = axes.ahead, axes.behind, axes.across
    order = (pair_far, far, pair_back, pair_front, back, front, pair, mine)
    offsets, used = {}, 0
    for name, size in (
        ("Y0", half), ("M0", quarter), ("P0", quarter), ("M1", half), ("Y1", half), ("Y2", half),
        ("P1", half), ("M2", half), ("P2", half), ("M3", rows), ("P3", rows), ("Y3", rows),
    ):
        offsets[name] = (used, size, len(offsets))
        used += size

    def landing(name):
        low, size, _ = offsets[name]
        return stage.at[pl.ds(low, size)]

    def send(name, which, low, device):
        _, size, index = offsets[name]
        line.send(index, part(which, low, size), landing(name), device)

    def add(name, which, low, device):
        _, size, index = offsets[name]
        line.take(index, landing(name), device)
        add_rows(part(which, low, size), landing(name), size)

    def join(*places):
        if twin is not None:
            for place in places:
                line.take(12 + place, twin[2](order[place]), twin[0])
                add_rows(part(order[place], 0, rows), twin[2](order[place]), rows)

    if twin is not None:
        for place, which in enumerate(order):
            line.send(12 + place, twin[1](which), twin[2](which), twin[0])
        yield
    join(0)
    send("Y0", pair_far, half, across)
    send("M0", pair_far, 0, behind)
    send("P0", pair_far, quarter, ahead)
    join(1)
    send("M1", far, 0, behind)
    join(2)
    send("Y1", pair_back, half, across)
    join(3)
    send("Y2", pair_front, half, across)
    yield
    add("M0", pair_back, 0, behind)
    send("M2", pair_back, 0, behind)
    add("P0", pair_front, quarter, ahead)
    send("P2", pair_front, 0, ahead)
    add("Y0", far, half, across)
    send("P1", far, half, ahead)
    join(4, 5, 6, 7)
    yield
    add("M1", back, 0, behind)
    add("Y1", back, half, across)
    send("M3", back, 0, behind)
    add("M2", pair, 0, behind)
    add("P2", pair, 0, ahead)
    send("Y3", pair, 0, across)
    add("P1", front, half, ahead)
    add("Y2", front, half, across)
    send("P3", front, 0, ahead)
    yield
    for name, device in (("M3", behind), ("P3", ahead), ("Y3", across)):
        line.take(offsets[name][2], landing(name), device)
    step = 16

    def body(index, carry):
        low = pl.multiple_of(index * step, step)
        total = part(mine, low, step)[...].astype(f32)
        for name in ("M3", "P3", "Y3"):
            total = total + stage[pl.ds(offsets[name][0] + low, step)].astype(f32)
        result[pl.ds(low, step)] = total.astype(result.dtype)
        return carry

    lax.fori_loop(0, rows // step, body, 0)
    line.finish()


def sems(count):
    return [pltpu.SemaphoreType.DMA((count,)), pltpu.SemaphoreType.DMA((count,))]


ANY = pl.BlockSpec(memory_space=pl.ANY)
IN_VMEM = pl.BlockSpec(memory_space=pltpu.VMEM)


def tokens_gather(place, line, own_ref, all_ref, local_sem):
    rows = own_ref.shape[0]
    axes, core = place.tokens, place.core

    def block(which, low, count, other=False):
        side, spot = which
        index = (side * RING + spot) * 2 + ((1 - core) if other else core)
        return all_ref.at[index, pl.ds(low, count)]

    return gather_parts(axes, line, own_ref, block, rows, local_sem, place.twin)


def copies_gather(place, line, own_ref, all_ref, local_sem):
    rows = own_ref.shape[0]

    def block(which, low, count, other=False):
        side, spot = which
        return all_ref.at[side * RING + spot, pl.ds(low, count)]

    return gather_parts(place.copies, line, own_ref, block, rows, local_sem)


def params(collective_id):
    return pltpu.CompilerParams(
        collective_id=collective_id, has_side_effects=True, vmem_limit_bytes=VMEM_LIMIT
    )


def gather_call(collective_id, over_tokens=None, over_copies=None):
    operands = [v for v in (over_tokens, over_copies) if v is not None]

    def kernel(*refs):
        count = len(operands)
        owns, alls, scratch = refs[:count], refs[count : 2 * count], list(refs[2 * count :])
        place = Place()
        friends, steps, at = [], [], 0
        for kind, value in (("tokens", over_tokens), ("copies", over_copies)):
            if value is None:
                continue
            send_sem, recv_sem, local_sem = scratch[3 * at : 3 * at + 3]
            line = Line(send_sem, recv_sem)
            if kind == "tokens":
                friends += place.tokens.neighbours() + [place.twin]
                steps.append(tokens_gather(place, line, owns[at], alls[at], local_sem))
            else:
                friends += place.copies.neighbours()
                steps.append(copies_gather(place, line, owns[at], alls[at], local_sem))
            at += 1
        greet(friends)
        abreast(*steps)

    sizes = []
    if over_tokens is not None:
        sizes.append(GROUP)
    if over_copies is not None:
        sizes.append(REPS)
    scratch = []
    for _ in operands:
        scratch += sems(GATHER_SEMS) + [pltpu.SemaphoreType.DMA]
    return pl.pallas_call(
        kernel,
        out_shape=[
            jax.ShapeDtypeStruct((size,) + v.shape, v.dtype) for size, v in zip(sizes, operands)
        ],
        in_specs=[ANY] * len(operands),
        out_specs=[ANY] * len(operands),
        scratch_shapes=scratch,
        compiler_params=params(collective_id),
    )(*operands)


def sum_call(collective_id, over_tokens=None, over_copies=None, result=f32):
    operands = [v for v in (over_tokens, over_copies) if v is not None]

    def kernel(*refs):
        count = len(operands)
        terms, outs, scratch = refs[:count], refs[count : 2 * count], list(refs[2 * count :])
        place = Place()
        friends, steps, at = [], [], 0
        if over_tokens is not None:
            friends += place.tokens.neighbours() + [place.twin]
        if over_copies is not None:
            friends += place.copies.neighbours()
        loads = []
        for kind, value in (("tokens", over_tokens), ("copies", over_copies)):
            if value is None:
                continue
            rows = value.shape[1]
            if kind == "tokens":
                held, staged, stage, send_sem, recv_sem, load_sem = scratch[:6]
                del scratch[:6]
                line = Line(send_sem, recv_sem)
                source = terms[at]
                core = place.core

                def index_of(which, c):
                    return (which[0] * RING + which[1]) * 2 + c

                def held_part(which, low, n, held=held):
                    return held.at[which[0] * RING + which[1], pl.ds(low, n)]

                def outgoing(which, source=source, core=core):
                    return source.at[index_of(which, 1 - core)]

                def landed(which, staged=staged):
                    return staged.at[which[0] * RING + which[1]]

                for block in range(8):
                    load = pltpu.make_async_copy(
                        source.at[2 * block + core], held.at[block], load_sem.at[block]
                    )
                    load.start()
                    loads.append(load)
                steps.append(
                    sum_parts(
                        place.tokens, line, held_part, stage, rows, outs[at],
                        (place.twin, outgoing, landed),
                    )
                )
            else:
                held, stage, send_sem, recv_sem, load_sem = scratch[:5]
                del scratch[:5]
                line = Line(send_sem, recv_sem)
                load = pltpu.make_async_copy(terms[at], held, load_sem)
                load.start()
                loads.append(load)

                def copies_part(which, low, n, held=held):
                    return held.at[which[0] * RING + which[1], pl.ds(low, n)]

                steps.append(
                    sum_parts(place.copies, line, copies_part, stage, rows, outs[at])
                )
            at += 1
        greet(friends)
        for load in loads:
            load.wait()
        abreast(*steps)

    scratch = []
    if over_tokens is not None:
        _, rows, columns = over_tokens.shape
        scratch += [
            pltpu.VMEM((8, rows, columns), bf16),
            pltpu.VMEM((8, rows, columns), bf16),
            pltpu.VMEM((stage_rows(rows), columns), bf16),
        ]
        scratch += sems(SUM_SEMS) + [pltpu.SemaphoreType.DMA((8,))]
    if over_copies is not None:
        _, rows, columns = over_copies.shape
        scratch += [
            pltpu.VMEM((8, rows, columns), bf16),
            pltpu.VMEM((stage_rows(rows), columns), bf16),
        ]
        scratch += sems(SUM_SEMS) + [pltpu.SemaphoreType.DMA]
    return pl.pallas_call(
        kernel,
        out_shape=[jax.ShapeDtypeStruct(v.shape[1:], result) for v in operands],
        in_specs=[ANY] * len(operands),
        out_specs=[IN_VMEM] * len(operands),
        scratch_shapes=scratch,
        compiler_params=params(collective_id),
    )(*operands)


def sum_gather_call(collective_id, over_tokens, over_copies):
    _, rows, columns = over_tokens.shape

    def kernel(terms, own, total, every, held, staged, stage, s1, r1, load_sem, s2, r2, local_sem):
        place = Place()
        core = place.core
        loads = []
        for block in range(8):
            load = pltpu.make_async_copy(
                terms.at[2 * block + core], held.at[block], load_sem.at[block]
            )
            load.start()
            loads.append(load)
        greet(place.tokens.neighbours() + [place.twin] + place.copies.neighbours())
        for load in loads:
            load.wait()

        def held_part(which, low, n):
            return held.at[which[0] * RING + which[1], pl.ds(low, n)]

        def outgoing(which):
            return terms.at[(which[0] * RING + which[1]) * 2 + 1 - core]

        def landed(which):
            return staged.at[which[0] * RING + which[1]]

        abreast(
            sum_parts(
                place.tokens, Line(s1, r1), held_part, stage, rows, total,
                (place.twin, outgoing, landed),
            ),
            copies_gather(place, Line(s2, r2), own, every, local_sem),
        )

    return pl.pallas_call(
        kernel,
        out_shape=[
            jax.ShapeDtypeStruct((rows, columns), f32),
            jax.ShapeDtypeStruct((REPS,) + over_copies.shape, over_copies.dtype),
        ],
        in_specs=[ANY, ANY],
        out_specs=[IN_VMEM, ANY],
        scratch_shapes=[
            pltpu.VMEM((8, rows, columns), bf16),
            pltpu.VMEM((8, rows, columns), bf16),
            pltpu.VMEM((stage_rows(rows), columns), bf16),
        ]
        + sems(SUM_SEMS)
        + [pltpu.SemaphoreType.DMA((8,))]
        + sems(GATHER_SEMS)
        + [pltpu.SemaphoreType.DMA],
        compiler_params=params(collective_id),
    )(over_tokens, over_copies)


def copies_total_call(collective_id, terms):
    _, rows, columns = terms.shape

    def kernel(terms_ref, every, held, stage, own, s1, r1, load_sem, s2, r2, local_sem):
        place = Place()
        load = pltpu.make_async_copy(terms_ref, held, load_sem)
        load.start()
        greet(place.copies.neighbours())
        load.wait()

        def held_part(which, low, n):
            return held.at[which[0] * RING + which[1], pl.ds(low, n)]

        abreast(sum_parts(place.copies, Line(s1, r1), held_part, stage, rows, own))
        abreast(copies_gather(place, Line(s2, r2), own, every, local_sem))

    return pl.pallas_call(
        kernel,
        out_shape=jax.ShapeDtypeStruct(terms.shape, bf16),
        in_specs=[ANY],
        out_specs=ANY,
        scratch_shapes=[
            pltpu.VMEM((8, rows, columns), bf16),
            pltpu.VMEM((stage_rows(rows), columns), bf16),
            pltpu.VMEM((rows, columns), bf16),
        ]
        + sems(SUM_SEMS)
        + [pltpu.SemaphoreType.DMA]
        + sems(GATHER_SEMS)
        + [pltpu.SemaphoreType.DMA],
        compiler_params=params(collective_id),
    )(terms)


def copies_total(own):
    rows, columns = own.shape
    wide = -(-columns // (128 * REPS)) * 128 * REPS
    cut = jnp.pad(own.astype(bf16), ((0, 0), (0, wide - columns)))
    cut = cut.reshape(rows, REPS, wide // REPS).transpose(1, 0, 2)
    total = copies_total_call(7, cut)
    return total.transpose(1, 0, 2).reshape(rows, wide)[:, :columns].astype(f32)


def rms_scale(values, gain):
    return values * lax.rsqrt(jnp.mean(values * values, axis=-1, keepdims=True) + norm_eps) * gain


def rotary_tables(positions, head_size):
    half_size = head_size // 2
    exponent = jnp.arange(half_size, dtype=f32) * (2.0 / head_size)
    frequency = rope_base ** (-exponent)
    angles = positions.astype(f32)[:, None] * frequency[None, :]
    cosine_table = jnp.concatenate([jnp.cos(angles), jnp.cos(angles)], axis=-1)
    sine_table = jnp.concatenate([jnp.sin(angles), jnp.sin(angles)], axis=-1)
    return (cosine_table, sine_table)


def rotate(values, cosine_table, sine_table):
    half_size = values.shape[-1] // 2
    turned = jnp.concatenate([-values[..., half_size:], values[..., :half_size]], axis=-1)
    return values * cosine_table[:, None, :] + turned * sine_table[:, None, :]


def piece_index(positions, starts):
    inside = (positions[:, None] >= starts[None, :]) & (positions[:, None] < starts[None, :] + PIC)
    labels = jnp.arange(1, starts.shape[0] + 1, dtype=jnp.int32)
    return jnp.sum(jnp.where(inside, labels[None, :], 0), axis=1) - 1


def allowed_mask(query_pos, key_pos, starts):
    query_piece = piece_index(query_pos, starts)
    key_piece = piece_index(key_pos, starts)
    causal = key_pos[None, :] <= query_pos[:, None]
    shared = (query_piece[:, None] == key_piece[None, :]) & (query_piece[:, None] >= 0)
    return causal | shared


def query_key(query_raw, key_raw, query_gain, key_gain, cosine_table, sine_table):
    row_count = query_raw.shape[0]
    query_rot = rotate(
        rms_scale(query_raw, query_gain).reshape(row_count, HEADS, HEAD_DIM),
        cosine_table,
        sine_table,
    )
    key_rot = rotate(
        rms_scale(key_raw, key_gain).reshape(row_count, KV_HEADS, HEAD_DIM),
        cosine_table,
        sine_table,
    )
    return (query_rot, key_rot)


def dot(a, b):
    return jnp.dot(a, b, preferred_element_type=f32)


def dot_nt(a, b):
    return lax.dot_general(a, b, (((1,), (1,)), ((), ())), preferred_element_type=f32)


def dot_tn(a, b):
    return lax.dot_general(a, b, (((0,), (0,)), ((), ())), preferred_element_type=f32)


SMALL = 128


def pack_rows(wide, router, gain_a, gain_q, gain_f, gain_k):
    rows = router.shape[0]
    short = jnp.concatenate([gain_k, jnp.zeros((rows - gain_k.shape[0],), gain_k.dtype)])
    small = jnp.concatenate(
        [router] + [v[:, None] for v in (gain_a, gain_q, gain_f, short)], axis=1
    )
    small = jnp.pad(small, ((0, 0), (0, SMALL - small.shape[1])))
    return jnp.concatenate(list(wide) + [small], axis=1)


def shards(
    tokens,
    cotangent,
    routes,
    picture_starts,
    attn_gain,
    query_weight,
    key_weight,
    value_weight,
    query_gain,
    key_gain,
    output_weight,
    ffn_gain,
    router_weight,
    expert_in,
    expert_down,
):
    seqs, positions, width = tokens.shape
    top = routes.shape[2]
    count = seqs * positions
    length = positions * REPS
    experts = GROUP
    hidden_width = expert_down.shape[1]
    group = HEADS // KV_HEADS
    query_width = HEADS * HEAD_DIM
    kv_width = KV_HEADS * HEAD_DIM
    score_scale = HEAD_DIM ** (-0.5)
    rows_own = query_weight.shape[0]
    kgain_own = key_gain.shape[0]
    shard = lax.axis_index("shard")
    query_pos = lax.axis_index("rep") * positions + jnp.arange(positions, dtype=jnp.int32)
    key_pos = jnp.arange(length, dtype=jnp.int32)
    cosine_one, sine_one = rotary_tables(query_pos, HEAD_DIM)
    cosine_table = jnp.tile(cosine_one, (seqs, 1))
    sine_table = jnp.tile(sine_one, (seqs, 1))

    packed = pack_rows(
        (query_weight, key_weight, value_weight, output_weight),
        router_weight,
        attn_gain,
        query_gain,
        ffn_gain,
        key_gain,
    )
    (dense,) = gather_call(1, packed)
    columns = packed.shape[1]
    dense = dense.reshape(GROUP * rows_own, columns)
    at_o = query_width + 2 * kv_width
    at_s = at_o + width
    weight_q = dense[:, :query_width]
    weight_k = dense[:, query_width : query_width + kv_width]
    weight_v = dense[:, query_width + kv_width : at_o]
    weight_o = dense[:, at_o:at_s]
    weight_r = dense[:, at_s : at_s + experts]
    gain_a = dense[:, at_s + experts].astype(f32)
    gain_q = dense[:, at_s + experts + 1].astype(f32)
    gain_f = dense[:, at_s + experts + 2].astype(f32)
    gain_k = (
        dense[:, at_s + experts + 3].reshape(GROUP, rows_own)[:, :kgain_own].reshape(-1).astype(f32)
    )

    inputs = tokens.reshape(count, width).astype(f32)
    grad_low = cotangent.reshape(count, width)
    grad_out = grad_low.astype(f32)
    attn_in = rms_scale(inputs, gain_a).astype(bf16)
    query_raw = dot(attn_in, weight_q)
    key_raw = dot(attn_in, weight_k)
    value_low = dot(attn_in, weight_v).astype(bf16)
    query_rot, key_rot = query_key(query_raw, key_raw, gain_q, gain_k, cosine_table, sine_table)
    query_low = query_rot.astype(bf16).reshape(seqs, positions, KV_HEADS, group, HEAD_DIM)
    key_low = key_rot.astype(bf16).reshape(count, kv_width)
    grad_all, pairs_all = gather_call(
        2, grad_low, jnp.concatenate([key_low, value_low], axis=1)
    )
    pairs_all = (
        pairs_all.reshape(REPS, seqs, positions, 2 * kv_width)
        .transpose(1, 0, 2, 3)
        .reshape(seqs, length, 2 * kv_width)
    )
    keys_all = pairs_all[..., :kv_width].reshape(seqs, length, KV_HEADS, HEAD_DIM)
    values_all = pairs_all[..., kv_width:].reshape(seqs, length, KV_HEADS, HEAD_DIM)
    allowed = jax.vmap(lambda starts: allowed_mask(query_pos, key_pos, starts))(picture_starts)

    def scores_of():
        scores = (
            jnp.einsum("bqkgd,bskd->bkgqs", query_low, keys_all, preferred_element_type=f32)
            * score_scale
        )
        return jnp.where(allowed[:, None, None], scores, masked_score)

    scores = scores_of()
    row_top = jnp.max(scores, axis=-1, keepdims=True)
    exponent = jnp.exp(scores - row_top)
    row_total = jnp.sum(exponent, axis=-1, keepdims=True)
    soft_low = (exponent / row_total).astype(bf16)
    log_total = row_top + jnp.log(row_total)
    mixed_low = (
        jnp.einsum("bkgqs,bskd->bqkgd", soft_low, values_all, preferred_element_type=f32)
        .reshape(count, query_width)
        .astype(bf16)
    )
    middle = inputs + dot(mixed_low, weight_o)
    ffn_in = rms_scale(middle, gain_f).astype(bf16)
    logits = dot(ffn_in, weight_r)
    route_ids = routes.reshape(count, top)
    picked = (
        jnp.sum((route_ids[:, :, None] == jnp.arange(experts)[None, None, :]).astype(f32), axis=1)
        > 0.5
    )
    shown = jnp.where(picked, logits, masked_score)
    raised = jnp.exp(shown - jnp.max(shown, axis=-1, keepdims=True))
    gates = raised / jnp.sum(raised, axis=-1, keepdims=True)
    gates_high = gates.astype(bf16)
    gates_rest = (gates - gates_high.astype(f32)).astype(bf16)
    sent = jnp.concatenate(
        [ffn_in, gates_high, gates_rest, jnp.zeros((count, SMALL - 2 * experts), bf16)], axis=1
    )
    (got,) = gather_call(3, sent)
    got = got.reshape(GROUP * count, width + SMALL)
    rows_in = got[:, :width]
    mine = (jnp.arange(SMALL) % experts == shard) & (jnp.arange(SMALL) < 2 * experts)
    gate = jnp.sum(
        jnp.where(mine[None, :], got[:, width:].astype(f32), 0.0), axis=1, keepdims=True
    )

    inner, outer = expert_in[0], expert_down[0]
    grad_rows_out = grad_all.reshape(GROUP * count, width)
    gate_up = dot(rows_in, inner)
    gate_part, up_part = gate_up[:, :hidden_width], gate_up[:, hidden_width:]
    sigmoid = jax.nn.sigmoid(gate_part)
    hidden = (gate_part * sigmoid * up_part).astype(bf16)
    expert_out = dot(hidden, outer).astype(bf16).astype(f32)
    out_terms = (gate * expert_out).astype(bf16)
    grad_expert = (gate * grad_rows_out.astype(f32)).astype(bf16)
    grad_gate_own = jnp.sum(expert_out * grad_rows_out.astype(f32), axis=1, keepdims=True)
    grad_hidden = dot_nt(grad_expert, outer)
    grad_gate_up = jnp.concatenate(
        [
            grad_hidden * up_part * sigmoid * (1.0 + gate_part * (1.0 - sigmoid)),
            grad_hidden * gate_part * sigmoid,
        ],
        axis=1,
    ).astype(bf16)
    grad_rows = dot_nt(grad_gate_up, inner).astype(bf16)
    inner_grad = dot_tn(rows_in, grad_gate_up).astype(bf16)
    outer_grad = dot_tn(hidden, grad_expert).astype(bf16)
    own_high = grad_gate_own.astype(bf16)
    own_rest = (grad_gate_own - own_high.astype(f32)).astype(bf16)
    lanes = jnp.arange(SMALL)[None, :]
    back_columns = jnp.where(lanes == shard, own_high, jnp.zeros((), bf16)) + jnp.where(
        lanes == shard + experts, own_rest, jnp.zeros((), bf16)
    )
    back = jnp.concatenate([grad_rows, back_columns], axis=1)
    expert_terms = jnp.concatenate([inner_grad, outer_grad], axis=0)
    returned, expert_own = sum_call(
        4,
        back.reshape(GROUP, count, width + SMALL),
        expert_terms.reshape(REPS, -1, width),
    )

    grad_gates = returned[:, width : width + experts] + returned[:, width + experts : width + 2 * experts]
    grad_chosen = gates * (grad_gates - jnp.sum(gates * grad_gates, axis=-1, keepdims=True))
    grad_logits = jnp.where(picked, grad_chosen, 0.0).astype(bf16)
    grad_router = dot_tn(ffn_in, grad_logits)
    grad_ffn_in = dot_nt(grad_logits, weight_r) + returned[:, :width]
    _, norm_pull = jax.vjp(rms_scale, middle, gain_f)
    grad_middle_part, grad_gain_f = norm_pull(grad_ffn_in)
    grad_middle = grad_out + grad_middle_part
    grad_attn = grad_middle.astype(bf16)
    grad_weight_o = dot_tn(mixed_low, grad_attn)
    grad_mixed = (
        dot_nt(grad_attn, weight_o).astype(bf16).reshape(seqs, positions, KV_HEADS, group, HEAD_DIM)
    )
    soft_full = jnp.exp(scores_of() - log_total)
    grad_soft = jnp.einsum("bqkgd,bskd->bkgqs", grad_mixed, values_all, preferred_element_type=f32)
    grad_values = jnp.einsum(
        "bkgqs,bqkgd->bskd", soft_full.astype(bf16), grad_mixed, preferred_element_type=f32
    )
    grad_scores = (
        soft_full * (grad_soft - jnp.sum(soft_full * grad_soft, axis=-1, keepdims=True))
    ).astype(bf16)
    grad_query_rot = (
        jnp.einsum("bkgqs,bskd->bqkgd", grad_scores, keys_all, preferred_element_type=f32)
        * score_scale
    )
    grad_keys = (
        jnp.einsum("bkgqs,bqkgd->bskd", grad_scores, query_low, preferred_element_type=f32)
        * score_scale
    )
    grad_pairs = (
        jnp.concatenate(
            [
                grad_keys.reshape(seqs, length, kv_width),
                grad_values.reshape(seqs, length, kv_width),
            ],
            axis=-1,
        )
        .astype(bf16)
        .reshape(seqs, REPS, positions, 2 * kv_width)
        .transpose(1, 0, 2, 3)
        .reshape(REPS, count, 2 * kv_width)
    )
    out_sum, pairs_own = sum_call(5, out_terms.reshape(GROUP, count, width), grad_pairs)
    block_out = (middle + out_sum).astype(bf16)

    grad_query_rot = grad_query_rot.astype(bf16).astype(f32).reshape(count, HEADS, HEAD_DIM)
    grad_key_rot = (
        pairs_own[:, :kv_width].astype(bf16).astype(f32).reshape(count, KV_HEADS, HEAD_DIM)
    )
    grad_value_low = pairs_own[:, kv_width:].astype(bf16)

    def turned_pair(query_in, key_in, query_scale, key_scale):
        return query_key(query_in, key_in, query_scale, key_scale, cosine_table, sine_table)

    _, pair_pull = jax.vjp(turned_pair, query_raw, key_raw, gain_q, gain_k)
    grad_query_raw, grad_key_raw, grad_gain_q, grad_gain_k = pair_pull(
        (grad_query_rot, grad_key_rot)
    )
    grad_query_low = grad_query_raw.astype(bf16)
    grad_key_low = grad_key_raw.astype(bf16)
    grad_weight_q = dot_tn(attn_in, grad_query_low)
    grad_weight_k = dot_tn(attn_in, grad_key_low)
    grad_weight_v = dot_tn(attn_in, grad_value_low)
    grad_attn_in = (
        dot_nt(grad_query_low, weight_q)
        + dot_nt(grad_key_low, weight_k)
        + dot_nt(grad_value_low, weight_v)
    )
    _, norm_pull = jax.vjp(rms_scale, inputs, gain_a)
    grad_inputs_part, grad_gain_a = norm_pull(grad_attn_in)
    tokens_grad = (grad_middle + grad_inputs_part).astype(bf16)

    gain_k_rows = jnp.pad(
        grad_gain_k.reshape(GROUP, kgain_own), ((0, 0), (0, rows_own - kgain_own))
    ).reshape(-1)
    dense_terms = pack_rows(
        tuple(v.astype(bf16) for v in (grad_weight_q, grad_weight_k, grad_weight_v, grad_weight_o)),
        grad_router.astype(bf16),
        grad_gain_a.astype(bf16),
        grad_gain_q.astype(bf16),
        grad_gain_f.astype(bf16),
        gain_k_rows.astype(bf16),
    ).reshape(GROUP, rows_own, columns)
    dense_own, expert_all = sum_gather_call(6, dense_terms, expert_own.astype(bf16))
    expert_all = expert_all.reshape(-1, width)
    inner_rows = expert_in.shape[1]
    expert_in_grad = expert_all[:inner_rows].astype(f32)[None]
    expert_down_grad = expert_all[inner_rows:].astype(f32)[None]
    dense_sum = copies_total(dense_own)
    return (
        block_out.reshape(tokens.shape),
        tokens_grad.reshape(tokens.shape),
        dense_sum[:, at_s + experts],
        dense_sum[:, :query_width],
        dense_sum[:, query_width : query_width + kv_width],
        dense_sum[:, query_width + kv_width : at_o],
        dense_sum[:, at_s + experts + 1],
        dense_sum[:kgain_own, at_s + experts + 3],
        dense_sum[:, at_o:at_s],
        dense_sum[:, at_s + experts + 2],
        dense_sum[:, at_s : at_s + experts],
        expert_in_grad,
        expert_down_grad,
    )


def solution(mesh):
    by_tokens = P("shard", "rep", None)
    rows, line, block = P("shard", None), P("shard"), P("shard", None, None)
    in_specs = (
        by_tokens, by_tokens, by_tokens, rows, line, rows, rows, rows, line, line, rows, line, rows, block, block,
    )
    out_specs = (
        by_tokens, by_tokens, line, rows, rows, rows, line, line, rows, line, rows, block, block,
    )
    return jax.shard_map(shards, mesh=mesh, in_specs=in_specs, out_specs=out_specs, check_vma=False)
```

```python
import functools

import jax
import jax.numpy as jnp
from jax import lax
from jax.experimental import pallas as pl
from jax.experimental.pallas import tpu as pltpu
from jax.sharding import PartitionSpec as P

HEADS = 16
KV_HEADS = 8
HEAD_DIM = 64
PIC = 256
RING = 4
GROUP = 16
REPS = 8
VMEM_LIMIT = 56 << 20

norm_eps = 1e-06
rope_base = 10000.0
masked_score = -1e30

bf16 = jnp.bfloat16
f32 = jnp.float32


class Place:
    def __init__(self):
        shard = lax.axis_index("shard")
        rep = lax.axis_index("rep")
        self.shard, self.rep = shard, rep
        core = lax.rem(shard, 2)
        ring_z = lax.rem(lax.div(shard, 2), RING)
        y_hi = lax.div(shard, 8)
        ring_x = lax.rem(rep, RING)
        y_lo = lax.div(rep, RING)
        self.core = core

        def shard_of(hi, z, c):
            return (hi * RING + z) * 2 + c

        def rep_of(lo, x):
            return lo * RING + x

        def up(v):
            return lax.rem(v + 1, RING)

        def down(v):
            return lax.rem(v + RING - 1, RING)

        self.twin = (shard_of(y_hi, ring_z, 1 - core), rep)
        self.tokens = Axes(
            y_hi,
            ring_z,
            (shard_of(y_hi, up(ring_z), core), rep),
            (shard_of(y_hi, down(ring_z), core), rep),
            (shard_of(1 - y_hi, ring_z, core), rep_of(1 - y_lo, ring_x)),
        )
        self.copies = Axes(
            y_lo,
            ring_x,
            (shard, rep_of(y_lo, up(ring_x))),
            (shard, rep_of(y_lo, down(ring_x))),
            (shard, rep_of(1 - y_lo, ring_x)),
        )


class Axes:
    def __init__(self, side, spot, ahead, behind, across):
        self.side, self.spot = side, spot
        self.ahead, self.behind, self.across = ahead, behind, across
        sides = (side, 1 - side)
        spots = [lax.rem(spot + step, RING) for step in range(RING)]
        self.places = [[(sides[flip], spots[step]) for step in range(RING)] for flip in range(2)]

    def at(self, flip, step):
        return self.places[flip][step % RING]

    def neighbours(self):
        return [self.ahead, self.behind, self.across]


def greet(devices):
    barrier = pltpu.get_barrier_semaphore()
    for device in devices:
        pl.semaphore_signal(barrier, inc=1, device_id=device, device_id_type=pl.DeviceIdType.MESH)
    pl.semaphore_wait(barrier, len(devices))


class Line:
    def __init__(self, send_sem, recv_sem):
        self.send_sem, self.recv_sem = send_sem, recv_sem
        self.sent = []

    def copy(self, index, source, target, device):
        return pltpu.make_async_remote_copy(
            src_ref=source(),
            dst_ref=target(),
            send_sem=self.send_sem.at[index],
            recv_sem=self.recv_sem.at[index],
            device_id=device,
            device_id_type=pl.DeviceIdType.MESH,
        )

    def send(self, index, source, target, device):
        self.copy(index, source, target, device).start()
        self.sent.append((index, source, target, device))

    def take(self, index, target, device):
        self.copy(index, target, target, device).wait_recv()

    def finish(self):
        for sent in self.sent:
            self.copy(*sent).wait_send()


def abreast(*parts):
    running = list(parts)
    while running:
        for part in list(running):
            try:
                next(part)
            except StopIteration:
                running.remove(part)


GATHER_SEMS = 20


def gather_parts(axes, line, own, block, rows, local_sem, twin=None, twin_later=False):
    half, quarter = rows // 2, rows // 4
    mine, back, front, far = axes.at(0, 0), axes.at(0, -1), axes.at(0, 1), axes.at(0, 2)
    pair, pair_back, pair_front, pair_far = (axes.at(1, n) for n in (0, -1, 1, 2))
    ahead, behind, across = axes.ahead, axes.behind, axes.across

    def rows_of(which, low=0, count=rows, other=False):
        return lambda: block(which, low, count, other)

    def first(index, device):
        line.send(index, lambda: own, rows_of(mine), device)

    def relay(index, device, which, low=0, count=rows):
        line.send(index, rows_of(which, low, count), rows_of(which, low, count), device)

    def share(index, which):
        if twin is not None:
            relay(12 + index, twin, which)

    def keep():
        return pltpu.make_async_copy(own, block(mine, 0, rows), local_sem)

    keep().start()
    if twin is not None:
        first(12, twin)
    first(0, ahead)
    first(1, behind)
    first(2, across)
    keep().wait()
    yield
    line.take(0, rows_of(back), ahead)
    relay(3, ahead, back, 0, half)
    relay(4, across, back, half, half)
    share(1, back)
    line.take(1, rows_of(front), behind)
    relay(5, behind, front, half, half)
    relay(6, across, front, half, half)
    share(2, front)
    line.take(2, rows_of(pair), across)
    relay(7, ahead, pair, 0, half)
    relay(8, behind, pair, 0, half)
    share(3, pair)
    yield
    line.take(3, rows_of(far, 0, half), ahead)
    line.take(5, rows_of(far, half, half), behind)
    relay(9, across, far, half, half)
    share(4, far)
    line.take(7, rows_of(pair_back, 0, half), ahead)
    relay(10, ahead, pair_back, 0, quarter)
    line.take(8, rows_of(pair_front, 0, half), behind)
    relay(11, behind, pair_front, quarter, quarter)
    line.take(4, rows_of(pair_back, half, half), across)
    share(5, pair_back)
    line.take(6, rows_of(pair_front, half, half), across)
    share(6, pair_front)
    yield
    line.take(10, rows_of(pair_far, 0, quarter), ahead)
    line.take(11, rows_of(pair_far, quarter, quarter), behind)
    line.take(9, rows_of(pair_far, half, half), across)
    share(7, pair_far)
    yield
    if twin is not None and not twin_later:
        for index, which in enumerate(gather_order(axes)):
            line.take(12 + index, rows_of(which, other=True), twin)
    line.finish()


SUM_SEMS = 20


def add_rows(target, source, rows):
    step = 16
    count = rows // step

    def body(index, carry):
        at = pl.ds(pl.multiple_of(index * step, step), step)
        target[at] = target[at] + source[at]
        return carry

    lax.fori_loop(0, count, body, 0)


def stage_rows(rows):
    return 7 * rows


def gather_order(axes):
    return [axes.at(*v) for v in ((0, 0), (0, -1), (0, 1), (1, 0), (0, 2), (1, -1), (1, 1), (1, 2))]


def sum_order(axes):
    return [axes.at(*v) for v in ((1, 2), (0, 2), (1, -1), (1, 1), (0, -1), (0, 1), (1, 0), (0, 0))]


def sum_parts(axes, line, part, stage, rows, result, twin=None):
    half, quarter = rows // 2, rows // 4
    mine, back, front, far = axes.at(0, 0), axes.at(0, -1), axes.at(0, 1), axes.at(0, 2)
    pair, pair_back, pair_front, pair_far = (axes.at(1, n) for n in (0, -1, 1, 2))
    ahead, behind, across = axes.ahead, axes.behind, axes.across
    order = sum_order(axes)
    offsets, used = {}, 0
    for name, size in (
        ("Y0", half), ("M0", quarter), ("P0", quarter), ("M1", half), ("Y1", half), ("Y2", half),
        ("P1", half), ("M2", half), ("P2", half), ("M3", rows), ("P3", rows), ("Y3", rows),
    ):
        offsets[name] = (used, size, len(offsets))
        used += size

    def landing(name):
        low, size, _ = offsets[name]
        return lambda: stage.at[pl.ds(low, size)]

    def send(name, which, low, device):
        _, size, index = offsets[name]
        line.send(index, lambda: part(which, low, size), landing(name), device)

    def add(name, which, low, device):
        _, size, index = offsets[name]
        line.take(index, landing(name), device)
        add_rows(part(which, low, size), landing(name)(), size)

    def join(*places):
        if twin is not None:
            for place in places:
                line.take(12 + place, lambda: twin[2](order[place]), twin[0])
                add_rows(part(order[place], 0, rows), twin[2](order[place]), rows)

    def hand(*places):
        if twin is not None:
            for place in places:
                which = order[place]
                line.send(
                    12 + place, lambda w=which: twin[1](w), lambda w=which: twin[2](w), twin[0]
                )

    hand(0, 1, 2, 3)
    yield
    join(0)
    send("Y0", pair_far, half, across)
    send("M0", pair_far, 0, behind)
    send("P0", pair_far, quarter, ahead)
    join(1)
    send("M1", far, 0, behind)
    join(2)
    send("Y1", pair_back, half, across)
    join(3)
    send("Y2", pair_front, half, across)
    yield
    hand(4, 5, 6, 7)
    add("M0", pair_back, 0, behind)
    send("M2", pair_back, 0, behind)
    add("P0", pair_front, quarter, ahead)
    send("P2", pair_front, 0, ahead)
    add("Y0", far, half, across)
    send("P1", far, half, ahead)
    yield
    join(4, 5, 6, 7)
    add("M1", back, 0, behind)
    add("Y1", back, half, across)
    send("M3", back, 0, behind)
    add("M2", pair, 0, behind)
    add("P2", pair, 0, ahead)
    send("Y3", pair, 0, across)
    add("P1", front, half, ahead)
    add("Y2", front, half, across)
    send("P3", front, 0, ahead)
    yield
    for name, device in (("M3", behind), ("P3", ahead), ("Y3", across)):
        line.take(offsets[name][2], landing(name), device)
    step = 16

    def body(index, carry):
        low = pl.multiple_of(index * step, step)
        total = part(mine, low, step)[...].astype(f32)
        for name in ("M3", "P3", "Y3"):
            total = total + stage[pl.ds(offsets[name][0] + low, step)].astype(f32)
        result[pl.ds(low, step)] = total.astype(result.dtype)
        return carry

    lax.fori_loop(0, rows // step, body, 0)
    line.finish()


def sems(count):
    return [pltpu.SemaphoreType.DMA((count,)), pltpu.SemaphoreType.DMA((count,))]


ANY = pl.BlockSpec(memory_space=pl.ANY)
IN_VMEM = pl.BlockSpec(memory_space=pltpu.VMEM)


def tokens_gather(place, line, own_ref, all_ref, local_sem):
    rows = own_ref.shape[0]
    axes, core = place.tokens, place.core

    def block(which, low, count, other=False):
        side, spot = which
        index = (side * RING + spot) * 2 + ((1 - core) if other else core)
        return all_ref.at[index, pl.ds(low, count)]

    return gather_parts(axes, line, own_ref, block, rows, local_sem, place.twin)


def copies_gather(place, line, own_ref, all_ref, local_sem):
    rows = own_ref.shape[0]

    def block(which, low, count, other=False):
        side, spot = which
        return all_ref.at[side * RING + spot, pl.ds(low, count)]

    return gather_parts(place.copies, line, own_ref, block, rows, local_sem)


def params(collective_id):
    return pltpu.CompilerParams(
        collective_id=collective_id, has_side_effects=True, vmem_limit_bytes=VMEM_LIMIT
    )


def gather_call(collective_id, over_tokens=None, over_copies=None):
    operands = [v for v in (over_tokens, over_copies) if v is not None]

    def kernel(*refs):
        count = len(operands)
        owns, alls, scratch = refs[:count], refs[count : 2 * count], list(refs[2 * count :])
        place = Place()
        friends, steps, at = [], [], 0
        for kind, value in (("tokens", over_tokens), ("copies", over_copies)):
            if value is None:
                continue
            send_sem, recv_sem, local_sem = scratch[3 * at : 3 * at + 3]
            line = Line(send_sem, recv_sem)
            if kind == "tokens":
                friends += place.tokens.neighbours() + [place.twin]
                steps.append(tokens_gather(place, line, owns[at], alls[at], local_sem))
            else:
                friends += place.copies.neighbours()
                steps.append(copies_gather(place, line, owns[at], alls[at], local_sem))
            at += 1
        greet(friends)
        abreast(*steps)

    sizes = []
    if over_tokens is not None:
        sizes.append(GROUP)
    if over_copies is not None:
        sizes.append(REPS)
    scratch = []
    for _ in operands:
        scratch += sems(GATHER_SEMS) + [pltpu.SemaphoreType.DMA]
    return pl.pallas_call(
        kernel,
        out_shape=[
            jax.ShapeDtypeStruct((size,) + v.shape, v.dtype) for size, v in zip(sizes, operands)
        ],
        in_specs=[ANY] * len(operands),
        out_specs=[ANY] * len(operands),
        scratch_shapes=scratch,
        compiler_params=params(collective_id),
    )(*operands)


def sum_call(collective_id, over_tokens=None, over_copies=None, result=f32):
    operands = [v for v in (over_tokens, over_copies) if v is not None]

    def kernel(*refs):
        count = len(operands)
        terms, outs, scratch = refs[:count], refs[count : 2 * count], list(refs[2 * count :])
        place = Place()
        friends, steps, at = [], [], 0
        if over_tokens is not None:
            friends += place.tokens.neighbours() + [place.twin]
        if over_copies is not None:
            friends += place.copies.neighbours()
        loads = []
        for kind, value in (("tokens", over_tokens), ("copies", over_copies)):
            if value is None:
                continue
            rows = value.shape[1]
            if kind == "tokens":
                held, staged, stage, send_sem, recv_sem, load_sem = scratch[:6]
                del scratch[:6]
                line = Line(send_sem, recv_sem)
                source = terms[at]
                core = place.core

                def index_of(which, c):
                    return (which[0] * RING + which[1]) * 2 + c

                def held_part(which, low, n, held=held):
                    return held.at[which[0] * RING + which[1], pl.ds(low, n)]

                def outgoing(which, source=source, core=core):
                    return source.at[index_of(which, 1 - core)]

                def landed(which, staged=staged):
                    return staged.at[which[0] * RING + which[1]]

                for block in range(8):
                    load = pltpu.make_async_copy(
                        source.at[2 * block + core], held.at[block], load_sem.at[block]
                    )
                    load.start()
                    loads.append(load)
                steps.append(
                    sum_parts(
                        place.tokens, line, held_part, stage, rows, outs[at],
                        (place.twin, outgoing, landed),
                    )
                )
            else:
                held, stage, send_sem, recv_sem, load_sem = scratch[:5]
                del scratch[:5]
                line = Line(send_sem, recv_sem)
                load = pltpu.make_async_copy(terms[at], held, load_sem)
                load.start()
                loads.append(load)

                def copies_part(which, low, n, held=held):
                    return held.at[which[0] * RING + which[1], pl.ds(low, n)]

                steps.append(
                    sum_parts(place.copies, line, copies_part, stage, rows, outs[at])
                )
            at += 1
        greet(friends)
        for load in loads:
            load.wait()
        abreast(*steps)

    scratch = []
    if over_tokens is not None:
        _, rows, columns = over_tokens.shape
        scratch += [
            pltpu.VMEM((8, rows, columns), bf16),
            pltpu.VMEM((8, rows, columns), bf16),
            pltpu.VMEM((stage_rows(rows), columns), bf16),
        ]
        scratch += sems(SUM_SEMS) + [pltpu.SemaphoreType.DMA((8,))]
    if over_copies is not None:
        _, rows, columns = over_copies.shape
        scratch += [
            pltpu.VMEM((8, rows, columns), bf16),
            pltpu.VMEM((stage_rows(rows), columns), bf16),
        ]
        scratch += sems(SUM_SEMS) + [pltpu.SemaphoreType.DMA]
    return pl.pallas_call(
        kernel,
        out_shape=[jax.ShapeDtypeStruct(v.shape[1:], result) for v in operands],
        in_specs=[ANY] * len(operands),
        out_specs=[IN_VMEM] * len(operands),
        scratch_shapes=scratch,
        compiler_params=params(collective_id),
    )(*operands)


def sum_gather_call(collective_id, over_tokens, over_copies):
    _, rows, columns = over_tokens.shape

    def kernel(terms, own, total, every, held, staged, stage, s1, r1, load_sem, s2, r2, local_sem):
        place = Place()
        core = place.core
        loads = []
        for block in range(8):
            load = pltpu.make_async_copy(
                terms.at[2 * block + core], held.at[block], load_sem.at[block]
            )
            load.start()
            loads.append(load)
        greet(place.tokens.neighbours() + [place.twin] + place.copies.neighbours())
        for load in loads:
            load.wait()

        def held_part(which, low, n):
            return held.at[which[0] * RING + which[1], pl.ds(low, n)]

        def outgoing(which):
            return terms.at[(which[0] * RING + which[1]) * 2 + 1 - core]

        def landed(which):
            return staged.at[which[0] * RING + which[1]]

        abreast(
            sum_parts(
                place.tokens, Line(s1, r1), held_part, stage, rows, total,
                (place.twin, outgoing, landed),
            ),
            copies_gather(place, Line(s2, r2), own, every, local_sem),
        )

    return pl.pallas_call(
        kernel,
        out_shape=[
            jax.ShapeDtypeStruct((rows, columns), f32),
            jax.ShapeDtypeStruct((REPS,) + over_copies.shape, over_copies.dtype),
        ],
        in_specs=[ANY, ANY],
        out_specs=[IN_VMEM, ANY],
        scratch_shapes=[
            pltpu.VMEM((8, rows, columns), bf16),
            pltpu.VMEM((8, rows, columns), bf16),
            pltpu.VMEM((stage_rows(rows), columns), bf16),
        ]
        + sems(SUM_SEMS)
        + [pltpu.SemaphoreType.DMA((8,))]
        + sems(GATHER_SEMS)
        + [pltpu.SemaphoreType.DMA],
        compiler_params=params(collective_id),
    )(over_tokens, over_copies)


def copies_total_call(collective_id, terms):
    _, rows, columns = terms.shape

    def kernel(terms_ref, every, held, stage, own, s1, r1, load_sem, s2, r2, local_sem):
        place = Place()
        load = pltpu.make_async_copy(terms_ref, held, load_sem)
        load.start()
        greet(place.copies.neighbours())
        load.wait()

        def held_part(which, low, n):
            return held.at[which[0] * RING + which[1], pl.ds(low, n)]

        abreast(sum_parts(place.copies, Line(s1, r1), held_part, stage, rows, own))
        abreast(copies_gather(place, Line(s2, r2), own, every, local_sem))

    return pl.pallas_call(
        kernel,
        out_shape=jax.ShapeDtypeStruct(terms.shape, bf16),
        in_specs=[ANY],
        out_specs=ANY,
        scratch_shapes=[
            pltpu.VMEM((8, rows, columns), bf16),
            pltpu.VMEM((stage_rows(rows), columns), bf16),
            pltpu.VMEM((rows, columns), bf16),
        ]
        + sems(SUM_SEMS)
        + [pltpu.SemaphoreType.DMA]
        + sems(GATHER_SEMS)
        + [pltpu.SemaphoreType.DMA],
        compiler_params=params(collective_id),
    )(terms)


def copies_total(own):
    rows, columns = own.shape
    wide = -(-columns // (128 * REPS)) * 128 * REPS
    cut = jnp.pad(own.astype(bf16), ((0, 0), (0, wide - columns)))
    cut = cut.reshape(rows, REPS, wide // REPS).transpose(1, 0, 2)
    total = copies_total_call(7, cut)
    return total.transpose(1, 0, 2).reshape(rows, wide)[:, :columns].astype(f32)


def dot(a, b):
    return jnp.dot(a, b, preferred_element_type=f32)


def dot_nt(a, b):
    return lax.dot_general(a, b, (((1,), (1,)), ((), ())), preferred_element_type=f32)


def dot_tn(a, b):
    return lax.dot_general(a, b, (((0,), (0,)), ((), ())), preferred_element_type=f32)


def pick(index, values):
    chosen = values[-1]
    for at in range(len(values) - 2, -1, -1):
        chosen = jnp.where(index == at, values[at], chosen)
    return chosen


def moe_call(collective_id, sent, grad_all, inner, outer):
    count, columns = sent.shape
    width = inner.shape[0]
    hidden_width = outer.shape[0]
    small = columns - width
    half = count // 2
    both = 2 * half
    chips = GROUP // 2

    def kernel(
        sent_ref, grad_ref, inner_ref, outer_ref,
        out_terms, returned, terms,
        rows_in, grads, hidden, back_gu, total, back, staged, stage, outbox,
        gs0, gr0, gs1, gr1, ss0, sr0, ss1, sr1, own_sem, grad_sem, out_sem,
    ):
        place = Place()
        axes, core, shard = place.tokens, place.core, place.shard
        gather_lines = (Line(gs0, gr0), Line(gs1, gr1))
        sum_lines = (Line(ss0, sr0), Line(ss1, sr1))

        def blocks(which, other=False):
            return (which[0] * RING + which[1]) * 2 + ((1 - core) if other else core)

        def gather_of(chunk):
            def block(which, low, n, other=False):
                return rows_in.at[chunk, blocks(which, other), pl.ds(low, n)]

            return gather_parts(
                axes, gather_lines[chunk], sent_ref.at[pl.ds(chunk * half, half)], block, half,
                own_sem.at[chunk], place.twin, twin_later=chunk == 0,
            )

        def sum_of(chunk):
            def part(which, low, n):
                return back.at[chunk, blocks(which), pl.ds(low, n)]

            def outgoing(which):
                return back.at[chunk, blocks(which, True)]

            def landed(which):
                return staged.at[chunk, which[0] * RING + which[1]]

            return sum_parts(
                axes, sum_lines[chunk], part, stage.at[chunk], half,
                returned.at[pl.ds(chunk * half, half)], (place.twin, outgoing, landed),
            )

        def grad_load(chunk):
            return pltpu.make_async_copy(
                grad_ref.at[:, pl.ds(chunk * half, half)], grads, grad_sem
            )

        def out_copy(chunk, chip, slot):
            return pltpu.make_async_copy(
                outbox.at[slot],
                out_terms.at[pl.ds(chip * 2, 2), pl.ds(chunk * half, half)],
                out_sem.at[slot],
            )

        lanes = lax.broadcasted_iota(jnp.int32, (both, small), 1)
        is_high, is_rest = lanes == shard, lanes == shard + GROUP

        def tile(chunk, chip, slot, wait_first):
            at = pl.ds(chip * 2, 2)
            row_block = rows_in[chunk, at].reshape(both, columns)
            rows = row_block[:, :width]
            gate = jnp.sum(
                jnp.where(is_high | is_rest, row_block[:, width:].astype(f32), 0.0),
                axis=1, keepdims=True,
            )
            gate_up = dot(rows, inner_ref[...])
            gate_part, up_part = gate_up[:, :hidden_width], gate_up[:, hidden_width:]
            sigmoid = 1.0 / (1.0 + jnp.exp(-gate_part))
            active = gate_part * sigmoid
            product = active * up_part
            hidden_low = product.astype(bf16)
            hidden[at] = hidden_low.reshape(2, half, hidden_width)
            out = (gate * dot(hidden_low, outer_ref[...])).astype(bf16)

            @pl.when(wait_first)
            def _():
                out_copy(chunk, chip, slot).wait()

            outbox[slot] = out.reshape(2, half, width)
            out_copy(chunk, chip, slot).start()
            grad = grads[at].reshape(both, width)
            grad_hidden = dot_nt(grad, outer_ref[...])
            grad_gate = jnp.sum(grad_hidden * product, axis=1, keepdims=True)
            grad_hidden = grad_hidden * gate
            grad_gate_up = jnp.concatenate(
                [
                    grad_hidden * up_part * sigmoid * (1.0 + gate_part * (1.0 - sigmoid)),
                    grad_hidden * active,
                ],
                axis=1,
            ).astype(bf16)
            back_gu[at] = grad_gate_up.reshape(2, half, 2 * hidden_width)
            grads[at] = (gate * grad.astype(f32)).astype(bf16).reshape(2, half, width)
            grad_rows = dot_nt(grad_gate_up, inner_ref[...]).astype(bf16)
            back[chunk, at, :, pl.ds(0, width)] = grad_rows.reshape(2, half, width)
            high = grad_gate.astype(bf16).astype(f32)
            tail = jnp.where(is_high, high, jnp.where(is_rest, grad_gate - high, 0.0))
            back[chunk, at, :, pl.ds(width, small)] = tail.astype(bf16).reshape(2, half, small)

        def weight_step(chunk, index):
            low = pl.multiple_of(index * 256, 256)
            terms_at = pl.ds(low, 256)
            rows = rows_in[chunk, :, :, pl.ds(low, 256)].reshape(GROUP * half, 256)
            return terms_at, dot_tn(rows, back_gu[...].reshape(GROUP * half, 2 * hidden_width))

        def down_step(index):
            low = pl.multiple_of(index * 256, 256)
            terms_at = pl.ds(width + low, 256)
            rows = hidden[:, :, pl.ds(low, 256)].reshape(GROUP * half, 256)
            return terms_at, dot_tn(rows, grads[...].reshape(GROUP * half, width))

        greet(axes.neighbours() + [place.twin])
        gather0, gather1, sum0, sum1 = gather_of(0), gather_of(1), sum_of(0), sum_of(1)
        next(gather0)
        grad_load(0).start()
        chips0 = [w[0] * RING + w[1] for w in gather_order(axes)]
        chips1 = [w[0] * RING + w[1] for w in sum_order(axes)]
        grad_load(0).wait()

        def first_tiles(t, carry):
            @pl.when(t == 1)
            def _():
                next(gather0)
                next(gather1)

            @pl.when(t == 4)
            def _():
                next(gather0)
                next(gather1)

            @pl.when(t == 7)
            def _():
                next(gather0)
                next(gather1)

            chip = pick(t, chips0)
            gather_lines[0].take(
                12 + t, lambda: rows_in.at[0, chip * 2 + 1 - core], place.twin
            )
            tile(0, chip, lax.rem(t, 2), t >= 2)
            return carry

        lax.fori_loop(0, chips, first_tiles, 0)
        for _ in gather0:
            pass
        next(sum0)

        def first_weights(index, carry):
            at, value = weight_step(0, index)
            total[at] = value
            return carry

        def first_downs(index, carry):
            at, value = down_step(index)
            total[at] = value
            return carry

        lax.fori_loop(0, width // 256, first_weights, 0)
        next(sum0)
        lax.fori_loop(0, hidden_width // 256, first_downs, 0)
        grad_load(1).start()
        for _ in gather1:
            pass
        grad_load(1).wait()

        def second_tiles(t, carry):
            @pl.when(t == 1)
            def _():
                next(sum0)

            @pl.when(t == 3)
            def _():
                next(sum0)

            @pl.when(t == 4)
            def _():
                next(sum1)

            @pl.when(t == 6)
            def _():
                for _ in sum0:
                    pass
                next(sum1)

            tile(1, pick(t, chips1), lax.rem(t, 2), t >= 0)
            return carry

        lax.fori_loop(0, chips, second_tiles, 0)
        next(sum1)

        def second_weights(index, carry):
            at, value = weight_step(1, index)
            terms[at] = (total[at] + value).astype(bf16)
            return carry

        def second_downs(index, carry):
            at, value = down_step(index)
            terms[at] = (total[at] + value).astype(bf16)
            return carry

        lax.fori_loop(0, width // 256, second_weights, 0)
        next(sum1)
        lax.fori_loop(0, hidden_width // 256, second_downs, 0)
        for _ in sum1:
            pass
        for slot in range(2):
            out_copy(1, 0, slot).wait()

    term_rows = width + hidden_width
    return pl.pallas_call(
        kernel,
        out_shape=[
            jax.ShapeDtypeStruct((GROUP, count, width), bf16),
            jax.ShapeDtypeStruct((count, columns), f32),
            jax.ShapeDtypeStruct((term_rows, width), bf16),
        ],
        in_specs=[ANY, ANY, IN_VMEM, IN_VMEM],
        out_specs=[ANY, IN_VMEM, IN_VMEM],
        scratch_shapes=[
            pltpu.VMEM((2, GROUP, half, columns), bf16),
            pltpu.VMEM((GROUP, half, width), bf16),
            pltpu.VMEM((GROUP, half, hidden_width), bf16),
            pltpu.VMEM((GROUP, half, 2 * hidden_width), bf16),
            pltpu.VMEM((term_rows, width), f32),
            pltpu.VMEM((2, GROUP, half, columns), bf16),
            pltpu.VMEM((2, chips, half, columns), bf16),
            pltpu.VMEM((2, stage_rows(half), columns), bf16),
            pltpu.VMEM((2, 2, half, width), bf16),
        ]
        + sems(GATHER_SEMS) * 2
        + sems(SUM_SEMS) * 2
        + [pltpu.SemaphoreType.DMA((2,)), pltpu.SemaphoreType.DMA, pltpu.SemaphoreType.DMA((2,))],
        compiler_params=params(collective_id),
    )(sent, grad_all, inner, outer)


def rms_scale(values, gain):
    return values * lax.rsqrt(jnp.mean(values * values, axis=-1, keepdims=True) + norm_eps) * gain


def rotary_tables(positions, head_size):
    half_size = head_size // 2
    exponent = jnp.arange(half_size, dtype=f32) * (2.0 / head_size)
    frequency = rope_base ** (-exponent)
    angles = positions.astype(f32)[:, None] * frequency[None, :]
    cosine_table = jnp.concatenate([jnp.cos(angles), jnp.cos(angles)], axis=-1)
    sine_table = jnp.concatenate([jnp.sin(angles), jnp.sin(angles)], axis=-1)
    return (cosine_table, sine_table)


def rotate(values, cosine_table, sine_table):
    half_size = values.shape[-1] // 2
    turned = jnp.concatenate([-values[..., half_size:], values[..., :half_size]], axis=-1)
    return values * cosine_table[:, None, :] + turned * sine_table[:, None, :]


def piece_index(positions, starts):
    inside = (positions[:, None] >= starts[None, :]) & (positions[:, None] < starts[None, :] + PIC)
    labels = jnp.arange(1, starts.shape[0] + 1, dtype=jnp.int32)
    return jnp.sum(jnp.where(inside, labels[None, :], 0), axis=1) - 1


def allowed_mask(query_pos, key_pos, starts):
    query_piece = piece_index(query_pos, starts)
    key_piece = piece_index(key_pos, starts)
    causal = key_pos[None, :] <= query_pos[:, None]
    shared = (query_piece[:, None] == key_piece[None, :]) & (query_piece[:, None] >= 0)
    return causal | shared


def query_key(query_raw, key_raw, query_gain, key_gain, cosine_table, sine_table):
    row_count = query_raw.shape[0]
    query_rot = rotate(
        rms_scale(query_raw, query_gain).reshape(row_count, HEADS, HEAD_DIM),
        cosine_table,
        sine_table,
    )
    key_rot = rotate(
        rms_scale(key_raw, key_gain).reshape(row_count, KV_HEADS, HEAD_DIM),
        cosine_table,
        sine_table,
    )
    return (query_rot, key_rot)


SMALL = 128


def pack_rows(wide, router, gain_a, gain_q, gain_f, gain_k):
    rows = router.shape[0]
    short = jnp.concatenate([gain_k, jnp.zeros((rows - gain_k.shape[0],), gain_k.dtype)])
    small = jnp.concatenate(
        [router] + [v[:, None] for v in (gain_a, gain_q, gain_f, short)], axis=1
    )
    small = jnp.pad(small, ((0, 0), (0, SMALL - small.shape[1])))
    return jnp.concatenate(list(wide) + [small], axis=1)


def shards(
    tokens,
    cotangent,
    routes,
    picture_starts,
    attn_gain,
    query_weight,
    key_weight,
    value_weight,
    query_gain,
    key_gain,
    output_weight,
    ffn_gain,
    router_weight,
    expert_in,
    expert_down,
):
    seqs, positions, width = tokens.shape
    top = routes.shape[2]
    count = seqs * positions
    length = positions * REPS
    experts = GROUP
    group = HEADS // KV_HEADS
    query_width = HEADS * HEAD_DIM
    kv_width = KV_HEADS * HEAD_DIM
    score_scale = HEAD_DIM ** (-0.5)
    rows_own = query_weight.shape[0]
    kgain_own = key_gain.shape[0]
    shard = lax.axis_index("shard")
    query_pos = lax.axis_index("rep") * positions + jnp.arange(positions, dtype=jnp.int32)
    key_pos = jnp.arange(length, dtype=jnp.int32)
    cosine_one, sine_one = rotary_tables(query_pos, HEAD_DIM)
    cosine_table = jnp.tile(cosine_one, (seqs, 1))
    sine_table = jnp.tile(sine_one, (seqs, 1))

    packed = pack_rows(
        (query_weight, key_weight, value_weight, output_weight),
        router_weight,
        attn_gain,
        query_gain,
        ffn_gain,
        key_gain,
    )
    (dense,) = gather_call(1, packed)
    columns = packed.shape[1]
    dense = dense.reshape(GROUP * rows_own, columns)
    at_o = query_width + 2 * kv_width
    at_s = at_o + width
    weight_q = dense[:, :query_width]
    weight_k = dense[:, query_width : query_width + kv_width]
    weight_v = dense[:, query_width + kv_width : at_o]
    weight_o = dense[:, at_o:at_s]
    weight_r = dense[:, at_s : at_s + experts]
    gain_a = dense[:, at_s + experts].astype(f32)
    gain_q = dense[:, at_s + experts + 1].astype(f32)
    gain_f = dense[:, at_s + experts + 2].astype(f32)
    gain_k = (
        dense[:, at_s + experts + 3].reshape(GROUP, rows_own)[:, :kgain_own].reshape(-1).astype(f32)
    )

    inputs = tokens.reshape(count, width).astype(f32)
    grad_low = cotangent.reshape(count, width)
    grad_out = grad_low.astype(f32)
    attn_in = rms_scale(inputs, gain_a).astype(bf16)
    query_raw = dot(attn_in, weight_q)
    key_raw = dot(attn_in, weight_k)
    value_low = dot(attn_in, weight_v).astype(bf16)
    query_rot, key_rot = query_key(query_raw, key_raw, gain_q, gain_k, cosine_table, sine_table)
    query_low = query_rot.astype(bf16).reshape(seqs, positions, KV_HEADS, group, HEAD_DIM)
    key_low = key_rot.astype(bf16).reshape(count, kv_width)
    grad_all, pairs_all = gather_call(
        2, grad_low, jnp.concatenate([key_low, value_low], axis=1)
    )
    pairs_all = (
        pairs_all.reshape(REPS, seqs, positions, 2 * kv_width)
        .transpose(1, 0, 2, 3)
        .reshape(seqs, length, 2 * kv_width)
    )
    keys_all = pairs_all[..., :kv_width].reshape(seqs, length, KV_HEADS, HEAD_DIM)
    values_all = pairs_all[..., kv_width:].reshape(seqs, length, KV_HEADS, HEAD_DIM)
    allowed = jax.vmap(lambda starts: allowed_mask(query_pos, key_pos, starts))(picture_starts)

    def scores_of():
        scores = (
            jnp.einsum("bqkgd,bskd->bkgqs", query_low, keys_all, preferred_element_type=f32)
            * score_scale
        )
        return jnp.where(allowed[:, None, None], scores, masked_score)

    scores = scores_of()
    row_top = jnp.max(scores, axis=-1, keepdims=True)
    exponent = jnp.exp(scores - row_top)
    row_total = jnp.sum(exponent, axis=-1, keepdims=True)
    soft_low = (exponent / row_total).astype(bf16)
    log_total = row_top + jnp.log(row_total)
    mixed_low = (
        jnp.einsum("bkgqs,bskd->bqkgd", soft_low, values_all, preferred_element_type=f32)
        .reshape(count, query_width)
        .astype(bf16)
    )
    middle = inputs + dot(mixed_low, weight_o)
    ffn_in = rms_scale(middle, gain_f).astype(bf16)
    logits = dot(ffn_in, weight_r)
    route_ids = routes.reshape(count, top)
    picked = (
        jnp.sum((route_ids[:, :, None] == jnp.arange(experts)[None, None, :]).astype(f32), axis=1)
        > 0.5
    )
    shown = jnp.where(picked, logits, masked_score)
    raised = jnp.exp(shown - jnp.max(shown, axis=-1, keepdims=True))
    gates = raised / jnp.sum(raised, axis=-1, keepdims=True)
    gates_high = gates.astype(bf16)
    gates_rest = (gates - gates_high.astype(f32)).astype(bf16)
    sent = jnp.concatenate(
        [ffn_in, gates_high, gates_rest, jnp.zeros((count, SMALL - 2 * experts), bf16)], axis=1
    )
    out_terms, returned, expert_terms = moe_call(
        3, sent, grad_all, expert_in[0], expert_down[0]
    )
    (expert_own,) = sum_call(4, None, expert_terms.reshape(REPS, -1, width))

    grad_gates = returned[:, width : width + experts] + returned[:, width + experts : width + 2 * experts]
    grad_chosen = gates * (grad_gates - jnp.sum(gates * grad_gates, axis=-1, keepdims=True))
    grad_logits = jnp.where(picked, grad_chosen, 0.0).astype(bf16)
    grad_router = dot_tn(ffn_in, grad_logits)
    grad_ffn_in = dot_nt(grad_logits, weight_r) + returned[:, :width]
    _, norm_pull = jax.vjp(rms_scale, middle, gain_f)
    grad_middle_part, grad_gain_f = norm_pull(grad_ffn_in)
    grad_middle = grad_out + grad_middle_part
    grad_attn = grad_middle.astype(bf16)
    grad_weight_o = dot_tn(mixed_low, grad_attn)
    grad_mixed = (
        dot_nt(grad_attn, weight_o).astype(bf16).reshape(seqs, positions, KV_HEADS, group, HEAD_DIM)
    )
    soft_full = jnp.exp(scores_of() - log_total)
    grad_soft = jnp.einsum("bqkgd,bskd->bkgqs", grad_mixed, values_all, preferred_element_type=f32)
    grad_values = jnp.einsum(
        "bkgqs,bqkgd->bskd", soft_full.astype(bf16), grad_mixed, preferred_element_type=f32
    )
    grad_scores = (
        soft_full * (grad_soft - jnp.sum(soft_full * grad_soft, axis=-1, keepdims=True))
    ).astype(bf16)
    grad_query_rot = (
        jnp.einsum("bkgqs,bskd->bqkgd", grad_scores, keys_all, preferred_element_type=f32)
        * score_scale
    )
    grad_keys = (
        jnp.einsum("bkgqs,bqkgd->bskd", grad_scores, query_low, preferred_element_type=f32)
        * score_scale
    )
    grad_pairs = (
        jnp.concatenate(
            [
                grad_keys.reshape(seqs, length, kv_width),
                grad_values.reshape(seqs, length, kv_width),
            ],
            axis=-1,
        )
        .astype(bf16)
        .reshape(seqs, REPS, positions, 2 * kv_width)
        .transpose(1, 0, 2, 3)
        .reshape(REPS, count, 2 * kv_width)
    )
    out_sum, pairs_own = sum_call(5, out_terms, grad_pairs)
    block_out = (middle + out_sum).astype(bf16)

    grad_query_rot = grad_query_rot.astype(bf16).astype(f32).reshape(count, HEADS, HEAD_DIM)
    grad_key_rot = (
        pairs_own[:, :kv_width].astype(bf16).astype(f32).reshape(count, KV_HEADS, HEAD_DIM)
    )
    grad_value_low = pairs_own[:, kv_width:].astype(bf16)

    def turned_pair(query_in, key_in, query_scale, key_scale):
        return query_key(query_in, key_in, query_scale, key_scale, cosine_table, sine_table)

    _, pair_pull = jax.vjp(turned_pair, query_raw, key_raw, gain_q, gain_k)
    grad_query_raw, grad_key_raw, grad_gain_q, grad_gain_k = pair_pull(
        (grad_query_rot, grad_key_rot)
    )
    grad_query_low = grad_query_raw.astype(bf16)
    grad_key_low = grad_key_raw.astype(bf16)
    grad_weight_q = dot_tn(attn_in, grad_query_low)
    grad_weight_k = dot_tn(attn_in, grad_key_low)
    grad_weight_v = dot_tn(attn_in, grad_value_low)
    grad_attn_in = (
        dot_nt(grad_query_low, weight_q)
        + dot_nt(grad_key_low, weight_k)
        + dot_nt(grad_value_low, weight_v)
    )
    _, norm_pull = jax.vjp(rms_scale, inputs, gain_a)
    grad_inputs_part, grad_gain_a = norm_pull(grad_attn_in)
    tokens_grad = (grad_middle + grad_inputs_part).astype(bf16)

    gain_k_rows = jnp.pad(
        grad_gain_k.reshape(GROUP, kgain_own), ((0, 0), (0, rows_own - kgain_own))
    ).reshape(-1)
    dense_terms = pack_rows(
        tuple(v.astype(bf16) for v in (grad_weight_q, grad_weight_k, grad_weight_v, grad_weight_o)),
        grad_router.astype(bf16),
        grad_gain_a.astype(bf16),
        grad_gain_q.astype(bf16),
        grad_gain_f.astype(bf16),
        gain_k_rows.astype(bf16),
    ).reshape(GROUP, rows_own, columns)
    dense_own, expert_all = sum_gather_call(6, dense_terms, expert_own.astype(bf16))
    expert_all = expert_all.reshape(-1, width)
    inner_rows = expert_in.shape[1]
    expert_in_grad = expert_all[:inner_rows].astype(f32)[None]
    expert_down_grad = expert_all[inner_rows:].astype(f32)[None]
    dense_sum = copies_total(dense_own)
    return (
        block_out.reshape(tokens.shape),
        tokens_grad.reshape(tokens.shape),
        dense_sum[:, at_s + experts],
        dense_sum[:, :query_width],
        dense_sum[:, query_width : query_width + kv_width],
        dense_sum[:, query_width + kv_width : at_o],
        dense_sum[:, at_s + experts + 1],
        dense_sum[:kgain_own, at_s + experts + 3],
        dense_sum[:, at_o:at_s],
        dense_sum[:, at_s + experts + 2],
        dense_sum[:, at_s : at_s + experts],
        expert_in_grad,
        expert_down_grad,
    )


def solution(mesh):
    by_tokens = P("shard", "rep", None)
    rows, line, block = P("shard", None), P("shard"), P("shard", None, None)
    in_specs = (
        by_tokens, by_tokens, by_tokens, rows, line, rows, rows, rows, line, line, rows, line, rows, block, block,
    )
    out_specs = (
        by_tokens, by_tokens, line, rows, rows, rows, line, line, rows, line, rows, block, block,
    )
    return jax.shard_map(shards, mesh=mesh, in_specs=in_specs, out_specs=out_specs, check_vma=False)
```

```python
import functools

import jax
import jax.numpy as jnp
from jax import lax
from jax.experimental import pallas as pl
from jax.experimental.pallas import tpu as pltpu
from jax.sharding import PartitionSpec as P

HEADS = 16
KV_HEADS = 8
HEAD_DIM = 64
PIC = 256
RING = 4
GROUP = 16
REPS = 8
VMEM_LIMIT = 56 << 20

norm_eps = 1e-06
rope_base = 10000.0
masked_score = -1e30

bf16 = jnp.bfloat16
f32 = jnp.float32


class Place:
    def __init__(self):
        shard = lax.axis_index("shard")
        rep = lax.axis_index("rep")
        self.shard, self.rep = shard, rep
        core = lax.rem(shard, 2)
        ring_z = lax.rem(lax.div(shard, 2), RING)
        y_hi = lax.div(shard, 8)
        ring_x = lax.rem(rep, RING)
        y_lo = lax.div(rep, RING)
        self.core = core

        def shard_of(hi, z, c):
            return (hi * RING + z) * 2 + c

        def rep_of(lo, x):
            return lo * RING + x

        def up(v):
            return lax.rem(v + 1, RING)

        def down(v):
            return lax.rem(v + RING - 1, RING)

        self.twin = (shard_of(y_hi, ring_z, 1 - core), rep)
        self.tokens = Axes(
            y_hi,
            ring_z,
            (shard_of(y_hi, up(ring_z), core), rep),
            (shard_of(y_hi, down(ring_z), core), rep),
            (shard_of(1 - y_hi, ring_z, core), rep_of(1 - y_lo, ring_x)),
        )
        self.copies = Axes(
            y_lo,
            ring_x,
            (shard, rep_of(y_lo, up(ring_x))),
            (shard, rep_of(y_lo, down(ring_x))),
            (shard, rep_of(1 - y_lo, ring_x)),
        )


class Axes:
    def __init__(self, side, spot, ahead, behind, across):
        self.side, self.spot = side, spot
        self.ahead, self.behind, self.across = ahead, behind, across
        sides = (side, 1 - side)
        spots = [lax.rem(spot + step, RING) for step in range(RING)]
        self.places = [[(sides[flip], spots[step]) for step in range(RING)] for flip in range(2)]

    def at(self, flip, step):
        return self.places[flip][step % RING]

    def neighbours(self):
        return [self.ahead, self.behind, self.across]


def greet(devices):
    barrier = pltpu.get_barrier_semaphore()
    for device in devices:
        pl.semaphore_signal(barrier, inc=1, device_id=device, device_id_type=pl.DeviceIdType.MESH)
    pl.semaphore_wait(barrier, len(devices))


class Line:
    def __init__(self, send_sem, recv_sem):
        self.send_sem, self.recv_sem = send_sem, recv_sem
        self.sent = []

    def copy(self, index, source, target, device):
        return pltpu.make_async_remote_copy(
            src_ref=source(),
            dst_ref=target(),
            send_sem=self.send_sem.at[index],
            recv_sem=self.recv_sem.at[index],
            device_id=device,
            device_id_type=pl.DeviceIdType.MESH,
        )

    def send(self, index, source, target, device):
        self.copy(index, source, target, device).start()
        self.sent.append((index, source, target, device))

    def take(self, index, target, device):
        self.copy(index, target, target, device).wait_recv()

    def finish(self):
        for sent in self.sent:
            self.copy(*sent).wait_send()


def abreast(*parts):
    running = list(parts)
    while running:
        for part in list(running):
            try:
                next(part)
            except StopIteration:
                running.remove(part)


GATHER_SEMS = 20


def gather_parts(axes, line, own, block, rows, local_sem, twin=None, twin_later=False):
    half, quarter = rows // 2, rows // 4
    mine, back, front, far = axes.at(0, 0), axes.at(0, -1), axes.at(0, 1), axes.at(0, 2)
    pair, pair_back, pair_front, pair_far = (axes.at(1, n) for n in (0, -1, 1, 2))
    ahead, behind, across = axes.ahead, axes.behind, axes.across

    def rows_of(which, low=0, count=rows, other=False):
        return lambda: block(which, low, count, other)

    def first(index, device):
        line.send(index, lambda: own, rows_of(mine), device)

    def relay(index, device, which, low=0, count=rows):
        line.send(index, rows_of(which, low, count), rows_of(which, low, count), device)

    def share(index, which):
        if twin is not None:
            relay(12 + index, twin, which)

    def keep():
        return pltpu.make_async_copy(own, block(mine, 0, rows), local_sem)

    keep().start()
    if twin is not None:
        first(12, twin)
    first(0, ahead)
    first(1, behind)
    first(2, across)
    keep().wait()
    yield
    line.take(0, rows_of(back), ahead)
    relay(3, ahead, back, 0, half)
    relay(4, across, back, half, half)
    share(1, back)
    line.take(1, rows_of(front), behind)
    relay(5, behind, front, half, half)
    relay(6, across, front, half, half)
    share(2, front)
    line.take(2, rows_of(pair), across)
    relay(7, ahead, pair, 0, half)
    relay(8, behind, pair, 0, half)
    share(3, pair)
    yield
    line.take(3, rows_of(far, 0, half), ahead)
    line.take(5, rows_of(far, half, half), behind)
    relay(9, across, far, half, half)
    share(4, far)
    line.take(7, rows_of(pair_back, 0, half), ahead)
    relay(10, ahead, pair_back, 0, quarter)
    line.take(8, rows_of(pair_front, 0, half), behind)
    relay(11, behind, pair_front, quarter, quarter)
    line.take(4, rows_of(pair_back, half, half), across)
    share(5, pair_back)
    line.take(6, rows_of(pair_front, half, half), across)
    share(6, pair_front)
    yield
    line.take(10, rows_of(pair_far, 0, quarter), ahead)
    line.take(11, rows_of(pair_far, quarter, quarter), behind)
    line.take(9, rows_of(pair_far, half, half), across)
    share(7, pair_far)
    yield
    if twin is not None and not twin_later:
        for index, which in enumerate(gather_order(axes)):
            line.take(12 + index, rows_of(which, other=True), twin)
    line.finish()


SUM_SEMS = 20


def add_rows(target, source, rows):
    step = 16
    count = rows // step

    def body(index, carry):
        at = pl.ds(pl.multiple_of(index * step, step), step)
        target[at] = target[at] + source[at]
        return carry

    lax.fori_loop(0, count, body, 0)


def stage_rows(rows):
    return 7 * rows


def gather_order(axes):
    return [axes.at(*v) for v in ((0, 0), (0, -1), (0, 1), (1, 0), (0, 2), (1, -1), (1, 1), (1, 2))]


def sum_order(axes):
    return [axes.at(*v) for v in ((1, 2), (0, 2), (1, -1), (1, 1), (0, -1), (0, 1), (1, 0), (0, 0))]


def sum_parts(axes, line, part, stage, rows, result, twin=None):
    half, quarter = rows // 2, rows // 4
    mine, back, front, far = axes.at(0, 0), axes.at(0, -1), axes.at(0, 1), axes.at(0, 2)
    pair, pair_back, pair_front, pair_far = (axes.at(1, n) for n in (0, -1, 1, 2))
    ahead, behind, across = axes.ahead, axes.behind, axes.across
    order = sum_order(axes)
    offsets, used = {}, 0
    for name, size in (
        ("Y0", half), ("M0", quarter), ("P0", quarter), ("M1", half), ("Y1", half), ("Y2", half),
        ("P1", half), ("M2", half), ("P2", half), ("M3", rows), ("P3", rows), ("Y3", rows),
    ):
        offsets[name] = (used, size, len(offsets))
        used += size

    def landing(name):
        low, size, _ = offsets[name]
        return lambda: stage.at[pl.ds(low, size)]

    def send(name, which, low, device):
        _, size, index = offsets[name]
        line.send(index, lambda: part(which, low, size), landing(name), device)

    def add(name, which, low, device):
        _, size, index = offsets[name]
        line.take(index, landing(name), device)
        add_rows(part(which, low, size), landing(name)(), size)

    def join(*places):
        if twin is not None:
            for place in places:
                line.take(12 + place, lambda: twin[2](order[place]), twin[0])
                add_rows(part(order[place], 0, rows), twin[2](order[place]), rows)

    def hand(*places):
        if twin is not None:
            for place in places:
                which = order[place]
                line.send(
                    12 + place, lambda w=which: twin[1](w), lambda w=which: twin[2](w), twin[0]
                )

    hand(0, 1, 2, 3)
    yield
    join(0)
    send("Y0", pair_far, half, across)
    send("M0", pair_far, 0, behind)
    send("P0", pair_far, quarter, ahead)
    join(1)
    send("M1", far, 0, behind)
    join(2)
    send("Y1", pair_back, half, across)
    join(3)
    send("Y2", pair_front, half, across)
    yield
    hand(4, 5, 6, 7)
    add("M0", pair_back, 0, behind)
    send("M2", pair_back, 0, behind)
    add("P0", pair_front, quarter, ahead)
    send("P2", pair_front, 0, ahead)
    add("Y0", far, half, across)
    send("P1", far, half, ahead)
    yield
    join(4, 5, 6, 7)
    add("M1", back, 0, behind)
    add("Y1", back, half, across)
    send("M3", back, 0, behind)
    add("M2", pair, 0, behind)
    add("P2", pair, 0, ahead)
    send("Y3", pair, 0, across)
    add("P1", front, half, ahead)
    add("Y2", front, half, across)
    send("P3", front, 0, ahead)
    yield
    for name, device in (("M3", behind), ("P3", ahead), ("Y3", across)):
        line.take(offsets[name][2], landing(name), device)
    step = 16

    def body(index, carry):
        low = pl.multiple_of(index * step, step)
        total = part(mine, low, step)[...].astype(f32)
        for name in ("M3", "P3", "Y3"):
            total = total + stage[pl.ds(offsets[name][0] + low, step)].astype(f32)
        result[pl.ds(low, step)] = total.astype(result.dtype)
        return carry

    lax.fori_loop(0, rows // step, body, 0)
    line.finish()


def sems(count):
    return [pltpu.SemaphoreType.DMA((count,)), pltpu.SemaphoreType.DMA((count,))]


ANY = pl.BlockSpec(memory_space=pl.ANY)
IN_VMEM = pl.BlockSpec(memory_space=pltpu.VMEM)


def tokens_gather(place, line, own_ref, all_ref, local_sem):
    rows = own_ref.shape[0]
    axes, core = place.tokens, place.core

    def block(which, low, count, other=False):
        side, spot = which
        index = (side * RING + spot) * 2 + ((1 - core) if other else core)
        return all_ref.at[index, pl.ds(low, count)]

    return gather_parts(axes, line, own_ref, block, rows, local_sem, place.twin)


def copies_gather(place, line, own_ref, all_ref, local_sem):
    rows = own_ref.shape[0]

    def block(which, low, count, other=False):
        side, spot = which
        return all_ref.at[side * RING + spot, pl.ds(low, count)]

    return gather_parts(place.copies, line, own_ref, block, rows, local_sem)


def params(collective_id):
    return pltpu.CompilerParams(
        collective_id=collective_id, has_side_effects=True, vmem_limit_bytes=VMEM_LIMIT
    )


def gather_call(collective_id, over_tokens=None, over_copies=None):
    operands = [v for v in (over_tokens, over_copies) if v is not None]

    def kernel(*refs):
        count = len(operands)
        owns, alls, scratch = refs[:count], refs[count : 2 * count], list(refs[2 * count :])
        place = Place()
        friends, steps, at = [], [], 0
        for kind, value in (("tokens", over_tokens), ("copies", over_copies)):
            if value is None:
                continue
            send_sem, recv_sem, local_sem = scratch[3 * at : 3 * at + 3]
            line = Line(send_sem, recv_sem)
            if kind == "tokens":
                friends += place.tokens.neighbours() + [place.twin]
                steps.append(tokens_gather(place, line, owns[at], alls[at], local_sem))
            else:
                friends += place.copies.neighbours()
                steps.append(copies_gather(place, line, owns[at], alls[at], local_sem))
            at += 1
        greet(friends)
        abreast(*steps)

    sizes = []
    if over_tokens is not None:
        sizes.append(GROUP)
    if over_copies is not None:
        sizes.append(REPS)
    scratch = []
    for _ in operands:
        scratch += sems(GATHER_SEMS) + [pltpu.SemaphoreType.DMA]
    return pl.pallas_call(
        kernel,
        out_shape=[
            jax.ShapeDtypeStruct((size,) + v.shape, v.dtype) for size, v in zip(sizes, operands)
        ],
        in_specs=[ANY] * len(operands),
        out_specs=[ANY] * len(operands),
        scratch_shapes=scratch,
        compiler_params=params(collective_id),
    )(*operands)


def sum_call(collective_id, over_tokens=None, over_copies=None, result=f32):
    operands = [v for v in (over_tokens, over_copies) if v is not None]

    def kernel(*refs):
        count = len(operands)
        terms, outs, scratch = refs[:count], refs[count : 2 * count], list(refs[2 * count :])
        place = Place()
        friends, steps, at = [], [], 0
        if over_tokens is not None:
            friends += place.tokens.neighbours() + [place.twin]
        if over_copies is not None:
            friends += place.copies.neighbours()
        loads = []
        for kind, value in (("tokens", over_tokens), ("copies", over_copies)):
            if value is None:
                continue
            rows = value.shape[1]
            if kind == "tokens":
                held, staged, stage, send_sem, recv_sem, load_sem = scratch[:6]
                del scratch[:6]
                line = Line(send_sem, recv_sem)
                source = terms[at]
                core = place.core

                def index_of(which, c):
                    return (which[0] * RING + which[1]) * 2 + c

                def held_part(which, low, n, held=held):
                    return held.at[which[0] * RING + which[1], pl.ds(low, n)]

                def outgoing(which, source=source, core=core):
                    return source.at[index_of(which, 1 - core)]

                def landed(which, staged=staged):
                    return staged.at[which[0] * RING + which[1]]

                for block in range(8):
                    load = pltpu.make_async_copy(
                        source.at[2 * block + core], held.at[block], load_sem.at[block]
                    )
                    load.start()
                    loads.append(load)
                steps.append(
                    sum_parts(
                        place.tokens, line, held_part, stage, rows, outs[at],
                        (place.twin, outgoing, landed),
                    )
                )
            else:
                held, stage, send_sem, recv_sem, load_sem = scratch[:5]
                del scratch[:5]
                line = Line(send_sem, recv_sem)
                load = pltpu.make_async_copy(terms[at], held, load_sem)
                load.start()
                loads.append(load)

                def copies_part(which, low, n, held=held):
                    return held.at[which[0] * RING + which[1], pl.ds(low, n)]

                steps.append(
                    sum_parts(place.copies, line, copies_part, stage, rows, outs[at])
                )
            at += 1
        greet(friends)
        for load in loads:
            load.wait()
        abreast(*steps)

    scratch = []
    if over_tokens is not None:
        _, rows, columns = over_tokens.shape
        scratch += [
            pltpu.VMEM((8, rows, columns), bf16),
            pltpu.VMEM((8, rows, columns), bf16),
            pltpu.VMEM((stage_rows(rows), columns), bf16),
        ]
        scratch += sems(SUM_SEMS) + [pltpu.SemaphoreType.DMA((8,))]
    if over_copies is not None:
        _, rows, columns = over_copies.shape
        scratch += [
            pltpu.VMEM((8, rows, columns), bf16),
            pltpu.VMEM((stage_rows(rows), columns), bf16),
        ]
        scratch += sems(SUM_SEMS) + [pltpu.SemaphoreType.DMA]
    return pl.pallas_call(
        kernel,
        out_shape=[jax.ShapeDtypeStruct(v.shape[1:], result) for v in operands],
        in_specs=[ANY] * len(operands),
        out_specs=[IN_VMEM] * len(operands),
        scratch_shapes=scratch,
        compiler_params=params(collective_id),
    )(*operands)


def sum_gather_call(collective_id, over_tokens, over_copies):
    _, rows, columns = over_tokens.shape

    def kernel(terms, own, total, every, held, staged, stage, s1, r1, load_sem, s2, r2, local_sem):
        place = Place()
        core = place.core
        loads = []
        for block in range(8):
            load = pltpu.make_async_copy(
                terms.at[2 * block + core], held.at[block], load_sem.at[block]
            )
            load.start()
            loads.append(load)
        greet(place.tokens.neighbours() + [place.twin] + place.copies.neighbours())
        for load in loads:
            load.wait()

        def held_part(which, low, n):
            return held.at[which[0] * RING + which[1], pl.ds(low, n)]

        def outgoing(which):
            return terms.at[(which[0] * RING + which[1]) * 2 + 1 - core]

        def landed(which):
            return staged.at[which[0] * RING + which[1]]

        abreast(
            sum_parts(
                place.tokens, Line(s1, r1), held_part, stage, rows, total,
                (place.twin, outgoing, landed),
            ),
            copies_gather(place, Line(s2, r2), own, every, local_sem),
        )

    return pl.pallas_call(
        kernel,
        out_shape=[
            jax.ShapeDtypeStruct((rows, columns), f32),
            jax.ShapeDtypeStruct((REPS,) + over_copies.shape, over_copies.dtype),
        ],
        in_specs=[ANY, ANY],
        out_specs=[IN_VMEM, ANY],
        scratch_shapes=[
            pltpu.VMEM((8, rows, columns), bf16),
            pltpu.VMEM((8, rows, columns), bf16),
            pltpu.VMEM((stage_rows(rows), columns), bf16),
        ]
        + sems(SUM_SEMS)
        + [pltpu.SemaphoreType.DMA((8,))]
        + sems(GATHER_SEMS)
        + [pltpu.SemaphoreType.DMA],
        compiler_params=params(collective_id),
    )(over_tokens, over_copies)


def copies_total_call(collective_id, terms):
    _, rows, columns = terms.shape

    def kernel(terms_ref, every, held, stage, own, s1, r1, load_sem, s2, r2, local_sem):
        place = Place()
        load = pltpu.make_async_copy(terms_ref, held, load_sem)
        load.start()
        greet(place.copies.neighbours())
        load.wait()

        def held_part(which, low, n):
            return held.at[which[0] * RING + which[1], pl.ds(low, n)]

        abreast(sum_parts(place.copies, Line(s1, r1), held_part, stage, rows, own))
        abreast(copies_gather(place, Line(s2, r2), own, every, local_sem))

    return pl.pallas_call(
        kernel,
        out_shape=jax.ShapeDtypeStruct(terms.shape, bf16),
        in_specs=[ANY],
        out_specs=ANY,
        scratch_shapes=[
            pltpu.VMEM((8, rows, columns), bf16),
            pltpu.VMEM((stage_rows(rows), columns), bf16),
            pltpu.VMEM((rows, columns), bf16),
        ]
        + sems(SUM_SEMS)
        + [pltpu.SemaphoreType.DMA]
        + sems(GATHER_SEMS)
        + [pltpu.SemaphoreType.DMA],
        compiler_params=params(collective_id),
    )(terms)


def copies_total(own):
    rows, columns = own.shape
    wide = -(-columns // (128 * REPS)) * 128 * REPS
    cut = jnp.pad(own.astype(bf16), ((0, 0), (0, wide - columns)))
    cut = cut.reshape(rows, REPS, wide // REPS).transpose(1, 0, 2)
    total = copies_total_call(7, cut)
    return total.transpose(1, 0, 2).reshape(rows, wide)[:, :columns].astype(f32)


def dot(a, b):
    return jnp.dot(a, b, preferred_element_type=f32)


def dot_nt(a, b):
    return lax.dot_general(a, b, (((1,), (1,)), ((), ())), preferred_element_type=f32)


def dot_tn(a, b):
    return lax.dot_general(a, b, (((0,), (0,)), ((), ())), preferred_element_type=f32)


def pick(index, values):
    chosen = values[-1]
    for at in range(len(values) - 2, -1, -1):
        chosen = jnp.where(index == at, values[at], chosen)
    return chosen


def moe_call(collective_id, sent, grad_all, inner, outer):
    count, columns = sent.shape
    width = inner.shape[0]
    hidden_width = outer.shape[0]
    small = columns - width
    half = count // 2
    both = 2 * half
    chips = GROUP // 2

    def kernel(
        sent_ref, grad_ref, inner_ref, outer_ref,
        out_terms, returned, terms,
        rows_in, grads, hidden, back_gu, total, back, staged, stage, outbox,
        gs0, gr0, gs1, gr1, ss0, sr0, ss1, sr1, own_sem, grad_sem, out_sem,
    ):
        place = Place()
        axes, core, shard = place.tokens, place.core, place.shard
        gather_lines = (Line(gs0, gr0), Line(gs1, gr1))
        sum_lines = (Line(ss0, sr0), Line(ss1, sr1))

        def blocks(which, other=False):
            return (which[0] * RING + which[1]) * 2 + ((1 - core) if other else core)

        def gather_of(chunk):
            def block(which, low, n, other=False):
                return rows_in.at[chunk, blocks(which, other), pl.ds(low, n)]

            return gather_parts(
                axes, gather_lines[chunk], sent_ref.at[pl.ds(chunk * half, half)], block, half,
                own_sem.at[chunk], place.twin, twin_later=chunk == 0,
            )

        def sum_of(chunk):
            def part(which, low, n):
                return back.at[chunk, blocks(which), pl.ds(low, n)]

            def outgoing(which):
                return back.at[chunk, blocks(which, True)]

            def landed(which):
                return staged.at[chunk, which[0] * RING + which[1]]

            return sum_parts(
                axes, sum_lines[chunk], part, stage.at[chunk], half,
                returned.at[pl.ds(chunk * half, half)], (place.twin, outgoing, landed),
            )

        def grad_load(chunk):
            return pltpu.make_async_copy(
                grad_ref.at[:, pl.ds(chunk * half, half)], grads, grad_sem
            )

        def out_copy(chunk, chip, slot):
            return pltpu.make_async_copy(
                outbox.at[slot],
                out_terms.at[pl.ds(chip * 2, 2), pl.ds(chunk * half, half)],
                out_sem.at[slot],
            )

        lanes = lax.broadcasted_iota(jnp.int32, (both, small), 1)
        is_high, is_rest = lanes == shard, lanes == shard + GROUP

        def tile(chunk, chip, slot, wait_first):
            at = pl.ds(chip * 2, 2)
            row_block = rows_in[chunk, at].reshape(both, columns)
            rows = row_block[:, :width]
            gate = jnp.sum(
                jnp.where(is_high | is_rest, row_block[:, width:].astype(f32), 0.0),
                axis=1, keepdims=True,
            )
            gate_up = dot(rows, inner_ref[...])
            gate_part, up_part = gate_up[:, :hidden_width], gate_up[:, hidden_width:]
            sigmoid = 1.0 / (1.0 + jnp.exp(-gate_part))
            active = gate_part * sigmoid
            product = active * up_part
            hidden_low = product.astype(bf16)
            hidden[at] = hidden_low.reshape(2, half, hidden_width)
            out = (gate * dot(hidden_low, outer_ref[...])).astype(bf16)

            @pl.when(wait_first)
            def _():
                out_copy(chunk, chip, slot).wait()

            outbox[slot] = out.reshape(2, half, width)
            out_copy(chunk, chip, slot).start()
            grad = grads[at].reshape(both, width)
            grad_hidden = dot_nt(grad, outer_ref[...])
            grad_gate = jnp.sum(grad_hidden * product, axis=1, keepdims=True)
            grad_hidden = grad_hidden * gate
            grad_gate_up = jnp.concatenate(
                [
                    grad_hidden * up_part * sigmoid * (1.0 + gate_part * (1.0 - sigmoid)),
                    grad_hidden * active,
                ],
                axis=1,
            ).astype(bf16)
            back_gu[at] = grad_gate_up.reshape(2, half, 2 * hidden_width)
            grads[at] = (gate * grad.astype(f32)).astype(bf16).reshape(2, half, width)
            grad_rows = dot_nt(grad_gate_up, inner_ref[...]).astype(bf16)
            back[chunk, at, :, pl.ds(0, width)] = grad_rows.reshape(2, half, width)
            high = grad_gate.astype(bf16).astype(f32)
            tail = jnp.where(is_high, high, jnp.where(is_rest, grad_gate - high, 0.0))
            back[chunk, at, :, pl.ds(width, small)] = tail.astype(bf16).reshape(2, half, small)

        def weight_step(chunk, index):
            low = pl.multiple_of(index * 256, 256)
            terms_at = pl.ds(low, 256)
            rows = rows_in[chunk, :, :, pl.ds(low, 256)].reshape(GROUP * half, 256)
            return terms_at, dot_tn(rows, back_gu[...].reshape(GROUP * half, 2 * hidden_width))

        def down_step(index):
            low = pl.multiple_of(index * 256, 256)
            terms_at = pl.ds(width + low, 256)
            rows = hidden[:, :, pl.ds(low, 256)].reshape(GROUP * half, 256)
            return terms_at, dot_tn(rows, grads[...].reshape(GROUP * half, width))

        greet(axes.neighbours() + [place.twin])
        gather0, gather1, sum0, sum1 = gather_of(0), gather_of(1), sum_of(0), sum_of(1)
        next(gather0)
        grad_load(0).start()
        chips0 = [w[0] * RING + w[1] for w in gather_order(axes)]
        chips1 = [w[0] * RING + w[1] for w in sum_order(axes)]
        grad_load(0).wait()

        def first_tiles(t, carry):
            @pl.when(t == 1)
            def _():
                next(gather0)
                next(gather1)

            @pl.when(t == 4)
            def _():
                next(gather0)
                next(gather1)

            @pl.when(t == 7)
            def _():
                next(gather0)
                next(gather1)

            chip = pick(t, chips0)
            gather_lines[0].take(
                12 + t, lambda: rows_in.at[0, chip * 2 + 1 - core], place.twin
            )
            tile(0, chip, lax.rem(t, 2), t >= 2)
            return carry

        lax.fori_loop(0, chips, first_tiles, 0)
        for _ in gather0:
            pass
        next(sum0)

        def first_weights(index, carry):
            at, value = weight_step(0, index)
            total[at] = value
            return carry

        def first_downs(index, carry):
            at, value = down_step(index)
            total[at] = value
            return carry

        lax.fori_loop(0, width // 256, first_weights, 0)
        next(sum0)
        lax.fori_loop(0, hidden_width // 256, first_downs, 0)
        grad_load(1).start()
        for _ in gather1:
            pass
        grad_load(1).wait()

        def second_tiles(t, carry):
            @pl.when(t == 1)
            def _():
                next(sum0)

            @pl.when(t == 3)
            def _():
                next(sum0)

            @pl.when(t == 4)
            def _():
                next(sum1)

            @pl.when(t == 6)
            def _():
                for _ in sum0:
                    pass
                next(sum1)

            tile(1, pick(t, chips1), lax.rem(t, 2), t >= 0)
            return carry

        lax.fori_loop(0, chips, second_tiles, 0)
        next(sum1)

        def second_weights(index, carry):
            at, value = weight_step(1, index)
            terms[at] = (total[at] + value).astype(bf16)
            return carry

        def second_downs(index, carry):
            at, value = down_step(index)
            terms[at] = (total[at] + value).astype(bf16)
            return carry

        lax.fori_loop(0, width // 256, second_weights, 0)
        next(sum1)
        lax.fori_loop(0, hidden_width // 256, second_downs, 0)
        for _ in sum1:
            pass
        for slot in range(2):
            out_copy(1, 0, slot).wait()

    term_rows = width + hidden_width
    return pl.pallas_call(
        kernel,
        out_shape=[
            jax.ShapeDtypeStruct((GROUP, count, width), bf16),
            jax.ShapeDtypeStruct((count, columns), f32),
            jax.ShapeDtypeStruct((term_rows, width), bf16),
        ],
        in_specs=[ANY, ANY, IN_VMEM, IN_VMEM],
        out_specs=[ANY, IN_VMEM, IN_VMEM],
        scratch_shapes=[
            pltpu.VMEM((2, GROUP, half, columns), bf16),
            pltpu.VMEM((GROUP, half, width), bf16),
            pltpu.VMEM((GROUP, half, hidden_width), bf16),
            pltpu.VMEM((GROUP, half, 2 * hidden_width), bf16),
            pltpu.VMEM((term_rows, width), f32),
            pltpu.VMEM((2, GROUP, half, columns), bf16),
            pltpu.VMEM((2, chips, half, columns), bf16),
            pltpu.VMEM((2, stage_rows(half), columns), bf16),
            pltpu.VMEM((2, 2, half, width), bf16),
        ]
        + sems(GATHER_SEMS) * 2
        + sems(SUM_SEMS) * 2
        + [pltpu.SemaphoreType.DMA((2,)), pltpu.SemaphoreType.DMA, pltpu.SemaphoreType.DMA((2,))],
        compiler_params=params(collective_id),
    )(sent, grad_all, inner, outer)


WIDTH = 1024
QUERY = HEADS * HEAD_DIM
KEY = KV_HEADS * HEAD_DIM
EXPERTS = 16
SMALL = 128
LANES = 128
AT_K = QUERY
AT_V = AT_K + KEY
AT_S = AT_V + KEY
AT_O = AT_S + SMALL
PACKED = AT_O + WIDTH
ROWS_OWN = WIDTH // GROUP
KGAIN_OWN = KEY // GROUP
HEAD_PAIRS = KV_HEADS // 2


def root_mean(values):
    return lax.rsqrt(jnp.mean(values * values, axis=1, keepdims=True) + norm_eps)


def lane_of(shape):
    return lax.broadcasted_iota(jnp.int32, shape, 1)


def turned(values, cosine, sine):
    first = lax.rem(lane_of(values.shape), HEAD_DIM) < HEAD_DIM // 2
    swapped = jnp.where(
        first, pltpu.roll(values, LANES - HEAD_DIM // 2, 1), pltpu.roll(values, HEAD_DIM // 2, 1)
    )
    return values * cosine + swapped * sine


def short_rows():
    row = lax.broadcasted_iota(jnp.int32, (WIDTH, KEY), 0)
    column = lax.broadcasted_iota(jnp.int32, (WIDTH, KEY), 1)
    same = (lax.div(row, ROWS_OWN) == lax.div(column, KGAIN_OWN)) & (
        lax.rem(row, ROWS_OWN) == lax.rem(column, KGAIN_OWN)
    )
    return jnp.where(same, 1.0, 0.0).astype(bf16)


def gain_rows(small):
    rows = jnp.transpose(small.astype(f32))
    gain_k = dot(rows[EXPERTS : EXPERTS + 8].astype(bf16), short_rows())[3:4]
    return rows[EXPERTS : EXPERTS + 1], rows[EXPERTS + 1 : EXPERTS + 2], rows[EXPERTS + 2 : EXPERTS + 3], gain_k


def four_heads(chunk_a, chunk_b):
    low = lane_of(chunk_a.shape) < HEAD_DIM
    zero = jnp.zeros_like(chunk_a)
    return jnp.concatenate(
        [
            jnp.where(low, chunk_a, zero),
            jnp.where(low, pltpu.roll(chunk_a, HEAD_DIM, 1), zero),
            jnp.where(low, zero, pltpu.roll(chunk_b, HEAD_DIM, 1)),
            jnp.where(low, zero, chunk_b),
        ],
        axis=0,
    )


def two_chunks(blocks):
    rows = blocks.shape[0] // 4
    one, two, three, four = (blocks[n * rows : (n + 1) * rows] for n in range(4))
    low = lane_of(one.shape) < HEAD_DIM
    return (
        jnp.where(low, one, pltpu.roll(two, HEAD_DIM, 1)),
        jnp.where(low, pltpu.roll(three, HEAD_DIM, 1), four),
    )


def chunk_at(index, base=0):
    return pl.ds(pl.multiple_of(base + index * LANES, LANES), LANES)


def front_call(collective_id, tokens, cotangent, packed, cosine, sine, bias, picked):
    count, width = tokens.shape
    seqs, positions, length = bias.shape
    score_scale = HEAD_DIM ** (-0.5)

    def kernel(
        tokens_ref, grad_ref, packed_ref, cos_ref, sin_ref, bias_ref, picked_ref,
        dense_out, grad_all, pairs_out, soft_out,
        attn_in, query_raw, key_raw, query_low, mixed, middle, sent, gates_out,
        dense, pairs, pair_own, soft_box,
        ws0, wr0, ws1, wr1, gs, gr, ks0, kr0, ks1, kr1, own_sem, out_sem, soft_sem,
    ):
        place = Place()
        core = place.core
        lines = [Line(*v) for v in ((ws0, wr0), (ws1, wr1), (gs, gr), (ks0, kr0), (ks1, kr1))]

        def weight_gather(index, low, size):
            def block(which, row, n, other=False):
                at = (which[0] * RING + which[1]) * 2 + ((1 - core) if other else core)
                return dense.at[at, pl.ds(row, n), pl.ds(low, size)]

            return gather_parts(
                place.tokens, lines[index], packed_ref.at[:, pl.ds(low, size)], block, ROWS_OWN,
                own_sem.at[index], place.twin,
            )

        def grad_block(which, row, n, other=False):
            at = (which[0] * RING + which[1]) * 2 + ((1 - core) if other else core)
            return grad_all.at[at, pl.ds(row, n)]

        def pair_gather(seq):
            def block(which, row, n, other=False):
                return pairs.at[seq, which[0] * RING + which[1], pl.ds(row, n)]

            return gather_parts(
                place.copies, lines[3 + seq], pair_own.at[pl.ds(seq * positions, positions)], block,
                positions, own_sem.at[3 + seq],
            )

        def soft_copy(seq, index, slot):
            return pltpu.make_async_copy(
                soft_box.at[slot], soft_out.at[seq, index], soft_sem.at[slot]
            )

        greet(place.tokens.neighbours() + place.copies.neighbours() + [place.twin])
        first = weight_gather(0, 0, AT_O)
        second = weight_gather(1, AT_O, WIDTH)
        grads = gather_parts(
            place.tokens, lines[2], grad_ref, grad_block, count, own_sem.at[2], place.twin
        )
        pair_gathers = [pair_gather(0), pair_gather(1)]
        next(first)
        inputs = tokens_ref[...].astype(f32)
        middle[...] = inputs * root_mean(inputs)
        next(first)
        next(second)
        next(first)
        next(second)
        for _ in first:
            pass
        next(second)
        next(grads)

        def weights(low, size):
            return dense[:, :, pl.ds(low, size)].reshape(width, size)

        small = weights(AT_S, SMALL)
        gain_a, gain_q, gain_f, gain_k = gain_rows(small)
        rows = (middle[...] * gain_a).astype(bf16)
        attn_in[...] = rows
        cos2 = jnp.concatenate([cos_ref[...]] * seqs, axis=0)
        sin2 = jnp.concatenate([sin_ref[...]] * seqs, axis=0)
        raw = dot(rows, weights(AT_K, KEY))
        key_raw[...] = raw
        scaled = raw * root_mean(raw) * gain_k
        for chunk in range(KEY // LANES):
            at = slice(chunk * LANES, (chunk + 1) * LANES)
            pair_own[:, at] = turned(scaled[:, at], cos2, sin2).astype(bf16)
        pair_own[:, KEY:] = dot(rows, weights(AT_V, KEY)).astype(bf16)
        next(pair_gathers[0])
        raw = dot(rows, weights(0, QUERY))
        query_raw[...] = raw
        scaled = raw * root_mean(raw) * gain_q
        for chunk in range(QUERY // LANES):
            at = slice(chunk * LANES, (chunk + 1) * LANES)
            query_low[:, at] = turned(scaled[:, at], cos2, sin2).astype(bf16)
        for _ in second:
            pass
        dense_copy = pltpu.make_async_copy(dense, dense_out, out_sem.at[0])
        dense_copy.start()
        next(pair_gathers[0])
        next(pair_gathers[1])
        next(pair_gathers[0])
        for _ in pair_gathers[0]:
            pass
        next(grads)
        next(pair_gathers[1])

        def attend(seq, index, slot, wait_first):
            rows_at = pl.ds(seq * positions, positions)
            queries = four_heads(
                query_low[rows_at, chunk_at(2 * index)].astype(f32),
                query_low[rows_at, chunk_at(2 * index + 1)].astype(f32),
            )
            queries = (queries * score_scale).astype(bf16)
            keys = pairs[seq, :, :, chunk_at(index)].reshape(length, LANES)
            scores = dot_nt(queries, keys).reshape(4, positions, length) + bias_ref[seq][None]
            scores = scores.reshape(4 * positions, length)
            raised = jnp.exp(scores - jnp.max(scores, axis=1, keepdims=True))
            soft = (raised * (1.0 / jnp.sum(raised, axis=1, keepdims=True))).astype(bf16)

            @pl.when(wait_first)
            def _():
                soft_copy(seq, index, slot).wait()

            soft_box[slot] = soft
            soft_copy(seq, index, slot).start()
            values = pairs[seq, :, :, chunk_at(index, KEY)].reshape(length, LANES)
            chunk_a, chunk_b = two_chunks(dot(soft, values))
            mixed[rows_at, chunk_at(2 * index)] = chunk_a.astype(bf16)
            mixed[rows_at, chunk_at(2 * index + 1)] = chunk_b.astype(bf16)

        def first_heads(index, carry):
            @pl.when(index == 3)
            def _():
                next(pair_gathers[1])

            attend(0, index, lax.rem(index, 2), index >= 2)
            return carry

        lax.fori_loop(0, HEAD_PAIRS, first_heads, 0)
        for _ in pair_gathers[1]:
            pass
        pairs_copy = pltpu.make_async_copy(pairs, pairs_out, out_sem.at[1])
        pairs_copy.start()

        def second_heads(index, carry):
            @pl.when(index == 0)
            def _():
                next(grads)

            @pl.when(index == 3)
            def _():
                next(grads)

            attend(1, index, lax.rem(index, 2), index >= 0)
            return carry

        lax.fori_loop(0, HEAD_PAIRS, second_heads, 0)
        total = tokens_ref[...].astype(f32) + dot(mixed[...], weights(AT_O, WIDTH))
        middle[...] = total
        ffn_in = (total * root_mean(total) * gain_f).astype(bf16)
        sent[:, pl.ds(0, width)] = ffn_in
        chosen = picked_ref[...] > 0.5
        logits = jnp.where(chosen, dot(ffn_in, small), masked_score)
        raised = jnp.exp(logits - jnp.max(logits, axis=1, keepdims=True))
        gates = raised * (1.0 / jnp.sum(raised, axis=1, keepdims=True))
        gates = jnp.where(chosen, gates, 0.0)
        gates_out[...] = gates
        high = gates.astype(bf16).astype(f32)
        tail = high + pltpu.roll(gates - high, EXPERTS, 1)
        sent[:, pl.ds(width, SMALL)] = tail.astype(bf16)
        for _ in grads:
            pass
        dense_copy.wait()
        pairs_copy.wait()
        for slot in range(2):
            soft_copy(1, 0, slot).wait()

    return pl.pallas_call(
        kernel,
        out_shape=[
            jax.ShapeDtypeStruct((GROUP, ROWS_OWN, PACKED), bf16),
            jax.ShapeDtypeStruct((GROUP, count, width), bf16),
            jax.ShapeDtypeStruct((seqs, REPS, positions, 2 * KEY), bf16),
            jax.ShapeDtypeStruct((seqs, HEAD_PAIRS, 4 * positions, length), bf16),
            jax.ShapeDtypeStruct((count, width), bf16),
            jax.ShapeDtypeStruct((count, QUERY), f32),
            jax.ShapeDtypeStruct((count, KEY), f32),
            jax.ShapeDtypeStruct((count, QUERY), bf16),
            jax.ShapeDtypeStruct((count, QUERY), bf16),
            jax.ShapeDtypeStruct((count, width), f32),
            jax.ShapeDtypeStruct((count, width + SMALL), bf16),
            jax.ShapeDtypeStruct((count, SMALL), f32),
        ],
        in_specs=[IN_VMEM, ANY, ANY, IN_VMEM, IN_VMEM, IN_VMEM, IN_VMEM],
        out_specs=[ANY] * 4 + [IN_VMEM] * 8,
        scratch_shapes=[
            pltpu.VMEM((GROUP, ROWS_OWN, PACKED), bf16),
            pltpu.VMEM((seqs, REPS, positions, 2 * KEY), bf16),
            pltpu.VMEM((count, 2 * KEY), bf16),
            pltpu.VMEM((2, 4 * positions, length), bf16),
        ]
        + sems(GATHER_SEMS) * 5
        + [
            pltpu.SemaphoreType.DMA((5,)),
            pltpu.SemaphoreType.DMA((2,)),
            pltpu.SemaphoreType.DMA((2,)),
        ],
        compiler_params=params(collective_id),
    )(tokens, cotangent, packed, cosine, sine, bias, picked)


def rms_scale(values, gain):
    return values * lax.rsqrt(jnp.mean(values * values, axis=-1, keepdims=True) + norm_eps) * gain


def rotary_tables(positions, head_size):
    half_size = head_size // 2
    exponent = jnp.arange(half_size, dtype=f32) * (2.0 / head_size)
    frequency = rope_base ** (-exponent)
    angles = positions.astype(f32)[:, None] * frequency[None, :]
    cosine_table = jnp.concatenate([jnp.cos(angles), jnp.cos(angles)], axis=-1)
    sine_table = jnp.concatenate([jnp.sin(angles), jnp.sin(angles)], axis=-1)
    return (cosine_table, sine_table)


def rotate(values, cosine_table, sine_table):
    half_size = values.shape[-1] // 2
    turned = jnp.concatenate([-values[..., half_size:], values[..., :half_size]], axis=-1)
    return values * cosine_table[:, None, :] + turned * sine_table[:, None, :]


def piece_index(positions, starts):
    inside = (positions[:, None] >= starts[None, :]) & (positions[:, None] < starts[None, :] + PIC)
    labels = jnp.arange(1, starts.shape[0] + 1, dtype=jnp.int32)
    return jnp.sum(jnp.where(inside, labels[None, :], 0), axis=1) - 1


def allowed_mask(query_pos, key_pos, starts):
    query_piece = piece_index(query_pos, starts)
    key_piece = piece_index(key_pos, starts)
    causal = key_pos[None, :] <= query_pos[:, None]
    shared = (query_piece[:, None] == key_piece[None, :]) & (query_piece[:, None] >= 0)
    return causal | shared


def query_key(query_raw, key_raw, query_gain, key_gain, cosine_table, sine_table):
    row_count = query_raw.shape[0]
    query_rot = rotate(
        rms_scale(query_raw, query_gain).reshape(row_count, HEADS, HEAD_DIM),
        cosine_table,
        sine_table,
    )
    key_rot = rotate(
        rms_scale(key_raw, key_gain).reshape(row_count, KV_HEADS, HEAD_DIM),
        cosine_table,
        sine_table,
    )
    return (query_rot, key_rot)


def pack_rows(wide, router, gain_a, gain_q, gain_f, gain_k):
    rows = router.shape[0]
    short = jnp.concatenate([gain_k, jnp.zeros((rows - gain_k.shape[0],), gain_k.dtype)])
    small = jnp.concatenate(
        [router] + [v[:, None] for v in (gain_a, gain_q, gain_f, short)], axis=1
    )
    small = jnp.pad(small, ((0, 0), (0, SMALL - small.shape[1])))
    return jnp.concatenate(list(wide[:3]) + [small, wide[3]], axis=1)


def shards(
    tokens,
    cotangent,
    routes,
    picture_starts,
    attn_gain,
    query_weight,
    key_weight,
    value_weight,
    query_gain,
    key_gain,
    output_weight,
    ffn_gain,
    router_weight,
    expert_in,
    expert_down,
):
    seqs, positions, width = tokens.shape
    top = routes.shape[2]
    count = seqs * positions
    length = positions * REPS
    experts = GROUP
    group = HEADS // KV_HEADS
    query_width = HEADS * HEAD_DIM
    kv_width = KV_HEADS * HEAD_DIM
    score_scale = HEAD_DIM ** (-0.5)
    rows_own = query_weight.shape[0]
    kgain_own = key_gain.shape[0]
    shard = lax.axis_index("shard")
    query_pos = lax.axis_index("rep") * positions + jnp.arange(positions, dtype=jnp.int32)
    key_pos = jnp.arange(length, dtype=jnp.int32)
    cosine_one, sine_one = rotary_tables(query_pos, HEAD_DIM)
    cosine_table = jnp.tile(cosine_one, (seqs, 1))
    sine_table = jnp.tile(sine_one, (seqs, 1))

    packed = pack_rows(
        (query_weight, key_weight, value_weight, output_weight),
        router_weight,
        attn_gain,
        query_gain,
        ffn_gain,
        key_gain,
    )
    allowed = jax.vmap(lambda starts: allowed_mask(query_pos, key_pos, starts))(picture_starts)
    bias = jnp.where(allowed, 0.0, masked_score).astype(f32)
    route_ids = routes.reshape(count, top)
    picked = jnp.sum(
        (route_ids[:, :, None] == jnp.arange(SMALL)[None, None, :]).astype(f32), axis=1
    )
    sign = jnp.where(jnp.arange(HEAD_DIM) < HEAD_DIM // 2, -1.0, 1.0).astype(f32)
    (
        dense, grad_all, pairs_all, soft_low,
        attn_in, query_raw, key_raw, query_low, mixed_low, middle, sent, gates,
    ) = front_call(
        1,
        tokens.reshape(count, width),
        cotangent.reshape(count, width),
        packed,
        jnp.tile(cosine_one, (1, 2)),
        jnp.tile(sine_one * sign[None, :], (1, 2)),
        bias,
        picked,
    )
    columns = packed.shape[1]
    dense = dense.reshape(GROUP * rows_own, columns)
    weight_q = dense[:, :AT_K]
    weight_k = dense[:, AT_K:AT_V]
    weight_v = dense[:, AT_V:AT_S]
    weight_o = dense[:, AT_O:]
    weight_r = dense[:, AT_S : AT_S + experts]
    gain_a = dense[:, AT_S + experts].astype(f32)
    gain_q = dense[:, AT_S + experts + 1].astype(f32)
    gain_f = dense[:, AT_S + experts + 2].astype(f32)
    gain_k = (
        dense[:, AT_S + experts + 3].reshape(GROUP, rows_own)[:, :kgain_own].reshape(-1).astype(f32)
    )
    inputs = tokens.reshape(count, width).astype(f32)
    grad_out = cotangent.reshape(count, width).astype(f32)
    query_low = query_low.reshape(seqs, positions, KV_HEADS, group, HEAD_DIM)
    pairs_all = pairs_all.reshape(seqs, length, 2 * kv_width)
    keys_all = pairs_all[..., :kv_width].reshape(seqs, length, KV_HEADS, HEAD_DIM)
    values_all = pairs_all[..., kv_width:].reshape(seqs, length, KV_HEADS, HEAD_DIM)
    gates = gates[:, :experts]
    picked = picked[:, :experts] > 0.5
    ffn_in = sent[:, :width]
    out_terms, returned, expert_terms = moe_call(
        3, sent, grad_all, expert_in[0], expert_down[0]
    )
    (expert_own,) = sum_call(4, None, expert_terms.reshape(REPS, -1, width))

    grad_gates = returned[:, width : width + experts] + returned[:, width + experts : width + 2 * experts]
    grad_chosen = gates * (grad_gates - jnp.sum(gates * grad_gates, axis=-1, keepdims=True))
    grad_logits = jnp.where(picked, grad_chosen, 0.0).astype(bf16)
    grad_router = dot_tn(ffn_in, grad_logits)
    grad_ffn_in = dot_nt(grad_logits, weight_r) + returned[:, :width]
    _, norm_pull = jax.vjp(rms_scale, middle, gain_f)
    grad_middle_part, grad_gain_f = norm_pull(grad_ffn_in)
    grad_middle = grad_out + grad_middle_part
    grad_attn = grad_middle.astype(bf16)
    grad_weight_o = dot_tn(mixed_low, grad_attn)
    grad_mixed = (
        dot_nt(grad_attn, weight_o).astype(bf16).reshape(seqs, positions, KV_HEADS, group, HEAD_DIM)
    )
    soft_full = soft_low.reshape(seqs, KV_HEADS, group, positions, length).astype(f32)
    grad_soft = jnp.einsum("bqkgd,bskd->bkgqs", grad_mixed, values_all, preferred_element_type=f32)
    grad_values = jnp.einsum(
        "bkgqs,bqkgd->bskd", soft_full.astype(bf16), grad_mixed, preferred_element_type=f32
    )
    grad_scores = (
        soft_full * (grad_soft - jnp.sum(soft_full * grad_soft, axis=-1, keepdims=True))
    ).astype(bf16)
    grad_query_rot = (
        jnp.einsum("bkgqs,bskd->bqkgd", grad_scores, keys_all, preferred_element_type=f32)
        * score_scale
    )
    grad_keys = (
        jnp.einsum("bkgqs,bqkgd->bskd", grad_scores, query_low, preferred_element_type=f32)
        * score_scale
    )
    grad_pairs = (
        jnp.concatenate(
            [
                grad_keys.reshape(seqs, length, kv_width),
                grad_values.reshape(seqs, length, kv_width),
            ],
            axis=-1,
        )
        .astype(bf16)
        .reshape(seqs, REPS, positions, 2 * kv_width)
        .transpose(1, 0, 2, 3)
        .reshape(REPS, count, 2 * kv_width)
    )
    out_sum, pairs_own = sum_call(5, out_terms, grad_pairs)
    block_out = (middle + out_sum).astype(bf16)

    grad_query_rot = grad_query_rot.astype(bf16).astype(f32).reshape(count, HEADS, HEAD_DIM)
    grad_key_rot = (
        pairs_own[:, :kv_width].astype(bf16).astype(f32).reshape(count, KV_HEADS, HEAD_DIM)
    )
    grad_value_low = pairs_own[:, kv_width:].astype(bf16)

    def turned_pair(query_in, key_in, query_scale, key_scale):
        return query_key(query_in, key_in, query_scale, key_scale, cosine_table, sine_table)

    _, pair_pull = jax.vjp(turned_pair, query_raw, key_raw, gain_q, gain_k)
    grad_query_raw, grad_key_raw, grad_gain_q, grad_gain_k = pair_pull(
        (grad_query_rot, grad_key_rot)
    )
    grad_query_low = grad_query_raw.astype(bf16)
    grad_key_low = grad_key_raw.astype(bf16)
    grad_weight_q = dot_tn(attn_in, grad_query_low)
    grad_weight_k = dot_tn(attn_in, grad_key_low)
    grad_weight_v = dot_tn(attn_in, grad_value_low)
    grad_attn_in = (
        dot_nt(grad_query_low, weight_q)
        + dot_nt(grad_key_low, weight_k)
        + dot_nt(grad_value_low, weight_v)
    )
    _, norm_pull = jax.vjp(rms_scale, inputs, gain_a)
    grad_inputs_part, grad_gain_a = norm_pull(grad_attn_in)
    tokens_grad = (grad_middle + grad_inputs_part).astype(bf16)

    gain_k_rows = jnp.pad(
        grad_gain_k.reshape(GROUP, kgain_own), ((0, 0), (0, rows_own - kgain_own))
    ).reshape(-1)
    dense_terms = pack_rows(
        tuple(v.astype(bf16) for v in (grad_weight_q, grad_weight_k, grad_weight_v, grad_weight_o)),
        grad_router.astype(bf16),
        grad_gain_a.astype(bf16),
        grad_gain_q.astype(bf16),
        grad_gain_f.astype(bf16),
        gain_k_rows.astype(bf16),
    ).reshape(GROUP, rows_own, columns)
    dense_own, expert_all = sum_gather_call(6, dense_terms, expert_own.astype(bf16))
    expert_all = expert_all.reshape(-1, width)
    inner_rows = expert_in.shape[1]
    expert_in_grad = expert_all[:inner_rows].astype(f32)[None]
    expert_down_grad = expert_all[inner_rows:].astype(f32)[None]
    dense_sum = copies_total(dense_own)
    return (
        block_out.reshape(tokens.shape),
        tokens_grad.reshape(tokens.shape),
        dense_sum[:, AT_S + experts],
        dense_sum[:, :AT_K],
        dense_sum[:, AT_K:AT_V],
        dense_sum[:, AT_V:AT_S],
        dense_sum[:, AT_S + experts + 1],
        dense_sum[:kgain_own, AT_S + experts + 3],
        dense_sum[:, AT_O:],
        dense_sum[:, AT_S + experts + 2],
        dense_sum[:, AT_S : AT_S + experts],
        expert_in_grad,
        expert_down_grad,
    )


def solution(mesh):
    by_tokens = P("shard", "rep", None)
    rows, line, block = P("shard", None), P("shard"), P("shard", None, None)
    in_specs = (
        by_tokens, by_tokens, by_tokens, rows, line, rows, rows, rows, line, line, rows, line, rows, block, block,
    )
    out_specs = (
        by_tokens, by_tokens, line, rows, rows, rows, line, line, rows, line, rows, block, block,
    )
    return jax.shard_map(shards, mesh=mesh, in_specs=in_specs, out_specs=out_specs, check_vma=False)
```

```python
import functools

import jax
import jax.numpy as jnp
from jax import lax
from jax.experimental import pallas as pl
from jax.experimental.pallas import tpu as pltpu
from jax.sharding import PartitionSpec as P

HEADS = 16
KV_HEADS = 8
HEAD_DIM = 64
PIC = 256
RING = 4
GROUP = 16
REPS = 8
VMEM_LIMIT = 62 << 20

norm_eps = 1e-06
rope_base = 10000.0
masked_score = -1e30

bf16 = jnp.bfloat16
f32 = jnp.float32


class Place:
    def __init__(self):
        shard = lax.axis_index("shard")
        rep = lax.axis_index("rep")
        self.shard, self.rep = shard, rep
        core = lax.rem(shard, 2)
        ring_z = lax.rem(lax.div(shard, 2), RING)
        y_hi = lax.div(shard, 8)
        ring_x = lax.rem(rep, RING)
        y_lo = lax.div(rep, RING)
        self.core = core

        def shard_of(hi, z, c):
            return (hi * RING + z) * 2 + c

        def rep_of(lo, x):
            return lo * RING + x

        def up(v):
            return lax.rem(v + 1, RING)

        def down(v):
            return lax.rem(v + RING - 1, RING)

        self.twin = (shard_of(y_hi, ring_z, 1 - core), rep)
        self.tokens = Axes(
            y_hi,
            ring_z,
            (shard_of(y_hi, up(ring_z), core), rep),
            (shard_of(y_hi, down(ring_z), core), rep),
            (shard_of(1 - y_hi, ring_z, core), rep_of(1 - y_lo, ring_x)),
        )
        self.copies = Axes(
            y_lo,
            ring_x,
            (shard, rep_of(y_lo, up(ring_x))),
            (shard, rep_of(y_lo, down(ring_x))),
            (shard, rep_of(1 - y_lo, ring_x)),
        )


class Axes:
    def __init__(self, side, spot, ahead, behind, across):
        self.side, self.spot = side, spot
        self.ahead, self.behind, self.across = ahead, behind, across
        sides = (side, 1 - side)
        spots = [lax.rem(spot + step, RING) for step in range(RING)]
        self.places = [[(sides[flip], spots[step]) for step in range(RING)] for flip in range(2)]

    def at(self, flip, step):
        return self.places[flip][step % RING]

    def neighbours(self):
        return [self.ahead, self.behind, self.across]


def greet(devices):
    barrier = pltpu.get_barrier_semaphore()
    for device in devices:
        pl.semaphore_signal(barrier, inc=1, device_id=device, device_id_type=pl.DeviceIdType.MESH)
    pl.semaphore_wait(barrier, len(devices))


class Line:
    def __init__(self, send_sem, recv_sem):
        self.send_sem, self.recv_sem = send_sem, recv_sem
        self.sent = []

    def copy(self, index, source, target, device):
        return pltpu.make_async_remote_copy(
            src_ref=source(),
            dst_ref=target(),
            send_sem=self.send_sem.at[index],
            recv_sem=self.recv_sem.at[index],
            device_id=device,
            device_id_type=pl.DeviceIdType.MESH,
        )

    def send(self, index, source, target, device):
        self.copy(index, source, target, device).start()
        self.sent.append((index, source, target, device))

    def take(self, index, target, device):
        self.copy(index, target, target, device).wait_recv()

    def finish(self):
        for sent in self.sent:
            self.copy(*sent).wait_send()


def abreast(*parts):
    running = list(parts)
    while running:
        for part in list(running):
            try:
                next(part)
            except StopIteration:
                running.remove(part)


GATHER_SEMS = 20


def gather_parts(axes, line, own, block, rows, local_sem, twin=None, twin_later=False):
    half, quarter = rows // 2, rows // 4
    mine, back, front, far = axes.at(0, 0), axes.at(0, -1), axes.at(0, 1), axes.at(0, 2)
    pair, pair_back, pair_front, pair_far = (axes.at(1, n) for n in (0, -1, 1, 2))
    ahead, behind, across = axes.ahead, axes.behind, axes.across

    def rows_of(which, low=0, count=rows, other=False):
        return lambda: block(which, low, count, other)

    def first(index, device):
        line.send(index, lambda: own, rows_of(mine), device)

    def relay(index, device, which, low=0, count=rows):
        line.send(index, rows_of(which, low, count), rows_of(which, low, count), device)

    def share(index, which):
        if twin is not None:
            relay(12 + index, twin, which)

    def keep():
        return pltpu.make_async_copy(own, block(mine, 0, rows), local_sem)

    keep().start()
    if twin is not None:
        first(12, twin)
    first(0, ahead)
    first(1, behind)
    first(2, across)
    keep().wait()
    yield
    line.take(0, rows_of(back), ahead)
    relay(3, ahead, back, 0, half)
    relay(4, across, back, half, half)
    share(1, back)
    line.take(1, rows_of(front), behind)
    relay(5, behind, front, half, half)
    relay(6, across, front, half, half)
    share(2, front)
    line.take(2, rows_of(pair), across)
    relay(7, ahead, pair, 0, half)
    relay(8, behind, pair, 0, half)
    share(3, pair)
    yield
    line.take(3, rows_of(far, 0, half), ahead)
    line.take(5, rows_of(far, half, half), behind)
    relay(9, across, far, half, half)
    share(4, far)
    line.take(7, rows_of(pair_back, 0, half), ahead)
    relay(10, ahead, pair_back, 0, quarter)
    line.take(8, rows_of(pair_front, 0, half), behind)
    relay(11, behind, pair_front, quarter, quarter)
    line.take(4, rows_of(pair_back, half, half), across)
    share(5, pair_back)
    line.take(6, rows_of(pair_front, half, half), across)
    share(6, pair_front)
    yield
    line.take(10, rows_of(pair_far, 0, quarter), ahead)
    line.take(11, rows_of(pair_far, quarter, quarter), behind)
    line.take(9, rows_of(pair_far, half, half), across)
    share(7, pair_far)
    yield
    if twin is not None and not twin_later:
        for index, which in enumerate(gather_order(axes)):
            line.take(12 + index, rows_of(which, other=True), twin)
    line.finish()


SUM_SEMS = 20


def add_rows(target, source, rows):
    step = 16
    count = rows // step

    def body(index, carry):
        at = pl.ds(pl.multiple_of(index * step, step), step)
        target[at] = target[at] + source[at]
        return carry

    lax.fori_loop(0, count, body, 0)


def stage_rows(rows):
    return 7 * rows


def gather_order(axes):
    return [axes.at(*v) for v in ((0, 0), (0, -1), (0, 1), (1, 0), (0, 2), (1, -1), (1, 1), (1, 2))]


def sum_order(axes):
    return [axes.at(*v) for v in ((1, 2), (0, 2), (1, -1), (1, 1), (0, -1), (0, 1), (1, 0), (0, 0))]


def sum_parts(axes, line, part, stage, rows, result, twin=None, store=None):
    half, quarter = rows // 2, rows // 4
    mine, back, front, far = axes.at(0, 0), axes.at(0, -1), axes.at(0, 1), axes.at(0, 2)
    pair, pair_back, pair_front, pair_far = (axes.at(1, n) for n in (0, -1, 1, 2))
    ahead, behind, across = axes.ahead, axes.behind, axes.across
    order = sum_order(axes)
    offsets, used = {}, 0
    for name, size in (
        ("Y0", half), ("M0", quarter), ("P0", quarter), ("M1", half), ("Y1", half), ("Y2", half),
        ("P1", half), ("M2", half), ("P2", half), ("M3", rows), ("P3", rows), ("Y3", rows),
    ):
        offsets[name] = (used, size, len(offsets))
        used += size

    def landing(name):
        low, size, _ = offsets[name]
        return lambda: stage.at[pl.ds(low, size)]

    def send(name, which, low, device):
        _, size, index = offsets[name]
        line.send(index, lambda: part(which, low, size), landing(name), device)

    def add(name, which, low, device):
        _, size, index = offsets[name]
        line.take(index, landing(name), device)
        add_rows(part(which, low, size), landing(name)(), size)

    def join(*places):
        if twin is not None:
            for place in places:
                line.take(12 + place, lambda: twin[2](order[place]), twin[0])
                add_rows(part(order[place], 0, rows), twin[2](order[place]), rows)

    def hand(*places):
        if twin is not None:
            for place in places:
                which = order[place]
                line.send(
                    12 + place, lambda w=which: twin[1](w), lambda w=which: twin[2](w), twin[0]
                )

    hand(0, 1, 2, 3)
    yield
    join(0)
    send("Y0", pair_far, half, across)
    send("M0", pair_far, 0, behind)
    send("P0", pair_far, quarter, ahead)
    join(1)
    send("M1", far, 0, behind)
    join(2)
    send("Y1", pair_back, half, across)
    join(3)
    send("Y2", pair_front, half, across)
    yield
    hand(4, 5, 6, 7)
    add("M0", pair_back, 0, behind)
    send("M2", pair_back, 0, behind)
    add("P0", pair_front, quarter, ahead)
    send("P2", pair_front, 0, ahead)
    add("Y0", far, half, across)
    send("P1", far, half, ahead)
    yield
    join(4, 5, 6, 7)
    add("M1", back, 0, behind)
    add("Y1", back, half, across)
    send("M3", back, 0, behind)
    add("M2", pair, 0, behind)
    add("P2", pair, 0, ahead)
    send("Y3", pair, 0, across)
    add("P1", front, half, ahead)
    add("Y2", front, half, across)
    send("P3", front, 0, ahead)
    yield
    for name, device in (("M3", behind), ("P3", ahead), ("Y3", across)):
        line.take(offsets[name][2], landing(name), device)
    step = 16

    def body(index, carry):
        low = pl.multiple_of(index * step, step)
        total = part(mine, low, step)[...].astype(f32)
        for name in ("M3", "P3", "Y3"):
            total = total + stage[pl.ds(offsets[name][0] + low, step)].astype(f32)
        if store is None:
            result[pl.ds(low, step)] = total.astype(result.dtype)
        else:
            store(low, step, total)
        return carry

    lax.fori_loop(0, rows // step, body, 0)
    line.finish()


def sems(count):
    return [pltpu.SemaphoreType.DMA((count,)), pltpu.SemaphoreType.DMA((count,))]


ANY = pl.BlockSpec(memory_space=pl.ANY)
IN_VMEM = pl.BlockSpec(memory_space=pltpu.VMEM)


def tokens_gather(place, line, own_ref, all_ref, local_sem):
    rows = own_ref.shape[0]
    axes, core = place.tokens, place.core

    def block(which, low, count, other=False):
        side, spot = which
        index = (side * RING + spot) * 2 + ((1 - core) if other else core)
        return all_ref.at[index, pl.ds(low, count)]

    return gather_parts(axes, line, own_ref, block, rows, local_sem, place.twin)


def copies_gather(place, line, own_ref, all_ref, local_sem):
    rows = own_ref.shape[0]

    def block(which, low, count, other=False):
        side, spot = which
        return all_ref.at[side * RING + spot, pl.ds(low, count)]

    return gather_parts(place.copies, line, own_ref, block, rows, local_sem)


def params(collective_id):
    return pltpu.CompilerParams(
        collective_id=collective_id, has_side_effects=True, vmem_limit_bytes=VMEM_LIMIT
    )


def gather_call(collective_id, over_tokens=None, over_copies=None):
    operands = [v for v in (over_tokens, over_copies) if v is not None]

    def kernel(*refs):
        count = len(operands)
        owns, alls, scratch = refs[:count], refs[count : 2 * count], list(refs[2 * count :])
        place = Place()
        friends, steps, at = [], [], 0
        for kind, value in (("tokens", over_tokens), ("copies", over_copies)):
            if value is None:
                continue
            send_sem, recv_sem, local_sem = scratch[3 * at : 3 * at + 3]
            line = Line(send_sem, recv_sem)
            if kind == "tokens":
                friends += place.tokens.neighbours() + [place.twin]
                steps.append(tokens_gather(place, line, owns[at], alls[at], local_sem))
            else:
                friends += place.copies.neighbours()
                steps.append(copies_gather(place, line, owns[at], alls[at], local_sem))
            at += 1
        greet(friends)
        abreast(*steps)

    sizes = []
    if over_tokens is not None:
        sizes.append(GROUP)
    if over_copies is not None:
        sizes.append(REPS)
    scratch = []
    for _ in operands:
        scratch += sems(GATHER_SEMS) + [pltpu.SemaphoreType.DMA]
    return pl.pallas_call(
        kernel,
        out_shape=[
            jax.ShapeDtypeStruct((size,) + v.shape, v.dtype) for size, v in zip(sizes, operands)
        ],
        in_specs=[ANY] * len(operands),
        out_specs=[ANY] * len(operands),
        scratch_shapes=scratch,
        compiler_params=params(collective_id),
    )(*operands)


def sum_call(collective_id, over_tokens=None, over_copies=None, result=f32):
    operands = [v for v in (over_tokens, over_copies) if v is not None]

    def kernel(*refs):
        count = len(operands)
        terms, outs, scratch = refs[:count], refs[count : 2 * count], list(refs[2 * count :])
        place = Place()
        friends, steps, at = [], [], 0
        if over_tokens is not None:
            friends += place.tokens.neighbours() + [place.twin]
        if over_copies is not None:
            friends += place.copies.neighbours()
        loads = []
        for kind, value in (("tokens", over_tokens), ("copies", over_copies)):
            if value is None:
                continue
            rows = value.shape[1]
            if kind == "tokens":
                held, staged, stage, send_sem, recv_sem, load_sem = scratch[:6]
                del scratch[:6]
                line = Line(send_sem, recv_sem)
                source = terms[at]
                core = place.core

                def index_of(which, c):
                    return (which[0] * RING + which[1]) * 2 + c

                def held_part(which, low, n, held=held):
                    return held.at[which[0] * RING + which[1], pl.ds(low, n)]

                def outgoing(which, source=source, core=core):
                    return source.at[index_of(which, 1 - core)]

                def landed(which, staged=staged):
                    return staged.at[which[0] * RING + which[1]]

                for block in range(8):
                    load = pltpu.make_async_copy(
                        source.at[2 * block + core], held.at[block], load_sem.at[block]
                    )
                    load.start()
                    loads.append(load)
                steps.append(
                    sum_parts(
                        place.tokens, line, held_part, stage, rows, outs[at],
                        (place.twin, outgoing, landed),
                    )
                )
            else:
                held, stage, send_sem, recv_sem, load_sem = scratch[:5]
                del scratch[:5]
                line = Line(send_sem, recv_sem)
                load = pltpu.make_async_copy(terms[at], held, load_sem)
                load.start()
                loads.append(load)

                def copies_part(which, low, n, held=held):
                    return held.at[which[0] * RING + which[1], pl.ds(low, n)]

                steps.append(
                    sum_parts(place.copies, line, copies_part, stage, rows, outs[at])
                )
            at += 1
        greet(friends)
        for load in loads:
            load.wait()
        abreast(*steps)

    scratch = []
    if over_tokens is not None:
        _, rows, columns = over_tokens.shape
        scratch += [
            pltpu.VMEM((8, rows, columns), bf16),
            pltpu.VMEM((8, rows, columns), bf16),
            pltpu.VMEM((stage_rows(rows), columns), bf16),
        ]
        scratch += sems(SUM_SEMS) + [pltpu.SemaphoreType.DMA((8,))]
    if over_copies is not None:
        _, rows, columns = over_copies.shape
        scratch += [
            pltpu.VMEM((8, rows, columns), bf16),
            pltpu.VMEM((stage_rows(rows), columns), bf16),
        ]
        scratch += sems(SUM_SEMS) + [pltpu.SemaphoreType.DMA]
    return pl.pallas_call(
        kernel,
        out_shape=[jax.ShapeDtypeStruct(v.shape[1:], result) for v in operands],
        in_specs=[ANY] * len(operands),
        out_specs=[IN_VMEM] * len(operands),
        scratch_shapes=scratch,
        compiler_params=params(collective_id),
    )(*operands)


def sum_gather_call(collective_id, over_tokens, over_copies):
    _, rows, columns = over_tokens.shape

    def kernel(terms, own, total, every, held, staged, stage, s1, r1, load_sem, s2, r2, local_sem):
        place = Place()
        core = place.core
        loads = []
        for block in range(8):
            load = pltpu.make_async_copy(
                terms.at[2 * block + core], held.at[block], load_sem.at[block]
            )
            load.start()
            loads.append(load)
        greet(place.tokens.neighbours() + [place.twin] + place.copies.neighbours())
        for load in loads:
            load.wait()

        def held_part(which, low, n):
            return held.at[which[0] * RING + which[1], pl.ds(low, n)]

        def outgoing(which):
            return terms.at[(which[0] * RING + which[1]) * 2 + 1 - core]

        def landed(which):
            return staged.at[which[0] * RING + which[1]]

        abreast(
            sum_parts(
                place.tokens, Line(s1, r1), held_part, stage, rows, total,
                (place.twin, outgoing, landed),
            ),
            copies_gather(place, Line(s2, r2), own, every, local_sem),
        )

    return pl.pallas_call(
        kernel,
        out_shape=[
            jax.ShapeDtypeStruct((rows, columns), f32),
            jax.ShapeDtypeStruct((REPS,) + over_copies.shape, over_copies.dtype),
        ],
        in_specs=[ANY, ANY],
        out_specs=[IN_VMEM, ANY],
        scratch_shapes=[
            pltpu.VMEM((8, rows, columns), bf16),
            pltpu.VMEM((8, rows, columns), bf16),
            pltpu.VMEM((stage_rows(rows), columns), bf16),
        ]
        + sems(SUM_SEMS)
        + [pltpu.SemaphoreType.DMA((8,))]
        + sems(GATHER_SEMS)
        + [pltpu.SemaphoreType.DMA],
        compiler_params=params(collective_id),
    )(over_tokens, over_copies)


def copies_total_call(collective_id, terms):
    _, rows, columns = terms.shape

    def kernel(terms_ref, every, held, stage, own, s1, r1, load_sem, s2, r2, local_sem):
        place = Place()
        load = pltpu.make_async_copy(terms_ref, held, load_sem)
        load.start()
        greet(place.copies.neighbours())
        load.wait()

        def held_part(which, low, n):
            return held.at[which[0] * RING + which[1], pl.ds(low, n)]

        abreast(sum_parts(place.copies, Line(s1, r1), held_part, stage, rows, own))
        abreast(copies_gather(place, Line(s2, r2), own, every, local_sem))

    return pl.pallas_call(
        kernel,
        out_shape=jax.ShapeDtypeStruct(terms.shape, bf16),
        in_specs=[ANY],
        out_specs=ANY,
        scratch_shapes=[
            pltpu.VMEM((8, rows, columns), bf16),
            pltpu.VMEM((stage_rows(rows), columns), bf16),
            pltpu.VMEM((rows, columns), bf16),
        ]
        + sems(SUM_SEMS)
        + [pltpu.SemaphoreType.DMA]
        + sems(GATHER_SEMS)
        + [pltpu.SemaphoreType.DMA],
        compiler_params=params(collective_id),
    )(terms)


def copies_total(own):
    rows, columns = own.shape
    wide = -(-columns // (128 * REPS)) * 128 * REPS
    cut = jnp.pad(own.astype(bf16), ((0, 0), (0, wide - columns)))
    cut = cut.reshape(rows, REPS, wide // REPS).transpose(1, 0, 2)
    total = copies_total_call(7, cut)
    return total.transpose(1, 0, 2).reshape(rows, wide)[:, :columns].astype(f32)


def dot(a, b):
    return jnp.dot(a, b, preferred_element_type=f32)


def dot_nt(a, b):
    return lax.dot_general(a, b, (((1,), (1,)), ((), ())), preferred_element_type=f32)


def dot_tn(a, b):
    return lax.dot_general(a, b, (((0,), (0,)), ((), ())), preferred_element_type=f32)


def pick(index, values):
    chosen = values[-1]
    for at in range(len(values) - 2, -1, -1):
        chosen = jnp.where(index == at, values[at], chosen)
    return chosen


def moe_call(collective_id, sent, grad_all, inner, outer):
    count, columns = sent.shape
    width = inner.shape[0]
    hidden_width = outer.shape[0]
    small = columns - width
    half = count // 2
    both = 2 * half
    chips = GROUP // 2

    def kernel(
        sent_ref, grad_ref, inner_ref, outer_ref,
        out_terms, returned, terms,
        rows_in, grads, hidden, back_gu, total, back, staged, stage, outbox,
        gs0, gr0, gs1, gr1, ss0, sr0, ss1, sr1, own_sem, grad_sem, out_sem,
    ):
        place = Place()
        axes, core, shard = place.tokens, place.core, place.shard
        gather_lines = (Line(gs0, gr0), Line(gs1, gr1))
        sum_lines = (Line(ss0, sr0), Line(ss1, sr1))

        def blocks(which, other=False):
            return (which[0] * RING + which[1]) * 2 + ((1 - core) if other else core)

        def gather_of(chunk):
            def block(which, low, n, other=False):
                return rows_in.at[chunk, blocks(which, other), pl.ds(low, n)]

            return gather_parts(
                axes, gather_lines[chunk], sent_ref.at[pl.ds(chunk * half, half)], block, half,
                own_sem.at[chunk], place.twin, twin_later=chunk == 0,
            )

        def sum_of(chunk):
            def part(which, low, n):
                return back.at[chunk, blocks(which), pl.ds(low, n)]

            def outgoing(which):
                return back.at[chunk, blocks(which, True)]

            def landed(which):
                return staged.at[chunk, which[0] * RING + which[1]]

            return sum_parts(
                axes, sum_lines[chunk], part, stage.at[chunk], half,
                returned.at[pl.ds(chunk * half, half)], (place.twin, outgoing, landed),
            )

        def grad_load(chunk):
            return pltpu.make_async_copy(
                grad_ref.at[:, pl.ds(chunk * half, half)], grads, grad_sem
            )

        def out_copy(chunk, chip, slot):
            return pltpu.make_async_copy(
                outbox.at[slot],
                out_terms.at[pl.ds(chip * 2, 2), pl.ds(chunk * half, half)],
                out_sem.at[slot],
            )

        lanes = lax.broadcasted_iota(jnp.int32, (both, small), 1)
        is_high, is_rest = lanes == shard, lanes == shard + GROUP

        def tile(chunk, chip, slot, wait_first):
            at = pl.ds(chip * 2, 2)
            row_block = rows_in[chunk, at].reshape(both, columns)
            rows = row_block[:, :width]
            gate = jnp.sum(
                jnp.where(is_high | is_rest, row_block[:, width:].astype(f32), 0.0),
                axis=1, keepdims=True,
            )
            gate_up = dot(rows, inner_ref[...])
            gate_part, up_part = gate_up[:, :hidden_width], gate_up[:, hidden_width:]
            sigmoid = 1.0 / (1.0 + jnp.exp(-gate_part))
            active = gate_part * sigmoid
            product = active * up_part
            hidden_low = product.astype(bf16)
            hidden[at] = hidden_low.reshape(2, half, hidden_width)
            out = (gate * dot(hidden_low, outer_ref[...])).astype(bf16)

            @pl.when(wait_first)
            def _():
                out_copy(chunk, chip, slot).wait()

            outbox[slot] = out.reshape(2, half, width)
            out_copy(chunk, chip, slot).start()
            grad = grads[at].reshape(both, width)
            grad_hidden = dot_nt(grad, outer_ref[...])
            grad_gate = jnp.sum(grad_hidden * product, axis=1, keepdims=True)
            grad_hidden = grad_hidden * gate
            grad_gate_up = jnp.concatenate(
                [
                    grad_hidden * up_part * sigmoid * (1.0 + gate_part * (1.0 - sigmoid)),
                    grad_hidden * active,
                ],
                axis=1,
            ).astype(bf16)
            back_gu[at] = grad_gate_up.reshape(2, half, 2 * hidden_width)
            grads[at] = (gate * grad.astype(f32)).astype(bf16).reshape(2, half, width)
            grad_rows = dot_nt(grad_gate_up, inner_ref[...]).astype(bf16)
            back[chunk, at, :, pl.ds(0, width)] = grad_rows.reshape(2, half, width)
            high = grad_gate.astype(bf16).astype(f32)
            tail = jnp.where(is_high, high, jnp.where(is_rest, grad_gate - high, 0.0))
            back[chunk, at, :, pl.ds(width, small)] = tail.astype(bf16).reshape(2, half, small)

        def weight_step(chunk, index):
            low = pl.multiple_of(index * 256, 256)
            terms_at = pl.ds(low, 256)
            rows = rows_in[chunk, :, :, pl.ds(low, 256)].reshape(GROUP * half, 256)
            return terms_at, dot_tn(rows, back_gu[...].reshape(GROUP * half, 2 * hidden_width))

        def down_step(index):
            low = pl.multiple_of(index * 256, 256)
            terms_at = pl.ds(width + low, 256)
            rows = hidden[:, :, pl.ds(low, 256)].reshape(GROUP * half, 256)
            return terms_at, dot_tn(rows, grads[...].reshape(GROUP * half, width))

        greet(axes.neighbours() + [place.twin])
        gather0, gather1, sum0, sum1 = gather_of(0), gather_of(1), sum_of(0), sum_of(1)
        next(gather0)
        grad_load(0).start()
        chips0 = [w[0] * RING + w[1] for w in gather_order(axes)]
        chips1 = [w[0] * RING + w[1] for w in sum_order(axes)]
        grad_load(0).wait()

        def first_tiles(t, carry):
            @pl.when(t == 1)
            def _():
                next(gather0)
                next(gather1)

            @pl.when(t == 4)
            def _():
                next(gather0)
                next(gather1)

            @pl.when(t == 7)
            def _():
                next(gather0)
                next(gather1)

            chip = pick(t, chips0)
            gather_lines[0].take(
                12 + t, lambda: rows_in.at[0, chip * 2 + 1 - core], place.twin
            )
            tile(0, chip, lax.rem(t, 2), t >= 2)
            return carry

        lax.fori_loop(0, chips, first_tiles, 0)
        for _ in gather0:
            pass
        next(sum0)

        def first_weights(index, carry):
            at, value = weight_step(0, index)
            total[at] = value
            return carry

        def first_downs(index, carry):
            at, value = down_step(index)
            total[at] = value
            return carry

        lax.fori_loop(0, width // 256, first_weights, 0)
        next(sum0)
        lax.fori_loop(0, hidden_width // 256, first_downs, 0)
        grad_load(1).start()
        for _ in gather1:
            pass
        grad_load(1).wait()

        def second_tiles(t, carry):
            @pl.when(t == 1)
            def _():
                next(sum0)

            @pl.when(t == 3)
            def _():
                next(sum0)

            @pl.when(t == 4)
            def _():
                next(sum1)

            @pl.when(t == 6)
            def _():
                for _ in sum0:
                    pass
                next(sum1)

            tile(1, pick(t, chips1), lax.rem(t, 2), t >= 0)
            return carry

        lax.fori_loop(0, chips, second_tiles, 0)
        next(sum1)

        def second_weights(index, carry):
            at, value = weight_step(1, index)
            terms[at] = (total[at] + value).astype(bf16)
            return carry

        def second_downs(index, carry):
            at, value = down_step(index)
            terms[at] = (total[at] + value).astype(bf16)
            return carry

        lax.fori_loop(0, width // 256, second_weights, 0)
        next(sum1)
        lax.fori_loop(0, hidden_width // 256, second_downs, 0)
        for _ in sum1:
            pass
        for slot in range(2):
            out_copy(1, 0, slot).wait()

    term_rows = width + hidden_width
    return pl.pallas_call(
        kernel,
        out_shape=[
            jax.ShapeDtypeStruct((GROUP, count, width), bf16),
            jax.ShapeDtypeStruct((count, columns), f32),
            jax.ShapeDtypeStruct((term_rows, width), bf16),
        ],
        in_specs=[ANY, ANY, IN_VMEM, IN_VMEM],
        out_specs=[ANY, IN_VMEM, IN_VMEM],
        scratch_shapes=[
            pltpu.VMEM((2, GROUP, half, columns), bf16),
            pltpu.VMEM((GROUP, half, width), bf16),
            pltpu.VMEM((GROUP, half, hidden_width), bf16),
            pltpu.VMEM((GROUP, half, 2 * hidden_width), bf16),
            pltpu.VMEM((term_rows, width), f32),
            pltpu.VMEM((2, GROUP, half, columns), bf16),
            pltpu.VMEM((2, chips, half, columns), bf16),
            pltpu.VMEM((2, stage_rows(half), columns), bf16),
            pltpu.VMEM((2, 2, half, width), bf16),
        ]
        + sems(GATHER_SEMS) * 2
        + sems(SUM_SEMS) * 2
        + [pltpu.SemaphoreType.DMA((2,)), pltpu.SemaphoreType.DMA, pltpu.SemaphoreType.DMA((2,))],
        compiler_params=params(collective_id),
    )(sent, grad_all, inner, outer)


WIDTH = 1024
QUERY = HEADS * HEAD_DIM
KEY = KV_HEADS * HEAD_DIM
EXPERTS = 16
SMALL = 128
LANES = 128
AT_K = QUERY
AT_V = AT_K + KEY
AT_S = AT_V + KEY
AT_O = AT_S + SMALL
PACKED = AT_O + WIDTH
ROWS_OWN = WIDTH // GROUP
KGAIN_OWN = KEY // GROUP
HEAD_PAIRS = KV_HEADS // 2


def root_mean(values):
    return lax.rsqrt(jnp.mean(values * values, axis=1, keepdims=True) + norm_eps)


def lane_of(shape):
    return lax.broadcasted_iota(jnp.int32, shape, 1)


def turned(values, cosine, sine):
    first = lax.rem(lane_of(values.shape), HEAD_DIM) < HEAD_DIM // 2
    swapped = jnp.where(
        first, pltpu.roll(values, LANES - HEAD_DIM // 2, 1), pltpu.roll(values, HEAD_DIM // 2, 1)
    )
    return values * cosine + swapped * sine


def short_rows():
    row = lax.broadcasted_iota(jnp.int32, (WIDTH, KEY), 0)
    column = lax.broadcasted_iota(jnp.int32, (WIDTH, KEY), 1)
    same = (lax.div(row, ROWS_OWN) == lax.div(column, KGAIN_OWN)) & (
        lax.rem(row, ROWS_OWN) == lax.rem(column, KGAIN_OWN)
    )
    return jnp.where(same, 1.0, 0.0).astype(bf16)


def gain_rows(small):
    rows = jnp.transpose(small.astype(f32))
    gain_k = dot(rows[EXPERTS : EXPERTS + 8].astype(bf16), short_rows())[3:4]
    return rows[EXPERTS : EXPERTS + 1], rows[EXPERTS + 1 : EXPERTS + 2], rows[EXPERTS + 2 : EXPERTS + 3], gain_k


def four_heads(chunk_a, chunk_b):
    low = lane_of(chunk_a.shape) < HEAD_DIM
    zero = jnp.zeros_like(chunk_a)
    return jnp.concatenate(
        [
            jnp.where(low, chunk_a, zero),
            jnp.where(low, pltpu.roll(chunk_a, HEAD_DIM, 1), zero),
            jnp.where(low, zero, pltpu.roll(chunk_b, HEAD_DIM, 1)),
            jnp.where(low, zero, chunk_b),
        ],
        axis=0,
    )


def two_chunks(blocks):
    rows = blocks.shape[0] // 4
    one, two, three, four = (blocks[n * rows : (n + 1) * rows] for n in range(4))
    low = lane_of(one.shape) < HEAD_DIM
    return (
        jnp.where(low, one, pltpu.roll(two, HEAD_DIM, 1)),
        jnp.where(low, pltpu.roll(three, HEAD_DIM, 1), four),
    )


def chunk_at(index, base=0):
    return pl.ds(pl.multiple_of(base + index * LANES, LANES), LANES)


def front_call(collective_id, tokens, cotangent, packed, cosine, sine, bias, picked):
    count, width = tokens.shape
    seqs, positions, length = bias.shape
    score_scale = HEAD_DIM ** (-0.5)

    def kernel(
        tokens_ref, grad_ref, packed_ref, cos_ref, sin_ref, bias_ref, picked_ref,
        dense_out, grad_all, pairs_out, soft_out,
        attn_in, query_raw, key_raw, query_low, mixed, middle, sent, gates_out,
        dense, pairs, pair_own, soft_box,
        ws0, wr0, ws1, wr1, gs, gr, ks0, kr0, ks1, kr1, own_sem, out_sem, soft_sem,
    ):
        place = Place()
        core = place.core
        lines = [Line(*v) for v in ((ws0, wr0), (ws1, wr1), (gs, gr), (ks0, kr0), (ks1, kr1))]

        def weight_gather(index, low, size):
            def block(which, row, n, other=False):
                at = (which[0] * RING + which[1]) * 2 + ((1 - core) if other else core)
                return dense.at[at, pl.ds(row, n), pl.ds(low, size)]

            return gather_parts(
                place.tokens, lines[index], packed_ref.at[:, pl.ds(low, size)], block, ROWS_OWN,
                own_sem.at[index], place.twin,
            )

        def grad_block(which, row, n, other=False):
            at = (which[0] * RING + which[1]) * 2 + ((1 - core) if other else core)
            return grad_all.at[at, pl.ds(row, n)]

        def pair_gather(seq):
            def block(which, row, n, other=False):
                return pairs.at[seq, which[0] * RING + which[1], pl.ds(row, n)]

            return gather_parts(
                place.copies, lines[3 + seq], pair_own.at[pl.ds(seq * positions, positions)], block,
                positions, own_sem.at[3 + seq],
            )

        def soft_copy(seq, index, slot):
            return pltpu.make_async_copy(
                soft_box.at[slot], soft_out.at[seq, index], soft_sem.at[slot]
            )

        greet(place.tokens.neighbours() + place.copies.neighbours() + [place.twin])
        first = weight_gather(0, 0, AT_O)
        second = weight_gather(1, AT_O, WIDTH)
        grads = gather_parts(
            place.tokens, lines[2], grad_ref, grad_block, count, own_sem.at[2], place.twin
        )
        pair_gathers = [pair_gather(0), pair_gather(1)]
        next(first)
        inputs = tokens_ref[...].astype(f32)
        middle[...] = inputs * root_mean(inputs)
        next(first)
        next(second)
        next(first)
        next(second)
        for _ in first:
            pass
        next(second)
        next(grads)

        def weights(low, size):
            return dense[:, :, pl.ds(low, size)].reshape(width, size)

        small = weights(AT_S, SMALL)
        gain_a, gain_q, gain_f, gain_k = gain_rows(small)
        rows = (middle[...] * gain_a).astype(bf16)
        attn_in[...] = rows
        cos2 = jnp.concatenate([cos_ref[...]] * seqs, axis=0)
        sin2 = jnp.concatenate([sin_ref[...]] * seqs, axis=0)
        raw = dot(rows, weights(AT_K, KEY))
        key_raw[...] = raw
        scaled = raw * root_mean(raw) * gain_k
        for chunk in range(KEY // LANES):
            at = slice(chunk * LANES, (chunk + 1) * LANES)
            pair_own[:, at] = turned(scaled[:, at], cos2, sin2).astype(bf16)
        pair_own[:, KEY:] = dot(rows, weights(AT_V, KEY)).astype(bf16)
        next(pair_gathers[0])
        raw = dot(rows, weights(0, QUERY))
        query_raw[...] = raw
        scaled = raw * root_mean(raw) * gain_q
        for chunk in range(QUERY // LANES):
            at = slice(chunk * LANES, (chunk + 1) * LANES)
            query_low[:, at] = turned(scaled[:, at], cos2, sin2).astype(bf16)
        for _ in second:
            pass
        dense_copy = pltpu.make_async_copy(dense, dense_out, out_sem.at[0])
        dense_copy.start()
        next(pair_gathers[0])
        next(pair_gathers[1])
        next(pair_gathers[0])
        for _ in pair_gathers[0]:
            pass
        next(grads)
        next(pair_gathers[1])

        def attend(seq, index, slot, wait_first):
            rows_at = pl.ds(seq * positions, positions)
            queries = four_heads(
                query_low[rows_at, chunk_at(2 * index)].astype(f32),
                query_low[rows_at, chunk_at(2 * index + 1)].astype(f32),
            )
            queries = (queries * score_scale).astype(bf16)
            keys = pairs[seq, :, :, chunk_at(index)].reshape(length, LANES)
            scores = dot_nt(queries, keys).reshape(4, positions, length) + bias_ref[seq][None]
            scores = scores.reshape(4 * positions, length)
            raised = jnp.exp(scores - jnp.max(scores, axis=1, keepdims=True))
            soft = (raised * (1.0 / jnp.sum(raised, axis=1, keepdims=True))).astype(bf16)

            @pl.when(wait_first)
            def _():
                soft_copy(seq, index, slot).wait()

            soft_box[slot] = soft
            soft_copy(seq, index, slot).start()
            values = pairs[seq, :, :, chunk_at(index, KEY)].reshape(length, LANES)
            chunk_a, chunk_b = two_chunks(dot(soft, values))
            mixed[rows_at, chunk_at(2 * index)] = chunk_a.astype(bf16)
            mixed[rows_at, chunk_at(2 * index + 1)] = chunk_b.astype(bf16)

        def first_heads(index, carry):
            @pl.when(index == 3)
            def _():
                next(pair_gathers[1])

            attend(0, index, lax.rem(index, 2), index >= 2)
            return carry

        lax.fori_loop(0, HEAD_PAIRS, first_heads, 0)
        for _ in pair_gathers[1]:
            pass
        pairs_copy = pltpu.make_async_copy(pairs, pairs_out, out_sem.at[1])
        pairs_copy.start()

        def second_heads(index, carry):
            @pl.when(index == 0)
            def _():
                next(grads)

            @pl.when(index == 3)
            def _():
                next(grads)

            attend(1, index, lax.rem(index, 2), index >= 0)
            return carry

        lax.fori_loop(0, HEAD_PAIRS, second_heads, 0)
        total = tokens_ref[...].astype(f32) + dot(mixed[...], weights(AT_O, WIDTH))
        middle[...] = total
        ffn_in = (total * root_mean(total) * gain_f).astype(bf16)
        sent[:, pl.ds(0, width)] = ffn_in
        chosen = picked_ref[...] > 0.5
        logits = jnp.where(chosen, dot(ffn_in, small), masked_score)
        raised = jnp.exp(logits - jnp.max(logits, axis=1, keepdims=True))
        gates = raised * (1.0 / jnp.sum(raised, axis=1, keepdims=True))
        gates = jnp.where(chosen, gates, 0.0)
        gates_out[...] = gates
        high = gates.astype(bf16).astype(f32)
        tail = high + pltpu.roll(gates - high, EXPERTS, 1)
        sent[:, pl.ds(width, SMALL)] = tail.astype(bf16)
        for _ in grads:
            pass
        dense_copy.wait()
        pairs_copy.wait()
        for slot in range(2):
            soft_copy(1, 0, slot).wait()

    return pl.pallas_call(
        kernel,
        out_shape=[
            jax.ShapeDtypeStruct((GROUP, ROWS_OWN, PACKED), bf16),
            jax.ShapeDtypeStruct((GROUP, count, width), bf16),
            jax.ShapeDtypeStruct((seqs, REPS, positions, 2 * KEY), bf16),
            jax.ShapeDtypeStruct((seqs, HEAD_PAIRS, 4 * positions, length), bf16),
            jax.ShapeDtypeStruct((count, width), bf16),
            jax.ShapeDtypeStruct((count, QUERY), f32),
            jax.ShapeDtypeStruct((count, KEY), f32),
            jax.ShapeDtypeStruct((count, QUERY), bf16),
            jax.ShapeDtypeStruct((count, QUERY), bf16),
            jax.ShapeDtypeStruct((count, width), f32),
            jax.ShapeDtypeStruct((count, width + SMALL), bf16),
            jax.ShapeDtypeStruct((count, SMALL), f32),
        ],
        in_specs=[IN_VMEM, ANY, ANY, IN_VMEM, IN_VMEM, IN_VMEM, IN_VMEM],
        out_specs=[ANY] * 4 + [IN_VMEM] * 8,
        scratch_shapes=[
            pltpu.VMEM((GROUP, ROWS_OWN, PACKED), bf16),
            pltpu.VMEM((seqs, REPS, positions, 2 * KEY), bf16),
            pltpu.VMEM((count, 2 * KEY), bf16),
            pltpu.VMEM((2, 4 * positions, length), bf16),
        ]
        + sems(GATHER_SEMS) * 5
        + [
            pltpu.SemaphoreType.DMA((5,)),
            pltpu.SemaphoreType.DMA((2,)),
            pltpu.SemaphoreType.DMA((2,)),
        ],
        compiler_params=params(collective_id),
    )(tokens, cotangent, packed, cosine, sine, bias, picked)


def norm_back(values, gain, grad):
    scale = root_mean(values)
    weighted = grad * gain
    mean = jnp.mean(values * weighted, axis=1, keepdims=True)
    inner = weighted * scale - values * (scale * scale * scale * mean)
    return inner, jnp.sum(grad * values * scale, axis=0, keepdims=True)


REST = 2 * KEY + SMALL


def back_call(
    collective_id, returned, gates, middle, sent, dense, cotangent, tokens, attn_in, query_raw, key_raw,
    query_low, mixed, pairs, soft, out_terms, expert_terms, cosine, sine,
):
    count, width = tokens.shape
    seqs, _, positions, _ = pairs.shape
    length = REPS * positions
    expert_rows = expert_terms.shape[0] // REPS
    score_scale = HEAD_DIM ** (-0.5)
    chips = GROUP // 2

    def kernel(
        returned_ref, gates_ref, middle_ref, sent_ref, dense_ref, grad_ref, tokens_ref, attn_ref,
        query_raw_ref, key_raw_ref, query_ref, mixed_ref, pairs_ref, soft_ref, out_ref, expert_ref,
        cos_ref, sin_ref,
        block_out, tokens_grad, dense_all, expert_all,
        weight_box, weight_rest, o_terms, rest_terms, dense_own,
        o_staged, q_staged, rest_staged, o_stage, q_stage, rest_stage,
        out_held, out_staged, out_stage, expert_held, expert_stage, expert_own,
        soft_box, key_box, value_box, pair_terms, pair_stage, pair_grads,
        grad_mixed, grad_query, grad_middle, grad_attn_in, gain_box,
        out_s, out_r, exp_s, exp_r, kv0_s, kv0_r, kv1_s, kv1_r, o_s, o_r, q_s, q_r, rest_s, rest_r,
        ge_s, ge_r, go_s, go_r, gq_s, gq_r, grest_s, grest_r,
        load_sem, out_load_sem, box_sem, own_sem,
    ):
        place = Place()
        core = place.core
        token_axes, copy_axes = place.tokens, place.copies
        q_terms = expert_held

        def chip_of(which):
            return which[0] * RING + which[1]

        def blocks(which, other=False):
            return chip_of(which) * 2 + ((1 - core) if other else core)

        def out_store(low, step, value):
            at = pl.ds(low, step)
            block_out[at] = (middle_ref[at] + value).astype(bf16)

        out_sum = sum_parts(
            token_axes, Line(out_s, out_r),
            lambda which, low, n: out_held.at[chip_of(which), pl.ds(low, n)],
            out_stage, count, None,
            (place.twin, lambda which: out_ref.at[blocks(which, True)],
             lambda which: out_staged.at[chip_of(which)]),
            store=out_store,
        )
        expert_sum = sum_parts(
            copy_axes, Line(exp_s, exp_r),
            lambda which, low, n: expert_held.at[pl.ds(chip_of(which) * expert_rows + low, n)],
            expert_stage, expert_rows, expert_own,
        )

        def pair_sum(seq, send_sem, recv_sem):
            return sum_parts(
                copy_axes, Line(send_sem, recv_sem),
                lambda which, low, n: pair_terms.at[seq, chip_of(which), pl.ds(low, n)],
                pair_stage.at[seq], positions, pair_grads.at[pl.ds(seq * positions, positions)],
            )

        pair_sums = [pair_sum(0, kv0_s, kv0_r), pair_sum(1, kv1_s, kv1_r)]

        def rows_of_block(terms, index, low, n):
            return terms.at[pl.ds(index * ROWS_OWN + low, n)]

        def dense_sum(terms, staged, stage, low, size, send_sem, recv_sem):
            return sum_parts(
                token_axes, Line(send_sem, recv_sem),
                lambda which, row, n: rows_of_block(terms, blocks(which), row, n),
                stage, ROWS_OWN, dense_own.at[:, pl.ds(low, size)],
                (place.twin, lambda which: rows_of_block(terms, blocks(which, True), 0, ROWS_OWN),
                 lambda which: staged.at[chip_of(which)]),
            )

        o_sum = dense_sum(o_terms, o_staged, o_stage, AT_O, width, o_s, o_r)
        q_sum = dense_sum(q_terms, q_staged, q_stage, 0, QUERY, q_s, q_r)
        rest_sum = dense_sum(rest_terms, rest_staged, rest_stage, AT_K, REST, rest_s, rest_r)

        def dense_gather(low, size, send_sem, recv_sem, index):
            return gather_parts(
                copy_axes, Line(send_sem, recv_sem), dense_own.at[:, pl.ds(low, size)],
                lambda which, row, n, other=False: dense_all.at[
                    chip_of(which), pl.ds(row, n), pl.ds(low, size)
                ],
                ROWS_OWN, own_sem.at[index],
            )

        o_gather = dense_gather(AT_O, width, go_s, go_r, 0)
        q_gather = dense_gather(0, QUERY, gq_s, gq_r, 1)
        rest_gather = dense_gather(AT_K, REST, grest_s, grest_r, 2)
        expert_gather = gather_parts(
            copy_axes, Line(ge_s, ge_r), expert_own,
            lambda which, row, n, other=False: expert_all.at[chip_of(which), pl.ds(row, n)],
            expert_rows, own_sem.at[3],
        )

        def weight_load(low, index):
            return pltpu.make_async_copy(
                dense_ref.at[:, :, pl.ds(low, width)], weight_box, load_sem.at[index]
            )

        rest_load = pltpu.make_async_copy(
            dense_ref.at[:, :, pl.ds(AT_K, REST)], weight_rest, load_sem.at[1]
        )
        expert_load = pltpu.make_async_copy(expert_ref, expert_held, load_sem.at[2])
        out_loads = [
            pltpu.make_async_copy(
                out_ref.at[2 * chip + core], out_held.at[chip], out_load_sem.at[chip]
            )
            for chip in range(chips)
        ]

        def box_loads(number, slot):
            seq, index = lax.div(number, HEAD_PAIRS), lax.rem(number, HEAD_PAIRS)
            return [
                pltpu.make_async_copy(
                    soft_ref.at[seq, index], soft_box.at[slot], box_sem.at[slot, 0]
                ),
                pltpu.make_async_copy(
                    pairs_ref.at[seq, :, :, chunk_at(index)], key_box.at[slot], box_sem.at[slot, 1]
                ),
                pltpu.make_async_copy(
                    pairs_ref.at[seq, :, :, chunk_at(index, KEY)],
                    value_box.at[slot],
                    box_sem.at[slot, 2],
                ),
            ]

        expert_load.start()
        rest_load.start()
        weight_load(AT_O, 0).start()
        for load in out_loads:
            load.start()
        for load in box_loads(0, 0):
            load.start()
        greet(token_axes.neighbours() + copy_axes.neighbours() + [place.twin])
        next(out_sum)
        expert_load.wait()
        next(expert_sum)
        next(expert_sum)
        rest_load.wait()

        small = weight_rest[:, :, pl.ds(2 * KEY, SMALL)].reshape(width, SMALL)
        gain_a, gain_q, gain_f, gain_k = gain_rows(small)
        gates = gates_ref[...]
        tail = returned_ref[:, pl.ds(width, SMALL)]
        grad_gates = tail + pltpu.roll(tail, SMALL - EXPERTS, 1)
        grad_logits = gates * (
            grad_gates - jnp.sum(gates * grad_gates, axis=1, keepdims=True)
        )
        grad_logits = grad_logits.astype(bf16)
        router_terms = dot_tn(sent_ref[:, pl.ds(0, width)], grad_logits)
        grad_ffn = returned_ref[:, pl.ds(0, width)] + dot_nt(grad_logits, small)
        inner, gain_f_terms = norm_back(middle_ref[...], gain_f, grad_ffn)
        inner = grad_ref[...].astype(f32) + inner
        grad_middle[...] = inner
        grad_attn = inner.astype(bf16)
        gain_box[...] = jnp.zeros_like(gain_box)
        gain_box[pl.ds(EXPERTS + 2, 1)] = gain_f_terms
        for load in out_loads:
            load.wait()
        next(out_sum)
        weight_load(AT_O, 0).wait()
        weight_o = weight_box[...].reshape(QUERY, width)
        grad_mixed[...] = dot_nt(grad_attn, weight_o).astype(bf16)
        weight_load(0, 3).start()

        def o_rows(index, carry):
            at = chunk_256(index)
            o_terms[at] = dot_tn(mixed_ref[:, at], grad_attn).astype(bf16)
            return carry

        lax.fori_loop(0, QUERY // 256, o_rows, 0)
        next(o_sum)
        next(o_sum)

        def attend_back(seq, index):
            number = seq * HEAD_PAIRS + index
            slot = lax.rem(number, 2)
            for load in box_loads(number, slot):
                load.wait()

            @pl.when(number + 1 < seqs * HEAD_PAIRS)
            def _():
                for load in box_loads(number + 1, 1 - slot):
                    load.start()

            rows_at = pl.ds(seq * positions, positions)
            first, second = chunk_at(2 * index), chunk_at(2 * index + 1)
            queries = four_heads(
                query_ref[rows_at, first].astype(f32), query_ref[rows_at, second].astype(f32)
            )
            queries = (queries * score_scale).astype(bf16)
            grads = four_heads(
                grad_mixed[rows_at, first].astype(f32), grad_mixed[rows_at, second].astype(f32)
            ).astype(bf16)
            keys = key_box[slot].reshape(length, LANES)
            values = value_box[slot].reshape(length, LANES)
            soft_low = soft_box[slot]
            value_terms = dot_tn(soft_low, grads)
            pair_terms[seq, :, :, chunk_at(index, KEY)] = value_terms.astype(bf16).reshape(
                REPS, positions, LANES
            )
            soft_full = soft_low.astype(f32)
            grad_soft = dot_nt(grads, values)
            weighted = soft_full * grad_soft
            grad_scores = (
                weighted - soft_full * jnp.sum(weighted, axis=1, keepdims=True)
            ).astype(bf16)
            key_terms = dot_tn(grad_scores, queries)
            pair_terms[seq, :, :, chunk_at(index)] = key_terms.astype(bf16).reshape(
                REPS, positions, LANES
            )
            chunk_a, chunk_b = two_chunks(dot(grad_scores, keys) * score_scale)
            grad_query[rows_at, first] = chunk_a.astype(bf16)
            grad_query[rows_at, second] = chunk_b.astype(bf16)

        def hooks(index, steps):
            for at, step in steps:
                pl.when(index == at)(step)

        def first_heads(index, carry):
            hooks(
                index,
                (
                    (1, lambda: next(expert_sum)),
                    (2, lambda: next(out_sum)),
                    (3, lambda: next(expert_sum)),
                ),
            )
            attend_back(0, index)
            return carry

        lax.fori_loop(0, HEAD_PAIRS, first_heads, 0)
        next(pair_sums[0])
        next(pair_sums[0])

        def drained(part):
            for _ in part:
                pass

        def second_heads(index, carry):
            hooks(
                index,
                (
                    (0, lambda: next(out_sum)),
                    (1, lambda: (drained(expert_sum), next(o_sum))[0]),
                    (2, lambda: next(pair_sums[0])),
                    (3, lambda: (drained(out_sum), next(o_sum))[0]),
                ),
            )
            attend_back(1, index)
            return carry

        lax.fori_loop(0, HEAD_PAIRS, second_heads, 0)
        next(pair_sums[0])
        next(pair_sums[1])
        next(pair_sums[1])

        cos2 = jnp.concatenate([cos_ref[...]] * seqs, axis=0)
        sin2 = -jnp.concatenate([sin_ref[...]] * seqs, axis=0)

        def turned_back(values):
            return jnp.concatenate(
                [
                    turned(values[:, low : low + LANES], cos2, sin2)
                    for low in range(0, values.shape[1], LANES)
                ],
                axis=1,
            )

        grad, gain_q_terms = norm_back(
            query_raw_ref[...], gain_q, turned_back(grad_query[...].astype(f32))
        )
        gain_box[pl.ds(EXPERTS + 1, 1)] = gain_q_terms
        grad_query_low = grad.astype(bf16)
        weight_load(0, 3).wait()
        grad_attn_in[...] = dot_nt(grad_query_low, weight_box[...].reshape(width, QUERY))

        def q_rows(index, carry):
            at = chunk_256(index)
            q_terms[at] = dot_tn(attn_ref[:, at], grad_query_low).astype(bf16)
            return carry

        lax.fori_loop(0, width // 256, q_rows, 0)
        next(q_sum)
        next(q_sum)
        drained(pair_sums[0])
        next(pair_sums[1])
        next(pair_sums[1])
        drained(o_sum)
        next(expert_gather)
        next(q_sum)
        drained(pair_sums[1])

        grads = pair_grads[...]
        grad, gain_k_terms = norm_back(
            key_raw_ref[...],
            gain_k,
            turned_back(grads[:, :KEY].astype(bf16).astype(f32)),
        )
        grad_pairs = jnp.concatenate([grad.astype(bf16), grads[:, KEY:].astype(bf16)], axis=1)
        gain_k_row = dot_nt(
            jnp.broadcast_to(gain_k_terms, (8, KEY)).astype(bf16), short_rows()
        )
        gain_box[pl.ds(EXPERTS + 3, 1)] = gain_k_row[:1]
        grad = grad_attn_in[...] + dot_nt(
            grad_pairs, weight_rest[:, :, pl.ds(0, 2 * KEY)].reshape(width, 2 * KEY)
        )
        values = tokens_ref[...].astype(f32)
        inner, gain_a_terms = norm_back(values, gain_a, grad)
        tokens_grad[...] = (grad_middle[...] + inner).astype(bf16)
        gain_box[pl.ds(EXPERTS, 1)] = gain_a_terms
        rest_terms[:, pl.ds(2 * KEY, SMALL)] = (
            router_terms + jnp.transpose(gain_box[...])
        ).astype(bf16)

        def rest_rows(index, carry):
            at = chunk_256(index)
            rest_terms[at, pl.ds(0, 2 * KEY)] = dot_tn(attn_ref[:, at], grad_pairs).astype(bf16)
            return carry

        lax.fori_loop(0, width // 256, rest_rows, 0)
        next(rest_sum)
        next(rest_sum)
        next(o_gather)
        next(expert_gather)
        next(q_sum)
        next(rest_sum)
        drained(q_sum)
        next(q_gather)
        next(o_gather)
        next(expert_gather)
        next(rest_sum)
        next(q_gather)
        next(o_gather)
        drained(rest_sum)
        next(rest_gather)
        abreast(expert_gather, o_gather, q_gather, rest_gather)

    block = pltpu.VMEM((GROUP, ROWS_OWN, width), bf16)
    scratch = [
        block,
        pltpu.VMEM((GROUP, ROWS_OWN, REST), bf16),
        pltpu.VMEM((width, width), bf16),
        pltpu.VMEM((width, REST), bf16),
        pltpu.VMEM((ROWS_OWN, PACKED), bf16),
        pltpu.VMEM((chips, ROWS_OWN, width), bf16),
        pltpu.VMEM((chips, ROWS_OWN, QUERY), bf16),
        pltpu.VMEM((chips, ROWS_OWN, REST), bf16),
        pltpu.VMEM((stage_rows(ROWS_OWN), width), bf16),
        pltpu.VMEM((stage_rows(ROWS_OWN), QUERY), bf16),
        pltpu.VMEM((stage_rows(ROWS_OWN), REST), bf16),
        pltpu.VMEM((chips, count, width), bf16),
        pltpu.VMEM((chips, count, width), bf16),
        pltpu.VMEM((stage_rows(count), width), bf16),
        pltpu.VMEM(expert_terms.shape, bf16),
        pltpu.VMEM((stage_rows(expert_rows), width), bf16),
        pltpu.VMEM((expert_rows, width), bf16),
        pltpu.VMEM((2, 4 * positions, length), bf16),
        pltpu.VMEM((2, REPS, positions, LANES), bf16),
        pltpu.VMEM((2, REPS, positions, LANES), bf16),
        pltpu.VMEM((seqs, REPS, positions, 2 * KEY), bf16),
        pltpu.VMEM((seqs, stage_rows(positions), 2 * KEY), bf16),
        pltpu.VMEM((count, 2 * KEY), f32),
        pltpu.VMEM((count, QUERY), bf16),
        pltpu.VMEM((count, QUERY), bf16),
        pltpu.VMEM((count, width), f32),
        pltpu.VMEM((count, width), f32),
        pltpu.VMEM((SMALL, width), f32),
    ]
    return pl.pallas_call(
        kernel,
        out_shape=[
            jax.ShapeDtypeStruct((count, width), bf16),
            jax.ShapeDtypeStruct((count, width), bf16),
            jax.ShapeDtypeStruct((REPS, ROWS_OWN, PACKED), bf16),
            jax.ShapeDtypeStruct((REPS, expert_rows, width), bf16),
        ],
        in_specs=[IN_VMEM] * 4 + [ANY] + [IN_VMEM] * 7 + [ANY] * 4 + [IN_VMEM] * 2,
        out_specs=[IN_VMEM, IN_VMEM, ANY, ANY],
        scratch_shapes=scratch
        + sems(SUM_SEMS) * 7
        + sems(GATHER_SEMS) * 4
        + [
            pltpu.SemaphoreType.DMA((4,)),
            pltpu.SemaphoreType.DMA((chips,)),
            pltpu.SemaphoreType.DMA((2, 3)),
            pltpu.SemaphoreType.DMA((4,)),
        ],
        compiler_params=params(collective_id),
    )(
        returned, gates, middle, sent, dense, cotangent, tokens, attn_in, query_raw, key_raw,
        query_low, mixed, pairs, soft, out_terms, expert_terms, cosine, sine,
    )


def chunk_256(index):
    return pl.ds(pl.multiple_of(index * 256, 256), 256)


def rms_scale(values, gain):
    return values * lax.rsqrt(jnp.mean(values * values, axis=-1, keepdims=True) + norm_eps) * gain


def rotary_tables(positions, head_size):
    half_size = head_size // 2
    exponent = jnp.arange(half_size, dtype=f32) * (2.0 / head_size)
    frequency = rope_base ** (-exponent)
    angles = positions.astype(f32)[:, None] * frequency[None, :]
    cosine_table = jnp.concatenate([jnp.cos(angles), jnp.cos(angles)], axis=-1)
    sine_table = jnp.concatenate([jnp.sin(angles), jnp.sin(angles)], axis=-1)
    return (cosine_table, sine_table)


def rotate(values, cosine_table, sine_table):
    half_size = values.shape[-1] // 2
    turned = jnp.concatenate([-values[..., half_size:], values[..., :half_size]], axis=-1)
    return values * cosine_table[:, None, :] + turned * sine_table[:, None, :]


def piece_index(positions, starts):
    inside = (positions[:, None] >= starts[None, :]) & (positions[:, None] < starts[None, :] + PIC)
    labels = jnp.arange(1, starts.shape[0] + 1, dtype=jnp.int32)
    return jnp.sum(jnp.where(inside, labels[None, :], 0), axis=1) - 1


def allowed_mask(query_pos, key_pos, starts):
    query_piece = piece_index(query_pos, starts)
    key_piece = piece_index(key_pos, starts)
    causal = key_pos[None, :] <= query_pos[:, None]
    shared = (query_piece[:, None] == key_piece[None, :]) & (query_piece[:, None] >= 0)
    return causal | shared


def query_key(query_raw, key_raw, query_gain, key_gain, cosine_table, sine_table):
    row_count = query_raw.shape[0]
    query_rot = rotate(
        rms_scale(query_raw, query_gain).reshape(row_count, HEADS, HEAD_DIM),
        cosine_table,
        sine_table,
    )
    key_rot = rotate(
        rms_scale(key_raw, key_gain).reshape(row_count, KV_HEADS, HEAD_DIM),
        cosine_table,
        sine_table,
    )
    return (query_rot, key_rot)


def pack_rows(wide, router, gain_a, gain_q, gain_f, gain_k):
    rows = router.shape[0]
    short = jnp.concatenate([gain_k, jnp.zeros((rows - gain_k.shape[0],), gain_k.dtype)])
    small = jnp.concatenate(
        [router] + [v[:, None] for v in (gain_a, gain_q, gain_f, short)], axis=1
    )
    small = jnp.pad(small, ((0, 0), (0, SMALL - small.shape[1])))
    return jnp.concatenate(list(wide[:3]) + [small, wide[3]], axis=1)


def shards(
    tokens,
    cotangent,
    routes,
    picture_starts,
    attn_gain,
    query_weight,
    key_weight,
    value_weight,
    query_gain,
    key_gain,
    output_weight,
    ffn_gain,
    router_weight,
    expert_in,
    expert_down,
):
    seqs, positions, width = tokens.shape
    top = routes.shape[2]
    count = seqs * positions
    length = positions * REPS
    experts = GROUP
    group = HEADS // KV_HEADS
    query_width = HEADS * HEAD_DIM
    kv_width = KV_HEADS * HEAD_DIM
    score_scale = HEAD_DIM ** (-0.5)
    rows_own = query_weight.shape[0]
    kgain_own = key_gain.shape[0]
    shard = lax.axis_index("shard")
    query_pos = lax.axis_index("rep") * positions + jnp.arange(positions, dtype=jnp.int32)
    key_pos = jnp.arange(length, dtype=jnp.int32)

    packed = pack_rows(
        (query_weight, key_weight, value_weight, output_weight),
        router_weight,
        attn_gain,
        query_gain,
        ffn_gain,
        key_gain,
    )
    allowed = jax.vmap(lambda starts: allowed_mask(query_pos, key_pos, starts))(picture_starts)
    bias = jnp.where(allowed, 0.0, masked_score).astype(f32)
    route_ids = routes.reshape(count, top)
    picked = jnp.sum(
        (route_ids[:, :, None] == jnp.arange(SMALL)[None, None, :]).astype(f32), axis=1
    )
    cosine_one, sine_one = rotary_tables(query_pos, HEAD_DIM)
    sign = jnp.where(jnp.arange(HEAD_DIM) < HEAD_DIM // 2, -1.0, 1.0).astype(f32)
    cosine_two = jnp.tile(cosine_one, (1, 2))
    sine_two = jnp.tile(sine_one * sign[None, :], (1, 2))
    (
        dense, grad_all, pairs_all, soft_low,
        attn_in, query_raw, key_raw, query_low, mixed_low, middle, sent, gates,
    ) = front_call(
        1,
        tokens.reshape(count, width),
        cotangent.reshape(count, width),
        packed,
        cosine_two,
        sine_two,
        bias,
        picked,
    )
    out_terms, returned, expert_terms = moe_call(
        3, sent, grad_all, expert_in[0], expert_down[0]
    )
    block_out, tokens_grad, dense_all, expert_all = back_call(
        2, returned, gates, middle, sent, dense, cotangent.reshape(count, width),
        tokens.reshape(count, width), attn_in, query_raw, key_raw, query_low, mixed_low, pairs_all,
        soft_low, out_terms, expert_terms, cosine_two, sine_two,
    )
    dense_sum = jnp.sum(dense_all.astype(f32), axis=0)
    expert_all = expert_all.reshape(-1, width)
    inner_rows = expert_in.shape[1]
    expert_in_grad = expert_all[:inner_rows].astype(f32)[None]
    expert_down_grad = expert_all[inner_rows:].astype(f32)[None]
    return (
        block_out.reshape(tokens.shape),
        tokens_grad.reshape(tokens.shape),
        dense_sum[:, AT_S + experts],
        dense_sum[:, :AT_K],
        dense_sum[:, AT_K:AT_V],
        dense_sum[:, AT_V:AT_S],
        dense_sum[:, AT_S + experts + 1],
        dense_sum[:kgain_own, AT_S + experts + 3],
        dense_sum[:, AT_O:],
        dense_sum[:, AT_S + experts + 2],
        dense_sum[:, AT_S : AT_S + experts],
        expert_in_grad,
        expert_down_grad,
    )


def solution(mesh):
    by_tokens = P("shard", "rep", None)
    rows, line, block = P("shard", None), P("shard"), P("shard", None, None)
    in_specs = (
        by_tokens, by_tokens, by_tokens, rows, line, rows, rows, rows, line, line, rows, line, rows, block, block,
    )
    out_specs = (
        by_tokens, by_tokens, line, rows, rows, rows, line, line, rows, line, rows, block, block,
    )
    return jax.shard_map(shards, mesh=mesh, in_specs=in_specs, out_specs=out_specs, check_vma=False)
```

```python
import jax
import jax.numpy as jnp
from jax import lax
from jax.experimental import pallas as pl
from jax.experimental.pallas import tpu as pltpu
from jax.sharding import PartitionSpec as P

HEADS = 16
KV_HEADS = 8
HEAD_DIM = 64
PIC = 256
RING = 4
GROUP = 16
REPS = 8
VMEM_LIMIT = 62 << 20

norm_eps = 1e-06
rope_base = 10000.0
masked_score = -1e30

bf16 = jnp.bfloat16
f32 = jnp.float32


class Place:
    def __init__(self):
        shard = lax.axis_index("shard")
        rep = lax.axis_index("rep")
        self.shard, self.rep = shard, rep
        core = lax.rem(shard, 2)
        ring_z = lax.rem(lax.div(shard, 2), RING)
        y_hi = lax.div(shard, 8)
        ring_x = lax.rem(rep, RING)
        y_lo = lax.div(rep, RING)
        self.core = core

        def shard_of(hi, z, c):
            return (hi * RING + z) * 2 + c

        def rep_of(lo, x):
            return lo * RING + x

        def up(v):
            return lax.rem(v + 1, RING)

        def down(v):
            return lax.rem(v + RING - 1, RING)

        self.twin = (shard_of(y_hi, ring_z, 1 - core), rep)
        self.tokens = Axes(
            y_hi,
            ring_z,
            (shard_of(y_hi, up(ring_z), core), rep),
            (shard_of(y_hi, down(ring_z), core), rep),
            (shard_of(1 - y_hi, ring_z, core), rep_of(1 - y_lo, ring_x)),
        )
        self.copies = Axes(
            y_lo,
            ring_x,
            (shard, rep_of(y_lo, up(ring_x))),
            (shard, rep_of(y_lo, down(ring_x))),
            (shard, rep_of(1 - y_lo, ring_x)),
        )


class Axes:
    def __init__(self, side, spot, ahead, behind, across):
        self.side, self.spot = side, spot
        self.ahead, self.behind, self.across = ahead, behind, across
        sides = (side, 1 - side)
        spots = [lax.rem(spot + step, RING) for step in range(RING)]
        self.places = [[(sides[flip], spots[step]) for step in range(RING)] for flip in range(2)]

    def at(self, flip, step):
        return self.places[flip][step % RING]

    def neighbours(self):
        return [self.ahead, self.behind, self.across]


def greet(devices):
    barrier = pltpu.get_barrier_semaphore()
    for device in devices:
        pl.semaphore_signal(barrier, inc=1, device_id=device, device_id_type=pl.DeviceIdType.MESH)
    pl.semaphore_wait(barrier, len(devices))


class Line:
    def __init__(self, send_sem, recv_sem):
        self.send_sem, self.recv_sem = send_sem, recv_sem
        self.sent = []

    def copy(self, index, source, target, device):
        return pltpu.make_async_remote_copy(
            src_ref=source(),
            dst_ref=target(),
            send_sem=self.send_sem.at[index],
            recv_sem=self.recv_sem.at[index],
            device_id=device,
            device_id_type=pl.DeviceIdType.MESH,
        )

    def send(self, index, source, target, device):
        self.copy(index, source, target, device).start()
        self.sent.append((index, source, target, device))

    def take(self, index, target, device):
        self.copy(index, target, target, device).wait_recv()

    def finish(self):
        for sent in self.sent:
            self.copy(*sent).wait_send()


def abreast(*parts):
    running = list(parts)
    while running:
        for part in list(running):
            try:
                next(part)
            except StopIteration:
                running.remove(part)


GATHER_SEMS = 20


def gather_parts(axes, line, own, block, rows, local_sem, twin=None, twin_later=False):
    half, quarter = rows // 2, rows // 4
    mine, back, front, far = axes.at(0, 0), axes.at(0, -1), axes.at(0, 1), axes.at(0, 2)
    pair, pair_back, pair_front, pair_far = (axes.at(1, n) for n in (0, -1, 1, 2))
    ahead, behind, across = axes.ahead, axes.behind, axes.across

    def rows_of(which, low=0, count=rows, other=False):
        return lambda: block(which, low, count, other)

    def first(index, device):
        line.send(index, lambda: own, rows_of(mine), device)

    def relay(index, device, which, low=0, count=rows):
        line.send(index, rows_of(which, low, count), rows_of(which, low, count), device)

    def share(index, which):
        if twin is not None:
            relay(12 + index, twin, which)

    def keep():
        return pltpu.make_async_copy(own, block(mine, 0, rows), local_sem)

    keep().start()
    if twin is not None:
        first(12, twin)
    first(0, ahead)
    first(1, behind)
    first(2, across)
    keep().wait()
    yield
    line.take(0, rows_of(back), ahead)
    relay(3, ahead, back, 0, half)
    relay(4, across, back, half, half)
    share(1, back)
    line.take(1, rows_of(front), behind)
    relay(5, behind, front, half, half)
    relay(6, across, front, half, half)
    share(2, front)
    line.take(2, rows_of(pair), across)
    relay(7, ahead, pair, 0, half)
    relay(8, behind, pair, 0, half)
    share(3, pair)
    yield
    line.take(3, rows_of(far, 0, half), ahead)
    line.take(5, rows_of(far, half, half), behind)
    relay(9, across, far, half, half)
    share(4, far)
    line.take(7, rows_of(pair_back, 0, half), ahead)
    relay(10, ahead, pair_back, 0, quarter)
    line.take(8, rows_of(pair_front, 0, half), behind)
    relay(11, behind, pair_front, quarter, quarter)
    line.take(4, rows_of(pair_back, half, half), across)
    share(5, pair_back)
    line.take(6, rows_of(pair_front, half, half), across)
    share(6, pair_front)
    yield
    line.take(10, rows_of(pair_far, 0, quarter), ahead)
    line.take(11, rows_of(pair_far, quarter, quarter), behind)
    line.take(9, rows_of(pair_far, half, half), across)
    share(7, pair_far)
    yield
    if twin is not None and not twin_later:
        for index, which in enumerate(gather_order(axes)):
            line.take(12 + index, rows_of(which, other=True), twin)
    line.finish()


SUM_SEMS = 20


def add_rows(target, source, rows):
    step = 16
    count = rows // step

    def body(index, carry):
        at = pl.ds(pl.multiple_of(index * step, step), step)
        target[at] = target[at] + source[at]
        return carry

    lax.fori_loop(0, count, body, 0)


def stage_rows(rows):
    return 7 * rows


def gather_order(axes):
    return [axes.at(*v) for v in ((0, 0), (0, -1), (0, 1), (1, 0), (0, 2), (1, -1), (1, 1), (1, 2))]


def sum_order(axes):
    return [axes.at(*v) for v in ((1, 2), (0, 2), (1, -1), (1, 1), (0, -1), (0, 1), (1, 0), (0, 0))]


def sum_parts(axes, line, part, stage, rows, result, twin=None, store=None):
    half, quarter = rows // 2, rows // 4
    mine, back, front, far = axes.at(0, 0), axes.at(0, -1), axes.at(0, 1), axes.at(0, 2)
    pair, pair_back, pair_front, pair_far = (axes.at(1, n) for n in (0, -1, 1, 2))
    ahead, behind, across = axes.ahead, axes.behind, axes.across
    order = sum_order(axes)
    offsets, used = {}, 0
    for name, size in (
        ("Y0", half), ("M0", quarter), ("P0", quarter), ("M1", half), ("Y1", half), ("Y2", half),
        ("P1", half), ("M2", half), ("P2", half), ("M3", rows), ("P3", rows), ("Y3", rows),
    ):
        offsets[name] = (used, size, len(offsets))
        used += size

    def landing(name):
        low, size, _ = offsets[name]
        return lambda: stage.at[pl.ds(low, size)]

    def send(name, which, low, device):
        _, size, index = offsets[name]
        line.send(index, lambda: part(which, low, size), landing(name), device)

    def add(name, which, low, device):
        _, size, index = offsets[name]
        line.take(index, landing(name), device)
        add_rows(part(which, low, size), landing(name)(), size)

    def join(*places):
        if twin is not None:
            for place in places:
                line.take(12 + place, lambda: twin[2](order[place]), twin[0])
                add_rows(part(order[place], 0, rows), twin[2](order[place]), rows)

    def hand(*places):
        if twin is not None:
            for place in places:
                which = order[place]
                line.send(
                    12 + place, lambda w=which: twin[1](w), lambda w=which: twin[2](w), twin[0]
                )

    hand(0, 1, 2, 3)
    yield
    join(0)
    send("Y0", pair_far, half, across)
    send("M0", pair_far, 0, behind)
    send("P0", pair_far, quarter, ahead)
    join(1)
    send("M1", far, 0, behind)
    join(2)
    send("Y1", pair_back, half, across)
    join(3)
    send("Y2", pair_front, half, across)
    yield
    hand(4, 5, 6, 7)
    add("M0", pair_back, 0, behind)
    send("M2", pair_back, 0, behind)
    add("P0", pair_front, quarter, ahead)
    send("P2", pair_front, 0, ahead)
    add("Y0", far, half, across)
    send("P1", far, half, ahead)
    yield
    join(4, 5, 6, 7)
    add("M1", back, 0, behind)
    add("Y1", back, half, across)
    send("M3", back, 0, behind)
    add("M2", pair, 0, behind)
    add("P2", pair, 0, ahead)
    send("Y3", pair, 0, across)
    add("P1", front, half, ahead)
    add("Y2", front, half, across)
    send("P3", front, 0, ahead)
    yield
    for name, device in (("M3", behind), ("P3", ahead), ("Y3", across)):
        line.take(offsets[name][2], landing(name), device)
    step = 16

    def body(index, carry):
        low = pl.multiple_of(index * step, step)
        total = part(mine, low, step)[...].astype(f32)
        for name in ("M3", "P3", "Y3"):
            total = total + stage[pl.ds(offsets[name][0] + low, step)].astype(f32)
        if store is None:
            result[pl.ds(low, step)] = total.astype(result.dtype)
        else:
            store(low, step, total)
        return carry

    lax.fori_loop(0, rows // step, body, 0)
    line.finish()


def sems(count):
    return [pltpu.SemaphoreType.DMA((count,)), pltpu.SemaphoreType.DMA((count,))]


ANY = pl.BlockSpec(memory_space=pl.ANY)
IN_VMEM = pl.BlockSpec(memory_space=pltpu.VMEM)


def params(collective_id):
    return pltpu.CompilerParams(
        collective_id=collective_id, has_side_effects=True, vmem_limit_bytes=VMEM_LIMIT
    )


def dot(a, b):
    return jnp.dot(a, b, preferred_element_type=f32)


def dot_nt(a, b):
    return lax.dot_general(a, b, (((1,), (1,)), ((), ())), preferred_element_type=f32)


def dot_tn(a, b):
    return lax.dot_general(a, b, (((0,), (0,)), ((), ())), preferred_element_type=f32)


def pick(index, values):
    chosen = values[-1]
    for at in range(len(values) - 2, -1, -1):
        chosen = jnp.where(index == at, values[at], chosen)
    return chosen


def moe_call(collective_id, sent, rows_first, grad_all, inner, outer):
    count, columns = sent.shape
    width = inner.shape[0]
    hidden_width = outer.shape[0]
    small = columns - width
    half = count // 2
    chips = GROUP // 2
    wide = 4

    def kernel(
        sent_ref, first_ref, grad_ref, inner_ref, outer_ref,
        returned, out_sum, back_terms, out_terms, terms,
        rows_in, grads, hidden, back_gu, back, back_staged, back_stage, out, out_staged, out_stage,
        back_box, out_box, term_box,
        gs, gr, bs, br, os, orr, own_sem, load_sem, box_sem, term_sem,
    ):
        place = Place()
        axes, core, shard = place.tokens, place.core, place.shard
        gather_line = Line(gs, gr)

        def chip_of(which):
            return which[0] * RING + which[1]

        def blocks(which, other=False):
            return chip_of(which) * 2 + ((1 - core) if other else core)

        gather = gather_parts(
            axes, gather_line, sent_ref.at[pl.ds(half, half)],
            lambda which, low, n, other=False: rows_in.at[1, blocks(which, other), pl.ds(low, n)],
            half, own_sem, place.twin, twin_later=True,
        )

        def sum_of(terms_ref, staged, stage, result, send_sem, recv_sem):
            return sum_parts(
                axes, Line(send_sem, recv_sem),
                lambda which, low, n: terms_ref.at[blocks(which), pl.ds(low, n)],
                stage, half, result,
                (place.twin, lambda which: terms_ref.at[blocks(which, True)],
                 lambda which: staged.at[chip_of(which)]),
            )

        back_sum = sum_of(back, back_staged, back_stage, returned, bs, br)
        outs_sum = sum_of(out, out_staged, out_stage, out_sum, os, orr)

        def loads(t):
            at = pl.ds(t * wide, wide)
            return [
                pltpu.make_async_copy(first_ref.at[at], rows_in.at[0, at], load_sem.at[t, 0]),
                pltpu.make_async_copy(
                    grad_ref.at[at, pl.ds(0, half)], grads.at[0, at], load_sem.at[t, 1]
                ),
            ]

        second_grads = pltpu.make_async_copy(
            grad_ref.at[:, pl.ds(half, half)], grads.at[1], load_sem.at[GROUP // wide, 0]
        )

        def box_copies(chip, slot):
            at = pl.ds(chip * 2, 2)
            return [
                pltpu.make_async_copy(back_box.at[slot], back_terms.at[at], box_sem.at[slot, 0]),
                pltpu.make_async_copy(out_box.at[slot], out_terms.at[at], box_sem.at[slot, 1]),
            ]

        def tile(chunk, first, number):
            rows_count = number * half
            at = pl.ds(first, number)
            lanes = lane_of((rows_count, small))
            is_high, is_rest = lanes == shard, lanes == shard + GROUP
            row_block = rows_in[chunk, at].reshape(rows_count, columns)
            gate = jnp.sum(
                jnp.where(is_high | is_rest, row_block[:, width:].astype(f32), 0.0),
                axis=1, keepdims=True,
            )
            gate_up = dot(row_block[:, :width], inner_ref[...])
            gate_part, up_part = gate_up[:, :hidden_width], gate_up[:, hidden_width:]
            sigmoid = 1.0 / (1.0 + jnp.exp(-gate_part))
            active = gate_part * sigmoid
            product = active * up_part
            hidden_low = product.astype(bf16)
            hidden[chunk, at] = hidden_low.reshape(number, half, hidden_width)
            out_rows = (gate * dot(hidden_low, outer_ref[...])).astype(bf16)
            grad = grads[chunk, at].reshape(rows_count, width)
            grad_hidden = dot_nt(grad, outer_ref[...])
            grad_gate = jnp.sum(grad_hidden * product, axis=1, keepdims=True)
            grad_hidden = grad_hidden * gate
            grad_gate_up = jnp.concatenate(
                [
                    grad_hidden * up_part * sigmoid * (1.0 + gate_part * (1.0 - sigmoid)),
                    grad_hidden * active,
                ],
                axis=1,
            ).astype(bf16)
            back_gu[chunk, at] = grad_gate_up.reshape(number, half, 2 * hidden_width)
            grads[chunk, at] = (gate * grad.astype(f32)).astype(bf16).reshape(number, half, width)
            grad_rows = dot_nt(grad_gate_up, inner_ref[...]).astype(bf16)
            high = grad_gate.astype(bf16).astype(f32)
            tail = jnp.where(is_high, high, jnp.where(is_rest, grad_gate - high, 0.0)).astype(bf16)
            return (
                out_rows.reshape(number, half, width),
                grad_rows.reshape(number, half, width),
                tail.reshape(number, half, small),
            )

        for t in range(GROUP // wide):
            for load in loads(t):
                load.start()
        second_grads.start()
        greet(axes.neighbours() + [place.twin])
        next(gather)

        def first_tiles(t, carry):
            hooks(t, ((2, lambda: next(gather)),))
            for load in loads(t):
                load.wait()
            at = pl.ds(t * wide, wide)
            out_rows, grad_rows, tail = tile(0, t * wide, wide)
            out[at] = out_rows
            back[at, :, pl.ds(0, width)] = grad_rows
            back[at, :, pl.ds(width, small)] = tail
            return carry

        lax.fori_loop(0, GROUP // wide, first_tiles, 0)
        next(back_sum)
        second_grads.wait()
        chips1 = [chip_of(which) for which in gather_order(axes)]

        def second_tiles(t, carry):
            hooks(
                t,
                (
                    (1, lambda: next(back_sum)),
                    (2, lambda: next(gather)),
                    (3, lambda: next(outs_sum)),
                    (4, lambda: next(back_sum)),
                    (5, lambda: next(outs_sum)),
                    (7, lambda: next(gather)),
                ),
            )
            chip, slot = pick(t, chips1), lax.rem(t, 2)
            gather_line.take(12 + t, lambda: rows_in.at[1, chip * 2 + 1 - core], place.twin)
            out_rows, grad_rows, tail = tile(1, chip * 2, 2)

            @pl.when(t >= 2)
            def _():
                for copy in box_copies(chip, slot):
                    copy.wait()

            out_box[slot] = out_rows
            back_box[slot, :, :, pl.ds(0, width)] = grad_rows
            back_box[slot, :, :, pl.ds(width, small)] = tail
            for copy in box_copies(chip, slot):
                copy.start()
            return carry

        lax.fori_loop(0, chips, second_tiles, 0)

        def term_copy(low, slot):
            return pltpu.make_async_copy(
                term_box.at[slot], terms.at[pl.ds(low, 256)], term_sem.at[slot]
            )

        every = 2 * GROUP * half

        def keep(index, low, value):
            slot = lax.rem(index, 2)

            @pl.when(index >= 2)
            def _():
                term_copy(low, slot).wait()

            term_box[slot] = value.astype(bf16)
            term_copy(low, slot).start()

        downs = hidden_width // 256

        def down_terms(index, carry):
            hooks(index, ((0, lambda: next(back_sum)), (1, lambda: next(outs_sum))))
            at = chunk_256(index)
            value = dot_tn(hidden[:, :, :, at].reshape(every, 256), grads[...].reshape(every, width))
            keep(index, pl.multiple_of(width + index * 256, 256), value)
            return carry

        lax.fori_loop(0, downs, down_terms, 0)

        def inner_terms(index, carry):
            hooks(
                index,
                (
                    (1, lambda: drained(back_sum)),
                    (2, lambda: next(outs_sum)),
                ),
            )
            at = chunk_256(index)
            value = dot_tn(
                rows_in[:, :, :, at].reshape(every, 256),
                back_gu[...].reshape(every, 2 * hidden_width),
            )
            keep(index + downs, pl.multiple_of(index * 256, 256), value)
            return carry

        lax.fori_loop(0, width // 256, inner_terms, 0)
        drained(outs_sum)
        drained(gather)
        for slot in range(2):
            for copy in box_copies(0, slot):
                copy.wait()
            term_copy(0, slot).wait()

    term_rows = width + hidden_width
    return pl.pallas_call(
        kernel,
        out_shape=[
            jax.ShapeDtypeStruct((half, columns), f32),
            jax.ShapeDtypeStruct((half, width), f32),
            jax.ShapeDtypeStruct((GROUP, half, columns), bf16),
            jax.ShapeDtypeStruct((GROUP, half, width), bf16),
            jax.ShapeDtypeStruct((term_rows, width), bf16),
        ],
        in_specs=[ANY, ANY, ANY, IN_VMEM, IN_VMEM],
        out_specs=[IN_VMEM, IN_VMEM, ANY, ANY, ANY],
        scratch_shapes=[
            pltpu.VMEM((2, GROUP, half, columns), bf16),
            pltpu.VMEM((2, GROUP, half, width), bf16),
            pltpu.VMEM((2, GROUP, half, hidden_width), bf16),
            pltpu.VMEM((2, GROUP, half, 2 * hidden_width), bf16),
            pltpu.VMEM((GROUP, half, columns), bf16),
            pltpu.VMEM((chips, half, columns), bf16),
            pltpu.VMEM((stage_rows(half), columns), bf16),
            pltpu.VMEM((GROUP, half, width), bf16),
            pltpu.VMEM((chips, half, width), bf16),
            pltpu.VMEM((stage_rows(half), width), bf16),
            pltpu.VMEM((2, 2, half, columns), bf16),
            pltpu.VMEM((2, 2, half, width), bf16),
            pltpu.VMEM((2, 256, width), bf16),
        ]
        + sems(GATHER_SEMS)
        + sems(SUM_SEMS) * 2
        + [
            pltpu.SemaphoreType.DMA,
            pltpu.SemaphoreType.DMA((GROUP // wide + 1, 2)),
            pltpu.SemaphoreType.DMA((2, 2)),
            pltpu.SemaphoreType.DMA((2,)),
        ],
        compiler_params=params(collective_id),
    )(sent, rows_first, grad_all, inner, outer)


WIDTH = 1024
QUERY = HEADS * HEAD_DIM
KEY = KV_HEADS * HEAD_DIM
EXPERTS = 16
SMALL = 128
LANES = 128
AT_K = QUERY
AT_V = AT_K + KEY
AT_S = AT_V + KEY
AT_O = AT_S + SMALL
PACKED = AT_O + WIDTH
ROWS_OWN = WIDTH // GROUP
KGAIN_OWN = KEY // GROUP
HEAD_PAIRS = KV_HEADS // 2
REST = 2 * KEY + SMALL


def drained(part):
    for _ in part:
        pass


def hooks(index, steps):
    for at, step in steps:
        pl.when(index == at)(step)


def chunk_256(index):
    return pl.ds(pl.multiple_of(index * 256, 256), 256)


def root_mean(values):
    return lax.rsqrt(jnp.mean(values * values, axis=1, keepdims=True) + norm_eps)


def lane_of(shape):
    return lax.broadcasted_iota(jnp.int32, shape, 1)


def turned(values, cosine, sine):
    first = lax.rem(lane_of(values.shape), HEAD_DIM) < HEAD_DIM // 2
    swapped = jnp.where(
        first, pltpu.roll(values, LANES - HEAD_DIM // 2, 1), pltpu.roll(values, HEAD_DIM // 2, 1)
    )
    return values * cosine + swapped * sine


def short_rows():
    row = lax.broadcasted_iota(jnp.int32, (WIDTH, KEY), 0)
    column = lax.broadcasted_iota(jnp.int32, (WIDTH, KEY), 1)
    same = (lax.div(row, ROWS_OWN) == lax.div(column, KGAIN_OWN)) & (
        lax.rem(row, ROWS_OWN) == lax.rem(column, KGAIN_OWN)
    )
    return jnp.where(same, 1.0, 0.0).astype(bf16)


def gain_rows(small):
    rows = jnp.transpose(small.astype(f32))
    gain_k = dot(rows[EXPERTS : EXPERTS + 8].astype(bf16), short_rows())[3:4]
    return rows[EXPERTS : EXPERTS + 1], rows[EXPERTS + 1 : EXPERTS + 2], rows[EXPERTS + 2 : EXPERTS + 3], gain_k


def four_heads(chunk_a, chunk_b):
    low = lane_of(chunk_a.shape) < HEAD_DIM
    zero = jnp.zeros_like(chunk_a)
    return jnp.concatenate(
        [
            jnp.where(low, chunk_a, zero),
            jnp.where(low, pltpu.roll(chunk_a, HEAD_DIM, 1), zero),
            jnp.where(low, zero, pltpu.roll(chunk_b, HEAD_DIM, 1)),
            jnp.where(low, zero, chunk_b),
        ],
        axis=0,
    )


def two_chunks(blocks):
    rows = blocks.shape[0] // 4
    one, two, three, four = (blocks[n * rows : (n + 1) * rows] for n in range(4))
    low = lane_of(one.shape) < HEAD_DIM
    return (
        jnp.where(low, one, pltpu.roll(two, HEAD_DIM, 1)),
        jnp.where(low, pltpu.roll(three, HEAD_DIM, 1), four),
    )


def chunk_at(index, base=0):
    return pl.ds(pl.multiple_of(base + index * LANES, LANES), LANES)


def front_call(collective_id, tokens, cotangent, weights_own, small_own, cosine, sine, routes, starts):
    count, width = tokens.shape
    seqs = starts.shape[0]
    positions = count // seqs
    length = REPS * positions
    score_scale = HEAD_DIM ** (-0.5)
    sent_width = width + SMALL

    def kernel(
        starts_ref, tokens_ref, grad_ref, query_w, key_w, value_w, output_w, small_ref,
        cos_ref, sin_ref, routes_ref,
        dense_out, grad_all, pairs_out, soft_out, rows_first,
        attn_in, query_raw, key_raw, query_low, mixed, middle, sent, gates_out,
        packed, dense, pairs, pair_own, soft_box, bias_box,
        ws0, wr0, ws1, wr1, ws2, wr2, gs, gr, ks0, kr0, ks1, kr1, rs, rr, own_sem, out_sem, soft_sem, pack_sem,
    ):
        place = Place()
        core = place.core
        packing = [
            pltpu.make_async_copy(
                source, packed.at[:, pl.ds(low, source.shape[1])], pack_sem.at[index]
            )
            for index, (source, low) in enumerate(
                ((key_w, AT_K), (value_w, AT_V), (small_ref, AT_S), (query_w, 0), (output_w, AT_O))
            )
        ]
        for copy in packing:
            copy.start()

        def token_block(index, low, size):
            def block(which, row, n, other=False):
                at = (which[0] * RING + which[1]) * 2 + ((1 - core) if other else core)
                return dense.at[at, pl.ds(row, n), pl.ds(low, size)]

            return block

        def weight_gather(index, low, size, send_sem, recv_sem):
            return gather_parts(
                place.tokens, Line(send_sem, recv_sem), packed.at[:, pl.ds(low, size)],
                token_block(index, low, size), ROWS_OWN, own_sem.at[index], place.twin,
            )

        def rows_of(target):
            def block(which, row, n, other=False):
                at = (which[0] * RING + which[1]) * 2 + ((1 - core) if other else core)
                return target.at[at, pl.ds(row, n)]

            return block

        def pair_gather(seq, send_sem, recv_sem):
            def block(which, row, n, other=False):
                return pairs.at[seq, which[0] * RING + which[1], pl.ds(row, n)]

            return gather_parts(
                place.copies, Line(send_sem, recv_sem),
                pair_own.at[pl.ds(seq * positions, positions)], block, positions, own_sem.at[3 + seq],
            )

        def soft_copy(seq, index, slot):
            return pltpu.make_async_copy(
                soft_box.at[slot], soft_out.at[seq, index], soft_sem.at[slot]
            )

        rest_gather = weight_gather(0, AT_K, REST, ws0, wr0)
        query_gather = weight_gather(1, 0, QUERY, ws1, wr1)
        output_gather = weight_gather(2, AT_O, WIDTH, ws2, wr2)
        grads = gather_parts(
            place.tokens, Line(gs, gr), grad_ref, rows_of(grad_all), count, own_sem.at[5], place.twin
        )
        first_rows = gather_parts(
            place.tokens, Line(rs, rr), sent.at[pl.ds(0, positions)], rows_of(rows_first), positions,
            own_sem.at[6], place.twin,
        )
        pair_gathers = [pair_gather(0, ks0, kr0), pair_gather(1, ks1, kr1)]

        greet(place.tokens.neighbours() + place.copies.neighbours() + [place.twin])
        for copy in packing:
            copy.wait()
        next(rest_gather)
        next(query_gather)
        inputs = tokens_ref[...].astype(f32)
        middle[...] = inputs * root_mean(inputs)
        next(rest_gather)
        next(query_gather)
        next(output_gather)
        query_at = place.rep * positions + lax.broadcasted_iota(jnp.int32, (positions, 1), 0)
        key_at = lax.broadcasted_iota(jnp.int32, (1, length), 1)
        for seq in range(seqs):
            allowed = key_at <= query_at
            for piece in range(starts_ref.shape[1]):
                start = starts_ref[seq, piece]
                query_inside = (query_at >= start) & (query_at < start + PIC)
                key_inside = (key_at >= start) & (key_at < start + PIC)
                allowed = allowed | (query_inside & key_inside)
            bias_box[seq] = jnp.where(allowed, 0.0, masked_score)
        next(rest_gather)
        next(query_gather)
        next(output_gather)
        drained(rest_gather)

        def weights(low, size):
            return dense[:, :, pl.ds(low, size)].reshape(width, size)

        small = weights(AT_S, SMALL)
        gain_a, gain_q, gain_f, gain_k = gain_rows(small)
        rows = (middle[...] * gain_a).astype(bf16)
        attn_in[...] = rows
        cos2 = jnp.concatenate([cos_ref[...]] * seqs, axis=0)
        sin2 = jnp.concatenate([sin_ref[...]] * seqs, axis=0)
        raw = dot(rows, weights(AT_K, KEY))
        key_raw[...] = raw
        scaled = raw * root_mean(raw) * gain_k
        for chunk in range(KEY // LANES):
            at = slice(chunk * LANES, (chunk + 1) * LANES)
            pair_own[:, at] = turned(scaled[:, at], cos2, sin2).astype(bf16)
        pair_own[:, KEY:] = dot(rows, weights(AT_V, KEY)).astype(bf16)
        next(pair_gathers[0])
        drained(query_gather)
        next(output_gather)
        next(grads)
        raw = dot(rows, weights(0, QUERY))
        query_raw[...] = raw
        scaled = raw * root_mean(raw) * gain_q
        for chunk in range(QUERY // LANES):
            at = slice(chunk * LANES, (chunk + 1) * LANES)
            query_low[:, at] = turned(scaled[:, at], cos2, sin2).astype(bf16)
        next(pair_gathers[0])
        next(pair_gathers[1])
        drained(output_gather)
        dense_copy = pltpu.make_async_copy(dense, dense_out, out_sem.at[0])
        dense_copy.start()
        next(pair_gathers[0])
        next(pair_gathers[1])
        drained(pair_gathers[0])
        next(grads)

        def attend(seq, index, slot, wait_first):
            rows_at = pl.ds(seq * positions, positions)
            queries = four_heads(
                query_low[rows_at, chunk_at(2 * index)].astype(f32),
                query_low[rows_at, chunk_at(2 * index + 1)].astype(f32),
            )
            queries = (queries * score_scale).astype(bf16)
            keys = pairs[seq, :, :, chunk_at(index)].reshape(length, LANES)
            scores = dot_nt(queries, keys).reshape(4, positions, length) + bias_box[seq][None]
            scores = scores.reshape(4 * positions, length)
            raised = jnp.exp(scores - jnp.max(scores, axis=1, keepdims=True))
            soft = (raised * (1.0 / jnp.sum(raised, axis=1, keepdims=True))).astype(bf16)

            @pl.when(wait_first)
            def _():
                soft_copy(seq, index, slot).wait()

            soft_box[slot] = soft
            soft_copy(seq, index, slot).start()
            values = pairs[seq, :, :, chunk_at(index, KEY)].reshape(length, LANES)
            chunk_a, chunk_b = two_chunks(dot(soft, values))
            mixed[rows_at, chunk_at(2 * index)] = chunk_a.astype(bf16)
            mixed[rows_at, chunk_at(2 * index + 1)] = chunk_b.astype(bf16)

        def features(seq):
            at = pl.ds(seq * positions, positions)
            total = tokens_ref[at].astype(f32) + dot(mixed[at], weights(AT_O, WIDTH))
            middle[at] = total
            ffn_in = (total * root_mean(total) * gain_f).astype(bf16)
            sent[at, pl.ds(0, width)] = ffn_in
            lanes = lane_of((positions, SMALL))
            named = routes_ref[at]
            chosen = lanes == named[:, :1]
            for choice in range(1, named.shape[1]):
                chosen = chosen | (lanes == named[:, choice : choice + 1])
            logits = jnp.where(chosen, dot(ffn_in, small), masked_score)
            raised = jnp.exp(logits - jnp.max(logits, axis=1, keepdims=True))
            gates = raised * (1.0 / jnp.sum(raised, axis=1, keepdims=True))
            gates = jnp.where(chosen, gates, 0.0)
            gates_out[at] = gates
            high = gates.astype(bf16).astype(f32)
            tail = high + pltpu.roll(gates - high, EXPERTS, 1)
            sent[at, pl.ds(width, SMALL)] = tail.astype(bf16)

        def first_heads(index, carry):
            hooks(index, ((2, lambda: next(pair_gathers[1])),))
            attend(0, index, lax.rem(index, 2), index >= 2)
            return carry

        lax.fori_loop(0, HEAD_PAIRS, first_heads, 0)
        features(0)
        next(first_rows)
        drained(pair_gathers[1])
        pairs_copy = pltpu.make_async_copy(pairs, pairs_out, out_sem.at[1])
        pairs_copy.start()
        next(grads)

        def second_heads(index, carry):
            hooks(
                index,
                (
                    (2, lambda: next(grads)),
                    (3, lambda: next(first_rows)),
                ),
            )
            attend(1, index, lax.rem(index, 2), index >= 0)
            return carry

        lax.fori_loop(0, HEAD_PAIRS, second_heads, 0)
        features(1)
        next(first_rows)
        drained(grads)
        drained(first_rows)
        dense_copy.wait()
        pairs_copy.wait()
        for slot in range(2):
            soft_copy(1, 0, slot).wait()

    return pl.pallas_call(
        kernel,
        out_shape=[
            jax.ShapeDtypeStruct((GROUP, ROWS_OWN, PACKED), bf16),
            jax.ShapeDtypeStruct((GROUP, count, width), bf16),
            jax.ShapeDtypeStruct((seqs, REPS, positions, 2 * KEY), bf16),
            jax.ShapeDtypeStruct((seqs, HEAD_PAIRS, 4 * positions, length), bf16),
            jax.ShapeDtypeStruct((GROUP, positions, sent_width), bf16),
            jax.ShapeDtypeStruct((count, width), bf16),
            jax.ShapeDtypeStruct((count, QUERY), f32),
            jax.ShapeDtypeStruct((count, KEY), f32),
            jax.ShapeDtypeStruct((count, QUERY), bf16),
            jax.ShapeDtypeStruct((count, QUERY), bf16),
            jax.ShapeDtypeStruct((count, width), f32),
            jax.ShapeDtypeStruct((count, width + SMALL), bf16),
            jax.ShapeDtypeStruct((count, SMALL), f32),
        ],
        in_specs=[pl.BlockSpec(memory_space=pltpu.SMEM), IN_VMEM] + [ANY] * 6 + [IN_VMEM] * 3,
        out_specs=[ANY] * 5 + [IN_VMEM] * 8,
        scratch_shapes=[
            pltpu.VMEM((ROWS_OWN, PACKED), bf16),
            pltpu.VMEM((GROUP, ROWS_OWN, PACKED), bf16),
            pltpu.VMEM((seqs, REPS, positions, 2 * KEY), bf16),
            pltpu.VMEM((count, 2 * KEY), bf16),
            pltpu.VMEM((2, 4 * positions, length), bf16),
            pltpu.VMEM((seqs, positions, length), f32),
        ]
        + sems(GATHER_SEMS) * 7
        + [
            pltpu.SemaphoreType.DMA((7,)),
            pltpu.SemaphoreType.DMA((2,)),
            pltpu.SemaphoreType.DMA((2,)),
            pltpu.SemaphoreType.DMA((5,)),
        ],
        compiler_params=params(collective_id),
    )(starts, tokens, cotangent, *weights_own, small_own, cosine, sine, routes)


def norm_back(values, gain, grad):
    scale = root_mean(values)
    weighted = grad * gain
    mean = jnp.mean(values * weighted, axis=1, keepdims=True)
    inner = weighted * scale - values * (scale * scale * scale * mean)
    return inner, jnp.sum(grad * values * scale, axis=0, keepdims=True)


def back_call(
    collective_id, returned, out_first, back_terms, gates, middle, sent, dense, cotangent, tokens, attn_in, query_raw, key_raw,
    query_low, mixed, pairs, soft, out_terms, expert_terms, cosine, sine,
):
    count, width = tokens.shape
    seqs, _, positions, _ = pairs.shape
    columns = back_terms.shape[2]
    length = REPS * positions
    expert_rows = expert_terms.shape[0] // REPS
    score_scale = HEAD_DIM ** (-0.5)
    chips = GROUP // 2

    def kernel(
        returned_ref, out_first_ref, back_ref, gates_ref, middle_ref, sent_ref, dense_ref, grad_ref, tokens_ref, attn_ref,
        query_raw_ref, key_raw_ref, query_ref, mixed_ref, pairs_ref, soft_ref, out_ref, expert_ref,
        cos_ref, sin_ref,
        block_out, tokens_grad, dense_all, expert_all,
        weight_box, weight_rest, rest_terms, dense_own,
        o_staged, q_staged, rest_staged, o_stage, q_stage, rest_stage,
        out_held, out_staged, out_stage, back_held, back_staged, back_stage, returned_second,
        expert_held, expert_stage, expert_own,
        soft_box, key_box, value_box, pair_terms, pair_stage, pair_grads,
        grad_mixed, grad_query, grad_middle, grad_attn, grad_attn_in, logit_box, gain_box,
        out_s, out_r, back_s, back_r, exp_s, exp_r, kv0_s, kv0_r, kv1_s, kv1_r, o_s, o_r, q_s, q_r, rest_s, rest_r,
        ge_s, ge_r, go_s, go_r, gq_s, gq_r, grest_s, grest_r,
        load_sem, held_sem, box_sem, own_sem,
    ):
        place = Place()
        core = place.core
        token_axes, copy_axes = place.tokens, place.copies
        q_terms = expert_held

        def chip_of(which):
            return which[0] * RING + which[1]

        def blocks(which, other=False):
            return chip_of(which) * 2 + ((1 - core) if other else core)

        def out_store(low, step, value):
            at = pl.ds(positions + low, step)
            block_out[at] = (middle_ref[at] + value).astype(bf16)

        def second_sum(source, held, staged, stage, send_sem, recv_sem, result, store=None):
            return sum_parts(
                token_axes, Line(send_sem, recv_sem),
                lambda which, low, n: held.at[chip_of(which), pl.ds(low, n)],
                stage, positions, result,
                (place.twin, lambda which: source.at[blocks(which, True)],
                 lambda which: staged.at[chip_of(which)]),
                store=store,
            )

        out_sum = second_sum(
            out_ref, out_held, out_staged, out_stage, out_s, out_r, None, store=out_store
        )
        back_sum = second_sum(
            back_ref, back_held, back_staged, back_stage, back_s, back_r, returned_second
        )
        expert_sum = sum_parts(
            copy_axes, Line(exp_s, exp_r),
            lambda which, low, n: expert_held.at[pl.ds(chip_of(which) * expert_rows + low, n)],
            expert_stage, expert_rows, expert_own,
        )

        def pair_sum(seq, send_sem, recv_sem):
            return sum_parts(
                copy_axes, Line(send_sem, recv_sem),
                lambda which, low, n: pair_terms.at[seq, chip_of(which), pl.ds(low, n)],
                pair_stage.at[seq], positions, pair_grads.at[pl.ds(seq * positions, positions)],
            )

        pair_sums = [pair_sum(0, kv0_s, kv0_r), pair_sum(1, kv1_s, kv1_r)]

        def rows_of_block(terms, index, low, n):
            return terms.at[pl.ds(index * ROWS_OWN + low, n)]

        def rows_of_pairs(terms, index, low, n):
            at = lax.rem(index, 2) * ROWS_OWN + low
            return terms.at[0, lax.div(index, 2), pl.ds(at, n)]

        def dense_sum(rows_of, terms, staged, stage, low, size, send_sem, recv_sem):
            return sum_parts(
                token_axes, Line(send_sem, recv_sem),
                lambda which, row, n: rows_of(terms, blocks(which), row, n),
                stage, ROWS_OWN, dense_own.at[:, pl.ds(low, size)],
                (place.twin, lambda which: rows_of(terms, blocks(which, True), 0, ROWS_OWN),
                 lambda which: staged.at[chip_of(which)]),
            )

        o_sum = dense_sum(rows_of_pairs, pair_terms, o_staged, o_stage, AT_O, width, o_s, o_r)
        q_sum = dense_sum(rows_of_block, q_terms, q_staged, q_stage, 0, QUERY, q_s, q_r)
        rest_sum = dense_sum(rows_of_block, rest_terms, rest_staged, rest_stage, AT_K, REST, rest_s, rest_r)

        def dense_gather(low, size, send_sem, recv_sem, index):
            return gather_parts(
                copy_axes, Line(send_sem, recv_sem), dense_own.at[:, pl.ds(low, size)],
                lambda which, row, n, other=False: dense_all.at[
                    chip_of(which), pl.ds(row, n), pl.ds(low, size)
                ],
                ROWS_OWN, own_sem.at[index],
            )

        o_gather = dense_gather(AT_O, width, go_s, go_r, 0)
        q_gather = dense_gather(0, QUERY, gq_s, gq_r, 1)
        rest_gather = dense_gather(AT_K, REST, grest_s, grest_r, 2)
        expert_gather = gather_parts(
            copy_axes, Line(ge_s, ge_r), expert_own,
            lambda which, row, n, other=False: expert_all.at[chip_of(which), pl.ds(row, n)],
            expert_rows, own_sem.at[3],
        )

        def weight_load(low, index):
            return pltpu.make_async_copy(
                dense_ref.at[:, :, pl.ds(low, width)], weight_box, load_sem.at[index]
            )

        rest_load = pltpu.make_async_copy(
            dense_ref.at[:, :, pl.ds(AT_K, REST)], weight_rest, load_sem.at[1]
        )
        expert_load = pltpu.make_async_copy(expert_ref, expert_held, load_sem.at[2])
        held_loads = [
            [
                pltpu.make_async_copy(
                    source.at[2 * chip + core], held.at[chip], held_sem.at[kind, chip]
                )
                for chip in range(chips)
            ]
            for kind, (source, held) in enumerate(((back_ref, back_held), (out_ref, out_held)))
        ]

        def box_loads(number, slot):
            seq, index = lax.div(number, HEAD_PAIRS), lax.rem(number, HEAD_PAIRS)
            return [
                pltpu.make_async_copy(
                    soft_ref.at[seq, index], soft_box.at[slot], box_sem.at[slot, 0]
                ),
                pltpu.make_async_copy(
                    pairs_ref.at[seq, :, :, chunk_at(index)], key_box.at[slot], box_sem.at[slot, 1]
                ),
                pltpu.make_async_copy(
                    pairs_ref.at[seq, :, :, chunk_at(index, KEY)],
                    value_box.at[slot],
                    box_sem.at[slot, 2],
                ),
            ]

        for load in held_loads[0]:
            load.start()
        expert_load.start()
        rest_load.start()
        weight_load(AT_O, 0).start()
        for load in held_loads[1]:
            load.start()
        for load in box_loads(0, 0):
            load.start()
        greet(token_axes.neighbours() + copy_axes.neighbours() + [place.twin])
        next(back_sum)
        expert_load.wait()
        next(expert_sum)
        next(expert_sum)
        for load in held_loads[0]:
            load.wait()
        next(back_sum)
        rest_load.wait()

        small = weight_rest[:, :, pl.ds(2 * KEY, SMALL)].reshape(width, SMALL)
        gain_a, gain_q, gain_f, gain_k = gain_rows(small)
        gain_box[...] = jnp.zeros_like(gain_box)

        def features_back(seq, source):
            at = pl.ds(seq * positions, positions)
            gates = gates_ref[at]
            tail = source[:, pl.ds(width, SMALL)]
            grad_gates = tail + pltpu.roll(tail, SMALL - EXPERTS, 1)
            grad_logits = gates * (
                grad_gates - jnp.sum(gates * grad_gates, axis=1, keepdims=True)
            )
            grad_logits = grad_logits.astype(bf16)
            logit_box[at] = grad_logits
            grad_ffn = source[:, pl.ds(0, width)] + dot_nt(grad_logits, small)
            inner, gain_terms = norm_back(middle_ref[at], gain_f, grad_ffn)
            inner = grad_ref[at].astype(f32) + inner
            grad_middle[at] = inner
            low = inner.astype(bf16)
            grad_attn[at] = low
            gain_at = pl.ds(EXPERTS + 2, 1)
            gain_box[gain_at] = gain_box[gain_at] + gain_terms
            weight_o = weight_box[...].reshape(QUERY, width)
            grad_mixed[at] = dot_nt(low, weight_o).astype(bf16)

        weight_load(AT_O, 0).wait()
        features_back(0, returned_ref)
        first_at = pl.ds(0, positions)
        block_out[first_at] = (middle_ref[first_at] + out_first_ref[...]).astype(bf16)

        def attend_back(seq, index):
            number = seq * HEAD_PAIRS + index
            slot = lax.rem(number, 2)
            for load in box_loads(number, slot):
                load.wait()

            @pl.when(number + 1 < seqs * HEAD_PAIRS)
            def _():
                for load in box_loads(number + 1, 1 - slot):
                    load.start()

            rows_at = pl.ds(seq * positions, positions)
            first, second = chunk_at(2 * index), chunk_at(2 * index + 1)
            queries = four_heads(
                query_ref[rows_at, first].astype(f32), query_ref[rows_at, second].astype(f32)
            )
            queries = (queries * score_scale).astype(bf16)
            grads = four_heads(
                grad_mixed[rows_at, first].astype(f32), grad_mixed[rows_at, second].astype(f32)
            ).astype(bf16)
            keys = key_box[slot].reshape(length, LANES)
            values = value_box[slot].reshape(length, LANES)
            soft_low = soft_box[slot]
            value_terms = dot_tn(soft_low, grads)
            pair_terms[seq, :, :, chunk_at(index, KEY)] = value_terms.astype(bf16).reshape(
                REPS, positions, LANES
            )
            soft_full = soft_low.astype(f32)
            grad_soft = dot_nt(grads, values)
            weighted = soft_full * grad_soft
            grad_scores = (
                weighted - soft_full * jnp.sum(weighted, axis=1, keepdims=True)
            ).astype(bf16)
            key_terms = dot_tn(grad_scores, queries)
            pair_terms[seq, :, :, chunk_at(index)] = key_terms.astype(bf16).reshape(
                REPS, positions, LANES
            )
            chunk_a, chunk_b = two_chunks(dot(grad_scores, keys) * score_scale)
            grad_query[rows_at, first] = chunk_a.astype(bf16)
            grad_query[rows_at, second] = chunk_b.astype(bf16)

        def first_heads(index, carry):
            hooks(index, ((2, lambda: next(back_sum)), (3, lambda: next(expert_sum))))
            attend_back(0, index)
            return carry

        lax.fori_loop(0, HEAD_PAIRS, first_heads, 0)
        next(pair_sums[0])
        next(pair_sums[0])
        next(back_sum)
        for load in held_loads[1]:
            load.wait()
        next(out_sum)
        next(expert_sum)
        next(out_sum)
        drained(expert_sum)
        next(pair_sums[0])
        drained(back_sum)
        features_back(1, returned_second)
        weight_load(0, 3).start()

        def second_heads(index, carry):
            hooks(
                index,
                (
                    (0, lambda: next(pair_sums[0])),
                    (1, lambda: next(out_sum)),
                    (2, lambda: (drained(pair_sums[0]), next(expert_gather))[0]),
                    (3, lambda: next(out_sum)),
                ),
            )
            attend_back(1, index)
            return carry

        lax.fori_loop(0, HEAD_PAIRS, second_heads, 0)
        next(pair_sums[1])
        next(pair_sums[1])
        drained(out_sum)
        next(expert_gather)

        def o_rows(index, carry):
            at = chunk_256(index)
            value = dot_tn(mixed_ref[:, at], grad_attn[...]).astype(bf16)
            pair_terms[0, pl.ds(2 * index, 2)] = value.reshape(2, positions, width)
            return carry

        lax.fori_loop(0, QUERY // 256, o_rows, 0)
        next(o_sum)
        next(o_sum)

        cos2 = jnp.concatenate([cos_ref[...]] * seqs, axis=0)
        sin2 = -jnp.concatenate([sin_ref[...]] * seqs, axis=0)

        def turned_back(values):
            return jnp.concatenate(
                [
                    turned(values[:, low : low + LANES], cos2, sin2)
                    for low in range(0, values.shape[1], LANES)
                ],
                axis=1,
            )

        grad, gain_q_terms = norm_back(
            query_raw_ref[...], gain_q, turned_back(grad_query[...].astype(f32))
        )
        gain_box[pl.ds(EXPERTS + 1, 1)] = gain_q_terms
        grad_query_low = grad.astype(bf16)
        weight_load(0, 3).wait()
        grad_attn_in[...] = dot_nt(grad_query_low, weight_box[...].reshape(width, QUERY))

        def q_rows(index, carry):
            at = chunk_256(index)
            q_terms[at] = dot_tn(attn_ref[:, at], grad_query_low).astype(bf16)
            return carry

        lax.fori_loop(0, width // 256, q_rows, 0)
        next(q_sum)
        next(pair_sums[1])
        next(q_sum)
        next(expert_gather)
        next(o_sum)
        next(pair_sums[1])
        next(o_sum)
        next(q_sum)
        router_terms = dot_tn(sent_ref[:, pl.ds(0, width)], logit_box[...])
        drained(o_sum)
        drained(pair_sums[1])
        next(o_gather)

        grads = pair_grads[...]
        grad, gain_k_terms = norm_back(
            key_raw_ref[...],
            gain_k,
            turned_back(grads[:, :KEY].astype(bf16).astype(f32)),
        )
        grad_pairs = jnp.concatenate([grad.astype(bf16), grads[:, KEY:].astype(bf16)], axis=1)
        gain_k_row = dot_nt(
            jnp.broadcast_to(gain_k_terms, (8, KEY)).astype(bf16), short_rows()
        )
        gain_box[pl.ds(EXPERTS + 3, 1)] = gain_k_row[:1]
        grad = grad_attn_in[...] + dot_nt(
            grad_pairs, weight_rest[:, :, pl.ds(0, 2 * KEY)].reshape(width, 2 * KEY)
        )
        values = tokens_ref[...].astype(f32)
        inner, gain_a_terms = norm_back(values, gain_a, grad)
        tokens_grad[...] = (grad_middle[...] + inner).astype(bf16)
        gain_box[pl.ds(EXPERTS, 1)] = gain_a_terms
        rest_terms[:, pl.ds(2 * KEY, SMALL)] = (
            router_terms + jnp.transpose(gain_box[...])
        ).astype(bf16)

        def rest_rows(index, carry):
            at = chunk_256(index)
            rest_terms[at, pl.ds(0, 2 * KEY)] = dot_tn(attn_ref[:, at], grad_pairs).astype(bf16)
            return carry

        lax.fori_loop(0, width // 256, rest_rows, 0)
        next(rest_sum)
        next(rest_sum)
        next(q_sum)
        next(o_gather)
        drained(q_sum)
        next(q_gather)
        next(rest_sum)
        drained(expert_gather)
        next(o_gather)
        next(q_gather)
        next(rest_sum)
        next(o_gather)
        next(q_gather)
        drained(rest_sum)
        next(rest_gather)
        abreast(o_gather, q_gather, rest_gather)

    block = pltpu.VMEM((GROUP, ROWS_OWN, width), bf16)
    scratch = [
        block,
        pltpu.VMEM((GROUP, ROWS_OWN, REST), bf16),
        pltpu.VMEM((width, REST), bf16),
        pltpu.VMEM((ROWS_OWN, PACKED), bf16),
        pltpu.VMEM((chips, ROWS_OWN, width), bf16),
        pltpu.VMEM((chips, ROWS_OWN, QUERY), bf16),
        pltpu.VMEM((chips, ROWS_OWN, REST), bf16),
        pltpu.VMEM((stage_rows(ROWS_OWN), width), bf16),
        pltpu.VMEM((stage_rows(ROWS_OWN), QUERY), bf16),
        pltpu.VMEM((stage_rows(ROWS_OWN), REST), bf16),
        pltpu.VMEM((chips, positions, width), bf16),
        pltpu.VMEM((chips, positions, width), bf16),
        pltpu.VMEM((stage_rows(positions), width), bf16),
        pltpu.VMEM((chips, positions, columns), bf16),
        pltpu.VMEM((chips, positions, columns), bf16),
        pltpu.VMEM((stage_rows(positions), columns), bf16),
        pltpu.VMEM((positions, columns), f32),
        pltpu.VMEM(expert_terms.shape, bf16),
        pltpu.VMEM((stage_rows(expert_rows), width), bf16),
        pltpu.VMEM((expert_rows, width), bf16),
        pltpu.VMEM((2, 4 * positions, length), bf16),
        pltpu.VMEM((2, REPS, positions, LANES), bf16),
        pltpu.VMEM((2, REPS, positions, LANES), bf16),
        pltpu.VMEM((seqs, REPS, positions, 2 * KEY), bf16),
        pltpu.VMEM((seqs, stage_rows(positions), 2 * KEY), bf16),
        pltpu.VMEM((count, 2 * KEY), f32),
        pltpu.VMEM((count, QUERY), bf16),
        pltpu.VMEM((count, QUERY), bf16),
        pltpu.VMEM((count, width), f32),
        pltpu.VMEM((count, width), bf16),
        pltpu.VMEM((count, width), f32),
        pltpu.VMEM((count, SMALL), bf16),
        pltpu.VMEM((SMALL, width), f32),
    ]
    return pl.pallas_call(
        kernel,
        out_shape=[
            jax.ShapeDtypeStruct((count, width), bf16),
            jax.ShapeDtypeStruct((count, width), bf16),
            jax.ShapeDtypeStruct((REPS, ROWS_OWN, PACKED), bf16),
            jax.ShapeDtypeStruct((REPS, expert_rows, width), bf16),
        ],
        in_specs=[IN_VMEM] * 2 + [ANY] + [IN_VMEM] * 3 + [ANY] + [IN_VMEM] * 7 + [ANY] * 4 + [IN_VMEM] * 2,
        out_specs=[IN_VMEM, IN_VMEM, ANY, ANY],
        scratch_shapes=scratch
        + sems(SUM_SEMS) * 8
        + sems(GATHER_SEMS) * 4
        + [
            pltpu.SemaphoreType.DMA((4,)),
            pltpu.SemaphoreType.DMA((2, chips)),
            pltpu.SemaphoreType.DMA((2, 3)),
            pltpu.SemaphoreType.DMA((4,)),
        ],
        compiler_params=params(collective_id),
    )(
        returned, out_first, back_terms, gates, middle, sent, dense, cotangent, tokens, attn_in, query_raw, key_raw,
        query_low, mixed, pairs, soft, out_terms, expert_terms, cosine, sine,
    )


def finish_call(dense_all, expert_all, inner_rows):
    total_rows, width = expert_all.shape
    step = 256
    inner_steps, steps = inner_rows // step, total_rows // step

    def kernel(dense_ref, expert_ref, inner, outer, query, key, value, output, small):
        at = pl.program_id(0)
        rows = expert_ref[...].astype(f32)

        @pl.when(at < inner_steps)
        def _():
            inner[...] = rows

        @pl.when(at >= inner_steps)
        def _():
            outer[...] = rows

        @pl.when(at == 1)
        def _():
            for low, target in ((0, query), (AT_K, key), (AT_V, value), (AT_O, output), (AT_S, small)):
                columns = pl.ds(low, target.shape[1])
                total = dense_ref[0, :, columns].astype(f32)
                for rep in range(1, REPS):
                    total = total + dense_ref[rep, :, columns].astype(f32)
                target[...] = total

    def whole(columns):
        return pl.BlockSpec((ROWS_OWN, columns), lambda i: (0, 0))

    sizes = (QUERY, KEY, KEY, WIDTH, SMALL)
    return pl.pallas_call(
        kernel,
        grid=(steps,),
        out_shape=[
            jax.ShapeDtypeStruct((inner_rows, width), f32),
            jax.ShapeDtypeStruct((total_rows - inner_rows, width), f32),
        ]
        + [jax.ShapeDtypeStruct((ROWS_OWN, size), f32) for size in sizes],
        in_specs=[
            pl.BlockSpec(dense_all.shape, lambda i: (0, 0, 0)),
            pl.BlockSpec((step, width), lambda i: (i, 0)),
        ],
        out_specs=[
            pl.BlockSpec((step, width), lambda i: (jnp.minimum(i, inner_steps - 1), 0)),
            pl.BlockSpec((step, width), lambda i: (jnp.maximum(i - inner_steps, 0), 0)),
        ]
        + [whole(size) for size in sizes],
        compiler_params=pltpu.CompilerParams(vmem_limit_bytes=VMEM_LIMIT),
    )(dense_all, expert_all)


def rotary_tables(positions):
    lane = jnp.arange(LANES, dtype=jnp.int32)
    half = HEAD_DIM // 2
    exponent = (lane % half).astype(f32) * (2.0 / HEAD_DIM)
    frequency = rope_base ** (-exponent)
    angles = positions.astype(f32)[:, None] * frequency[None, :]
    sign = jnp.where(lane % HEAD_DIM < half, -1.0, 1.0).astype(f32)
    return jnp.cos(angles), jnp.sin(angles) * sign[None, :]


def small_columns(router, gain_a, gain_q, gain_f, gain_k):
    rows = router.shape[0]
    lane = jnp.arange(SMALL)[None, :]
    small = jnp.pad(router, ((0, 0), (0, SMALL - EXPERTS)))
    short = jnp.pad(gain_k, (0, rows - gain_k.shape[0]))
    for at, gain in enumerate((gain_a, gain_q, gain_f, short)):
        small = jnp.where(lane == EXPERTS + at, gain[:, None], small)
    return small


def shards(
    tokens,
    cotangent,
    routes,
    picture_starts,
    attn_gain,
    query_weight,
    key_weight,
    value_weight,
    query_gain,
    key_gain,
    output_weight,
    ffn_gain,
    router_weight,
    expert_in,
    expert_down,
):
    seqs, positions, width = tokens.shape
    count = seqs * positions
    query_pos = lax.axis_index("rep") * positions + jnp.arange(positions, dtype=jnp.int32)
    cosine, sine = rotary_tables(query_pos)
    rows = tokens.reshape(count, width)
    grad_rows = cotangent.reshape(count, width)
    (
        dense, grad_all, pairs, soft, rows_first,
        attn_in, query_raw, key_raw, query_low, mixed, middle, sent, gates,
    ) = front_call(
        1, rows, grad_rows, (query_weight, key_weight, value_weight, output_weight),
        small_columns(router_weight, attn_gain, query_gain, ffn_gain, key_gain),
        cosine, sine, routes.reshape(count, routes.shape[2]), picture_starts,
    )
    returned, out_first, back_terms, out_terms, expert_terms = moe_call(
        2, sent, rows_first, grad_all, expert_in[0], expert_down[0]
    )
    block_out, tokens_grad, dense_all, expert_all = back_call(
        3, returned, out_first, back_terms, gates, middle, sent, dense, grad_rows, rows, attn_in,
        query_raw, key_raw, query_low, mixed, pairs, soft, out_terms, expert_terms, cosine, sine,
    )
    inner, outer, query, key, value, output, small = finish_call(
        dense_all, expert_all.reshape(-1, width), expert_in.shape[1]
    )
    return (
        block_out.reshape(tokens.shape),
        tokens_grad.reshape(tokens.shape),
        small[:, EXPERTS],
        query,
        key,
        value,
        small[:, EXPERTS + 1],
        small[: key_gain.shape[0], EXPERTS + 3],
        output,
        small[:, EXPERTS + 2],
        small[:, :EXPERTS],
        inner[None],
        outer[None],
    )


def solution(mesh):
    by_tokens = P("shard", "rep", None)
    rows, line, block = P("shard", None), P("shard"), P("shard", None, None)
    in_specs = (
        by_tokens, by_tokens, by_tokens, rows, line, rows, rows, rows, line, line, rows, line, rows, block, block,
    )
    out_specs = (
        by_tokens, by_tokens, line, rows, rows, rows, line, line, rows, line, rows, block, block,
    )
    return jax.shard_map(shards, mesh=mesh, in_specs=in_specs, out_specs=out_specs, check_vma=False)
```

```python
import jax
import jax.numpy as jnp
from jax import lax
from jax.experimental import pallas as pl
from jax.experimental.pallas import tpu as pltpu
from jax.sharding import PartitionSpec as P

HEADS = 16
KV_HEADS = 8
HEAD_DIM = 64
PIC = 256
RING = 4
GROUP = 16
REPS = 8
VMEM_LIMIT = 62 << 20

norm_eps = 1e-06
rope_base = 10000.0
masked_score = -1e30

bf16 = jnp.bfloat16
f32 = jnp.float32


class Place:
    def __init__(self):
        shard = lax.axis_index("shard")
        rep = lax.axis_index("rep")
        self.shard, self.rep = shard, rep
        core = lax.rem(shard, 2)
        ring_z = lax.rem(lax.div(shard, 2), RING)
        y_hi = lax.div(shard, 8)
        ring_x = lax.rem(rep, RING)
        y_lo = lax.div(rep, RING)
        self.core = core

        def shard_of(hi, z, c):
            return (hi * RING + z) * 2 + c

        def rep_of(lo, x):
            return lo * RING + x

        def up(v):
            return lax.rem(v + 1, RING)

        def down(v):
            return lax.rem(v + RING - 1, RING)

        self.twin = (shard_of(y_hi, ring_z, 1 - core), rep)
        self.others = [lax.rem(rep + step, REPS) for step in range(REPS)]
        self.tokens = Axes(
            y_hi,
            ring_z,
            (shard_of(y_hi, up(ring_z), core), rep),
            (shard_of(y_hi, down(ring_z), core), rep),
            (shard_of(1 - y_hi, ring_z, core), rep_of(1 - y_lo, ring_x)),
        )
        self.copies = Axes(
            y_lo,
            ring_x,
            (shard, rep_of(y_lo, up(ring_x))),
            (shard, rep_of(y_lo, down(ring_x))),
            (shard, rep_of(1 - y_lo, ring_x)),
        )


class Axes:
    def __init__(self, side, spot, ahead, behind, across):
        self.side, self.spot = side, spot
        self.ahead, self.behind, self.across = ahead, behind, across
        sides = (side, 1 - side)
        spots = [lax.rem(spot + step, RING) for step in range(RING)]
        self.places = [[(sides[flip], spots[step]) for step in range(RING)] for flip in range(2)]

    def at(self, flip, step):
        return self.places[flip][step % RING]

    def neighbours(self):
        return [self.ahead, self.behind, self.across]


def greet(devices):
    barrier = pltpu.get_barrier_semaphore()
    for device in devices:
        pl.semaphore_signal(barrier, inc=1, device_id=device, device_id_type=pl.DeviceIdType.MESH)
    pl.semaphore_wait(barrier, len(devices))


class Line:
    def __init__(self, send_sem, recv_sem):
        self.send_sem, self.recv_sem = send_sem, recv_sem
        self.sent = []

    def copy(self, index, source, target, device):
        return pltpu.make_async_remote_copy(
            src_ref=source(),
            dst_ref=target(),
            send_sem=self.send_sem.at[index],
            recv_sem=self.recv_sem.at[index],
            device_id=device,
            device_id_type=pl.DeviceIdType.MESH,
        )

    def send(self, index, source, target, device):
        self.copy(index, source, target, device).start()
        self.sent.append((index, source, target, device))

    def take(self, index, target, device):
        self.copy(index, target, target, device).wait_recv()

    def finish(self):
        for sent in self.sent:
            self.copy(*sent).wait_send()


def abreast(*parts):
    running = list(parts)
    while running:
        for part in list(running):
            try:
                next(part)
            except StopIteration:
                running.remove(part)


GATHER_SEMS = 20


def gather_parts(axes, line, own, block, rows, local_sem, twin=None, twin_later=False):
    half, quarter = rows // 2, rows // 4
    mine, back, front, far = axes.at(0, 0), axes.at(0, -1), axes.at(0, 1), axes.at(0, 2)
    pair, pair_back, pair_front, pair_far = (axes.at(1, n) for n in (0, -1, 1, 2))
    ahead, behind, across = axes.ahead, axes.behind, axes.across

    def rows_of(which, low=0, count=rows, other=False):
        return lambda: block(which, low, count, other)

    def first(index, device):
        line.send(index, lambda: own, rows_of(mine), device)

    def relay(index, device, which, low=0, count=rows):
        line.send(index, rows_of(which, low, count), rows_of(which, low, count), device)

    def share(index, which):
        if twin is not None:
            relay(12 + index, twin, which)

    def keep():
        return pltpu.make_async_copy(own, block(mine, 0, rows), local_sem)

    keep().start()
    if twin is not None:
        first(12, twin)
    first(0, ahead)
    first(1, behind)
    first(2, across)
    keep().wait()
    yield
    line.take(0, rows_of(back), ahead)
    relay(3, ahead, back, 0, half)
    relay(4, across, back, half, half)
    share(1, back)
    line.take(1, rows_of(front), behind)
    relay(5, behind, front, half, half)
    relay(6, across, front, half, half)
    share(2, front)
    line.take(2, rows_of(pair), across)
    relay(7, ahead, pair, 0, half)
    relay(8, behind, pair, 0, half)
    share(3, pair)
    yield
    line.take(3, rows_of(far, 0, half), ahead)
    line.take(5, rows_of(far, half, half), behind)
    relay(9, across, far, half, half)
    share(4, far)
    line.take(7, rows_of(pair_back, 0, half), ahead)
    relay(10, ahead, pair_back, 0, quarter)
    line.take(8, rows_of(pair_front, 0, half), behind)
    relay(11, behind, pair_front, quarter, quarter)
    line.take(4, rows_of(pair_back, half, half), across)
    share(5, pair_back)
    line.take(6, rows_of(pair_front, half, half), across)
    share(6, pair_front)
    yield
    line.take(10, rows_of(pair_far, 0, quarter), ahead)
    line.take(11, rows_of(pair_far, quarter, quarter), behind)
    line.take(9, rows_of(pair_far, half, half), across)
    share(7, pair_far)
    yield
    if twin is not None and not twin_later:
        for index, which in enumerate(gather_order(axes)):
            line.take(12 + index, rows_of(which, other=True), twin)
    line.finish()


SUM_SEMS = 20
TOTAL_SEMS = 24


def total_parts(place, line, own, got, total, target, local_sem, tail=None):
    rep = place.rep
    steps = range(1, REPS)
    peers = {step: (place.shard, place.others[step]) for step in steps}
    before = {step: place.others[REPS - step] for step in steps}

    def added(mine, received):
        value = mine[...].astype(f32)
        for step in steps:
            value = value + received[before[step]].astype(f32)
        return value.astype(bf16)

    def kept(index, source, place_of):
        return pltpu.make_async_copy(source, place_of, local_sem.at[index])

    for step in steps:
        line.send(
            step, lambda p=place.others[step]: own(p), lambda: got.at[rep], peers[step]
        )
        if tail is not None:
            line.send(16 + step, lambda: tail[0], lambda: tail[1].at[rep], peers[step])
    yield
    for step in steps:
        line.take(step, lambda b=before[step]: got.at[b], peers[step])
    total[...] = added(own(rep), got)
    kept(0, total, target(rep)).start()
    for step in steps:
        line.send(8 + step, lambda: total, lambda: target(rep), peers[step])
    if tail is not None:
        for step in steps:
            line.take(16 + step, lambda b=before[step]: tail[1].at[b], peers[step])
        tail[2][...] = added(tail[0], tail[1])
        kept(1, tail[2], tail[3]).start()
    yield
    for step in steps:
        line.take(8 + step, lambda b=before[step]: target(b), peers[step])
    kept(0, total, target(rep)).wait()
    if tail is not None:
        kept(1, tail[2], tail[3]).wait()
    line.finish()


def add_rows(target, source, rows):
    step = 16
    count = rows // step

    def body(index, carry):
        at = pl.ds(pl.multiple_of(index * step, step), step)
        target[at] = target[at] + source[at]
        return carry

    lax.fori_loop(0, count, body, 0)


def stage_rows(rows):
    return 7 * rows


def gather_order(axes):
    return [axes.at(*v) for v in ((0, 0), (0, -1), (0, 1), (1, 0), (0, 2), (1, -1), (1, 1), (1, 2))]


def sum_order(axes):
    return [axes.at(*v) for v in ((1, 2), (0, 2), (1, -1), (1, 1), (0, -1), (0, 1), (1, 0), (0, 0))]


def sum_parts(axes, line, part, stage, rows, result, twin=None, store=None):
    half, quarter = rows // 2, rows // 4
    mine, back, front, far = axes.at(0, 0), axes.at(0, -1), axes.at(0, 1), axes.at(0, 2)
    pair, pair_back, pair_front, pair_far = (axes.at(1, n) for n in (0, -1, 1, 2))
    ahead, behind, across = axes.ahead, axes.behind, axes.across
    order = sum_order(axes)
    offsets, used = {}, 0
    for name, size in (
        ("Y0", half), ("M0", quarter), ("P0", quarter), ("M1", half), ("Y1", half), ("Y2", half),
        ("P1", half), ("M2", half), ("P2", half), ("M3", rows), ("P3", rows), ("Y3", rows),
    ):
        offsets[name] = (used, size, len(offsets))
        used += size

    def landing(name):
        low, size, _ = offsets[name]
        return lambda: stage.at[pl.ds(low, size)]

    def send(name, which, low, device):
        _, size, index = offsets[name]
        line.send(index, lambda: part(which, low, size), landing(name), device)

    def add(name, which, low, device):
        _, size, index = offsets[name]
        line.take(index, landing(name), device)
        add_rows(part(which, low, size), landing(name)(), size)

    def join(*places):
        if twin is not None:
            for place in places:
                line.take(12 + place, lambda: twin[2](order[place]), twin[0])
                add_rows(part(order[place], 0, rows), twin[2](order[place]), rows)

    def hand(*places):
        if twin is not None:
            for place in places:
                which = order[place]
                line.send(
                    12 + place, lambda w=which: twin[1](w), lambda w=which: twin[2](w), twin[0]
                )

    hand(0, 1, 2, 3)
    yield
    join(0)
    send("Y0", pair_far, half, across)
    send("M0", pair_far, 0, behind)
    send("P0", pair_far, quarter, ahead)
    join(1)
    send("M1", far, 0, behind)
    join(2)
    send("Y1", pair_back, half, across)
    join(3)
    send("Y2", pair_front, half, across)
    yield
    hand(4, 5, 6, 7)
    yield
    add("M0", pair_back, 0, behind)
    send("M2", pair_back, 0, behind)
    add("P0", pair_front, quarter, ahead)
    send("P2", pair_front, 0, ahead)
    add("Y0", far, half, across)
    send("P1", far, half, ahead)
    yield
    join(4, 5, 6, 7)
    add("M1", back, 0, behind)
    add("Y1", back, half, across)
    send("M3", back, 0, behind)
    add("M2", pair, 0, behind)
    add("P2", pair, 0, ahead)
    send("Y3", pair, 0, across)
    add("P1", front, half, ahead)
    add("Y2", front, half, across)
    send("P3", front, 0, ahead)
    yield
    for name, device in (("M3", behind), ("P3", ahead), ("Y3", across)):
        line.take(offsets[name][2], landing(name), device)
    step = 16

    def body(index, carry):
        low = pl.multiple_of(index * step, step)
        total = part(mine, low, step)[...].astype(f32)
        for name in ("M3", "P3", "Y3"):
            total = total + stage[pl.ds(offsets[name][0] + low, step)].astype(f32)
        if store is None:
            result[pl.ds(low, step)] = total.astype(result.dtype)
        else:
            store(low, step, total)
        return carry

    lax.fori_loop(0, rows // step, body, 0)
    line.finish()


def sems(count):
    return [pltpu.SemaphoreType.DMA((count,)), pltpu.SemaphoreType.DMA((count,))]


ANY = pl.BlockSpec(memory_space=pl.ANY)
IN_VMEM = pl.BlockSpec(memory_space=pltpu.VMEM)


def params(collective_id):
    return pltpu.CompilerParams(
        collective_id=collective_id, has_side_effects=True, vmem_limit_bytes=VMEM_LIMIT
    )


def dot(a, b):
    return jnp.dot(a, b, preferred_element_type=f32)


def dot_nt(a, b):
    return lax.dot_general(a, b, (((1,), (1,)), ((), ())), preferred_element_type=f32)


def dot_tn(a, b):
    return lax.dot_general(a, b, (((0,), (0,)), ((), ())), preferred_element_type=f32)


def pick(index, values):
    chosen = values[-1]
    for at in range(len(values) - 2, -1, -1):
        chosen = jnp.where(index == at, values[at], chosen)
    return chosen


def moe_call(collective_id, sent, rows_first, grad_all, inner, outer):
    count, columns = sent.shape
    width = inner.shape[0]
    hidden_width = outer.shape[0]
    small = columns - width
    half = count // 2
    chips = GROUP // 2
    wide = 4
    rounds = GROUP // wide

    def kernel(
        sent_ref, first_ref, grad_ref, inner_ref, outer_ref,
        returned, out_terms, terms,
        rows_in, grads, hidden, back_gu, back, back_staged, back_stage, out_box, term_box,
        gs, gr, bs0, br0, bs1, br1, own_sem, load_sem, box_sem, term_sem,
    ):
        place = Place()
        axes, core, shard = place.tokens, place.core, place.shard
        gather_line = Line(gs, gr)

        def chip_of(which):
            return which[0] * RING + which[1]

        def blocks(which, other=False):
            return chip_of(which) * 2 + ((1 - core) if other else core)

        gather = gather_parts(
            axes, gather_line, sent_ref.at[pl.ds(half, half)],
            lambda which, low, n, other=False: rows_in.at[1, blocks(which, other), pl.ds(low, n)],
            half, own_sem, place.twin, twin_later=True,
        )

        def sum_of(chunk, send_sem, recv_sem):
            return sum_parts(
                axes, Line(send_sem, recv_sem),
                lambda which, low, n: back.at[chunk, blocks(which), pl.ds(low, n)],
                back_stage.at[chunk], half, returned.at[pl.ds(chunk * half, half)],
                (place.twin, lambda which: back.at[chunk, blocks(which, True)],
                 lambda which: back_staged.at[chunk, chip_of(which)]),
            )

        sums = [sum_of(0, bs0, br0), sum_of(1, bs1, br1)]

        def loads(t):
            at = pl.ds(t * wide, wide)
            return [
                pltpu.make_async_copy(first_ref.at[at], rows_in.at[0, at], load_sem.at[t, 0]),
                pltpu.make_async_copy(
                    grad_ref.at[at, pl.ds(0, half)], grads.at[0, at], load_sem.at[t, 1]
                ),
            ]

        second_grads = pltpu.make_async_copy(
            grad_ref.at[:, pl.ds(half, half)], grads.at[1], load_sem.at[rounds, 0]
        )

        def box_copy(chunk, first, slot):
            return pltpu.make_async_copy(
                out_box.at[slot],
                out_terms.at[pl.ds(first, wide), pl.ds(chunk * half, half)],
                box_sem.at[slot],
            )

        rows_count = wide * half
        lanes = lane_of((rows_count, small))
        is_high, is_rest = lanes == shard, lanes == shard + GROUP

        def tile(chunk, first, slot, wait_first):
            at = pl.ds(first, wide)
            row_block = rows_in[chunk, at].reshape(rows_count, columns)
            gate = jnp.sum(
                jnp.where(is_high | is_rest, row_block[:, width:].astype(f32), 0.0),
                axis=1, keepdims=True,
            )
            gate_up = dot(row_block[:, :width], inner_ref[...])
            gate_part, up_part = gate_up[:, :hidden_width], gate_up[:, hidden_width:]
            sigmoid = 1.0 / (1.0 + jnp.exp(-gate_part))
            active = gate_part * sigmoid
            product = active * up_part
            hidden_low = product.astype(bf16)
            hidden[chunk, at] = hidden_low.reshape(wide, half, hidden_width)
            out_rows = (gate * dot(hidden_low, outer_ref[...])).astype(bf16)

            @pl.when(wait_first)
            def _():
                box_copy(chunk, first, slot).wait()

            out_box[slot] = out_rows.reshape(wide, half, width)
            box_copy(chunk, first, slot).start()
            grad = grads[chunk, at].reshape(rows_count, width)
            grad_hidden = dot_nt(grad, outer_ref[...])
            grad_gate = jnp.sum(grad_hidden * product, axis=1, keepdims=True)
            grad_hidden = grad_hidden * gate
            grad_gate_up = jnp.concatenate(
                [
                    grad_hidden * up_part * sigmoid * (1.0 + gate_part * (1.0 - sigmoid)),
                    grad_hidden * active,
                ],
                axis=1,
            ).astype(bf16)
            back_gu[chunk, at] = grad_gate_up.reshape(wide, half, 2 * hidden_width)
            grads[chunk, at] = (gate * grad.astype(f32)).astype(bf16).reshape(wide, half, width)
            grad_rows = dot_nt(grad_gate_up, inner_ref[...]).astype(bf16)
            back[chunk, at, :, pl.ds(0, width)] = grad_rows.reshape(wide, half, width)
            high = grad_gate.astype(bf16).astype(f32)
            tail = jnp.where(is_high, high, jnp.where(is_rest, grad_gate - high, 0.0))
            back[chunk, at, :, pl.ds(width, small)] = tail.astype(bf16).reshape(wide, half, small)

        for t in range(rounds):
            for load in loads(t):
                load.start()
        second_grads.start()
        greet(axes.neighbours() + [place.twin])
        next(gather)

        def first_tiles(t, carry):
            hooks(t, ((2, lambda: next(gather)),))
            for load in loads(t):
                load.wait()
            tile(0, t * wide, lax.rem(t, 2), t >= 2)
            return carry

        lax.fori_loop(0, rounds, first_tiles, 0)
        next(sums[0])
        next(gather)
        second_grads.wait()
        near, beyond = lax.div(axes.spot, 2), 1 - lax.div(axes.spot, 2)
        chips_per_round = wide // 2
        firsts = [
            (side * RING + part * chips_per_round) * 2
            for side, part in (
                (axes.side, beyond), (1 - axes.side, near), (1 - axes.side, beyond), (axes.side, near),
            )
        ]
        arrivals = gather_order(axes)

        def arrived(*numbers):
            for number in numbers:
                gather_line.take(
                    12 + number, lambda: rows_in.at[1, blocks(arrivals[number], True)], place.twin
                )

        def second_tiles(t, carry):
            hooks(
                t,
                (
                    (0, lambda: arrived(0, 1, 2, 4)),
                    (1, lambda: (next(sums[0]), next(sums[0]), arrived(3, 5, 6))[2]),
                    (2, lambda: (next(gather), arrived(7))[1]),
                    (3, lambda: (next(sums[1]), next(sums[0]))[0]),
                ),
            )
            tile(1, pick(t, firsts), lax.rem(t, 2), t >= 0)
            return carry

        lax.fori_loop(0, rounds, second_tiles, 0)
        next(sums[1])
        next(sums[1])

        def term_copy(low, slot):
            return pltpu.make_async_copy(
                term_box.at[slot], terms.at[pl.ds(low, 256)], term_sem.at[slot]
            )

        every = 2 * GROUP * half

        def keep(index, low, value):
            slot = lax.rem(index, 2)

            @pl.when(index >= 2)
            def _():
                term_copy(low, slot).wait()

            term_box[slot] = value.astype(bf16)
            term_copy(low, slot).start()

        downs = hidden_width // 256

        def down_terms(index, carry):
            at = chunk_256(index)
            value = dot_tn(hidden[:, :, :, at].reshape(every, 256), grads[...].reshape(every, width))
            keep(index, pl.multiple_of(width + index * 256, 256), value)
            return carry

        lax.fori_loop(0, downs, down_terms, 0)

        def inner_terms(index, carry):
            hooks(
                index,
                (
                    (0, lambda: next(sums[0])),
                    (1, lambda: next(sums[1])),
                ),
            )
            at = chunk_256(index)
            value = dot_tn(
                rows_in[:, :, :, at].reshape(every, 256),
                back_gu[...].reshape(every, 2 * hidden_width),
            )
            keep(index + downs, pl.multiple_of(index * 256, 256), value)
            return carry

        lax.fori_loop(0, width // 256, inner_terms, 0)
        drained(sums[0])
        drained(sums[1])
        drained(gather)
        for slot in range(2):
            box_copy(1, 0, slot).wait()
            term_copy(0, slot).wait()

    term_rows = width + hidden_width
    return pl.pallas_call(
        kernel,
        out_shape=[
            jax.ShapeDtypeStruct((count, columns), f32),
            jax.ShapeDtypeStruct((GROUP, count, width), bf16),
            jax.ShapeDtypeStruct((term_rows, width), bf16),
        ],
        in_specs=[ANY, ANY, ANY, IN_VMEM, IN_VMEM],
        out_specs=[IN_VMEM, ANY, ANY],
        scratch_shapes=[
            pltpu.VMEM((2, GROUP, half, columns), bf16),
            pltpu.VMEM((2, GROUP, half, width), bf16),
            pltpu.VMEM((2, GROUP, half, hidden_width), bf16),
            pltpu.VMEM((2, GROUP, half, 2 * hidden_width), bf16),
            pltpu.VMEM((2, GROUP, half, columns), bf16),
            pltpu.VMEM((2, chips, half, columns), bf16),
            pltpu.VMEM((2, stage_rows(half), columns), bf16),
            pltpu.VMEM((2, wide, half, width), bf16),
            pltpu.VMEM((2, 256, width), bf16),
        ]
        + sems(GATHER_SEMS)
        + sems(SUM_SEMS) * 2
        + [
            pltpu.SemaphoreType.DMA,
            pltpu.SemaphoreType.DMA((rounds + 1, 2)),
            pltpu.SemaphoreType.DMA((2,)),
            pltpu.SemaphoreType.DMA((2,)),
        ],
        compiler_params=params(collective_id),
    )(sent, rows_first, grad_all, inner, outer)


WIDTH = 1024
QUERY = HEADS * HEAD_DIM
KEY = KV_HEADS * HEAD_DIM
EXPERTS = 16
SMALL = 128
LANES = 128
AT_K = QUERY
AT_V = AT_K + KEY
AT_S = AT_V + KEY
AT_O = AT_S + SMALL
PACKED = AT_O + WIDTH
ROWS_OWN = WIDTH // GROUP
KGAIN_OWN = KEY // GROUP
HEAD_PAIRS = KV_HEADS // 2
REST = 2 * KEY + SMALL


def drained(part):
    for _ in part:
        pass


def hooks(index, steps):
    for at, step in steps:
        pl.when(index == at)(step)


def chunk_256(index):
    return pl.ds(pl.multiple_of(index * 256, 256), 256)


def root_mean(values):
    return lax.rsqrt(jnp.mean(values * values, axis=1, keepdims=True) + norm_eps)


def lane_of(shape):
    return lax.broadcasted_iota(jnp.int32, shape, 1)


def turned(values, cosine, sine):
    first = lax.rem(lane_of(values.shape), HEAD_DIM) < HEAD_DIM // 2
    swapped = jnp.where(
        first, pltpu.roll(values, LANES - HEAD_DIM // 2, 1), pltpu.roll(values, HEAD_DIM // 2, 1)
    )
    return values * cosine + swapped * sine


def short_rows():
    row = lax.broadcasted_iota(jnp.int32, (WIDTH, KEY), 0)
    column = lax.broadcasted_iota(jnp.int32, (WIDTH, KEY), 1)
    same = (lax.div(row, ROWS_OWN) == lax.div(column, KGAIN_OWN)) & (
        lax.rem(row, ROWS_OWN) == lax.rem(column, KGAIN_OWN)
    )
    return jnp.where(same, 1.0, 0.0).astype(bf16)


def gain_rows(small):
    rows = jnp.transpose(small.astype(f32))
    gain_k = dot(rows[EXPERTS : EXPERTS + 8].astype(bf16), short_rows())[3:4]
    return rows[EXPERTS : EXPERTS + 1], rows[EXPERTS + 1 : EXPERTS + 2], rows[EXPERTS + 2 : EXPERTS + 3], gain_k


def four_heads(chunk_a, chunk_b):
    low = lane_of(chunk_a.shape) < HEAD_DIM
    zero = jnp.zeros_like(chunk_a)
    return jnp.concatenate(
        [
            jnp.where(low, chunk_a, zero),
            jnp.where(low, pltpu.roll(chunk_a, HEAD_DIM, 1), zero),
            jnp.where(low, zero, pltpu.roll(chunk_b, HEAD_DIM, 1)),
            jnp.where(low, zero, chunk_b),
        ],
        axis=0,
    )


def two_chunks(blocks):
    rows = blocks.shape[0] // 4
    one, two, three, four = (blocks[n * rows : (n + 1) * rows] for n in range(4))
    low = lane_of(one.shape) < HEAD_DIM
    return (
        jnp.where(low, one, pltpu.roll(two, HEAD_DIM, 1)),
        jnp.where(low, pltpu.roll(three, HEAD_DIM, 1), four),
    )


def chunk_at(index, base=0):
    return pl.ds(pl.multiple_of(base + index * LANES, LANES), LANES)


def front_call(collective_id, tokens, cotangent, weights_own, small_own, cosine, sine, routes, starts):
    count, width = tokens.shape
    seqs = starts.shape[0]
    positions = count // seqs
    length = REPS * positions
    score_scale = HEAD_DIM ** (-0.5)
    sent_width = width + SMALL

    def kernel(
        starts_ref, tokens_ref, grad_ref, query_w, key_w, value_w, output_w, small_ref,
        cos_ref, sin_ref, routes_ref,
        dense_out, grad_all, pairs_out, soft_out, rows_first,
        attn_in, query_raw, key_raw, query_low, mixed, middle, sent, gates_out,
        packed, dense, pairs, pair_own, soft_box, bias_box,
        ws0, wr0, ws1, wr1, ws2, wr2, gs0, gr0, gs1, gr1, ks0, kr0, ks1, kr1, rs, rr, own_sem, out_sem, soft_sem, pack_sem,
    ):
        place = Place()
        core = place.core
        packing = [
            pltpu.make_async_copy(
                source, packed.at[:, pl.ds(low, source.shape[1])], pack_sem.at[index]
            )
            for index, (source, low) in enumerate(
                ((key_w, AT_K), (value_w, AT_V), (small_ref, AT_S), (query_w, 0), (output_w, AT_O))
            )
        ]
        for copy in packing:
            copy.start()

        def token_block(index, low, size):
            def block(which, row, n, other=False):
                at = (which[0] * RING + which[1]) * 2 + ((1 - core) if other else core)
                return dense.at[at, pl.ds(row, n), pl.ds(low, size)]

            return block

        def weight_gather(index, low, size, send_sem, recv_sem):
            return gather_parts(
                place.tokens, Line(send_sem, recv_sem), packed.at[:, pl.ds(low, size)],
                token_block(index, low, size), ROWS_OWN, own_sem.at[index], place.twin,
            )

        def rows_of(target):
            def block(which, row, n, other=False):
                at = (which[0] * RING + which[1]) * 2 + ((1 - core) if other else core)
                return target.at[at, pl.ds(row, n)]

            return block

        def pair_gather(seq, send_sem, recv_sem):
            def block(which, row, n, other=False):
                return pairs.at[seq, which[0] * RING + which[1], pl.ds(row, n)]

            return gather_parts(
                place.copies, Line(send_sem, recv_sem),
                pair_own.at[pl.ds(seq * positions, positions)], block, positions, own_sem.at[3 + seq],
            )

        def soft_copy(seq, index, slot):
            return pltpu.make_async_copy(
                soft_box.at[slot], soft_out.at[seq, index], soft_sem.at[slot]
            )

        rest_gather = weight_gather(0, AT_K, REST, ws0, wr0)
        query_gather = weight_gather(1, 0, QUERY, ws1, wr1)
        output_gather = weight_gather(2, AT_O, WIDTH, ws2, wr2)
        def grad_gather(seq, send_sem, recv_sem):
            base = seq * positions

            def block(which, row, n, other=False):
                at = (which[0] * RING + which[1]) * 2 + ((1 - core) if other else core)
                return grad_all.at[at, pl.ds(base + row, n)]

            return gather_parts(
                place.tokens, Line(send_sem, recv_sem), grad_ref.at[pl.ds(base, positions)], block,
                positions, own_sem.at[5 + seq], place.twin,
            )

        grads = [grad_gather(0, gs0, gr0), grad_gather(1, gs1, gr1)]
        first_rows = gather_parts(
            place.tokens, Line(rs, rr), sent.at[pl.ds(0, positions)], rows_of(rows_first), positions,
            own_sem.at[7], place.twin,
        )
        pair_gathers = [pair_gather(0, ks0, kr0), pair_gather(1, ks1, kr1)]

        greet(place.tokens.neighbours() + place.copies.neighbours() + [place.twin])
        for copy in packing:
            copy.wait()
        next(rest_gather)
        next(query_gather)
        inputs = tokens_ref[...].astype(f32)
        middle[...] = inputs * root_mean(inputs)
        next(rest_gather)
        next(query_gather)
        next(output_gather)
        query_at = place.rep * positions + lax.broadcasted_iota(jnp.int32, (positions, 1), 0)
        key_at = lax.broadcasted_iota(jnp.int32, (1, length), 1)
        for seq in range(seqs):
            allowed = key_at <= query_at
            for piece in range(starts_ref.shape[1]):
                start = starts_ref[seq, piece]
                query_inside = (query_at >= start) & (query_at < start + PIC)
                key_inside = (key_at >= start) & (key_at < start + PIC)
                allowed = allowed | (query_inside & key_inside)
            bias_box[seq] = jnp.where(allowed, 0.0, masked_score)
        next(rest_gather)
        next(query_gather)
        next(output_gather)
        drained(rest_gather)

        def weights(low, size):
            return dense[:, :, pl.ds(low, size)].reshape(width, size)

        small = weights(AT_S, SMALL)
        gain_a, gain_q, gain_f, gain_k = gain_rows(small)
        rows = (middle[...] * gain_a).astype(bf16)
        attn_in[...] = rows
        cos2 = jnp.concatenate([cos_ref[...]] * seqs, axis=0)
        sin2 = jnp.concatenate([sin_ref[...]] * seqs, axis=0)
        raw = dot(rows, weights(AT_K, KEY))
        key_raw[...] = raw
        scaled = raw * root_mean(raw) * gain_k
        for chunk in range(KEY // LANES):
            at = slice(chunk * LANES, (chunk + 1) * LANES)
            pair_own[:, at] = turned(scaled[:, at], cos2, sin2).astype(bf16)
        pair_own[:, KEY:] = dot(rows, weights(AT_V, KEY)).astype(bf16)
        next(pair_gathers[0])
        drained(query_gather)
        next(output_gather)
        next(grads[0])
        raw = dot(rows, weights(0, QUERY))
        query_raw[...] = raw
        scaled = raw * root_mean(raw) * gain_q
        for chunk in range(QUERY // LANES):
            at = slice(chunk * LANES, (chunk + 1) * LANES)
            query_low[:, at] = turned(scaled[:, at], cos2, sin2).astype(bf16)
        next(pair_gathers[0])
        next(pair_gathers[1])
        drained(output_gather)
        dense_copy = pltpu.make_async_copy(dense, dense_out, out_sem.at[0])
        dense_copy.start()
        next(grads[0])
        next(grads[1])
        next(pair_gathers[0])
        next(pair_gathers[1])
        next(grads[0])
        drained(pair_gathers[0])
        next(grads[1])

        def attend(seq, index, slot, wait_first):
            rows_at = pl.ds(seq * positions, positions)
            queries = four_heads(
                query_low[rows_at, chunk_at(2 * index)].astype(f32),
                query_low[rows_at, chunk_at(2 * index + 1)].astype(f32),
            )
            queries = (queries * score_scale).astype(bf16)
            keys = pairs[seq, :, :, chunk_at(index)].reshape(length, LANES)
            scores = dot_nt(queries, keys).reshape(4, positions, length) + bias_box[seq][None]
            scores = scores.reshape(4 * positions, length)
            raised = jnp.exp(scores - jnp.max(scores, axis=1, keepdims=True))
            soft = (raised * (1.0 / jnp.sum(raised, axis=1, keepdims=True))).astype(bf16)

            @pl.when(wait_first)
            def _():
                soft_copy(seq, index, slot).wait()

            soft_box[slot] = soft
            soft_copy(seq, index, slot).start()
            values = pairs[seq, :, :, chunk_at(index, KEY)].reshape(length, LANES)
            chunk_a, chunk_b = two_chunks(dot(soft, values))
            mixed[rows_at, chunk_at(2 * index)] = chunk_a.astype(bf16)
            mixed[rows_at, chunk_at(2 * index + 1)] = chunk_b.astype(bf16)

        def features(seq):
            at = pl.ds(seq * positions, positions)
            total = tokens_ref[at].astype(f32) + dot(mixed[at], weights(AT_O, WIDTH))
            middle[at] = total
            ffn_in = (total * root_mean(total) * gain_f).astype(bf16)
            sent[at, pl.ds(0, width)] = ffn_in
            lanes = lane_of((positions, SMALL))
            named = routes_ref[at]
            chosen = lanes == named[:, :1]
            for choice in range(1, named.shape[1]):
                chosen = chosen | (lanes == named[:, choice : choice + 1])
            logits = jnp.where(chosen, dot(ffn_in, small), masked_score)
            raised = jnp.exp(logits - jnp.max(logits, axis=1, keepdims=True))
            gates = raised * (1.0 / jnp.sum(raised, axis=1, keepdims=True))
            gates = jnp.where(chosen, gates, 0.0)
            gates_out[at] = gates
            high = gates.astype(bf16).astype(f32)
            tail = high + pltpu.roll(gates - high, EXPERTS, 1)
            sent[at, pl.ds(width, SMALL)] = tail.astype(bf16)

        def first_heads(index, carry):
            hooks(
                index,
                (
                    (1, lambda: next(grads[0])),
                    (2, lambda: next(pair_gathers[1])),
                    (3, lambda: next(grads[1])),
                ),
            )
            attend(0, index, lax.rem(index, 2), index >= 2)
            return carry

        lax.fori_loop(0, HEAD_PAIRS, first_heads, 0)
        features(0)
        next(first_rows)
        drained(pair_gathers[1])
        pairs_copy = pltpu.make_async_copy(pairs, pairs_out, out_sem.at[1])
        pairs_copy.start()

        def second_heads(index, carry):
            hooks(
                index,
                (
                    (1, lambda: next(grads[1])),
                    (3, lambda: next(first_rows)),
                ),
            )
            attend(1, index, lax.rem(index, 2), index >= 0)
            return carry

        lax.fori_loop(0, HEAD_PAIRS, second_heads, 0)
        features(1)
        next(first_rows)
        drained(grads[0])
        drained(grads[1])
        drained(first_rows)
        dense_copy.wait()
        pairs_copy.wait()
        for slot in range(2):
            soft_copy(1, 0, slot).wait()

    return pl.pallas_call(
        kernel,
        out_shape=[
            jax.ShapeDtypeStruct((GROUP, ROWS_OWN, PACKED), bf16),
            jax.ShapeDtypeStruct((GROUP, count, width), bf16),
            jax.ShapeDtypeStruct((seqs, REPS, positions, 2 * KEY), bf16),
            jax.ShapeDtypeStruct((seqs, HEAD_PAIRS, 4 * positions, length), bf16),
            jax.ShapeDtypeStruct((GROUP, positions, sent_width), bf16),
            jax.ShapeDtypeStruct((count, width), bf16),
            jax.ShapeDtypeStruct((count, QUERY), f32),
            jax.ShapeDtypeStruct((count, KEY), f32),
            jax.ShapeDtypeStruct((count, QUERY), bf16),
            jax.ShapeDtypeStruct((count, QUERY), bf16),
            jax.ShapeDtypeStruct((count, width), f32),
            jax.ShapeDtypeStruct((count, width + SMALL), bf16),
            jax.ShapeDtypeStruct((count, SMALL), f32),
        ],
        in_specs=[pl.BlockSpec(memory_space=pltpu.SMEM), IN_VMEM] + [ANY] * 6 + [IN_VMEM] * 3,
        out_specs=[ANY] * 5 + [IN_VMEM] * 8,
        scratch_shapes=[
            pltpu.VMEM((ROWS_OWN, PACKED), bf16),
            pltpu.VMEM((GROUP, ROWS_OWN, PACKED), bf16),
            pltpu.VMEM((seqs, REPS, positions, 2 * KEY), bf16),
            pltpu.VMEM((count, 2 * KEY), bf16),
            pltpu.VMEM((2, 4 * positions, length), bf16),
            pltpu.VMEM((seqs, positions, length), f32),
        ]
        + sems(GATHER_SEMS) * 8
        + [
            pltpu.SemaphoreType.DMA((8,)),
            pltpu.SemaphoreType.DMA((2,)),
            pltpu.SemaphoreType.DMA((2,)),
            pltpu.SemaphoreType.DMA((5,)),
        ],
        compiler_params=params(collective_id),
    )(starts, tokens, cotangent, *weights_own, small_own, cosine, sine, routes)


def norm_back(values, gain, grad):
    scale = root_mean(values)
    weighted = grad * gain
    mean = jnp.mean(values * weighted, axis=1, keepdims=True)
    inner = weighted * scale - values * (scale * scale * scale * mean)
    return inner, jnp.sum(grad * values * scale, axis=0, keepdims=True)


def back_call(
    collective_id, returned, gates, middle, sent, dense, cotangent, tokens, attn_in, query_raw, key_raw,
    query_low, mixed, pairs, soft, out_terms, expert_terms, cosine, sine,
):
    count, width = tokens.shape
    seqs, _, positions, _ = pairs.shape
    length = REPS * positions
    expert_rows = expert_terms.shape[0] // REPS
    score_scale = HEAD_DIM ** (-0.5)
    chips = GROUP // 2

    def kernel(
        returned_ref, gates_ref, middle_ref, sent_ref, dense_ref, grad_ref, tokens_ref, attn_ref,
        query_raw_ref, key_raw_ref, query_ref, mixed_ref, pairs_ref, soft_ref, out_ref, expert_ref,
        cos_ref, sin_ref,
        block_out, tokens_grad, dense_out, expert_all,
        weight_box, weight_rest, rest_terms, dense_own,
        o_staged, q_staged, rest_staged, o_stage, q_stage, rest_stage,
        out_held, out_staged, out_stage, expert_held, expert_stage, expert_own,
        soft_box, key_box, value_box, pair_terms, pair_stage, pair_grads,
        grad_mixed, grad_query, grad_middle, grad_attn, grad_attn_in, gain_box,
        o_got, q_got, rest_got, small_got, totals,
        out_s, out_r, exp_s, exp_r, kv0_s, kv0_r, kv1_s, kv1_r, o_s, o_r, q_s, q_r, rest_s, rest_r,
        ge_s, ge_r, go_s, go_r, gq_s, gq_r, grest_s, grest_r,
        load_sem, held_sem, box_sem, own_sem, total_sem,
    ):
        place = Place()
        core = place.core
        token_axes, copy_axes = place.tokens, place.copies
        q_terms = expert_held

        def chip_of(which):
            return which[0] * RING + which[1]

        def blocks(which, other=False):
            return chip_of(which) * 2 + ((1 - core) if other else core)

        def out_store(low, step, value):
            at = pl.ds(low, step)
            block_out[at] = (middle_ref[at] + value).astype(bf16)

        out_sum = sum_parts(
            token_axes, Line(out_s, out_r),
            lambda which, low, n: out_held.at[chip_of(which), pl.ds(low, n)],
            out_stage, count, None,
            (place.twin, lambda which: out_ref.at[blocks(which, True)],
             lambda which: out_staged.at[chip_of(which)]),
            store=out_store,
        )
        expert_sum = sum_parts(
            copy_axes, Line(exp_s, exp_r),
            lambda which, low, n: expert_held.at[pl.ds(chip_of(which) * expert_rows + low, n)],
            expert_stage, expert_rows, expert_own,
        )

        def pair_sum(seq, send_sem, recv_sem):
            return sum_parts(
                copy_axes, Line(send_sem, recv_sem),
                lambda which, low, n: pair_terms.at[seq, chip_of(which), pl.ds(low, n)],
                pair_stage.at[seq], positions, pair_grads.at[pl.ds(seq * positions, positions)],
            )

        pair_sums = [pair_sum(0, kv0_s, kv0_r), pair_sum(1, kv1_s, kv1_r)]

        def rows_of_block(terms, index, low, n):
            return terms.at[pl.ds(index * ROWS_OWN + low, n)]

        def rows_of_pairs(terms, index, low, n):
            at = lax.rem(index, 2) * ROWS_OWN + low
            return terms.at[0, lax.div(index, 2), pl.ds(at, n)]

        def dense_sum(rows_of, terms, staged, stage, low, size, send_sem, recv_sem):
            return sum_parts(
                token_axes, Line(send_sem, recv_sem),
                lambda which, row, n: rows_of(terms, blocks(which), row, n),
                stage, ROWS_OWN, dense_own.at[:, pl.ds(low, size)],
                (place.twin, lambda which: rows_of(terms, blocks(which, True), 0, ROWS_OWN),
                 lambda which: staged.at[chip_of(which)]),
            )

        o_sum = dense_sum(rows_of_pairs, pair_terms, o_staged, o_stage, AT_O, width, o_s, o_r)
        q_sum = dense_sum(rows_of_block, q_terms, q_staged, q_stage, 0, QUERY, q_s, q_r)
        rest_sum = dense_sum(rows_of_block, rest_terms, rest_staged, rest_stage, AT_K, REST, rest_s, rest_r)

        def dense_total(index, low, got, send_sem, recv_sem, tail=None):
            def own(rep):
                return dense_own.at[:, chunk_at(rep, low)]

            def target(rep):
                return dense_out.at[:, chunk_at(rep, low)]

            return total_parts(
                place, Line(send_sem, recv_sem), own, got, totals.at[index], target,
                total_sem.at[index], tail,
            )

        o_total = dense_total(0, AT_O, o_got, go_s, go_r)
        q_total = dense_total(1, 0, q_got, gq_s, gq_r)
        small_at = pl.ds(AT_S, SMALL)
        rest_total = dense_total(
            2, AT_K, rest_got, grest_s, grest_r,
            (dense_own.at[:, small_at], small_got, totals.at[3], dense_out.at[:, small_at]),
        )
        expert_gather = gather_parts(
            copy_axes, Line(ge_s, ge_r), expert_own,
            lambda which, row, n, other=False: expert_all.at[chip_of(which), pl.ds(row, n)],
            expert_rows, own_sem,
        )

        def weight_load(low, index):
            return pltpu.make_async_copy(
                dense_ref.at[:, :, pl.ds(low, width)], weight_box, load_sem.at[index]
            )

        rest_load = pltpu.make_async_copy(
            dense_ref.at[:, :, pl.ds(AT_K, REST)], weight_rest, load_sem.at[1]
        )
        expert_load = pltpu.make_async_copy(expert_ref, expert_held, load_sem.at[2])
        held_loads = [
            pltpu.make_async_copy(
                out_ref.at[2 * chip + core], out_held.at[chip], held_sem.at[chip]
            )
            for chip in range(chips)
        ]

        def box_loads(number, slot):
            seq, index = lax.div(number, HEAD_PAIRS), lax.rem(number, HEAD_PAIRS)
            return [
                pltpu.make_async_copy(
                    soft_ref.at[seq, index], soft_box.at[slot], box_sem.at[slot, 0]
                ),
                pltpu.make_async_copy(
                    pairs_ref.at[seq, :, :, chunk_at(index)], key_box.at[slot], box_sem.at[slot, 1]
                ),
                pltpu.make_async_copy(
                    pairs_ref.at[seq, :, :, chunk_at(index, KEY)],
                    value_box.at[slot],
                    box_sem.at[slot, 2],
                ),
            ]

        expert_load.start()
        rest_load.start()
        weight_load(AT_O, 0).start()
        for load in held_loads + box_loads(0, 0):
            load.start()
        greet(
            token_axes.neighbours()
            + [place.twin]
            + [(place.shard, other) for other in place.others[1:]]
        )
        next(out_sum)
        expert_load.wait()
        next(expert_sum)
        next(expert_sum)
        next(expert_sum)
        rest_load.wait()

        small = weight_rest[:, :, pl.ds(2 * KEY, SMALL)].reshape(width, SMALL)
        gain_a, gain_q, gain_f, gain_k = gain_rows(small)
        gates = gates_ref[...]
        tail = returned_ref[:, pl.ds(width, SMALL)]
        grad_gates = tail + pltpu.roll(tail, SMALL - EXPERTS, 1)
        grad_logits = gates * (grad_gates - jnp.sum(gates * grad_gates, axis=1, keepdims=True))
        grad_logits = grad_logits.astype(bf16)
        grad_ffn = returned_ref[:, pl.ds(0, width)] + dot_nt(grad_logits, small)
        inner, gain_f_terms = norm_back(middle_ref[...], gain_f, grad_ffn)
        inner = grad_ref[...].astype(f32) + inner
        grad_middle[...] = inner
        grad_attn[...] = inner.astype(bf16)
        gain_box[...] = jnp.zeros_like(gain_box)
        gain_box[pl.ds(EXPERTS + 2, 1)] = gain_f_terms
        weight_load(AT_O, 0).wait()
        grad_mixed[...] = dot_nt(
            grad_attn[...], weight_box[...].reshape(QUERY, width)
        ).astype(bf16)
        weight_load(0, 3).start()

        def attend_back(seq, index):
            number = seq * HEAD_PAIRS + index
            slot = lax.rem(number, 2)
            for load in box_loads(number, slot):
                load.wait()

            @pl.when(number + 1 < seqs * HEAD_PAIRS)
            def _():
                for load in box_loads(number + 1, 1 - slot):
                    load.start()

            rows_at = pl.ds(seq * positions, positions)
            first, second = chunk_at(2 * index), chunk_at(2 * index + 1)
            queries = four_heads(
                query_ref[rows_at, first].astype(f32), query_ref[rows_at, second].astype(f32)
            )
            queries = (queries * score_scale).astype(bf16)
            grads = four_heads(
                grad_mixed[rows_at, first].astype(f32), grad_mixed[rows_at, second].astype(f32)
            ).astype(bf16)
            keys = key_box[slot].reshape(length, LANES)
            values = value_box[slot].reshape(length, LANES)
            soft_low = soft_box[slot]
            value_terms = dot_tn(soft_low, grads)
            pair_terms[seq, :, :, chunk_at(index, KEY)] = value_terms.astype(bf16).reshape(
                REPS, positions, LANES
            )
            soft_full = soft_low.astype(f32)
            grad_soft = dot_nt(grads, values)
            weighted = soft_full * grad_soft
            grad_scores = (
                weighted - soft_full * jnp.sum(weighted, axis=1, keepdims=True)
            ).astype(bf16)
            key_terms = dot_tn(grad_scores, queries)
            pair_terms[seq, :, :, chunk_at(index)] = key_terms.astype(bf16).reshape(
                REPS, positions, LANES
            )
            chunk_a, chunk_b = two_chunks(dot(grad_scores, keys) * score_scale)
            grad_query[rows_at, first] = chunk_a.astype(bf16)
            grad_query[rows_at, second] = chunk_b.astype(bf16)

        def out_ready():
            for load in held_loads:
                load.wait()
            next(out_sum)
            next(out_sum)

        def first_heads(index, carry):
            hooks(index, ((2, lambda: next(expert_sum)), (3, out_ready)))
            attend_back(0, index)
            return carry

        lax.fori_loop(0, HEAD_PAIRS, first_heads, 0)
        next(pair_sums[0])
        next(pair_sums[0])
        next(pair_sums[0])

        def second_heads(index, carry):
            hooks(index, ((3, lambda: next(out_sum)),))
            attend_back(1, index)
            return carry

        lax.fori_loop(0, HEAD_PAIRS, second_heads, 0)
        next(pair_sums[1])
        next(pair_sums[1])
        next(pair_sums[1])
        next(pair_sums[0])
        router_terms = dot_tn(sent_ref[:, pl.ds(0, width)], grad_logits)

        cos2 = jnp.concatenate([cos_ref[...]] * seqs, axis=0)
        sin2 = -jnp.concatenate([sin_ref[...]] * seqs, axis=0)

        def turned_back(values):
            return jnp.concatenate(
                [
                    turned(values[:, low : low + LANES], cos2, sin2)
                    for low in range(0, values.shape[1], LANES)
                ],
                axis=1,
            )

        grad, gain_q_terms = norm_back(
            query_raw_ref[...], gain_q, turned_back(grad_query[...].astype(f32))
        )
        gain_box[pl.ds(EXPERTS + 1, 1)] = gain_q_terms
        grad_query_low = grad.astype(bf16)
        weight_load(0, 3).wait()
        grad_attn_in[...] = dot_nt(grad_query_low, weight_box[...].reshape(width, QUERY))

        next(pair_sums[1])
        next(expert_sum)
        next(out_sum)
        next(pair_sums[0])
        drained(pair_sums[0])
        next(pair_sums[1])

        def o_rows(index, carry):
            at = chunk_256(index)
            value = dot_tn(mixed_ref[:, at], grad_attn[...]).astype(bf16)
            pair_terms[0, pl.ds(2 * index, 2)] = value.reshape(2, positions, width)
            return carry

        lax.fori_loop(0, QUERY // 256, o_rows, 0)
        next(o_sum)
        drained(expert_sum)
        next(expert_gather)

        def q_rows(index, carry):
            at = chunk_256(index)
            q_terms[at] = dot_tn(attn_ref[:, at], grad_query_low).astype(bf16)
            return carry

        lax.fori_loop(0, width // 256, q_rows, 0)
        next(q_sum)
        next(o_sum)
        next(o_sum)
        drained(out_sum)
        next(q_sum)
        next(q_sum)
        next(o_sum)
        drained(pair_sums[1])

        grads = pair_grads[...]
        grad, gain_k_terms = norm_back(
            key_raw_ref[...],
            gain_k,
            turned_back(grads[:, :KEY].astype(bf16).astype(f32)),
        )
        grad_pairs = jnp.concatenate([grad.astype(bf16), grads[:, KEY:].astype(bf16)], axis=1)
        gain_k_row = dot_nt(
            jnp.broadcast_to(gain_k_terms, (8, KEY)).astype(bf16), short_rows()
        )
        gain_box[pl.ds(EXPERTS + 3, 1)] = gain_k_row[:1]
        grad = grad_attn_in[...] + dot_nt(
            grad_pairs, weight_rest[:, :, pl.ds(0, 2 * KEY)].reshape(width, 2 * KEY)
        )
        values = tokens_ref[...].astype(f32)
        inner, gain_a_terms = norm_back(values, gain_a, grad)
        tokens_grad[...] = (grad_middle[...] + inner).astype(bf16)
        gain_box[pl.ds(EXPERTS, 1)] = gain_a_terms
        rest_terms[:, pl.ds(2 * KEY, SMALL)] = (
            router_terms + jnp.transpose(gain_box[...])
        ).astype(bf16)

        def rest_rows(index, carry):
            at = chunk_256(index)
            rest_terms[at, pl.ds(0, 2 * KEY)] = dot_tn(attn_ref[:, at], grad_pairs).astype(bf16)
            return carry

        lax.fori_loop(0, width // 256, rest_rows, 0)
        next(rest_sum)
        next(rest_sum)
        next(rest_sum)
        next(q_sum)
        next(o_sum)
        next(expert_gather)
        next(rest_sum)
        drained(o_sum)
        next(o_total)
        next(q_sum)
        next(expert_gather)
        next(rest_sum)
        next(o_total)
        drained(q_sum)
        next(q_total)
        drained(rest_sum)
        next(rest_total)
        next(q_total)
        next(rest_total)
        drained(o_total)
        drained(q_total)
        drained(expert_gather)
        drained(rest_total)

    block = pltpu.VMEM((GROUP, ROWS_OWN, width), bf16)
    scratch = [
        block,
        pltpu.VMEM((GROUP, ROWS_OWN, REST), bf16),
        pltpu.VMEM((width, REST), bf16),
        pltpu.VMEM((ROWS_OWN, PACKED), bf16),
        pltpu.VMEM((chips, ROWS_OWN, width), bf16),
        pltpu.VMEM((chips, ROWS_OWN, QUERY), bf16),
        pltpu.VMEM((chips, ROWS_OWN, REST), bf16),
        pltpu.VMEM((stage_rows(ROWS_OWN), width), bf16),
        pltpu.VMEM((stage_rows(ROWS_OWN), QUERY), bf16),
        pltpu.VMEM((stage_rows(ROWS_OWN), REST), bf16),
        pltpu.VMEM((chips, count, width), bf16),
        pltpu.VMEM((chips, count, width), bf16),
        pltpu.VMEM((stage_rows(count), width), bf16),
        pltpu.VMEM(expert_terms.shape, bf16),
        pltpu.VMEM((stage_rows(expert_rows), width), bf16),
        pltpu.VMEM((expert_rows, width), bf16),
        pltpu.VMEM((2, 4 * positions, length), bf16),
        pltpu.VMEM((2, REPS, positions, LANES), bf16),
        pltpu.VMEM((2, REPS, positions, LANES), bf16),
        pltpu.VMEM((seqs, REPS, positions, 2 * KEY), bf16),
        pltpu.VMEM((seqs, stage_rows(positions), 2 * KEY), bf16),
        pltpu.VMEM((count, 2 * KEY), f32),
        pltpu.VMEM((count, QUERY), bf16),
        pltpu.VMEM((count, QUERY), bf16),
        pltpu.VMEM((count, width), f32),
        pltpu.VMEM((count, width), bf16),
        pltpu.VMEM((count, width), f32),
        pltpu.VMEM((SMALL, width), f32),
    ]
    scratch += [pltpu.VMEM((REPS, ROWS_OWN, LANES), bf16)] * 4
    scratch += [pltpu.VMEM((4, ROWS_OWN, LANES), bf16)]
    return pl.pallas_call(
        kernel,
        out_shape=[
            jax.ShapeDtypeStruct((count, width), bf16),
            jax.ShapeDtypeStruct((count, width), bf16),
            jax.ShapeDtypeStruct((ROWS_OWN, PACKED), bf16),
            jax.ShapeDtypeStruct((REPS, expert_rows, width), bf16),
        ],
        in_specs=[IN_VMEM] * 4 + [ANY] + [IN_VMEM] * 7 + [ANY] * 4 + [IN_VMEM] * 2,
        out_specs=[IN_VMEM, IN_VMEM, ANY, ANY],
        scratch_shapes=scratch
        + sems(SUM_SEMS) * 7
        + sems(GATHER_SEMS)
        + sems(TOTAL_SEMS) * 3
        + [
            pltpu.SemaphoreType.DMA((4,)),
            pltpu.SemaphoreType.DMA((chips,)),
            pltpu.SemaphoreType.DMA((2, 3)),
            pltpu.SemaphoreType.DMA,
            pltpu.SemaphoreType.DMA((3, 2)),
        ],
        compiler_params=params(collective_id),
    )(
        returned, gates, middle, sent, dense, cotangent, tokens, attn_in, query_raw, key_raw,
        query_low, mixed, pairs, soft, out_terms, expert_terms, cosine, sine,
    )


def finish_call(dense_own, expert_all, inner_rows):
    total_rows, width = expert_all.shape
    step = 256
    inner_steps, steps = inner_rows // step, total_rows // step

    def kernel(dense_ref, expert_ref, inner, outer, query, key, value, output, small):
        at = pl.program_id(0)
        rows = expert_ref[...].astype(f32)

        @pl.when(at < inner_steps)
        def _():
            inner[...] = rows

        @pl.when(at >= inner_steps)
        def _():
            outer[...] = rows

        @pl.when(at == 1)
        def _():
            for low, target in ((0, query), (AT_K, key), (AT_V, value), (AT_O, output), (AT_S, small)):
                target[...] = dense_ref[:, pl.ds(low, target.shape[1])].astype(f32)

    def whole(columns):
        return pl.BlockSpec((ROWS_OWN, columns), lambda i: (0, 0))

    sizes = (QUERY, KEY, KEY, WIDTH, SMALL)
    return pl.pallas_call(
        kernel,
        grid=(steps,),
        out_shape=[
            jax.ShapeDtypeStruct((inner_rows, width), f32),
            jax.ShapeDtypeStruct((total_rows - inner_rows, width), f32),
        ]
        + [jax.ShapeDtypeStruct((ROWS_OWN, size), f32) for size in sizes],
        in_specs=[
            pl.BlockSpec(dense_own.shape, lambda i: (0, 0)),
            pl.BlockSpec((step, width), lambda i: (i, 0)),
        ],
        out_specs=[
            pl.BlockSpec((step, width), lambda i: (jnp.minimum(i, inner_steps - 1), 0)),
            pl.BlockSpec((step, width), lambda i: (jnp.maximum(i - inner_steps, 0), 0)),
        ]
        + [whole(size) for size in sizes],
        compiler_params=pltpu.CompilerParams(vmem_limit_bytes=VMEM_LIMIT),
    )(dense_own, expert_all)


def rotary_tables(positions):
    lane = jnp.arange(LANES, dtype=jnp.int32)
    half = HEAD_DIM // 2
    exponent = (lane % half).astype(f32) * (2.0 / HEAD_DIM)
    frequency = rope_base ** (-exponent)
    angles = positions.astype(f32)[:, None] * frequency[None, :]
    sign = jnp.where(lane % HEAD_DIM < half, -1.0, 1.0).astype(f32)
    return jnp.cos(angles), jnp.sin(angles) * sign[None, :]


def small_columns(router, gain_a, gain_q, gain_f, gain_k):
    rows = router.shape[0]
    lane = jnp.arange(SMALL)[None, :]
    small = jnp.pad(router, ((0, 0), (0, SMALL - EXPERTS)))
    short = jnp.pad(gain_k, (0, rows - gain_k.shape[0]))
    for at, gain in enumerate((gain_a, gain_q, gain_f, short)):
        small = jnp.where(lane == EXPERTS + at, gain[:, None], small)
    return small


def shards(
    tokens,
    cotangent,
    routes,
    picture_starts,
    attn_gain,
    query_weight,
    key_weight,
    value_weight,
    query_gain,
    key_gain,
    output_weight,
    ffn_gain,
    router_weight,
    expert_in,
    expert_down,
):
    seqs, positions, width = tokens.shape
    count = seqs * positions
    query_pos = lax.axis_index("rep") * positions + jnp.arange(positions, dtype=jnp.int32)
    cosine, sine = rotary_tables(query_pos)
    rows = tokens.reshape(count, width)
    grad_rows = cotangent.reshape(count, width)
    (
        dense, grad_all, pairs, soft, rows_first,
        attn_in, query_raw, key_raw, query_low, mixed, middle, sent, gates,
    ) = front_call(
        1, rows, grad_rows, (query_weight, key_weight, value_weight, output_weight),
        small_columns(router_weight, attn_gain, query_gain, ffn_gain, key_gain),
        cosine, sine, routes.reshape(count, routes.shape[2]), picture_starts,
    )
    returned, out_terms, expert_terms = moe_call(
        2, sent, rows_first, grad_all, expert_in[0], expert_down[0]
    )
    block_out, tokens_grad, dense_out, expert_all = back_call(
        3, returned, gates, middle, sent, dense, grad_rows, rows, attn_in,
        query_raw, key_raw, query_low, mixed, pairs, soft, out_terms, expert_terms, cosine, sine,
    )
    inner, outer, query, key, value, output, small = finish_call(
        dense_out, expert_all.reshape(-1, width), expert_in.shape[1]
    )
    return (
        block_out.reshape(tokens.shape),
        tokens_grad.reshape(tokens.shape),
        small[:, EXPERTS],
        query,
        key,
        value,
        small[:, EXPERTS + 1],
        small[: key_gain.shape[0], EXPERTS + 3],
        output,
        small[:, EXPERTS + 2],
        small[:, :EXPERTS],
        inner[None],
        outer[None],
    )


def solution(mesh):
    by_tokens = P("shard", "rep", None)
    rows, line, block = P("shard", None), P("shard"), P("shard", None, None)
    in_specs = (
        by_tokens, by_tokens, by_tokens, rows, line, rows, rows, rows, line, line, rows, line, rows, block, block,
    )
    out_specs = (
        by_tokens, by_tokens, line, rows, rows, rows, line, line, rows, line, rows, block, block,
    )
    return jax.shard_map(shards, mesh=mesh, in_specs=in_specs, out_specs=out_specs, check_vma=False)
```

```python
import jax
import jax.numpy as jnp
from jax import lax
from jax.experimental import pallas as pl
from jax.experimental.pallas import tpu as pltpu
from jax.sharding import PartitionSpec as P

HEADS = 16
KV_HEADS = 8
HEAD_DIM = 64
PIC = 256
RING = 4
GROUP = 16
REPS = 8
VMEM_LIMIT = 63 << 20

norm_eps = 1e-06
rope_base = 10000.0
masked_score = -1e30

bf16 = jnp.bfloat16
f32 = jnp.float32


class Place:
    def __init__(self):
        shard = lax.axis_index("shard")
        rep = lax.axis_index("rep")
        self.shard, self.rep = shard, rep
        core = lax.rem(shard, 2)
        ring_z = lax.rem(lax.div(shard, 2), RING)
        y_hi = lax.div(shard, 8)
        ring_x = lax.rem(rep, RING)
        y_lo = lax.div(rep, RING)
        self.core = core

        def shard_of(hi, z, c):
            return (hi * RING + z) * 2 + c

        def rep_of(lo, x):
            return lo * RING + x

        def up(v):
            return lax.rem(v + 1, RING)

        def down(v):
            return lax.rem(v + RING - 1, RING)

        self.twin = (shard_of(y_hi, ring_z, 1 - core), rep)
        self.others = [lax.rem(rep + step, REPS) for step in range(REPS)]
        self.tokens = Axes(
            y_hi,
            ring_z,
            (shard_of(y_hi, up(ring_z), core), rep),
            (shard_of(y_hi, down(ring_z), core), rep),
            (shard_of(1 - y_hi, ring_z, core), rep_of(1 - y_lo, ring_x)),
        )
        self.copies = Axes(
            y_lo,
            ring_x,
            (shard, rep_of(y_lo, up(ring_x))),
            (shard, rep_of(y_lo, down(ring_x))),
            (shard, rep_of(1 - y_lo, ring_x)),
        )


class Axes:
    def __init__(self, side, spot, ahead, behind, across):
        self.side, self.spot = side, spot
        self.ahead, self.behind, self.across = ahead, behind, across
        sides = (side, 1 - side)
        spots = [lax.rem(spot + step, RING) for step in range(RING)]
        self.places = [[(sides[flip], spots[step]) for step in range(RING)] for flip in range(2)]

    def at(self, flip, step):
        return self.places[flip][step % RING]

    def neighbours(self):
        return [self.ahead, self.behind, self.across]


def greet(devices):
    barrier = pltpu.get_barrier_semaphore()
    for device in devices:
        pl.semaphore_signal(barrier, inc=1, device_id=device, device_id_type=pl.DeviceIdType.MESH)
    pl.semaphore_wait(barrier, len(devices))


class Line:
    def __init__(self, send_sem, recv_sem):
        self.send_sem, self.recv_sem = send_sem, recv_sem
        self.sent = []

    def copy(self, index, source, target, device):
        return pltpu.make_async_remote_copy(
            src_ref=source(),
            dst_ref=target(),
            send_sem=self.send_sem.at[index],
            recv_sem=self.recv_sem.at[index],
            device_id=device,
            device_id_type=pl.DeviceIdType.MESH,
        )

    def send(self, index, source, target, device):
        self.copy(index, source, target, device).start()
        self.sent.append((index, source, target, device))

    def take(self, index, target, device):
        self.copy(index, target, target, device).wait_recv()

    def finish(self):
        for sent in self.sent:
            self.copy(*sent).wait_send()


def abreast(*parts):
    running = list(parts)
    while running:
        for part in list(running):
            try:
                next(part)
            except StopIteration:
                running.remove(part)


GATHER_SEMS = 20


def gather_parts(axes, line, own, block, rows, local_sem, twin=None, twin_later=False):
    half, quarter = rows // 2, rows // 4
    mine, back, front, far = axes.at(0, 0), axes.at(0, -1), axes.at(0, 1), axes.at(0, 2)
    pair, pair_back, pair_front, pair_far = (axes.at(1, n) for n in (0, -1, 1, 2))
    ahead, behind, across = axes.ahead, axes.behind, axes.across

    def rows_of(which, low=0, count=rows, other=False):
        return lambda: block(which, low, count, other)

    def first(index, device):
        line.send(index, lambda: own, rows_of(mine), device)

    def relay(index, device, which, low=0, count=rows):
        line.send(index, rows_of(which, low, count), rows_of(which, low, count), device)

    def share(index, which):
        if twin is not None:
            relay(12 + index, twin, which)

    def keep():
        return pltpu.make_async_copy(own, block(mine, 0, rows), local_sem)

    keep().start()
    if twin is not None:
        first(12, twin)
    first(0, ahead)
    first(1, behind)
    first(2, across)
    keep().wait()
    yield
    line.take(0, rows_of(back), ahead)
    relay(3, ahead, back, 0, half)
    relay(4, across, back, half, half)
    share(1, back)
    line.take(1, rows_of(front), behind)
    relay(5, behind, front, half, half)
    relay(6, across, front, half, half)
    share(2, front)
    line.take(2, rows_of(pair), across)
    relay(7, ahead, pair, 0, half)
    relay(8, behind, pair, 0, half)
    share(3, pair)
    yield
    line.take(3, rows_of(far, 0, half), ahead)
    line.take(5, rows_of(far, half, half), behind)
    relay(9, across, far, half, half)
    share(4, far)
    line.take(7, rows_of(pair_back, 0, half), ahead)
    relay(10, ahead, pair_back, 0, quarter)
    line.take(8, rows_of(pair_front, 0, half), behind)
    relay(11, behind, pair_front, quarter, quarter)
    line.take(4, rows_of(pair_back, half, half), across)
    share(5, pair_back)
    line.take(6, rows_of(pair_front, half, half), across)
    share(6, pair_front)
    yield
    line.take(10, rows_of(pair_far, 0, quarter), ahead)
    line.take(11, rows_of(pair_far, quarter, quarter), behind)
    line.take(9, rows_of(pair_far, half, half), across)
    share(7, pair_far)
    yield
    if twin is not None and not twin_later:
        for index, which in enumerate(gather_order(axes)):
            line.take(12 + index, rows_of(which, other=True), twin)
    line.finish()


SUM_SEMS = 20
TOTAL_SEMS = 16


def total_parts(place, line, own, got, total, target, local_sem):
    rep = place.rep
    steps = range(1, REPS)
    peers = {step: (place.shard, place.others[step]) for step in steps}
    before = {step: place.others[REPS - step] for step in steps}

    def kept():
        return pltpu.make_async_copy(total, target(rep), local_sem)

    for step in steps:
        line.send(step, lambda p=place.others[step]: own(p), lambda: got.at[rep], peers[step])
    yield
    value = own(rep)[...].astype(f32)
    for step in steps:
        line.take(step, lambda b=before[step]: got.at[b], peers[step])
        value = value + got[before[step]].astype(f32)
    total[...] = value.astype(bf16)
    kept().start()
    for step in steps:
        line.send(8 + step, lambda: total, lambda: target(rep), peers[step])
    yield
    for step in steps:
        line.take(8 + step, lambda b=before[step]: target(b), peers[step])
    kept().wait()
    line.finish()


def spread_parts(place, line, own, got, total):
    rep = place.rep
    steps = range(1, REPS)
    for step in steps:
        peer = (place.shard, place.others[step])
        line.send(step, lambda: own, lambda: got.at[rep], peer)
    yield
    value = own[...].astype(f32)
    for step in steps:
        before = place.others[REPS - step]
        line.take(step, lambda: got.at[before], (place.shard, place.others[step]))
        value = value + got[before].astype(f32)
    total[...] = value
    line.finish()


def add_rows(target, source, rows):
    step = 16
    count = rows // step

    def body(index, carry):
        at = pl.ds(pl.multiple_of(index * step, step), step)
        target[at] = target[at] + source[at]
        return carry

    lax.fori_loop(0, count, body, 0)


def stage_rows(rows):
    return 7 * rows


def gather_order(axes):
    return [axes.at(*v) for v in ((0, 0), (0, -1), (0, 1), (1, 0), (0, 2), (1, -1), (1, 1), (1, 2))]


def sum_order(axes):
    return [axes.at(*v) for v in ((1, 2), (0, 2), (1, -1), (1, 1), (0, -1), (0, 1), (1, 0), (0, 0))]


def sum_parts(axes, line, part, stage, rows, result, twin=None, store=None):
    half, quarter = rows // 2, rows // 4
    mine, back, front, far = axes.at(0, 0), axes.at(0, -1), axes.at(0, 1), axes.at(0, 2)
    pair, pair_back, pair_front, pair_far = (axes.at(1, n) for n in (0, -1, 1, 2))
    ahead, behind, across = axes.ahead, axes.behind, axes.across
    order = sum_order(axes)
    offsets, used = {}, 0
    for name, size in (
        ("Y0", half), ("M0", quarter), ("P0", quarter), ("M1", half), ("Y1", half), ("Y2", half),
        ("P1", half), ("M2", half), ("P2", half), ("M3", rows), ("P3", rows), ("Y3", rows),
    ):
        offsets[name] = (used, size, len(offsets))
        used += size

    def landing(name):
        low, size, _ = offsets[name]
        return lambda: stage.at[pl.ds(low, size)]

    def send(name, which, low, device):
        _, size, index = offsets[name]
        line.send(index, lambda: part(which, low, size), landing(name), device)

    def add(name, which, low, device):
        _, size, index = offsets[name]
        line.take(index, landing(name), device)
        add_rows(part(which, low, size), landing(name)(), size)

    def join(*places):
        if twin is not None:
            for place in places:
                line.take(12 + place, lambda: twin[2](order[place]), twin[0])
                add_rows(part(order[place], 0, rows), twin[2](order[place]), rows)

    def hand(*places):
        if twin is not None:
            for place in places:
                which = order[place]
                line.send(
                    12 + place, lambda w=which: twin[1](w), lambda w=which: twin[2](w), twin[0]
                )

    hand(0, 1, 2, 3)
    yield
    join(0)
    send("Y0", pair_far, half, across)
    send("M0", pair_far, 0, behind)
    send("P0", pair_far, quarter, ahead)
    join(1)
    send("M1", far, 0, behind)
    join(2)
    send("Y1", pair_back, half, across)
    join(3)
    send("Y2", pair_front, half, across)
    yield
    hand(4, 5, 6, 7)
    yield
    add("M0", pair_back, 0, behind)
    send("M2", pair_back, 0, behind)
    add("P0", pair_front, quarter, ahead)
    send("P2", pair_front, 0, ahead)
    add("Y0", far, half, across)
    send("P1", far, half, ahead)
    yield
    join(4, 5, 6, 7)
    add("M1", back, 0, behind)
    add("Y1", back, half, across)
    send("M3", back, 0, behind)
    add("M2", pair, 0, behind)
    add("P2", pair, 0, ahead)
    send("Y3", pair, 0, across)
    add("P1", front, half, ahead)
    add("Y2", front, half, across)
    send("P3", front, 0, ahead)
    yield
    for name, device in (("M3", behind), ("P3", ahead), ("Y3", across)):
        line.take(offsets[name][2], landing(name), device)
    step = 16

    def body(index, carry):
        low = pl.multiple_of(index * step, step)
        total = part(mine, low, step)[...].astype(f32)
        for name in ("M3", "P3", "Y3"):
            total = total + stage[pl.ds(offsets[name][0] + low, step)].astype(f32)
        if store is None:
            result[pl.ds(low, step)] = total.astype(result.dtype)
        else:
            store(low, step, total)
        return carry

    lax.fori_loop(0, rows // step, body, 0)
    line.finish()


def sems(count):
    return [pltpu.SemaphoreType.DMA((count,)), pltpu.SemaphoreType.DMA((count,))]


ANY = pl.BlockSpec(memory_space=pl.ANY)
IN_VMEM = pl.BlockSpec(memory_space=pltpu.VMEM)


def params(collective_id):
    return pltpu.CompilerParams(
        collective_id=collective_id, has_side_effects=True, vmem_limit_bytes=VMEM_LIMIT
    )


def dot(a, b):
    return jnp.dot(a, b, preferred_element_type=f32)


def dot_nt(a, b):
    return lax.dot_general(a, b, (((1,), (1,)), ((), ())), preferred_element_type=f32)


def dot_tn(a, b):
    return lax.dot_general(a, b, (((0,), (0,)), ((), ())), preferred_element_type=f32)


def pick(index, values):
    chosen = values[-1]
    for at in range(len(values) - 2, -1, -1):
        chosen = jnp.where(index == at, values[at], chosen)
    return chosen


def moe_call(collective_id, sent, rows_first, grad_all, inner, outer):
    count, columns = sent.shape
    width = inner.shape[0]
    hidden_width = outer.shape[0]
    small = columns - width
    half = count // 2
    chips = GROUP // 2
    wide = 4
    rounds = GROUP // wide

    def kernel(
        sent_ref, first_ref, grad_ref, inner_ref, outer_ref,
        returned, expert_own, out_terms,
        rows_in, grads, hidden, back_gu, back, back_staged, back_stage, out_box,
        inner_stage, down_stage,
        gs, gr, bs0, br0, bs1, br1, is_, ir, ds_, dr, own_sem, load_sem, box_sem,
    ):
        place = Place()
        axes, core, shard = place.tokens, place.core, place.shard
        gather_line = Line(gs, gr)

        def chip_of(which):
            return which[0] * RING + which[1]

        def blocks(which, other=False):
            return chip_of(which) * 2 + ((1 - core) if other else core)

        gather = gather_parts(
            axes, gather_line, sent_ref.at[pl.ds(half, half)],
            lambda which, low, n, other=False: rows_in.at[1, blocks(which, other), pl.ds(low, n)],
            half, own_sem, place.twin, twin_later=True,
        )

        def sum_of(chunk, send_sem, recv_sem):
            return sum_parts(
                axes, Line(send_sem, recv_sem),
                lambda which, low, n: back.at[chunk, blocks(which), pl.ds(low, n)],
                back_stage.at[chunk], half, returned.at[pl.ds(chunk * half, half)],
                (place.twin, lambda which: back.at[chunk, blocks(which, True)],
                 lambda which: back_staged.at[chunk, chip_of(which)]),
            )

        sums = [sum_of(0, bs0, br0), sum_of(1, bs1, br1)]
        inner_rows, down_rows = width // REPS, hidden_width // REPS

        def inner_part(which, low, n):
            at = chip_of(which)
            return out_box.at[lax.div(at, wide), lax.rem(at, wide), pl.ds(low, n)]

        def down_part(which, low, n):
            at = chip_of(which)
            row = lax.rem(at, 2) * down_rows + low
            return back_gu.at[0, lax.div(at, 2), pl.ds(row, n)]

        inner_sum = sum_parts(
            place.copies, Line(is_, ir), inner_part, inner_stage, inner_rows,
            expert_own.at[pl.ds(0, inner_rows)],
        )
        down_sum = sum_parts(
            place.copies, Line(ds_, dr), down_part, down_stage, down_rows,
            expert_own.at[pl.ds(inner_rows, down_rows)],
        )

        def loads(t):
            at = pl.ds(t * wide, wide)
            return [
                pltpu.make_async_copy(first_ref.at[at], rows_in.at[0, at], load_sem.at[t, 0]),
                pltpu.make_async_copy(
                    grad_ref.at[at, pl.ds(0, half)], grads.at[0, at], load_sem.at[t, 1]
                ),
            ]

        second_grads = pltpu.make_async_copy(
            grad_ref.at[:, pl.ds(half, half)], grads.at[1], load_sem.at[rounds, 0]
        )

        def box_copy(chunk, first, slot):
            return pltpu.make_async_copy(
                out_box.at[slot],
                out_terms.at[pl.ds(first, wide), pl.ds(chunk * half, half)],
                box_sem.at[slot],
            )

        rows_count = wide * half
        lanes = lane_of((rows_count, small))
        is_high, is_rest = lanes == shard, lanes == shard + GROUP

        def tile(chunk, first, slot, wait_first):
            at = pl.ds(first, wide)
            row_block = rows_in[chunk, at].reshape(rows_count, columns)
            gate = jnp.sum(
                jnp.where(is_high | is_rest, row_block[:, width:].astype(f32), 0.0),
                axis=1, keepdims=True,
            )
            gate_up = dot(row_block[:, :width], inner_ref[...])
            gate_part, up_part = gate_up[:, :hidden_width], gate_up[:, hidden_width:]
            sigmoid = 1.0 / (1.0 + jnp.exp(-gate_part))
            active = gate_part * sigmoid
            product = active * up_part
            hidden_low = product.astype(bf16)
            hidden[chunk, at] = hidden_low.reshape(wide, half, hidden_width)
            out_rows = (gate * dot(hidden_low, outer_ref[...])).astype(bf16)

            @pl.when(wait_first)
            def _():
                box_copy(chunk, first, slot).wait()

            out_box[slot] = out_rows.reshape(wide, half, width)
            box_copy(chunk, first, slot).start()
            grad = grads[chunk, at].reshape(rows_count, width)
            grad_hidden = dot_nt(grad, outer_ref[...])
            grad_gate = jnp.sum(grad_hidden * product, axis=1, keepdims=True)
            grad_hidden = grad_hidden * gate
            grad_gate_up = jnp.concatenate(
                [
                    grad_hidden * up_part * sigmoid * (1.0 + gate_part * (1.0 - sigmoid)),
                    grad_hidden * active,
                ],
                axis=1,
            ).astype(bf16)
            back_gu[chunk, at] = grad_gate_up.reshape(wide, half, 2 * hidden_width)
            grads[chunk, at] = (gate * grad.astype(f32)).astype(bf16).reshape(wide, half, width)
            grad_rows = dot_nt(grad_gate_up, inner_ref[...]).astype(bf16)
            back[chunk, at, :, pl.ds(0, width)] = grad_rows.reshape(wide, half, width)
            high = grad_gate.astype(bf16).astype(f32)
            tail = jnp.where(is_high, high, jnp.where(is_rest, grad_gate - high, 0.0))
            back[chunk, at, :, pl.ds(width, small)] = tail.astype(bf16).reshape(wide, half, small)

        for t in range(rounds):
            for load in loads(t):
                load.start()
        second_grads.start()
        greet(axes.neighbours() + place.copies.neighbours() + [place.twin])
        next(gather)

        def first_tiles(t, carry):
            hooks(t, ((2, lambda: next(gather)),))
            for load in loads(t):
                load.wait()
            tile(0, t * wide, lax.rem(t, 2), t >= 2)
            return carry

        lax.fori_loop(0, rounds, first_tiles, 0)
        next(sums[0])
        next(gather)
        second_grads.wait()
        near, beyond = lax.div(axes.spot, 2), 1 - lax.div(axes.spot, 2)
        chips_per_round = wide // 2
        firsts = [
            (side * RING + part * chips_per_round) * 2
            for side, part in (
                (axes.side, beyond), (1 - axes.side, near), (1 - axes.side, beyond), (axes.side, near),
            )
        ]
        arrivals = gather_order(axes)

        def arrived(*numbers):
            for number in numbers:
                gather_line.take(
                    12 + number, lambda: rows_in.at[1, blocks(arrivals[number], True)], place.twin
                )

        def second_tiles(t, carry):
            hooks(
                t,
                (
                    (0, lambda: arrived(0, 1, 2, 4)),
                    (1, lambda: (next(sums[0]), next(sums[0]), arrived(3, 5, 6))[2]),
                    (2, lambda: (next(gather), arrived(7))[1]),
                    (3, lambda: (next(sums[1]), next(sums[0]))[0]),
                ),
            )
            tile(1, pick(t, firsts), lax.rem(t, 2), t >= 0)
            return carry

        lax.fori_loop(0, rounds, second_tiles, 0)
        next(sums[1])
        next(sums[1])

        every = 2 * GROUP * half
        for slot in range(2):
            box_copy(1, 0, slot).wait()

        def inner_terms(index, carry):
            hooks(index, ((2, lambda: next(sums[0])), (3, lambda: next(sums[1]))))
            at = chunk_256(index)
            value = dot_tn(
                rows_in[:, :, :, at].reshape(every, 256),
                back_gu[...].reshape(every, 2 * hidden_width),
            )
            out_box[lax.div(index, 2), pl.ds(2 * lax.rem(index, 2), 2)] = value.astype(bf16).reshape(
                2, half, width
            )
            return carry

        lax.fori_loop(0, width // 256, inner_terms, 0)
        for _ in range(3):
            next(inner_sum)

        def down_terms(index, carry):
            at = chunk_256(index)
            value = dot_tn(hidden[:, :, :, at].reshape(every, 256), grads[...].reshape(every, width))
            back_gu[0, pl.ds(2 * index, 2)] = value.astype(bf16).reshape(2, half, width)
            return carry

        lax.fori_loop(0, hidden_width // 256, down_terms, 0)
        for _ in range(3):
            next(down_sum)
        drained(sums[0])
        next(inner_sum)
        next(sums[1])
        next(down_sum)
        next(inner_sum)
        next(down_sum)
        drained(sums[1])
        drained(inner_sum)
        drained(down_sum)
        drained(gather)

    own_rows = (width + hidden_width) // REPS
    return pl.pallas_call(
        kernel,
        out_shape=[
            jax.ShapeDtypeStruct((count, columns), bf16),
            jax.ShapeDtypeStruct((own_rows, width), bf16),
            jax.ShapeDtypeStruct((GROUP, count, width), bf16),
        ],
        in_specs=[ANY, ANY, ANY, IN_VMEM, IN_VMEM],
        out_specs=[IN_VMEM, IN_VMEM, ANY],
        scratch_shapes=[
            pltpu.VMEM((2, GROUP, half, columns), bf16),
            pltpu.VMEM((2, GROUP, half, width), bf16),
            pltpu.VMEM((2, GROUP, half, hidden_width), bf16),
            pltpu.VMEM((2, GROUP, half, 2 * hidden_width), bf16),
            pltpu.VMEM((2, GROUP, half, columns), bf16),
            pltpu.VMEM((2, chips, half, columns), bf16),
            pltpu.VMEM((2, stage_rows(half), columns), bf16),
            pltpu.VMEM((2, wide, half, width), bf16),
            pltpu.VMEM((stage_rows(width // REPS), width), bf16),
            pltpu.VMEM((stage_rows(hidden_width // REPS), width), bf16),
        ]
        + sems(GATHER_SEMS)
        + sems(SUM_SEMS) * 4
        + [
            pltpu.SemaphoreType.DMA,
            pltpu.SemaphoreType.DMA((rounds + 1, 2)),
            pltpu.SemaphoreType.DMA((2,)),
        ],
        compiler_params=params(collective_id),
    )(sent, rows_first, grad_all, inner, outer)


WIDTH = 1024
QUERY = HEADS * HEAD_DIM
KEY = KV_HEADS * HEAD_DIM
EXPERTS = 16
SMALL = 128
LANES = 128
AT_K = QUERY
AT_V = AT_K + KEY
AT_S = AT_V + KEY
AT_O = AT_S + SMALL
PACKED = AT_O + WIDTH
ROWS_OWN = WIDTH // GROUP
KGAIN_OWN = KEY // GROUP
HEAD_PAIRS = KV_HEADS // 2
REST = 2 * KEY + SMALL


def drained(part):
    for _ in part:
        pass


def hooks(index, steps):
    for at, step in steps:
        pl.when(index == at)(step)


def chunk_256(index):
    return pl.ds(pl.multiple_of(index * 256, 256), 256)


def root_mean(values):
    return lax.rsqrt(jnp.mean(values * values, axis=1, keepdims=True) + norm_eps)


def lane_of(shape):
    return lax.broadcasted_iota(jnp.int32, shape, 1)


def turned(values, cosine, sine):
    first = (lane_of(values.shape) & (HEAD_DIM - 1)) < HEAD_DIM // 2
    swapped = jnp.where(
        first, pltpu.roll(values, LANES - HEAD_DIM // 2, 1), pltpu.roll(values, HEAD_DIM // 2, 1)
    )
    return values * cosine + swapped * sine


def gain_rows(small):
    rows = jnp.transpose(small.astype(f32))
    short = small.reshape(GROUP, ROWS_OWN, SMALL)[:, :KGAIN_OWN].reshape(KEY, SMALL)
    gain_k = jnp.transpose(short.astype(f32))[EXPERTS + 3 : EXPERTS + 4]
    return rows[EXPERTS : EXPERTS + 1], rows[EXPERTS + 1 : EXPERTS + 2], rows[EXPERTS + 2 : EXPERTS + 3], gain_k


def long_column(columns):
    cut = columns.reshape(GROUP, KGAIN_OWN, SMALL)
    return jnp.concatenate([cut, jnp.zeros_like(cut)], axis=1).reshape(WIDTH, SMALL)


def four_heads(chunk_a, chunk_b):
    low = lane_of(chunk_a.shape) < HEAD_DIM
    zero = jnp.zeros_like(chunk_a)
    return jnp.concatenate(
        [
            jnp.where(low, chunk_a, zero),
            jnp.where(low, pltpu.roll(chunk_a, HEAD_DIM, 1), zero),
            jnp.where(low, zero, pltpu.roll(chunk_b, HEAD_DIM, 1)),
            jnp.where(low, zero, chunk_b),
        ],
        axis=0,
    )


def two_chunks(blocks):
    rows = blocks.shape[0] // 4
    one, two, three, four = (blocks[n * rows : (n + 1) * rows] for n in range(4))
    low = lane_of(one.shape) < HEAD_DIM
    return (
        jnp.where(low, one, pltpu.roll(two, HEAD_DIM, 1)),
        jnp.where(low, pltpu.roll(three, HEAD_DIM, 1), four),
    )


def chunk_at(index, base=0):
    return pl.ds(pl.multiple_of(base + index * LANES, LANES), LANES)


def front_call(collective_id, tokens, cotangent, weights_own, gains, router, cosine, sine, routes, starts):
    count, width = tokens.shape
    seqs = starts.shape[0]
    positions = count // seqs
    length = REPS * positions
    score_scale = HEAD_DIM ** (-0.5)
    sent_width = width + SMALL

    def kernel(
        starts_ref, tokens_ref, grad_ref, query_w, key_w, value_w, output_w,
        gain_a_ref, gain_q_ref, gain_f_ref, gain_k_ref, router_ref, cos_ref, sin_ref, routes_ref,
        dense_out, grad_all, pairs_out, soft_out, rows_first,
        attn_in, query_raw, key_raw, query_low, mixed, middle, sent, gates_out,
        packed, small_box, dense, pairs, pair_own, soft_box, bias_box,
        ws0, wr0, ws1, wr1, ws2, wr2, gs0, gr0, gs1, gr1, ks0, kr0, ks1, kr1, rs, rr, own_sem, out_sem, soft_sem, pack_sem,
    ):
        place = Place()
        core = place.core
        packing = [
            pltpu.make_async_copy(
                source, packed.at[:, pl.ds(low, source.shape[1])], pack_sem.at[index]
            )
            for index, (source, low) in enumerate(
                ((key_w, AT_K), (value_w, AT_V), (query_w, 0), (output_w, AT_O))
            )
        ]
        for copy in packing:
            copy.start()
        small_box[...] = jnp.zeros_like(small_box)
        small_box[pl.ds(0, EXPERTS), pl.ds(0, ROWS_OWN)] = router_ref[...].astype(f32)
        for at, ref in enumerate((gain_a_ref, gain_q_ref, gain_f_ref, gain_k_ref)):
            size = ref.shape[0]
            small_box[pl.ds(EXPERTS + at, 1), pl.ds(0, size)] = (
                ref[...].astype(f32).reshape(1, size)
            )
        packed[:, pl.ds(AT_S, SMALL)] = jnp.transpose(small_box[...])[:ROWS_OWN].astype(bf16)

        def token_block(index, low, size):
            def block(which, row, n, other=False):
                at = (which[0] * RING + which[1]) * 2 + ((1 - core) if other else core)
                return dense.at[at, pl.ds(row, n), pl.ds(low, size)]

            return block

        def weight_gather(index, low, size, send_sem, recv_sem):
            return gather_parts(
                place.tokens, Line(send_sem, recv_sem), packed.at[:, pl.ds(low, size)],
                token_block(index, low, size), ROWS_OWN, own_sem.at[index], place.twin,
            )

        def rows_of(target):
            def block(which, row, n, other=False):
                at = (which[0] * RING + which[1]) * 2 + ((1 - core) if other else core)
                return target.at[at, pl.ds(row, n)]

            return block

        def pair_gather(seq, send_sem, recv_sem):
            def block(which, row, n, other=False):
                return pairs.at[seq, which[0] * RING + which[1], pl.ds(row, n)]

            return gather_parts(
                place.copies, Line(send_sem, recv_sem),
                pair_own.at[pl.ds(seq * positions, positions)], block, positions, own_sem.at[3 + seq],
            )

        def soft_copy(seq, index, slot):
            return pltpu.make_async_copy(
                soft_box.at[slot], soft_out.at[seq, index], soft_sem.at[slot]
            )

        rest_gather = weight_gather(0, AT_K, REST, ws0, wr0)
        query_gather = weight_gather(1, 0, QUERY, ws1, wr1)
        output_gather = weight_gather(2, AT_O, WIDTH, ws2, wr2)
        def grad_gather(seq, send_sem, recv_sem):
            base = seq * positions

            def block(which, row, n, other=False):
                at = (which[0] * RING + which[1]) * 2 + ((1 - core) if other else core)
                return grad_all.at[at, pl.ds(base + row, n)]

            return gather_parts(
                place.tokens, Line(send_sem, recv_sem), grad_ref.at[pl.ds(base, positions)], block,
                positions, own_sem.at[5 + seq], place.twin,
            )

        grads = [grad_gather(0, gs0, gr0), grad_gather(1, gs1, gr1)]
        first_rows = gather_parts(
            place.tokens, Line(rs, rr), sent.at[pl.ds(0, positions)], rows_of(rows_first), positions,
            own_sem.at[7], place.twin,
        )
        pair_gathers = [pair_gather(0, ks0, kr0), pair_gather(1, ks1, kr1)]

        greet(place.tokens.neighbours() + place.copies.neighbours() + [place.twin])
        for copy in packing:
            copy.wait()
        next(rest_gather)
        inputs = tokens_ref[...].astype(f32)
        middle[...] = inputs * root_mean(inputs)
        next(rest_gather)
        next(query_gather)
        query_at = place.rep * positions + lax.broadcasted_iota(jnp.int32, (positions, 1), 0)
        key_at = lax.broadcasted_iota(jnp.int32, (1, length), 1)
        for seq in range(seqs):
            allowed = key_at <= query_at
            for piece in range(starts_ref.shape[1]):
                start = starts_ref[seq, piece]
                query_inside = (query_at >= start) & (query_at < start + PIC)
                key_inside = (key_at >= start) & (key_at < start + PIC)
                allowed = allowed | (query_inside & key_inside)
            bias_box[seq] = jnp.where(allowed, 0.0, masked_score)
        next(rest_gather)
        next(query_gather)
        next(output_gather)
        drained(rest_gather)
        next(query_gather)
        next(output_gather)

        def weights(low, size):
            return dense[:, :, pl.ds(low, size)].reshape(width, size)

        small = weights(AT_S, SMALL)
        gain_a, gain_q, gain_f, gain_k = gain_rows(small)
        rows = (middle[...] * gain_a).astype(bf16)
        attn_in[...] = rows
        cos2 = jnp.concatenate([cos_ref[...]] * seqs, axis=0)
        sin2 = jnp.concatenate([sin_ref[...]] * seqs, axis=0)
        raw = dot(rows, weights(AT_K, KEY))
        key_raw[...] = raw
        scaled = raw * root_mean(raw) * gain_k
        for chunk in range(KEY // LANES):
            at = slice(chunk * LANES, (chunk + 1) * LANES)
            pair_own[:, at] = turned(scaled[:, at], cos2, sin2).astype(bf16)
        pair_own[:, KEY:] = dot(rows, weights(AT_V, KEY)).astype(bf16)
        next(pair_gathers[0])
        drained(query_gather)
        next(output_gather)
        next(grads[0])
        raw = dot(rows, weights(0, QUERY))
        query_raw[...] = raw
        scaled = raw * root_mean(raw) * gain_q
        for chunk in range(QUERY // LANES):
            at = slice(chunk * LANES, (chunk + 1) * LANES)
            query_low[:, at] = turned(scaled[:, at], cos2, sin2).astype(bf16)
        next(pair_gathers[0])
        next(pair_gathers[1])
        drained(output_gather)
        dense_copy = pltpu.make_async_copy(dense, dense_out, out_sem.at[0])
        dense_copy.start()
        next(grads[0])
        next(grads[1])
        next(pair_gathers[0])
        next(pair_gathers[1])
        next(grads[0])
        drained(pair_gathers[0])
        next(grads[1])

        def attend(seq, index, slot, wait_first):
            rows_at = pl.ds(seq * positions, positions)
            queries = four_heads(
                query_low[rows_at, chunk_at(2 * index)].astype(f32),
                query_low[rows_at, chunk_at(2 * index + 1)].astype(f32),
            )
            queries = (queries * score_scale).astype(bf16)
            keys = pairs[seq, :, :, chunk_at(index)].reshape(length, LANES)
            scores = dot_nt(queries, keys).reshape(4, positions, length) + bias_box[seq][None]
            scores = scores.reshape(4 * positions, length)
            raised = jnp.exp(scores - jnp.max(scores, axis=1, keepdims=True))
            soft = (raised * (1.0 / jnp.sum(raised, axis=1, keepdims=True))).astype(bf16)

            @pl.when(wait_first)
            def _():
                soft_copy(seq, index, slot).wait()

            soft_box[slot] = soft
            soft_copy(seq, index, slot).start()
            values = pairs[seq, :, :, chunk_at(index, KEY)].reshape(length, LANES)
            chunk_a, chunk_b = two_chunks(dot(soft, values))
            mixed[rows_at, chunk_at(2 * index)] = chunk_a.astype(bf16)
            mixed[rows_at, chunk_at(2 * index + 1)] = chunk_b.astype(bf16)

        def features(seq):
            at = pl.ds(seq * positions, positions)
            total = tokens_ref[at].astype(f32) + dot(mixed[at], weights(AT_O, WIDTH))
            middle[at] = total
            ffn_in = (total * root_mean(total) * gain_f).astype(bf16)
            sent[at, pl.ds(0, width)] = ffn_in
            lanes = lane_of((positions, SMALL))
            named = jnp.transpose(routes_ref[seq].astype(f32)).astype(jnp.int32)
            chosen = lanes == named[:, :1]
            for choice in range(1, named.shape[1]):
                chosen = chosen | (lanes == named[:, choice : choice + 1])
            logits = jnp.where(chosen, dot(ffn_in, small), masked_score)
            raised = jnp.exp(logits - jnp.max(logits, axis=1, keepdims=True))
            gates = raised * (1.0 / jnp.sum(raised, axis=1, keepdims=True))
            gates = jnp.where(chosen, gates, 0.0)
            gates_out[at] = gates
            high = gates.astype(bf16).astype(f32)
            tail = high + pltpu.roll(gates - high, EXPERTS, 1)
            sent[at, pl.ds(width, SMALL)] = tail.astype(bf16)

        def first_heads(index, carry):
            hooks(
                index,
                (
                    (1, lambda: next(grads[0])),
                    (2, lambda: next(pair_gathers[1])),
                    (3, lambda: next(grads[1])),
                ),
            )
            attend(0, index, lax.rem(index, 2), index >= 2)
            return carry

        lax.fori_loop(0, HEAD_PAIRS, first_heads, 0)
        features(0)
        next(first_rows)
        drained(pair_gathers[1])
        pairs_copy = pltpu.make_async_copy(pairs, pairs_out, out_sem.at[1])
        pairs_copy.start()

        def second_heads(index, carry):
            hooks(
                index,
                (
                    (1, lambda: next(grads[1])),
                    (3, lambda: next(first_rows)),
                ),
            )
            attend(1, index, lax.rem(index, 2), index >= 0)
            return carry

        lax.fori_loop(0, HEAD_PAIRS, second_heads, 0)
        features(1)
        next(first_rows)
        drained(grads[0])
        drained(grads[1])
        drained(first_rows)
        dense_copy.wait()
        pairs_copy.wait()
        for slot in range(2):
            soft_copy(1, 0, slot).wait()

    return pl.pallas_call(
        kernel,
        out_shape=[
            jax.ShapeDtypeStruct((GROUP, ROWS_OWN, PACKED), bf16),
            jax.ShapeDtypeStruct((GROUP, count, width), bf16),
            jax.ShapeDtypeStruct((seqs, REPS, positions, 2 * KEY), bf16),
            jax.ShapeDtypeStruct((seqs, HEAD_PAIRS, 4 * positions, length), bf16),
            jax.ShapeDtypeStruct((GROUP, positions, sent_width), bf16),
            jax.ShapeDtypeStruct((count, width), bf16),
            jax.ShapeDtypeStruct((count, QUERY), f32),
            jax.ShapeDtypeStruct((count, KEY), f32),
            jax.ShapeDtypeStruct((count, QUERY), bf16),
            jax.ShapeDtypeStruct((count, QUERY), bf16),
            jax.ShapeDtypeStruct((count, width), f32),
            jax.ShapeDtypeStruct((count, width + SMALL), bf16),
            jax.ShapeDtypeStruct((count, SMALL), f32),
        ],
        in_specs=[pl.BlockSpec(memory_space=pltpu.SMEM), IN_VMEM] + [ANY] * 5 + [IN_VMEM] * 8,
        out_specs=[ANY] * 5 + [IN_VMEM] * 8,
        scratch_shapes=[
            pltpu.VMEM((ROWS_OWN, PACKED), bf16),
            pltpu.VMEM((SMALL, LANES), f32),
            pltpu.VMEM((GROUP, ROWS_OWN, PACKED), bf16),
            pltpu.VMEM((seqs, REPS, positions, 2 * KEY), bf16),
            pltpu.VMEM((count, 2 * KEY), bf16),
            pltpu.VMEM((2, 4 * positions, length), bf16),
            pltpu.VMEM((seqs, positions, length), f32),
        ]
        + sems(GATHER_SEMS) * 8
        + [
            pltpu.SemaphoreType.DMA((8,)),
            pltpu.SemaphoreType.DMA((2,)),
            pltpu.SemaphoreType.DMA((2,)),
            pltpu.SemaphoreType.DMA((4,)),
        ],
        compiler_params=params(collective_id),
    )(starts, tokens, cotangent, *weights_own, *gains, router, cosine, sine, routes)


def norm_back(values, gain, grad):
    scale = root_mean(values)
    weighted = grad * gain
    mean = jnp.mean(values * weighted, axis=1, keepdims=True)
    inner = weighted * scale - values * (scale * scale * scale * mean)
    return inner, jnp.sum(grad * values * scale, axis=0, keepdims=True)


def back_call(
    collective_id, returned, gates, middle, sent, dense, cotangent, tokens, attn_in, query_raw, key_raw,
    query_low, mixed, pairs, soft, out_terms, expert_own, cosine, sine,
):
    count, width = tokens.shape
    seqs, _, positions, _ = pairs.shape
    length = REPS * positions
    expert_rows = expert_own.shape[0]
    score_scale = HEAD_DIM ** (-0.5)
    chips = GROUP // 2

    def kernel(
        returned_ref, gates_ref, middle_ref, sent_ref, dense_ref, grad_ref, tokens_ref, attn_ref,
        query_raw_ref, key_raw_ref, query_ref, mixed_ref, pairs_ref, soft_ref, out_ref, expert_ref,
        cos_ref, sin_ref,
        block_out, tokens_grad, small_out, dense_out, expert_all,
        weight_box, weight_rest, rest_terms, dense_own,
        o_staged, q_staged, rest_staged, o_stage, q_stage, rest_stage,
        out_held, out_staged, out_stage, small_terms, small_staged, small_stage, small_own, q_terms,
        soft_box, key_box, value_box, pair_terms, pair_stage, pair_grads,
        grad_mixed, grad_query, grad_middle, grad_attn, grad_attn_in, gain_box,
        o_got, q_got, rest_got, small_got, totals,
        out_s, out_r, small_s, small_r, kv0_s, kv0_r, kv1_s, kv1_r, o_s, o_r, q_s, q_r, rest_s, rest_r,
        ge_s, ge_r, go_s, go_r, gq_s, gq_r, grest_s, grest_r, gsmall_s, gsmall_r,
        load_sem, held_sem, box_sem, own_sem, total_sem,
    ):
        place = Place()
        core = place.core
        token_axes, copy_axes = place.tokens, place.copies

        def chip_of(which):
            return which[0] * RING + which[1]

        def blocks(which, other=False):
            return chip_of(which) * 2 + ((1 - core) if other else core)

        def out_store(low, step, value):
            at = pl.ds(low, step)
            block_out[at] = (middle_ref[at] + value).astype(bf16)

        out_sum = sum_parts(
            token_axes, Line(out_s, out_r),
            lambda which, low, n: out_held.at[chip_of(which), pl.ds(low, n)],
            out_stage, count, None,
            (place.twin, lambda which: out_ref.at[blocks(which, True)],
             lambda which: out_staged.at[chip_of(which)]),
            store=out_store,
        )
        def pair_sum(seq, send_sem, recv_sem):
            return sum_parts(
                copy_axes, Line(send_sem, recv_sem),
                lambda which, low, n: pair_terms.at[seq, chip_of(which), pl.ds(low, n)],
                pair_stage.at[seq], positions, pair_grads.at[pl.ds(seq * positions, positions)],
            )

        pair_sums = [pair_sum(0, kv0_s, kv0_r), pair_sum(1, kv1_s, kv1_r)]

        def rows_of_block(terms, index, low, n):
            return terms.at[pl.ds(index * ROWS_OWN + low, n)]

        def rows_of_pairs(terms, index, low, n):
            at = lax.rem(index, 2) * ROWS_OWN + low
            return terms.at[0, lax.div(index, 2), pl.ds(at, n)]

        def dense_sum(rows_of, terms, staged, stage, own, send_sem, recv_sem):
            return sum_parts(
                token_axes, Line(send_sem, recv_sem),
                lambda which, row, n: rows_of(terms, blocks(which), row, n),
                stage, ROWS_OWN, own,
                (place.twin, lambda which: rows_of(terms, blocks(which, True), 0, ROWS_OWN),
                 lambda which: staged.at[chip_of(which)]),
            )

        def own_columns(low):
            return dense_own.at[:, pl.ds(low, width)]

        o_sum = dense_sum(rows_of_pairs, pair_terms, o_staged, o_stage, own_columns(AT_O), o_s, o_r)
        q_sum = dense_sum(rows_of_block, q_terms, q_staged, q_stage, own_columns(0), q_s, q_r)
        rest_sum = dense_sum(
            rows_of_block, rest_terms, rest_staged, rest_stage, own_columns(AT_K), rest_s, rest_r
        )
        small_sum = dense_sum(
            rows_of_block, small_terms, small_staged, small_stage, small_own, small_s, small_r
        )

        def dense_total(index, low, got, send_sem, recv_sem):
            def own(rep):
                return dense_own.at[:, chunk_at(rep, low)]

            def target(rep):
                return dense_out.at[:, chunk_at(rep, low)]

            return total_parts(
                place, Line(send_sem, recv_sem), own, got, totals.at[index], target,
                total_sem.at[index],
            )

        o_total = dense_total(0, AT_O, o_got, go_s, go_r)
        q_total = dense_total(1, 0, q_got, gq_s, gq_r)
        rest_total = dense_total(2, AT_K, rest_got, grest_s, grest_r)
        small_total = spread_parts(place, Line(gsmall_s, gsmall_r), small_own, small_got, small_out)
        expert_gather = gather_parts(
            copy_axes, Line(ge_s, ge_r), expert_ref,
            lambda which, row, n, other=False: expert_all.at[chip_of(which), pl.ds(row, n)],
            expert_rows, own_sem,
        )

        def weight_load(low, index):
            return pltpu.make_async_copy(
                dense_ref.at[:, :, pl.ds(low, width)], weight_box, load_sem.at[index]
            )

        rest_load = pltpu.make_async_copy(
            dense_ref.at[:, :, pl.ds(AT_K, REST)], weight_rest, load_sem.at[1]
        )
        held_loads = [
            pltpu.make_async_copy(
                out_ref.at[2 * chip + core], out_held.at[chip], held_sem.at[chip]
            )
            for chip in range(chips)
        ]

        def box_loads(number, slot):
            seq, index = lax.div(number, HEAD_PAIRS), lax.rem(number, HEAD_PAIRS)
            return [
                pltpu.make_async_copy(
                    soft_ref.at[seq, index], soft_box.at[slot], box_sem.at[slot, 0]
                ),
                pltpu.make_async_copy(
                    pairs_ref.at[seq, :, :, chunk_at(index)], key_box.at[slot], box_sem.at[slot, 1]
                ),
                pltpu.make_async_copy(
                    pairs_ref.at[seq, :, :, chunk_at(index, KEY)],
                    value_box.at[slot],
                    box_sem.at[slot, 2],
                ),
            ]

        rest_load.start()
        weight_load(AT_O, 0).start()
        for load in held_loads + box_loads(0, 0):
            load.start()
        greet(
            token_axes.neighbours()
            + [place.twin]
            + [(place.shard, other) for other in place.others[1:]]
        )
        next(out_sum)
        next(expert_gather)
        rest_load.wait()

        small = weight_rest[:, :, pl.ds(2 * KEY, SMALL)].reshape(width, SMALL)
        gain_a, gain_q, gain_f, gain_k = gain_rows(small)
        gates = gates_ref[...]
        tail = returned_ref[:, pl.ds(width, SMALL)].astype(f32)
        grad_gates = tail + pltpu.roll(tail, SMALL - EXPERTS, 1)
        grad_logits = gates * (grad_gates - jnp.sum(gates * grad_gates, axis=1, keepdims=True))
        grad_logits = grad_logits.astype(bf16)
        grad_ffn = returned_ref[:, pl.ds(0, width)].astype(f32) + dot_nt(grad_logits, small)
        inner, gain_f_terms = norm_back(middle_ref[...], gain_f, grad_ffn)
        inner = grad_ref[...].astype(f32) + inner
        grad_middle[...] = inner
        grad_attn[...] = inner.astype(bf16)
        gain_box[...] = jnp.zeros_like(gain_box)
        gain_box[pl.ds(EXPERTS + 2, 1)] = gain_f_terms
        weight_load(AT_O, 0).wait()
        grad_mixed[...] = dot_nt(
            grad_attn[...], weight_box[...].reshape(QUERY, width)
        ).astype(bf16)
        weight_load(0, 3).start()

        def attend_back(seq, index):
            number = seq * HEAD_PAIRS + index
            slot = lax.rem(number, 2)
            for load in box_loads(number, slot):
                load.wait()

            @pl.when(number + 1 < seqs * HEAD_PAIRS)
            def _():
                for load in box_loads(number + 1, 1 - slot):
                    load.start()

            rows_at = pl.ds(seq * positions, positions)
            first, second = chunk_at(2 * index), chunk_at(2 * index + 1)
            queries = four_heads(
                query_ref[rows_at, first].astype(f32), query_ref[rows_at, second].astype(f32)
            )
            queries = (queries * score_scale).astype(bf16)
            grads = four_heads(
                grad_mixed[rows_at, first].astype(f32), grad_mixed[rows_at, second].astype(f32)
            ).astype(bf16)
            keys = key_box[slot].reshape(length, LANES)
            values = value_box[slot].reshape(length, LANES)
            soft_low = soft_box[slot]
            value_terms = dot_tn(soft_low, grads)
            pair_terms[seq, :, :, chunk_at(index, KEY)] = value_terms.astype(bf16).reshape(
                REPS, positions, LANES
            )
            soft_full = soft_low.astype(f32)
            grad_soft = dot_nt(grads, values)
            weighted = soft_full * grad_soft
            grad_scores = (
                weighted - soft_full * jnp.sum(weighted, axis=1, keepdims=True)
            ).astype(bf16)
            key_terms = dot_tn(grad_scores, queries)
            pair_terms[seq, :, :, chunk_at(index)] = key_terms.astype(bf16).reshape(
                REPS, positions, LANES
            )
            chunk_a, chunk_b = two_chunks(dot(grad_scores, keys) * score_scale)
            grad_query[rows_at, first] = chunk_a.astype(bf16)
            grad_query[rows_at, second] = chunk_b.astype(bf16)

        def out_ready():
            for load in held_loads:
                load.wait()
            next(out_sum)
            next(out_sum)

        def first_heads(index, carry):
            hooks(index, ((2, out_ready), (3, lambda: next(expert_gather))))
            attend_back(0, index)
            return carry

        lax.fori_loop(0, HEAD_PAIRS, first_heads, 0)
        next(pair_sums[0])
        next(pair_sums[0])
        next(pair_sums[0])

        def second_heads(index, carry):
            hooks(index, ((2, lambda: next(out_sum)), (3, lambda: next(expert_gather))))
            attend_back(1, index)
            return carry

        lax.fori_loop(0, HEAD_PAIRS, second_heads, 0)
        next(pair_sums[1])
        next(pair_sums[1])
        next(pair_sums[1])
        next(pair_sums[0])
        router_terms = dot_tn(sent_ref[:, pl.ds(0, width)], grad_logits)

        cos2 = jnp.concatenate([cos_ref[...]] * seqs, axis=0)
        sin2 = -jnp.concatenate([sin_ref[...]] * seqs, axis=0)

        def turned_back(values):
            return jnp.concatenate(
                [
                    turned(values[:, low : low + LANES], cos2, sin2)
                    for low in range(0, values.shape[1], LANES)
                ],
                axis=1,
            )

        grad, gain_q_terms = norm_back(
            query_raw_ref[...], gain_q, turned_back(grad_query[...].astype(f32))
        )
        gain_box[pl.ds(EXPERTS + 1, 1)] = gain_q_terms
        grad_query_low = grad.astype(bf16)
        weight_load(0, 3).wait()
        grad_attn_in[...] = dot_nt(grad_query_low, weight_box[...].reshape(width, QUERY))

        next(pair_sums[0])
        next(pair_sums[1])
        next(out_sum)
        drained(pair_sums[0])

        def o_rows(index, carry):
            at = chunk_256(index)
            value = dot_tn(mixed_ref[:, at], grad_attn[...]).astype(bf16)
            pair_terms[0, pl.ds(2 * index, 2)] = value.reshape(2, positions, width)
            return carry

        lax.fori_loop(0, QUERY // 256, o_rows, 0)
        next(o_sum)
        next(pair_sums[1])

        def q_rows(index, carry):
            at = chunk_256(index)
            q_terms[at] = dot_tn(attn_ref[:, at], grad_query_low).astype(bf16)
            return carry

        lax.fori_loop(0, width // 256, q_rows, 0)
        next(q_sum)
        next(o_sum)
        next(o_sum)
        drained(out_sum)
        next(q_sum)
        next(q_sum)
        next(o_sum)
        next(expert_gather)
        drained(pair_sums[1])

        grads = pair_grads[...]
        grad, gain_k_terms = norm_back(
            key_raw_ref[...],
            gain_k,
            turned_back(grads[:, :KEY].astype(bf16).astype(f32)),
        )
        grad_pairs = jnp.concatenate([grad.astype(bf16), grads[:, KEY:].astype(bf16)], axis=1)

        def rest_rows(index, carry):
            at = chunk_256(index)
            rest_terms[at] = dot_tn(attn_ref[:, at], grad_pairs).astype(bf16)
            return carry

        lax.fori_loop(0, width // 256, rest_rows, 0)
        next(rest_sum)
        grad = grad_attn_in[...] + dot_nt(
            grad_pairs, weight_rest[:, :, pl.ds(0, 2 * KEY)].reshape(width, 2 * KEY)
        )
        next(rest_sum)
        next(rest_sum)
        values = tokens_ref[...].astype(f32)
        inner, gain_a_terms = norm_back(values, gain_a, grad)
        gain_box[pl.ds(EXPERTS, 1)] = gain_a_terms
        lanes = lane_of((KEY, SMALL))
        gain_k_column = jnp.where(
            lanes == EXPERTS + 3,
            jnp.transpose(jnp.broadcast_to(gain_k_terms, (SMALL, KEY))),
            0.0,
        )
        small_terms[...] = (
            router_terms + jnp.transpose(gain_box[...]) + long_column(gain_k_column)
        ).astype(bf16)
        next(small_sum)
        tokens_grad[...] = (grad_middle[...] + inner).astype(bf16)
        next(small_sum)
        next(small_sum)
        next(q_sum)
        next(rest_sum)
        next(small_sum)
        next(o_sum)
        next(small_sum)
        next(q_sum)
        next(rest_sum)
        drained(o_sum)
        next(o_total)
        drained(small_sum)
        next(small_total)
        drained(q_sum)
        next(q_total)
        next(o_total)
        drained(rest_sum)
        next(rest_total)
        next(q_total)
        drained(small_total)
        next(rest_total)
        drained(expert_gather)
        drained(o_total)
        drained(q_total)
        drained(rest_total)

    block = pltpu.VMEM((GROUP, ROWS_OWN, width), bf16)
    scratch = [
        block,
        pltpu.VMEM((GROUP, ROWS_OWN, REST), bf16),
        pltpu.VMEM((width, 2 * KEY), bf16),
        pltpu.VMEM((ROWS_OWN, PACKED), bf16),
        pltpu.VMEM((chips, ROWS_OWN, width), bf16),
        pltpu.VMEM((chips, ROWS_OWN, QUERY), bf16),
        pltpu.VMEM((chips, ROWS_OWN, 2 * KEY), bf16),
        pltpu.VMEM((stage_rows(ROWS_OWN), width), bf16),
        pltpu.VMEM((stage_rows(ROWS_OWN), QUERY), bf16),
        pltpu.VMEM((stage_rows(ROWS_OWN), 2 * KEY), bf16),
        pltpu.VMEM((chips, count, width), bf16),
        pltpu.VMEM((chips, count, width), bf16),
        pltpu.VMEM((stage_rows(count), width), bf16),
        pltpu.VMEM((width, SMALL), bf16),
        pltpu.VMEM((chips, ROWS_OWN, SMALL), bf16),
        pltpu.VMEM((stage_rows(ROWS_OWN), SMALL), bf16),
        pltpu.VMEM((ROWS_OWN, SMALL), bf16),
        pltpu.VMEM((width, QUERY), bf16),
        pltpu.VMEM((2, 4 * positions, length), bf16),
        pltpu.VMEM((2, REPS, positions, LANES), bf16),
        pltpu.VMEM((2, REPS, positions, LANES), bf16),
        pltpu.VMEM((seqs, REPS, positions, 2 * KEY), bf16),
        pltpu.VMEM((seqs, stage_rows(positions), 2 * KEY), bf16),
        pltpu.VMEM((count, 2 * KEY), f32),
        pltpu.VMEM((count, QUERY), bf16),
        pltpu.VMEM((count, QUERY), bf16),
        pltpu.VMEM((count, width), f32),
        pltpu.VMEM((count, width), bf16),
        pltpu.VMEM((count, width), f32),
        pltpu.VMEM((SMALL, width), f32),
    ]
    scratch += [pltpu.VMEM((REPS, ROWS_OWN, LANES), bf16)] * 4
    scratch += [pltpu.VMEM((3, ROWS_OWN, LANES), bf16)]
    return pl.pallas_call(
        kernel,
        out_shape=[
            jax.ShapeDtypeStruct((count, width), bf16),
            jax.ShapeDtypeStruct((count, width), bf16),
            jax.ShapeDtypeStruct((ROWS_OWN, SMALL), f32),
            jax.ShapeDtypeStruct((ROWS_OWN, PACKED), bf16),
            jax.ShapeDtypeStruct((REPS, expert_rows, width), bf16),
        ],
        in_specs=[IN_VMEM] * 4 + [ANY] + [IN_VMEM] * 7 + [ANY] * 4 + [IN_VMEM] * 2,
        out_specs=[IN_VMEM, IN_VMEM, IN_VMEM, ANY, ANY],
        scratch_shapes=scratch
        + sems(SUM_SEMS) * 7
        + sems(GATHER_SEMS)
        + sems(TOTAL_SEMS) * 4
        + [
            pltpu.SemaphoreType.DMA((4,)),
            pltpu.SemaphoreType.DMA((chips,)),
            pltpu.SemaphoreType.DMA((2, 3)),
            pltpu.SemaphoreType.DMA,
            pltpu.SemaphoreType.DMA((3,)),
        ],
        compiler_params=params(collective_id),
    )(
        returned, gates, middle, sent, dense, cotangent, tokens, attn_in, query_raw, key_raw,
        query_low, mixed, pairs, soft, out_terms, expert_own, cosine, sine,
    )


def finish_call(small_sum, dense_own, expert_all, inner_rows):
    reps, expert_rows, width = expert_all.shape
    inner_own = inner_rows // reps
    outer_own = expert_rows - inner_own

    def kernel(
        small_ref, dense_ref, expert_ref,
        inner, outer, query, key, value, output, router, gain_a, gain_q, gain_f, gain_k,
    ):
        inner[...] = expert_ref[0, :inner_own].astype(f32)
        outer[...] = expert_ref[0, inner_own:].astype(f32)

        @pl.when(pl.program_id(0) == 1)
        def _():
            for low, target in ((0, query), (AT_K, key), (AT_V, value), (AT_O, output)):
                target[...] = dense_ref[:, pl.ds(low, target.shape[1])].astype(f32)
            rows = jnp.transpose(small_ref[...])
            router[...] = rows[:EXPERTS, :ROWS_OWN]
            for at, target in enumerate((gain_a, gain_q, gain_f, gain_k)):
                size = target.shape[0]
                target[...] = rows[EXPERTS + at, :size].reshape(size)

    def whole(*shape):
        return pl.BlockSpec(shape, lambda i: (0,) * len(shape))

    shapes = [(ROWS_OWN, QUERY), (ROWS_OWN, KEY), (ROWS_OWN, KEY), (ROWS_OWN, WIDTH)]
    shapes += [(EXPERTS, ROWS_OWN), (ROWS_OWN,), (ROWS_OWN,), (ROWS_OWN,), (KGAIN_OWN,)]
    return pl.pallas_call(
        kernel,
        grid=(reps,),
        out_shape=[
            jax.ShapeDtypeStruct((inner_rows, width), f32),
            jax.ShapeDtypeStruct((reps * outer_own, width), f32),
        ]
        + [jax.ShapeDtypeStruct(shape, f32) for shape in shapes],
        in_specs=[
            whole(*small_sum.shape),
            whole(*dense_own.shape),
            pl.BlockSpec((1, expert_rows, width), lambda i: (i, 0, 0)),
        ],
        out_specs=[
            pl.BlockSpec((inner_own, width), lambda i: (i, 0)),
            pl.BlockSpec((outer_own, width), lambda i: (i, 0)),
        ]
        + [whole(*shape) for shape in shapes],
        compiler_params=pltpu.CompilerParams(vmem_limit_bytes=VMEM_LIMIT),
    )(small_sum, dense_own, expert_all)


def rotary_tables(positions):
    lane = jnp.arange(LANES, dtype=jnp.int32)
    half = HEAD_DIM // 2
    exponent = (lane % half).astype(f32) * (2.0 / HEAD_DIM)
    frequency = rope_base ** (-exponent)
    angles = positions.astype(f32)[:, None] * frequency[None, :]
    sign = jnp.where(lane % HEAD_DIM < half, -1.0, 1.0).astype(f32)
    return jnp.cos(angles), jnp.sin(angles) * sign[None, :]


def shards(
    tokens,
    cotangent,
    routes,
    picture_starts,
    attn_gain,
    query_weight,
    key_weight,
    value_weight,
    query_gain,
    key_gain,
    output_weight,
    ffn_gain,
    router_weight,
    expert_in,
    expert_down,
):
    seqs, positions, width = tokens.shape
    count = seqs * positions
    query_pos = lax.axis_index("rep") * positions + jnp.arange(positions, dtype=jnp.int32)
    cosine, sine = rotary_tables(query_pos)
    rows = tokens.reshape(count, width)
    grad_rows = cotangent.reshape(count, width)
    (
        dense, grad_all, pairs, soft, rows_first,
        attn_in, query_raw, key_raw, query_low, mixed, middle, sent, gates,
    ) = front_call(
        1, rows, grad_rows, (query_weight, key_weight, value_weight, output_weight),
        (attn_gain, query_gain, ffn_gain, key_gain), router_weight.T,
        cosine, sine, jnp.transpose(routes, (0, 2, 1)), picture_starts,
    )
    returned, expert_own, out_terms = moe_call(
        2, sent, rows_first, grad_all, expert_in[0], expert_down[0]
    )
    block_out, tokens_grad, small_sum, dense_out, expert_all = back_call(
        3, returned, gates, middle, sent, dense, grad_rows, rows, attn_in,
        query_raw, key_raw, query_low, mixed, pairs, soft, out_terms, expert_own, cosine, sine,
    )
    inner, outer, query, key, value, output, router, gain_a, gain_q, gain_f, gain_k = finish_call(
        small_sum, dense_out, expert_all, expert_in.shape[1]
    )
    return (
        block_out.reshape(tokens.shape),
        tokens_grad.reshape(tokens.shape),
        gain_a,
        query,
        key,
        value,
        gain_q,
        gain_k,
        output,
        gain_f,
        router.T,
        inner[None],
        outer[None],
    )


def solution(mesh):
    by_tokens = P("shard", "rep", None)
    rows, line, block = P("shard", None), P("shard"), P("shard", None, None)
    in_specs = (
        by_tokens, by_tokens, by_tokens, rows, line, rows, rows, rows, line, line, rows, line, rows, block, block,
    )
    out_specs = (
        by_tokens, by_tokens, line, rows, rows, rows, line, line, rows, line, rows, block, block,
    )
    return jax.shard_map(shards, mesh=mesh, in_specs=in_specs, out_specs=out_specs, check_vma=False)
```

```python
import jax
import jax.numpy as jnp
from jax import lax
from jax.experimental import pallas as pl
from jax.experimental.pallas import tpu as pltpu
from jax.sharding import PartitionSpec as P

HEADS = 16
KV_HEADS = 8
HEAD_DIM = 64
PIC = 256
RING = 4
GROUP = 16
REPS = 8
VMEM_LIMIT = 63 << 20

norm_eps = 1e-06
rope_base = 10000.0
masked_score = -1e30

bf16 = jnp.bfloat16
f32 = jnp.float32


class Place:
    def __init__(self):
        shard = lax.axis_index("shard")
        rep = lax.axis_index("rep")
        self.shard, self.rep = shard, rep
        core = lax.rem(shard, 2)
        ring_z = lax.rem(lax.div(shard, 2), RING)
        y_hi = lax.div(shard, 8)
        ring_x = lax.rem(rep, RING)
        y_lo = lax.div(rep, RING)
        self.core = core

        def shard_of(hi, z, c):
            return (hi * RING + z) * 2 + c

        def rep_of(lo, x):
            return lo * RING + x

        def up(v):
            return lax.rem(v + 1, RING)

        def down(v):
            return lax.rem(v + RING - 1, RING)

        self.twin = (shard_of(y_hi, ring_z, 1 - core), rep)
        self.others = [lax.rem(rep + step, REPS) for step in range(REPS)]
        self.tokens = Axes(
            y_hi,
            ring_z,
            (shard_of(y_hi, up(ring_z), core), rep),
            (shard_of(y_hi, down(ring_z), core), rep),
            (shard_of(1 - y_hi, ring_z, core), rep_of(1 - y_lo, ring_x)),
        )
        self.copies = Axes(
            y_lo,
            ring_x,
            (shard, rep_of(y_lo, up(ring_x))),
            (shard, rep_of(y_lo, down(ring_x))),
            (shard, rep_of(1 - y_lo, ring_x)),
        )


class Axes:
    def __init__(self, side, spot, ahead, behind, across):
        self.side, self.spot = side, spot
        self.ahead, self.behind, self.across = ahead, behind, across
        sides = (side, 1 - side)
        spots = [lax.rem(spot + step, RING) for step in range(RING)]
        self.places = [[(sides[flip], spots[step]) for step in range(RING)] for flip in range(2)]

    def at(self, flip, step):
        return self.places[flip][step % RING]

    def neighbours(self):
        return [self.ahead, self.behind, self.across]


def greet(devices):
    barrier = pltpu.get_barrier_semaphore()
    for device in devices:
        pl.semaphore_signal(barrier, inc=1, device_id=device, device_id_type=pl.DeviceIdType.MESH)
    pl.semaphore_wait(barrier, len(devices))


class Line:
    def __init__(self, send_sem, recv_sem):
        self.send_sem, self.recv_sem = send_sem, recv_sem
        self.sent = []

    def copy(self, index, source, target, device):
        return pltpu.make_async_remote_copy(
            src_ref=source(),
            dst_ref=target(),
            send_sem=self.send_sem.at[index],
            recv_sem=self.recv_sem.at[index],
            device_id=device,
            device_id_type=pl.DeviceIdType.MESH,
        )

    def send(self, index, source, target, device):
        self.copy(index, source, target, device).start()
        self.sent.append((index, source, target, device))

    def take(self, index, target, device):
        self.copy(index, target, target, device).wait_recv()

    def finish(self):
        for sent in self.sent:
            self.copy(*sent).wait_send()


def abreast(*parts):
    running = list(parts)
    while running:
        for part in list(running):
            try:
                next(part)
            except StopIteration:
                running.remove(part)


GATHER_SEMS = 20


def gather_parts(axes, line, own, block, rows, local_sem, twin=None, twin_later=False):
    half, quarter = rows // 2, rows // 4
    mine, back, front, far = axes.at(0, 0), axes.at(0, -1), axes.at(0, 1), axes.at(0, 2)
    pair, pair_back, pair_front, pair_far = (axes.at(1, n) for n in (0, -1, 1, 2))
    ahead, behind, across = axes.ahead, axes.behind, axes.across

    def rows_of(which, low=0, count=rows, other=False):
        return lambda: block(which, low, count, other)

    def first(index, device):
        line.send(index, lambda: own, rows_of(mine), device)

    def relay(index, device, which, low=0, count=rows):
        line.send(index, rows_of(which, low, count), rows_of(which, low, count), device)

    def share(index, which):
        if twin is not None:
            relay(12 + index, twin, which)

    def keep():
        return pltpu.make_async_copy(own, block(mine, 0, rows), local_sem)

    keep().start()
    if twin is not None:
        first(12, twin)
    first(0, ahead)
    first(1, behind)
    first(2, across)
    keep().wait()
    yield
    line.take(0, rows_of(back), ahead)
    relay(3, ahead, back, 0, half)
    relay(4, across, back, half, half)
    share(1, back)
    line.take(1, rows_of(front), behind)
    relay(5, behind, front, half, half)
    relay(6, across, front, half, half)
    share(2, front)
    line.take(2, rows_of(pair), across)
    relay(7, ahead, pair, 0, half)
    relay(8, behind, pair, 0, half)
    share(3, pair)
    yield
    line.take(3, rows_of(far, 0, half), ahead)
    line.take(5, rows_of(far, half, half), behind)
    relay(9, across, far, half, half)
    share(4, far)
    line.take(7, rows_of(pair_back, 0, half), ahead)
    relay(10, ahead, pair_back, 0, quarter)
    line.take(8, rows_of(pair_front, 0, half), behind)
    relay(11, behind, pair_front, quarter, quarter)
    line.take(4, rows_of(pair_back, half, half), across)
    share(5, pair_back)
    line.take(6, rows_of(pair_front, half, half), across)
    share(6, pair_front)
    yield
    line.take(10, rows_of(pair_far, 0, quarter), ahead)
    line.take(11, rows_of(pair_far, quarter, quarter), behind)
    line.take(9, rows_of(pair_far, half, half), across)
    share(7, pair_far)
    yield
    if twin is not None and not twin_later:
        for index, which in enumerate(gather_order(axes)):
            line.take(12 + index, rows_of(which, other=True), twin)
    line.finish()


SUM_SEMS = 20
TOTAL_SEMS = 16


def total_parts(place, line, own, got, total, target, local_sem):
    rep = place.rep
    steps = range(1, REPS)
    peers = {step: (place.shard, place.others[step]) for step in steps}
    before = {step: place.others[REPS - step] for step in steps}

    def kept():
        return pltpu.make_async_copy(total, target(rep), local_sem)

    for step in steps:
        line.send(step, lambda p=place.others[step]: own(p), lambda: got.at[rep], peers[step])
    yield
    value = own(rep)[...].astype(f32)
    for step in steps:
        line.take(step, lambda b=before[step]: got.at[b], peers[step])
        value = value + got[before[step]].astype(f32)
    total[...] = value.astype(bf16)
    kept().start()
    for step in steps:
        line.send(8 + step, lambda: total, lambda: target(rep), peers[step])
    yield
    for step in steps:
        line.take(8 + step, lambda b=before[step]: target(b), peers[step])
    kept().wait()
    line.finish()


def spread_parts(place, line, own, got, total):
    rep = place.rep
    steps = range(1, REPS)
    for step in steps:
        peer = (place.shard, place.others[step])
        line.send(step, lambda: own, lambda: got.at[rep], peer)
    yield
    value = own[...].astype(f32)
    for step in steps:
        before = place.others[REPS - step]
        line.take(step, lambda: got.at[before], (place.shard, place.others[step]))
        value = value + got[before].astype(f32)
    total[...] = value
    line.finish()


def add_rows(target, source, rows):
    step = 16
    count = rows // step

    def body(index, carry):
        at = pl.ds(pl.multiple_of(index * step, step), step)
        target[at] = target[at] + source[at]
        return carry

    lax.fori_loop(0, count, body, 0)


def stage_rows(rows):
    return 7 * rows


def gather_order(axes):
    return [axes.at(*v) for v in ((0, 0), (0, -1), (0, 1), (1, 0), (0, 2), (1, -1), (1, 1), (1, 2))]


def sum_order(axes):
    return [axes.at(*v) for v in ((1, 2), (0, 2), (1, -1), (1, 1), (0, -1), (0, 1), (1, 0), (0, 0))]


def sum_parts(axes, line, part, stage, rows, result, twin=None, store=None):
    half, quarter = rows // 2, rows // 4
    mine, back, front, far = axes.at(0, 0), axes.at(0, -1), axes.at(0, 1), axes.at(0, 2)
    pair, pair_back, pair_front, pair_far = (axes.at(1, n) for n in (0, -1, 1, 2))
    ahead, behind, across = axes.ahead, axes.behind, axes.across
    order = sum_order(axes)
    offsets, used = {}, 0
    for name, size in (
        ("Y0", half), ("M0", quarter), ("P0", quarter), ("M1", half), ("Y1", half), ("Y2", half),
        ("P1", half), ("M2", half), ("P2", half), ("M3", rows), ("P3", rows), ("Y3", rows),
    ):
        offsets[name] = (used, size, len(offsets))
        used += size

    def landing(name):
        low, size, _ = offsets[name]
        return lambda: stage.at[pl.ds(low, size)]

    def send(name, which, low, device):
        _, size, index = offsets[name]
        line.send(index, lambda: part(which, low, size), landing(name), device)

    def add(name, which, low, device):
        _, size, index = offsets[name]
        line.take(index, landing(name), device)
        add_rows(part(which, low, size), landing(name)(), size)

    def join(*places):
        if twin is not None:
            for place in places:
                line.take(12 + place, lambda: twin[2](order[place]), twin[0])
                add_rows(part(order[place], 0, rows), twin[2](order[place]), rows)

    def hand(*places):
        if twin is not None:
            for place in places:
                which = order[place]
                line.send(
                    12 + place, lambda w=which: twin[1](w), lambda w=which: twin[2](w), twin[0]
                )

    hand(0, 1, 2, 3)
    yield
    join(0)
    send("Y0", pair_far, half, across)
    send("M0", pair_far, 0, behind)
    send("P0", pair_far, quarter, ahead)
    join(1)
    send("M1", far, 0, behind)
    join(2)
    send("Y1", pair_back, half, across)
    join(3)
    send("Y2", pair_front, half, across)
    yield
    hand(4, 5, 6, 7)
    yield
    add("M0", pair_back, 0, behind)
    send("M2", pair_back, 0, behind)
    add("P0", pair_front, quarter, ahead)
    send("P2", pair_front, 0, ahead)
    add("Y0", far, half, across)
    send("P1", far, half, ahead)
    yield
    join(4, 5, 6, 7)
    add("M1", back, 0, behind)
    add("Y1", back, half, across)
    send("M3", back, 0, behind)
    add("M2", pair, 0, behind)
    add("P2", pair, 0, ahead)
    send("Y3", pair, 0, across)
    add("P1", front, half, ahead)
    add("Y2", front, half, across)
    send("P3", front, 0, ahead)
    yield
    for name, device in (("M3", behind), ("P3", ahead), ("Y3", across)):
        line.take(offsets[name][2], landing(name), device)
    step = 16

    def body(index, carry):
        low = pl.multiple_of(index * step, step)
        total = part(mine, low, step)[...].astype(f32)
        for name in ("M3", "P3", "Y3"):
            total = total + stage[pl.ds(offsets[name][0] + low, step)].astype(f32)
        if store is None:
            result[pl.ds(low, step)] = total.astype(result.dtype)
        else:
            store(low, step, total)
        return carry

    lax.fori_loop(0, rows // step, body, 0)
    line.finish()


def sems(count):
    return [pltpu.SemaphoreType.DMA((count,)), pltpu.SemaphoreType.DMA((count,))]


ANY = pl.BlockSpec(memory_space=pl.ANY)
IN_VMEM = pl.BlockSpec(memory_space=pltpu.VMEM)


def params(collective_id):
    return pltpu.CompilerParams(
        collective_id=collective_id, has_side_effects=True, vmem_limit_bytes=VMEM_LIMIT
    )


def dot(a, b):
    return jnp.dot(a, b, preferred_element_type=f32)


def dot_nt(a, b):
    return lax.dot_general(a, b, (((1,), (1,)), ((), ())), preferred_element_type=f32)


def dot_tn(a, b):
    return lax.dot_general(a, b, (((0,), (0,)), ((), ())), preferred_element_type=f32)


def pick(index, values):
    chosen = values[-1]
    for at in range(len(values) - 2, -1, -1):
        chosen = jnp.where(index == at, values[at], chosen)
    return chosen


def moe_call(collective_id, sent, rows_first, grad_all, inner, outer):
    count, columns = sent.shape
    width = inner.shape[0]
    hidden_width = outer.shape[0]
    small = columns - width
    half = count // 2
    chips = GROUP // 2
    wide = 4
    rounds = GROUP // wide

    def kernel(
        sent_ref, first_ref, grad_ref, inner_ref, outer_ref,
        returned, expert_own, out_terms,
        rows_in, grads, hidden, back_gu, back, back_staged, back_stage, out_box,
        term_stage,
        gs, gr, bs0, br0, bs1, br1, ia, ja, ib, jb, ds_, dr, own_sem, load_sem, box_sem,
    ):
        place = Place()
        axes, core, shard = place.tokens, place.core, place.shard
        gather_line = Line(gs, gr)

        def chip_of(which):
            return which[0] * RING + which[1]

        def blocks(which, other=False):
            return chip_of(which) * 2 + ((1 - core) if other else core)

        gather = gather_parts(
            axes, gather_line, sent_ref.at[pl.ds(half, half)],
            lambda which, low, n, other=False: rows_in.at[1, blocks(which, other), pl.ds(low, n)],
            half, own_sem, place.twin, twin_later=True,
        )

        def sum_of(chunk, send_sem, recv_sem):
            return sum_parts(
                axes, Line(send_sem, recv_sem),
                lambda which, low, n: back.at[chunk, blocks(which), pl.ds(low, n)],
                back_stage.at[chunk], half, returned.at[pl.ds(chunk * half, half)],
                (place.twin, lambda which: back.at[chunk, blocks(which, True)],
                 lambda which: back_staged.at[chunk, chip_of(which)]),
            )

        sums = [sum_of(0, bs0, br0), sum_of(1, bs1, br1)]
        piece = hidden_width // REPS

        def inner_part(part):
            def rows(which, low, n):
                at = chip_of(which)
                return out_box.at[part, lax.div(at, 2), pl.ds(lax.rem(at, 2) * piece + low, n)]

            return rows

        def down_part(which, low, n):
            at = chip_of(which)
            return back_gu.at[0, lax.div(at, 2), pl.ds(lax.rem(at, 2) * piece + low, n)]

        inner_sums = [
            sum_parts(
                place.copies, Line(send_sem, recv_sem), inner_part(part), term_stage.at[part], piece,
                expert_own.at[pl.ds(part * piece, piece)],
            )
            for part, (send_sem, recv_sem) in enumerate(((ia, ja), (ib, jb)))
        ]
        down_sum = sum_parts(
            place.copies, Line(ds_, dr), down_part, term_stage.at[2], piece,
            expert_own.at[pl.ds(2 * piece, piece)],
        )

        def loads(t):
            at = pl.ds(t * wide, wide)
            return [
                pltpu.make_async_copy(first_ref.at[at], rows_in.at[0, at], load_sem.at[t, 0]),
                pltpu.make_async_copy(
                    grad_ref.at[at, pl.ds(0, half)], grads.at[0, at], load_sem.at[t, 1]
                ),
            ]

        second_grads = pltpu.make_async_copy(
            grad_ref.at[:, pl.ds(half, half)], grads.at[1], load_sem.at[rounds, 0]
        )

        def box_copy(chunk, first, slot):
            return pltpu.make_async_copy(
                out_box.at[slot],
                out_terms.at[pl.ds(first, wide), pl.ds(chunk * half, half)],
                box_sem.at[slot],
            )

        rows_count = wide * half
        lanes = lane_of((rows_count, small))
        is_high, is_rest = lanes == shard, lanes == shard + GROUP

        def tile(chunk, first, slot, wait_first):
            at = pl.ds(first, wide)
            row_block = rows_in[chunk, at].reshape(rows_count, columns)
            gate = jnp.sum(
                jnp.where(is_high | is_rest, row_block[:, width:].astype(f32), 0.0),
                axis=1, keepdims=True,
            )
            gate_up = dot(row_block[:, :width], inner_ref[...])
            gate_part, up_part = gate_up[:, :hidden_width], gate_up[:, hidden_width:]
            sigmoid = 1.0 / (1.0 + jnp.exp(-gate_part))
            active = gate_part * sigmoid
            product = active * up_part
            hidden_low = product.astype(bf16)
            hidden[chunk, at] = hidden_low.reshape(wide, half, hidden_width)
            out_rows = (gate * dot(hidden_low, outer_ref[...])).astype(bf16)

            @pl.when(wait_first)
            def _():
                box_copy(chunk, first, slot).wait()

            out_box[slot] = out_rows.reshape(wide, half, width)
            box_copy(chunk, first, slot).start()
            grad = grads[chunk, at].reshape(rows_count, width)
            grad_hidden = dot_nt(grad, outer_ref[...])
            grad_gate = jnp.sum(grad_hidden * product, axis=1, keepdims=True)
            grad_hidden = grad_hidden * gate
            grad_gate_up = jnp.concatenate(
                [
                    grad_hidden * up_part * sigmoid * (1.0 + gate_part * (1.0 - sigmoid)),
                    grad_hidden * active,
                ],
                axis=1,
            ).astype(bf16)
            back_gu[chunk, at] = grad_gate_up.reshape(wide, half, 2 * hidden_width)
            grads[chunk, at] = (gate * grad.astype(f32)).astype(bf16).reshape(wide, half, width)
            grad_rows = dot_nt(grad_gate_up, inner_ref[...]).astype(bf16)
            back[chunk, at, :, pl.ds(0, width)] = grad_rows.reshape(wide, half, width)
            high = grad_gate.astype(bf16).astype(f32)
            tail = jnp.where(is_high, high, jnp.where(is_rest, grad_gate - high, 0.0))
            back[chunk, at, :, pl.ds(width, small)] = tail.astype(bf16).reshape(wide, half, small)

        for t in range(rounds):
            for load in loads(t):
                load.start()
        second_grads.start()
        greet(axes.neighbours() + place.copies.neighbours() + [place.twin])
        next(gather)

        def first_tiles(t, carry):
            hooks(t, ((2, lambda: next(gather)),))
            for load in loads(t):
                load.wait()
            tile(0, t * wide, lax.rem(t, 2), t >= 2)
            return carry

        lax.fori_loop(0, rounds, first_tiles, 0)
        next(sums[0])
        next(gather)
        second_grads.wait()
        near, beyond = lax.div(axes.spot, 2), 1 - lax.div(axes.spot, 2)
        chips_per_round = wide // 2
        firsts = [
            (side * RING + part * chips_per_round) * 2
            for side, part in (
                (axes.side, beyond), (1 - axes.side, near), (1 - axes.side, beyond), (axes.side, near),
            )
        ]
        arrivals = gather_order(axes)

        def arrived(*numbers):
            for number in numbers:
                gather_line.take(
                    12 + number, lambda: rows_in.at[1, blocks(arrivals[number], True)], place.twin
                )

        def second_tiles(t, carry):
            hooks(
                t,
                (
                    (0, lambda: arrived(0, 1, 2, 4)),
                    (1, lambda: (next(sums[0]), next(sums[0]), arrived(3, 5, 6))[2]),
                    (2, lambda: (next(gather), arrived(7))[1]),
                    (3, lambda: (next(sums[1]), next(sums[0]))[0]),
                ),
            )
            tile(1, pick(t, firsts), lax.rem(t, 2), t >= 0)
            return carry

        lax.fori_loop(0, rounds, second_tiles, 0)
        next(sums[1])
        next(sums[1])

        every = 2 * GROUP * half
        for slot in range(2):
            box_copy(1, 0, slot).wait()

        def begin(part):
            for _ in range(3):
                next(part)

        def inner_terms(index, carry):
            hooks(
                index,
                (
                    (2, lambda: (begin(inner_sums[0]), next(sums[0]))[0]),
                    (3, lambda: next(sums[1])),
                ),
            )
            at = chunk_256(index)
            value = dot_tn(
                rows_in[:, :, :, at].reshape(every, 256),
                back_gu[...].reshape(every, 2 * hidden_width),
            )
            out_box[lax.div(index, 2), pl.ds(2 * lax.rem(index, 2), 2)] = value.astype(bf16).reshape(
                2, half, width
            )
            return carry

        lax.fori_loop(0, width // 256, inner_terms, 0)
        begin(inner_sums[1])

        def down_terms(index, carry):
            hooks(index, ((1, lambda: next(inner_sums[0])),))
            at = chunk_256(index)
            value = dot_tn(hidden[:, :, :, at].reshape(every, 256), grads[...].reshape(every, width))
            back_gu[0, pl.ds(2 * index, 2)] = value.astype(bf16).reshape(2, half, width)
            return carry

        lax.fori_loop(0, hidden_width // 256, down_terms, 0)
        begin(down_sum)
        drained(sums[0])
        next(inner_sums[1])
        next(inner_sums[0])
        next(sums[1])
        next(down_sum)
        next(inner_sums[1])
        drained(inner_sums[0])
        next(down_sum)
        drained(sums[1])
        drained(inner_sums[1])
        drained(down_sum)
        drained(gather)

    own_rows = (width + hidden_width) // REPS
    return pl.pallas_call(
        kernel,
        out_shape=[
            jax.ShapeDtypeStruct((count, columns), bf16),
            jax.ShapeDtypeStruct((own_rows, width), bf16),
            jax.ShapeDtypeStruct((GROUP, count, width), bf16),
        ],
        in_specs=[ANY, ANY, ANY, IN_VMEM, IN_VMEM],
        out_specs=[IN_VMEM, IN_VMEM, ANY],
        scratch_shapes=[
            pltpu.VMEM((2, GROUP, half, columns), bf16),
            pltpu.VMEM((2, GROUP, half, width), bf16),
            pltpu.VMEM((2, GROUP, half, hidden_width), bf16),
            pltpu.VMEM((2, GROUP, half, 2 * hidden_width), bf16),
            pltpu.VMEM((2, GROUP, half, columns), bf16),
            pltpu.VMEM((2, chips, half, columns), bf16),
            pltpu.VMEM((2, stage_rows(half), columns), bf16),
            pltpu.VMEM((2, wide, half, width), bf16),
            pltpu.VMEM((3, stage_rows(hidden_width // REPS), width), bf16),
        ]
        + sems(GATHER_SEMS)
        + sems(SUM_SEMS) * 5
        + [
            pltpu.SemaphoreType.DMA,
            pltpu.SemaphoreType.DMA((rounds + 1, 2)),
            pltpu.SemaphoreType.DMA((2,)),
        ],
        compiler_params=params(collective_id),
    )(sent, rows_first, grad_all, inner, outer)


WIDTH = 1024
QUERY = HEADS * HEAD_DIM
KEY = KV_HEADS * HEAD_DIM
EXPERTS = 16
SMALL = 128
LANES = 128
AT_K = QUERY
AT_V = AT_K + KEY
AT_S = AT_V + KEY
AT_O = AT_S + SMALL
PACKED = AT_O + WIDTH
ROWS_OWN = WIDTH // GROUP
KGAIN_OWN = KEY // GROUP
HEAD_PAIRS = KV_HEADS // 2
REST = 2 * KEY + SMALL


def drained(part):
    for _ in part:
        pass


def hooks(index, steps):
    for at, step in steps:
        pl.when(index == at)(step)


def chunk_256(index):
    return pl.ds(pl.multiple_of(index * 256, 256), 256)


def root_mean(values):
    return lax.rsqrt(jnp.mean(values * values, axis=1, keepdims=True) + norm_eps)


def lane_of(shape):
    return lax.broadcasted_iota(jnp.int32, shape, 1)


def turned(values, cosine, sine):
    first = (lane_of(values.shape) & (HEAD_DIM - 1)) < HEAD_DIM // 2
    swapped = jnp.where(
        first, pltpu.roll(values, LANES - HEAD_DIM // 2, 1), pltpu.roll(values, HEAD_DIM // 2, 1)
    )
    return values * cosine + swapped * sine


def gain_rows(small):
    rows = jnp.transpose(small.astype(f32))
    short = small.reshape(GROUP, ROWS_OWN, SMALL)[:, :KGAIN_OWN].reshape(KEY, SMALL)
    gain_k = jnp.transpose(short.astype(f32))[EXPERTS + 3 : EXPERTS + 4]
    return rows[EXPERTS : EXPERTS + 1], rows[EXPERTS + 1 : EXPERTS + 2], rows[EXPERTS + 2 : EXPERTS + 3], gain_k


def long_column(columns):
    cut = columns.reshape(GROUP, KGAIN_OWN, SMALL)
    return jnp.concatenate([cut, jnp.zeros_like(cut)], axis=1).reshape(WIDTH, SMALL)


def four_heads(chunk_a, chunk_b):
    low = lane_of(chunk_a.shape) < HEAD_DIM
    zero = jnp.zeros_like(chunk_a)
    return jnp.concatenate(
        [
            jnp.where(low, chunk_a, zero),
            jnp.where(low, pltpu.roll(chunk_a, HEAD_DIM, 1), zero),
            jnp.where(low, zero, pltpu.roll(chunk_b, HEAD_DIM, 1)),
            jnp.where(low, zero, chunk_b),
        ],
        axis=0,
    )


def two_chunks(blocks):
    rows = blocks.shape[0] // 4
    one, two, three, four = (blocks[n * rows : (n + 1) * rows] for n in range(4))
    low = lane_of(one.shape) < HEAD_DIM
    return (
        jnp.where(low, one, pltpu.roll(two, HEAD_DIM, 1)),
        jnp.where(low, pltpu.roll(three, HEAD_DIM, 1), four),
    )


def chunk_at(index, base=0):
    return pl.ds(pl.multiple_of(base + index * LANES, LANES), LANES)


def key_low(index):
    return (index // 2) * KEY + (index % 2) * LANES


def key_chunk(index, base=0):
    low = lax.div(index, 2) * KEY + lax.rem(index, 2) * LANES + base
    return pl.ds(pl.multiple_of(low, LANES), LANES)


def front_call(collective_id, tokens, cotangent, weights_own, gains, router, cosine, sine, routes, starts):
    count, width = tokens.shape
    seqs = starts.shape[0]
    positions = count // seqs
    length = REPS * positions
    score_scale = HEAD_DIM ** (-0.5)
    sent_width = width + SMALL

    def kernel(
        starts_ref, tokens_ref, grad_ref, query_w, key_w, value_w, output_w,
        gain_a_ref, gain_q_ref, gain_f_ref, gain_k_ref, router_ref, cos_ref, sin_ref, routes_ref,
        dense_out, grad_all, pairs_out, soft_out, rows_first,
        attn_in, query_raw, key_raw, query_low, mixed, middle, sent, gates_out,
        packed, small_box, dense, pairs, pair_own, soft_box, bias_box,
        ws0, wr0, ws1, wr1, ws2, wr2, gs0, gr0, gs1, gr1,
        ka0, la0, kb0, lb0, ka1, la1, kb1, lb1, rs, rr, own_sem, out_sem, soft_sem, pack_sem,
    ):
        place = Place()
        core = place.core
        packing = [
            pltpu.make_async_copy(
                source, packed.at[:, pl.ds(low, source.shape[1])], pack_sem.at[index]
            )
            for index, (source, low) in enumerate(
                ((key_w, AT_K), (value_w, AT_V), (query_w, 0), (output_w, AT_O))
            )
        ]
        for copy in packing:
            copy.start()
        small_box[...] = jnp.zeros_like(small_box)
        small_box[pl.ds(0, EXPERTS), pl.ds(0, ROWS_OWN)] = router_ref[...].astype(f32)
        for at, ref in enumerate((gain_a_ref, gain_q_ref, gain_f_ref, gain_k_ref)):
            size = ref.shape[0]
            small_box[pl.ds(EXPERTS + at, 1), pl.ds(0, size)] = (
                ref[...].astype(f32).reshape(1, size)
            )
        packed[:, pl.ds(AT_S, SMALL)] = jnp.transpose(small_box[...])[:ROWS_OWN].astype(bf16)

        def token_block(index, low, size):
            def block(which, row, n, other=False):
                at = (which[0] * RING + which[1]) * 2 + ((1 - core) if other else core)
                return dense.at[at, pl.ds(row, n), pl.ds(low, size)]

            return block

        def weight_gather(index, low, size, send_sem, recv_sem):
            return gather_parts(
                place.tokens, Line(send_sem, recv_sem), packed.at[:, pl.ds(low, size)],
                token_block(index, low, size), ROWS_OWN, own_sem.at[index], place.twin,
            )

        def rows_of(target):
            def block(which, row, n, other=False):
                at = (which[0] * RING + which[1]) * 2 + ((1 - core) if other else core)
                return target.at[at, pl.ds(row, n)]

            return block

        def pair_gather(seq, part, send_sem, recv_sem):
            columns = pl.ds(part * KEY, KEY)

            def block(which, row, n, other=False):
                return pairs.at[seq, which[0] * RING + which[1], pl.ds(row, n), columns]

            return gather_parts(
                place.copies, Line(send_sem, recv_sem),
                pair_own.at[pl.ds(seq * positions, positions), columns], block, positions,
                own_sem.at[8 + 2 * seq + part],
            )

        def soft_copy(seq, index, slot):
            return pltpu.make_async_copy(
                soft_box.at[slot], soft_out.at[seq, index], soft_sem.at[slot]
            )

        rest_gather = weight_gather(0, AT_K, REST, ws0, wr0)
        query_gather = weight_gather(1, 0, QUERY, ws1, wr1)
        output_gather = weight_gather(2, AT_O, WIDTH, ws2, wr2)
        def grad_gather(seq, send_sem, recv_sem):
            base = seq * positions

            def block(which, row, n, other=False):
                at = (which[0] * RING + which[1]) * 2 + ((1 - core) if other else core)
                return grad_all.at[at, pl.ds(base + row, n)]

            return gather_parts(
                place.tokens, Line(send_sem, recv_sem), grad_ref.at[pl.ds(base, positions)], block,
                positions, own_sem.at[5 + seq], place.twin,
            )

        grads = [grad_gather(0, gs0, gr0), grad_gather(1, gs1, gr1)]
        first_rows = gather_parts(
            place.tokens, Line(rs, rr), sent.at[pl.ds(0, positions)], rows_of(rows_first), positions,
            own_sem.at[7], place.twin,
        )
        heads_a0, heads_b0 = pair_gather(0, 0, ka0, la0), pair_gather(0, 1, kb0, lb0)
        heads_a1, heads_b1 = pair_gather(1, 0, ka1, la1), pair_gather(1, 1, kb1, lb1)

        greet(place.tokens.neighbours() + place.copies.neighbours() + [place.twin])
        for copy in packing:
            copy.wait()
        next(rest_gather)
        inputs = tokens_ref[...].astype(f32)
        middle[...] = inputs * root_mean(inputs)
        next(rest_gather)
        next(query_gather)
        query_at = place.rep * positions + lax.broadcasted_iota(jnp.int32, (positions, 1), 0)
        key_at = lax.broadcasted_iota(jnp.int32, (1, length), 1)
        for seq in range(seqs):
            allowed = key_at <= query_at
            for piece in range(starts_ref.shape[1]):
                start = starts_ref[seq, piece]
                query_inside = (query_at >= start) & (query_at < start + PIC)
                key_inside = (key_at >= start) & (key_at < start + PIC)
                allowed = allowed | (query_inside & key_inside)
            bias_box[seq] = jnp.where(allowed, 0.0, masked_score)
        next(rest_gather)
        next(query_gather)
        next(output_gather)
        drained(rest_gather)
        next(query_gather)
        next(output_gather)

        def weights(low, size):
            return dense[:, :, pl.ds(low, size)].reshape(width, size)

        small = weights(AT_S, SMALL)
        gain_a, gain_q, gain_f, gain_k = gain_rows(small)
        rows = (middle[...] * gain_a).astype(bf16)
        attn_in[...] = rows
        cos2 = jnp.concatenate([cos_ref[...]] * seqs, axis=0)
        sin2 = jnp.concatenate([sin_ref[...]] * seqs, axis=0)
        raw = dot(rows, weights(AT_K, KEY))
        key_raw[...] = raw
        scaled = raw * root_mean(raw) * gain_k
        for chunk in range(KEY // LANES):
            at = slice(chunk * LANES, (chunk + 1) * LANES)
            pair_own[:, pl.ds(key_low(chunk), LANES)] = turned(scaled[:, at], cos2, sin2).astype(bf16)
        raw = dot(rows, weights(AT_V, KEY)).astype(bf16)
        for chunk in range(KEY // LANES):
            at = slice(chunk * LANES, (chunk + 1) * LANES)
            pair_own[:, pl.ds(key_low(chunk) + KEY // 2, LANES)] = raw[:, at]
        next(heads_a0)
        next(heads_b0)
        drained(query_gather)
        next(output_gather)
        next(grads[0])
        raw = dot(rows, weights(0, QUERY))
        query_raw[...] = raw
        scaled = raw * root_mean(raw) * gain_q
        for chunk in range(QUERY // LANES):
            at = slice(chunk * LANES, (chunk + 1) * LANES)
            query_low[:, at] = turned(scaled[:, at], cos2, sin2).astype(bf16)
        next(heads_a0)
        next(heads_b0)
        next(heads_a1)
        drained(output_gather)
        dense_copy = pltpu.make_async_copy(dense, dense_out, out_sem.at[0])
        dense_copy.start()
        next(heads_a0)
        next(grads[0])
        next(grads[1])
        next(heads_b0)
        next(heads_b1)
        drained(heads_a0)

        def attend(seq, index, slot, wait_first):
            rows_at = pl.ds(seq * positions, positions)
            queries = four_heads(
                query_low[rows_at, chunk_at(2 * index)].astype(f32),
                query_low[rows_at, chunk_at(2 * index + 1)].astype(f32),
            )
            queries = (queries * score_scale).astype(bf16)
            keys = pairs[seq, :, :, key_chunk(index)].reshape(length, LANES)
            scores = dot_nt(queries, keys).reshape(4, positions, length) + bias_box[seq][None]
            scores = scores.reshape(4 * positions, length)
            raised = jnp.exp(scores - jnp.max(scores, axis=1, keepdims=True))
            soft = (raised * (1.0 / jnp.sum(raised, axis=1, keepdims=True))).astype(bf16)

            @pl.when(wait_first)
            def _():
                soft_copy(seq, index, slot).wait()

            soft_box[slot] = soft
            soft_copy(seq, index, slot).start()
            values = pairs[seq, :, :, key_chunk(index, KEY // 2)].reshape(length, LANES)
            chunk_a, chunk_b = two_chunks(dot(soft, values))
            mixed[rows_at, chunk_at(2 * index)] = chunk_a.astype(bf16)
            mixed[rows_at, chunk_at(2 * index + 1)] = chunk_b.astype(bf16)

        def features(seq):
            at = pl.ds(seq * positions, positions)
            total = tokens_ref[at].astype(f32) + dot(mixed[at], weights(AT_O, WIDTH))
            middle[at] = total
            ffn_in = (total * root_mean(total) * gain_f).astype(bf16)
            sent[at, pl.ds(0, width)] = ffn_in
            lanes = lane_of((positions, SMALL))
            named = jnp.transpose(routes_ref[seq].astype(f32)).astype(jnp.int32)
            chosen = lanes == named[:, :1]
            for choice in range(1, named.shape[1]):
                chosen = chosen | (lanes == named[:, choice : choice + 1])
            logits = jnp.where(chosen, dot(ffn_in, small), masked_score)
            raised = jnp.exp(logits - jnp.max(logits, axis=1, keepdims=True))
            gates = raised * (1.0 / jnp.sum(raised, axis=1, keepdims=True))
            gates = jnp.where(chosen, gates, 0.0)
            gates_out[at] = gates
            high = gates.astype(bf16).astype(f32)
            tail = high + pltpu.roll(gates - high, EXPERTS, 1)
            sent[at, pl.ds(width, SMALL)] = tail.astype(bf16)

        def first_heads(index, carry):
            hooks(
                index,
                (
                    (0, lambda: next(heads_a1)),
                    (1, lambda: next(grads[0])),
                    (2, lambda: (drained(heads_b0), next(heads_a1))[0]),
                    (3, lambda: (next(heads_b1), next(grads[1]))[0]),
                ),
            )
            attend(0, index, lax.rem(index, 2), index >= 2)
            return carry

        lax.fori_loop(0, HEAD_PAIRS, first_heads, 0)
        features(0)
        next(first_rows)
        next(heads_b1)
        drained(heads_a1)
        next(grads[0])

        def second_heads(index, carry):
            hooks(
                index,
                (
                    (1, lambda: next(grads[1])),
                    (2, lambda: drained(heads_b1)),
                    (3, lambda: next(first_rows)),
                ),
            )
            attend(1, index, lax.rem(index, 2), index >= 0)
            return carry

        lax.fori_loop(0, HEAD_PAIRS, second_heads, 0)
        pairs_copy = pltpu.make_async_copy(pairs, pairs_out, out_sem.at[1])
        pairs_copy.start()
        features(1)
        next(first_rows)
        drained(grads[0])
        drained(grads[1])
        drained(first_rows)
        dense_copy.wait()
        pairs_copy.wait()
        for slot in range(2):
            soft_copy(1, 0, slot).wait()

    return pl.pallas_call(
        kernel,
        out_shape=[
            jax.ShapeDtypeStruct((GROUP, ROWS_OWN, PACKED), bf16),
            jax.ShapeDtypeStruct((GROUP, count, width), bf16),
            jax.ShapeDtypeStruct((seqs, REPS, positions, 2 * KEY), bf16),
            jax.ShapeDtypeStruct((seqs, HEAD_PAIRS, 4 * positions, length), bf16),
            jax.ShapeDtypeStruct((GROUP, positions, sent_width), bf16),
            jax.ShapeDtypeStruct((count, width), bf16),
            jax.ShapeDtypeStruct((count, QUERY), f32),
            jax.ShapeDtypeStruct((count, KEY), f32),
            jax.ShapeDtypeStruct((count, QUERY), bf16),
            jax.ShapeDtypeStruct((count, QUERY), bf16),
            jax.ShapeDtypeStruct((count, width), f32),
            jax.ShapeDtypeStruct((count, width + SMALL), bf16),
            jax.ShapeDtypeStruct((count, SMALL), f32),
        ],
        in_specs=[pl.BlockSpec(memory_space=pltpu.SMEM), IN_VMEM] + [ANY] * 5 + [IN_VMEM] * 8,
        out_specs=[ANY] * 5 + [IN_VMEM] * 8,
        scratch_shapes=[
            pltpu.VMEM((ROWS_OWN, PACKED), bf16),
            pltpu.VMEM((SMALL, LANES), f32),
            pltpu.VMEM((GROUP, ROWS_OWN, PACKED), bf16),
            pltpu.VMEM((seqs, REPS, positions, 2 * KEY), bf16),
            pltpu.VMEM((count, 2 * KEY), bf16),
            pltpu.VMEM((2, 4 * positions, length), bf16),
            pltpu.VMEM((seqs, positions, length), f32),
        ]
        + sems(GATHER_SEMS) * 10
        + [
            pltpu.SemaphoreType.DMA((12,)),
            pltpu.SemaphoreType.DMA((2,)),
            pltpu.SemaphoreType.DMA((2,)),
            pltpu.SemaphoreType.DMA((4,)),
        ],
        compiler_params=params(collective_id),
    )(starts, tokens, cotangent, *weights_own, *gains, router, cosine, sine, routes)


def norm_back(values, gain, grad):
    scale = root_mean(values)
    weighted = grad * gain
    mean = jnp.mean(values * weighted, axis=1, keepdims=True)
    inner = weighted * scale - values * (scale * scale * scale * mean)
    return inner, jnp.sum(grad * values * scale, axis=0, keepdims=True)


def back_call(
    collective_id, returned, gates, middle, sent, dense, cotangent, tokens, attn_in, query_raw, key_raw,
    query_low, mixed, pairs, soft, out_terms, expert_own, cosine, sine,
):
    count, width = tokens.shape
    seqs, _, positions, _ = pairs.shape
    length = REPS * positions
    expert_rows = expert_own.shape[0]
    score_scale = HEAD_DIM ** (-0.5)
    chips = GROUP // 2

    def kernel(
        returned_ref, gates_ref, middle_ref, sent_ref, dense_ref, grad_ref, tokens_ref, attn_ref,
        query_raw_ref, key_raw_ref, query_ref, mixed_ref, pairs_ref, soft_ref, out_ref, expert_ref,
        cos_ref, sin_ref,
        block_out, tokens_grad, small_out, dense_out, expert_all,
        weight_box, weight_rest, rest_terms, dense_own,
        o_staged, q_staged, rest_staged, o_stage, q_stage, rest_stage,
        out_held, out_staged, out_stage, small_terms, small_staged, small_stage, small_own, q_terms,
        soft_box, key_box, value_box, pair_terms, pair_stage, pair_grads,
        grad_mixed, grad_query, grad_middle, grad_attn, grad_attn_in, gain_box,
        o_got, q_got, rest_got, small_got, totals,
        out_s, out_r, small_s, small_r, kv0_s, kv0_r, kva_s, kva_r, kvb_s, kvb_r, o_s, o_r, q_s, q_r, rest_s, rest_r,
        ge_s, ge_r, go_s, go_r, gq_s, gq_r, grest_s, grest_r, gsmall_s, gsmall_r,
        load_sem, held_sem, box_sem, own_sem, total_sem,
    ):
        place = Place()
        core = place.core
        token_axes, copy_axes = place.tokens, place.copies

        def chip_of(which):
            return which[0] * RING + which[1]

        def blocks(which, other=False):
            return chip_of(which) * 2 + ((1 - core) if other else core)

        def out_store(low, step, value):
            at = pl.ds(low, step)
            block_out[at] = (middle_ref[at] + value).astype(bf16)

        out_sum = sum_parts(
            token_axes, Line(out_s, out_r),
            lambda which, low, n: out_held.at[chip_of(which), pl.ds(low, n)],
            out_stage, count, None,
            (place.twin, lambda which: out_ref.at[blocks(which, True)],
             lambda which: out_staged.at[chip_of(which)]),
            store=out_store,
        )
        def pair_sum(seq, low, size, index, send_sem, recv_sem):
            columns = pl.ds(low, size)
            return sum_parts(
                copy_axes, Line(send_sem, recv_sem),
                lambda which, row, n: pair_terms.at[seq, chip_of(which), pl.ds(row, n), columns],
                pair_stage.at[index, :, columns], positions,
                pair_grads.at[pl.ds(seq * positions, positions), columns],
            )

        first_pairs = pair_sum(0, 0, 2 * KEY, 0, kv0_s, kv0_r)
        second_pairs = [
            pair_sum(1, 0, KEY, 1, kva_s, kva_r), pair_sum(1, KEY, KEY, 1, kvb_s, kvb_r)
        ]

        def rows_of_block(terms, index, low, n):
            return terms.at[pl.ds(index * ROWS_OWN + low, n)]

        def rows_of_pairs(terms, index, low, n):
            at = lax.rem(index, 2) * ROWS_OWN + low
            return terms.at[0, lax.div(index, 2), pl.ds(at, n)]

        def dense_sum(rows_of, terms, staged, stage, own, send_sem, recv_sem):
            return sum_parts(
                token_axes, Line(send_sem, recv_sem),
                lambda which, row, n: rows_of(terms, blocks(which), row, n),
                stage, ROWS_OWN, own,
                (place.twin, lambda which: rows_of(terms, blocks(which, True), 0, ROWS_OWN),
                 lambda which: staged.at[chip_of(which)]),
            )

        def own_columns(low):
            return dense_own.at[:, pl.ds(low, width)]

        o_sum = dense_sum(rows_of_pairs, pair_terms, o_staged, o_stage, own_columns(AT_O), o_s, o_r)
        q_sum = dense_sum(rows_of_block, q_terms, q_staged, q_stage, own_columns(0), q_s, q_r)
        rest_sum = dense_sum(
            rows_of_block, rest_terms, rest_staged, rest_stage, own_columns(AT_K), rest_s, rest_r
        )
        small_sum = dense_sum(
            rows_of_block, small_terms, small_staged, small_stage, small_own, small_s, small_r
        )

        def dense_total(index, low, got, send_sem, recv_sem):
            def own(rep):
                return dense_own.at[:, chunk_at(rep, low)]

            def target(rep):
                return dense_out.at[:, chunk_at(rep, low)]

            return total_parts(
                place, Line(send_sem, recv_sem), own, got, totals.at[index], target,
                total_sem.at[index],
            )

        o_total = dense_total(0, AT_O, o_got, go_s, go_r)
        q_total = dense_total(1, 0, q_got, gq_s, gq_r)
        rest_total = dense_total(2, AT_K, rest_got, grest_s, grest_r)
        small_total = spread_parts(place, Line(gsmall_s, gsmall_r), small_own, small_got, small_out)
        expert_gather = gather_parts(
            copy_axes, Line(ge_s, ge_r), expert_ref,
            lambda which, row, n, other=False: expert_all.at[chip_of(which), pl.ds(row, n)],
            expert_rows, own_sem,
        )

        def weight_load(low, index):
            return pltpu.make_async_copy(
                dense_ref.at[:, :, pl.ds(low, width)], weight_box, load_sem.at[index]
            )

        rest_load = pltpu.make_async_copy(
            dense_ref.at[:, :, pl.ds(AT_K, REST)], weight_rest, load_sem.at[1]
        )
        held_loads = [
            pltpu.make_async_copy(
                out_ref.at[2 * chip + core], out_held.at[chip], held_sem.at[chip]
            )
            for chip in range(chips)
        ]

        def box_loads(number, slot):
            seq, index = lax.div(number, HEAD_PAIRS), lax.rem(number, HEAD_PAIRS)
            return [
                pltpu.make_async_copy(
                    soft_ref.at[seq, index], soft_box.at[slot], box_sem.at[slot, 0]
                ),
                pltpu.make_async_copy(
                    pairs_ref.at[seq, :, :, key_chunk(index)], key_box.at[slot], box_sem.at[slot, 1]
                ),
                pltpu.make_async_copy(
                    pairs_ref.at[seq, :, :, key_chunk(index, KEY // 2)],
                    value_box.at[slot],
                    box_sem.at[slot, 2],
                ),
            ]

        rest_load.start()
        weight_load(AT_O, 0).start()
        for load in held_loads + box_loads(0, 0):
            load.start()
        greet(
            token_axes.neighbours()
            + [place.twin]
            + [(place.shard, other) for other in place.others[1:]]
        )
        next(out_sum)
        next(expert_gather)
        rest_load.wait()

        small = weight_rest[:, :, pl.ds(2 * KEY, SMALL)].reshape(width, SMALL)
        gain_a, gain_q, gain_f, gain_k = gain_rows(small)
        gates = gates_ref[...]
        tail = returned_ref[:, pl.ds(width, SMALL)].astype(f32)
        grad_gates = tail + pltpu.roll(tail, SMALL - EXPERTS, 1)
        grad_logits = gates * (grad_gates - jnp.sum(gates * grad_gates, axis=1, keepdims=True))
        grad_logits = grad_logits.astype(bf16)
        grad_ffn = returned_ref[:, pl.ds(0, width)].astype(f32) + dot_nt(grad_logits, small)
        inner, gain_f_terms = norm_back(middle_ref[...], gain_f, grad_ffn)
        inner = grad_ref[...].astype(f32) + inner
        grad_middle[...] = inner
        grad_attn[...] = inner.astype(bf16)
        gain_box[...] = jnp.zeros_like(gain_box)
        gain_box[pl.ds(EXPERTS + 2, 1)] = gain_f_terms
        weight_load(AT_O, 0).wait()
        grad_mixed[...] = dot_nt(
            grad_attn[...], weight_box[...].reshape(QUERY, width)
        ).astype(bf16)
        weight_load(0, 3).start()

        def attend_back(seq, index):
            number = seq * HEAD_PAIRS + index
            slot = lax.rem(number, 2)
            for load in box_loads(number, slot):
                load.wait()

            @pl.when(number + 1 < seqs * HEAD_PAIRS)
            def _():
                for load in box_loads(number + 1, 1 - slot):
                    load.start()

            rows_at = pl.ds(seq * positions, positions)
            first, second = chunk_at(2 * index), chunk_at(2 * index + 1)
            queries = four_heads(
                query_ref[rows_at, first].astype(f32), query_ref[rows_at, second].astype(f32)
            )
            queries = (queries * score_scale).astype(bf16)
            grads = four_heads(
                grad_mixed[rows_at, first].astype(f32), grad_mixed[rows_at, second].astype(f32)
            ).astype(bf16)
            keys = key_box[slot].reshape(length, LANES)
            values = value_box[slot].reshape(length, LANES)
            soft_low = soft_box[slot]
            value_terms = dot_tn(soft_low, grads)
            pair_terms[seq, :, :, key_chunk(index, KEY // 2)] = value_terms.astype(bf16).reshape(
                REPS, positions, LANES
            )
            soft_full = soft_low.astype(f32)
            grad_soft = dot_nt(grads, values)
            weighted = soft_full * grad_soft
            grad_scores = (
                weighted - soft_full * jnp.sum(weighted, axis=1, keepdims=True)
            ).astype(bf16)
            key_terms = dot_tn(grad_scores, queries)
            pair_terms[seq, :, :, key_chunk(index)] = key_terms.astype(bf16).reshape(
                REPS, positions, LANES
            )
            chunk_a, chunk_b = two_chunks(dot(grad_scores, keys) * score_scale)
            grad_query[rows_at, first] = chunk_a.astype(bf16)
            grad_query[rows_at, second] = chunk_b.astype(bf16)

        def out_ready():
            for load in held_loads:
                load.wait()
            next(out_sum)
            next(out_sum)

        def begin(part):
            for _ in range(3):
                next(part)

        def first_heads(index, carry):
            hooks(index, ((2, out_ready),))
            attend_back(0, index)
            return carry

        lax.fori_loop(0, HEAD_PAIRS, first_heads, 0)
        begin(first_pairs)

        def second_heads(index, carry):
            hooks(
                index,
                (
                    (1, lambda: next(out_sum)),
                    (2, lambda: begin(second_pairs[0])),
                    (3, lambda: next(first_pairs)),
                ),
            )
            attend_back(1, index)
            return carry

        lax.fori_loop(0, HEAD_PAIRS, second_heads, 0)
        begin(second_pairs[1])
        next(second_pairs[0])
        router_terms = dot_tn(sent_ref[:, pl.ds(0, width)], grad_logits)

        cos2 = jnp.concatenate([cos_ref[...]] * seqs, axis=0)
        sin2 = -jnp.concatenate([sin_ref[...]] * seqs, axis=0)

        def turned_back(values):
            return jnp.concatenate(
                [
                    turned(values[:, low : low + LANES], cos2, sin2)
                    for low in range(0, values.shape[1], LANES)
                ],
                axis=1,
            )

        grad, gain_q_terms = norm_back(
            query_raw_ref[...], gain_q, turned_back(grad_query[...].astype(f32))
        )
        gain_box[pl.ds(EXPERTS + 1, 1)] = gain_q_terms
        grad_query_low = grad.astype(bf16)
        weight_load(0, 3).wait()
        grad_attn_in[...] = dot_nt(grad_query_low, weight_box[...].reshape(width, QUERY))

        next(second_pairs[1])
        next(first_pairs)
        next(second_pairs[0])
        next(second_pairs[1])
        next(expert_gather)
        next(out_sum)
        drained(first_pairs)

        def o_rows(index, carry):
            at = chunk_256(index)
            value = dot_tn(mixed_ref[:, at], grad_attn[...]).astype(bf16)
            pair_terms[0, pl.ds(2 * index, 2)] = value.reshape(2, positions, width)
            return carry

        lax.fori_loop(0, QUERY // 256, o_rows, 0)
        next(o_sum)

        def q_rows(index, carry):
            at = chunk_256(index)
            q_terms[at] = dot_tn(attn_ref[:, at], grad_query_low).astype(bf16)
            return carry

        lax.fori_loop(0, width // 256, q_rows, 0)
        next(q_sum)
        next(o_sum)
        next(o_sum)
        drained(second_pairs[0])
        drained(second_pairs[1])

        grads = pair_grads[...]
        half = KEY // 2
        key_grads = jnp.concatenate([grads[:, :half], grads[:, KEY : KEY + half]], axis=1)
        value_grads = jnp.concatenate([grads[:, half:KEY], grads[:, KEY + half :]], axis=1)
        grad, gain_k_terms = norm_back(
            key_raw_ref[...], gain_k, turned_back(key_grads.astype(bf16).astype(f32))
        )
        grad_pairs = jnp.concatenate([grad.astype(bf16), value_grads.astype(bf16)], axis=1)

        def rest_rows(index, carry):
            at = chunk_256(index)
            rest_terms[at] = dot_tn(attn_ref[:, at], grad_pairs).astype(bf16)
            return carry

        lax.fori_loop(0, width // 256, rest_rows, 0)
        next(rest_sum)
        grad = grad_attn_in[...] + dot_nt(
            grad_pairs, weight_rest[:, :, pl.ds(0, 2 * KEY)].reshape(width, 2 * KEY)
        )
        next(rest_sum)
        next(rest_sum)
        values = tokens_ref[...].astype(f32)
        inner, gain_a_terms = norm_back(values, gain_a, grad)
        gain_box[pl.ds(EXPERTS, 1)] = gain_a_terms
        lanes = lane_of((KEY, SMALL))
        gain_k_column = jnp.where(
            lanes == EXPERTS + 3,
            jnp.transpose(jnp.broadcast_to(gain_k_terms, (SMALL, KEY))),
            0.0,
        )
        small_terms[...] = (
            router_terms + jnp.transpose(gain_box[...]) + long_column(gain_k_column)
        ).astype(bf16)
        next(small_sum)
        tokens_grad[...] = (grad_middle[...] + inner).astype(bf16)
        next(small_sum)
        next(small_sum)
        next(q_sum)
        next(q_sum)
        next(rest_sum)
        next(o_sum)
        next(small_sum)
        next(expert_gather)
        next(q_sum)
        next(o_sum)
        next(small_sum)
        next(rest_sum)
        next(q_sum)
        drained(out_sum)
        drained(o_sum)
        next(o_total)
        drained(small_sum)
        next(small_total)
        drained(q_sum)
        next(q_total)
        next(o_total)
        drained(rest_sum)
        next(rest_total)
        next(q_total)
        drained(small_total)
        next(expert_gather)
        next(rest_total)
        drained(expert_gather)
        drained(o_total)
        drained(q_total)
        drained(rest_total)

    block = pltpu.VMEM((GROUP, ROWS_OWN, width), bf16)
    scratch = [
        block,
        pltpu.VMEM((GROUP, ROWS_OWN, REST), bf16),
        pltpu.VMEM((width, 2 * KEY), bf16),
        pltpu.VMEM((ROWS_OWN, PACKED), bf16),
        pltpu.VMEM((chips, ROWS_OWN, width), bf16),
        pltpu.VMEM((chips, ROWS_OWN, QUERY), bf16),
        pltpu.VMEM((chips, ROWS_OWN, 2 * KEY), bf16),
        pltpu.VMEM((stage_rows(ROWS_OWN), width), bf16),
        pltpu.VMEM((stage_rows(ROWS_OWN), QUERY), bf16),
        pltpu.VMEM((stage_rows(ROWS_OWN), 2 * KEY), bf16),
        pltpu.VMEM((chips, count, width), bf16),
        pltpu.VMEM((chips, count, width), bf16),
        pltpu.VMEM((stage_rows(count), width), bf16),
        pltpu.VMEM((width, SMALL), bf16),
        pltpu.VMEM((chips, ROWS_OWN, SMALL), bf16),
        pltpu.VMEM((stage_rows(ROWS_OWN), SMALL), bf16),
        pltpu.VMEM((ROWS_OWN, SMALL), bf16),
        pltpu.VMEM((width, QUERY), bf16),
        pltpu.VMEM((2, 4 * positions, length), bf16),
        pltpu.VMEM((2, REPS, positions, LANES), bf16),
        pltpu.VMEM((2, REPS, positions, LANES), bf16),
        pltpu.VMEM((seqs, REPS, positions, 2 * KEY), bf16),
        pltpu.VMEM((seqs, stage_rows(positions), 2 * KEY), bf16),
        pltpu.VMEM((count, 2 * KEY), f32),
        pltpu.VMEM((count, QUERY), bf16),
        pltpu.VMEM((count, QUERY), bf16),
        pltpu.VMEM((count, width), f32),
        pltpu.VMEM((count, width), bf16),
        pltpu.VMEM((count, width), f32),
        pltpu.VMEM((SMALL, width), f32),
    ]
    scratch += [pltpu.VMEM((REPS, ROWS_OWN, LANES), bf16)] * 4
    scratch += [pltpu.VMEM((3, ROWS_OWN, LANES), bf16)]
    return pl.pallas_call(
        kernel,
        out_shape=[
            jax.ShapeDtypeStruct((count, width), bf16),
            jax.ShapeDtypeStruct((count, width), bf16),
            jax.ShapeDtypeStruct((ROWS_OWN, SMALL), f32),
            jax.ShapeDtypeStruct((ROWS_OWN, PACKED), bf16),
            jax.ShapeDtypeStruct((REPS, expert_rows, width), bf16),
        ],
        in_specs=[IN_VMEM] * 4 + [ANY] + [IN_VMEM] * 7 + [ANY] * 4 + [IN_VMEM] * 2,
        out_specs=[IN_VMEM, IN_VMEM, IN_VMEM, ANY, ANY],
        scratch_shapes=scratch
        + sems(SUM_SEMS) * 8
        + sems(GATHER_SEMS)
        + sems(TOTAL_SEMS) * 4
        + [
            pltpu.SemaphoreType.DMA((4,)),
            pltpu.SemaphoreType.DMA((chips,)),
            pltpu.SemaphoreType.DMA((2, 3)),
            pltpu.SemaphoreType.DMA,
            pltpu.SemaphoreType.DMA((3,)),
        ],
        compiler_params=params(collective_id),
    )(
        returned, gates, middle, sent, dense, cotangent, tokens, attn_in, query_raw, key_raw,
        query_low, mixed, pairs, soft, out_terms, expert_own, cosine, sine,
    )


def finish_call(block_out, tokens_grad, small_sum, dense_own, expert_all):
    reps, expert_rows, width = expert_all.shape
    piece = expert_rows // 3
    rows = block_out.shape[0] // reps

    def kernel(
        block_ref, tokens_ref, small_ref, dense_ref, expert_ref,
        block, tokens, inner, outer, query, key, value, output, router, gain_a, gain_q, gain_f, gain_k,
    ):
        block[...] = block_ref[...]
        tokens[...] = tokens_ref[...]
        inner[0] = expert_ref[0, :piece].astype(f32)
        inner[1] = expert_ref[0, piece : 2 * piece].astype(f32)
        outer[...] = expert_ref[0, 2 * piece :].astype(f32)

        @pl.when(pl.program_id(0) == 1)
        def _():
            for low, target in ((0, query), (AT_K, key), (AT_V, value), (AT_O, output)):
                target[...] = dense_ref[:, pl.ds(low, target.shape[1])].astype(f32)
            turned_small = jnp.transpose(small_ref[...])
            router[...] = turned_small[:EXPERTS, :ROWS_OWN]
            for at, target in enumerate((gain_a, gain_q, gain_f, gain_k)):
                size = target.shape[0]
                target[...] = turned_small[EXPERTS + at, :size].reshape(size)

    def whole(*shape):
        return pl.BlockSpec(shape, lambda i: (0,) * len(shape))

    by_rows = pl.BlockSpec((rows, width), lambda i: (i, 0))
    shapes = [(ROWS_OWN, QUERY), (ROWS_OWN, KEY), (ROWS_OWN, KEY), (ROWS_OWN, WIDTH)]
    shapes += [(EXPERTS, ROWS_OWN), (ROWS_OWN,), (ROWS_OWN,), (ROWS_OWN,), (KGAIN_OWN,)]
    return pl.pallas_call(
        kernel,
        grid=(reps,),
        out_shape=[
            jax.ShapeDtypeStruct(block_out.shape, bf16),
            jax.ShapeDtypeStruct(tokens_grad.shape, bf16),
            jax.ShapeDtypeStruct((2, reps * piece, width), f32),
            jax.ShapeDtypeStruct((reps * piece, width), f32),
        ]
        + [jax.ShapeDtypeStruct(shape, f32) for shape in shapes],
        in_specs=[
            by_rows,
            by_rows,
            whole(*small_sum.shape),
            whole(*dense_own.shape),
            pl.BlockSpec((1, expert_rows, width), lambda i: (i, 0, 0)),
        ],
        out_specs=[
            by_rows,
            by_rows,
            pl.BlockSpec((2, piece, width), lambda i: (0, i, 0)),
            pl.BlockSpec((piece, width), lambda i: (i, 0)),
        ]
        + [whole(*shape) for shape in shapes],
        compiler_params=pltpu.CompilerParams(vmem_limit_bytes=VMEM_LIMIT),
    )(block_out, tokens_grad, small_sum, dense_own, expert_all)


def rotary_tables(positions):
    lane = jnp.arange(LANES, dtype=jnp.int32)
    half = HEAD_DIM // 2
    exponent = (lane % half).astype(f32) * (2.0 / HEAD_DIM)
    frequency = rope_base ** (-exponent)
    angles = positions.astype(f32)[:, None] * frequency[None, :]
    sign = jnp.where(lane % HEAD_DIM < half, -1.0, 1.0).astype(f32)
    return jnp.cos(angles), jnp.sin(angles) * sign[None, :]


def shards(
    tokens,
    cotangent,
    routes,
    picture_starts,
    attn_gain,
    query_weight,
    key_weight,
    value_weight,
    query_gain,
    key_gain,
    output_weight,
    ffn_gain,
    router_weight,
    expert_in,
    expert_down,
):
    seqs, positions, width = tokens.shape
    count = seqs * positions
    query_pos = lax.axis_index("rep") * positions + jnp.arange(positions, dtype=jnp.int32)
    cosine, sine = rotary_tables(query_pos)
    rows = tokens.reshape(count, width)
    grad_rows = cotangent.reshape(count, width)
    (
        dense, grad_all, pairs, soft, rows_first,
        attn_in, query_raw, key_raw, query_low, mixed, middle, sent, gates,
    ) = front_call(
        1, rows, grad_rows, (query_weight, key_weight, value_weight, output_weight),
        (attn_gain, query_gain, ffn_gain, key_gain), router_weight.T,
        cosine, sine, jnp.transpose(routes, (0, 2, 1)), picture_starts,
    )
    returned, expert_own, out_terms = moe_call(
        2, sent, rows_first, grad_all, expert_in[0], expert_down[0]
    )
    block_out, tokens_grad, small_sum, dense_out, expert_all = back_call(
        3, returned, gates, middle, sent, dense, grad_rows, rows, attn_in,
        query_raw, key_raw, query_low, mixed, pairs, soft, out_terms, expert_own, cosine, sine,
    )
    (
        block_out, tokens_grad, inner, outer, query, key, value, output, router, gain_a, gain_q, gain_f, gain_k,
    ) = finish_call(block_out, tokens_grad, small_sum, dense_out, expert_all)
    return (
        block_out.reshape(tokens.shape),
        tokens_grad.reshape(tokens.shape),
        gain_a,
        query,
        key,
        value,
        gain_q,
        gain_k,
        output,
        gain_f,
        router.T,
        inner.reshape(expert_in.shape),
        outer[None],
    )


def solution(mesh):
    by_tokens = P("shard", "rep", None)
    rows, line, block = P("shard", None), P("shard"), P("shard", None, None)
    in_specs = (
        by_tokens, by_tokens, by_tokens, rows, line, rows, rows, rows, line, line, rows, line, rows, block, block,
    )
    out_specs = (
        by_tokens, by_tokens, line, rows, rows, rows, line, line, rows, line, rows, block, block,
    )
    return jax.shard_map(shards, mesh=mesh, in_specs=in_specs, out_specs=out_specs, check_vma=False)
```

```python
import jax
import jax.numpy as jnp
from jax import lax
from jax.experimental import pallas as pl
from jax.experimental.pallas import tpu as pltpu
from jax.sharding import PartitionSpec as P

HEADS = 16
KV_HEADS = 8
HEAD_DIM = 64
PIC = 256
RING = 4
GROUP = 16
REPS = 8
VMEM_LIMIT = 63 << 20

norm_eps = 1e-06
rope_base = 10000.0
masked_score = -1e30

bf16 = jnp.bfloat16
f32 = jnp.float32


class Place:
    def __init__(self):
        shard = lax.axis_index("shard")
        rep = lax.axis_index("rep")
        self.shard, self.rep = shard, rep
        core = lax.rem(shard, 2)
        ring_z = lax.rem(lax.div(shard, 2), RING)
        y_hi = lax.div(shard, 8)
        ring_x = lax.rem(rep, RING)
        y_lo = lax.div(rep, RING)
        self.core = core

        def shard_of(hi, z, c):
            return (hi * RING + z) * 2 + c

        def rep_of(lo, x):
            return lo * RING + x

        def up(v):
            return lax.rem(v + 1, RING)

        def down(v):
            return lax.rem(v + RING - 1, RING)

        self.twin = (shard_of(y_hi, ring_z, 1 - core), rep)
        self.others = [lax.rem(rep + step, REPS) for step in range(REPS)]
        self.tokens = Axes(
            y_hi,
            ring_z,
            (shard_of(y_hi, up(ring_z), core), rep),
            (shard_of(y_hi, down(ring_z), core), rep),
            (shard_of(1 - y_hi, ring_z, core), rep_of(1 - y_lo, ring_x)),
        )
        self.copies = Axes(
            y_lo,
            ring_x,
            (shard, rep_of(y_lo, up(ring_x))),
            (shard, rep_of(y_lo, down(ring_x))),
            (shard, rep_of(1 - y_lo, ring_x)),
        )


class Axes:
    def __init__(self, side, spot, ahead, behind, across):
        self.side, self.spot = side, spot
        self.ahead, self.behind, self.across = ahead, behind, across
        sides = (side, 1 - side)
        spots = [lax.rem(spot + step, RING) for step in range(RING)]
        self.places = [[(sides[flip], spots[step]) for step in range(RING)] for flip in range(2)]

    def at(self, flip, step):
        return self.places[flip][step % RING]

    def neighbours(self):
        return [self.ahead, self.behind, self.across]


def greet(devices):
    barrier = pltpu.get_barrier_semaphore()
    for device in devices:
        pl.semaphore_signal(barrier, inc=1, device_id=device, device_id_type=pl.DeviceIdType.MESH)
    pl.semaphore_wait(barrier, len(devices))


class Line:
    def __init__(self, send_sem, recv_sem):
        self.send_sem, self.recv_sem = send_sem, recv_sem
        self.sent = []

    def copy(self, index, source, target, device):
        return pltpu.make_async_remote_copy(
            src_ref=source(),
            dst_ref=target(),
            send_sem=self.send_sem.at[index],
            recv_sem=self.recv_sem.at[index],
            device_id=device,
            device_id_type=pl.DeviceIdType.MESH,
        )

    def send(self, index, source, target, device):
        self.copy(index, source, target, device).start()
        self.sent.append((index, source, target, device))

    def take(self, index, target, device):
        self.copy(index, target, target, device).wait_recv()

    def finish(self):
        for sent in self.sent:
            self.copy(*sent).wait_send()


def abreast(*parts):
    running = list(parts)
    while running:
        for part in list(running):
            try:
                next(part)
            except StopIteration:
                running.remove(part)


GATHER_SEMS = 20


def gather_parts(axes, line, own, block, rows, local_sem, twin=None, twin_later=False):
    half, quarter = rows // 2, rows // 4
    mine, back, front, far = axes.at(0, 0), axes.at(0, -1), axes.at(0, 1), axes.at(0, 2)
    pair, pair_back, pair_front, pair_far = (axes.at(1, n) for n in (0, -1, 1, 2))
    ahead, behind, across = axes.ahead, axes.behind, axes.across

    def rows_of(which, low=0, count=rows, other=False):
        return lambda: block(which, low, count, other)

    def first(index, device):
        line.send(index, lambda: own, rows_of(mine), device)

    def relay(index, device, which, low=0, count=rows):
        line.send(index, rows_of(which, low, count), rows_of(which, low, count), device)

    def share(index, which):
        if twin is not None:
            relay(12 + index, twin, which)

    def keep():
        return pltpu.make_async_copy(own, block(mine, 0, rows), local_sem)

    keep().start()
    if twin is not None:
        first(12, twin)
    first(0, ahead)
    first(1, behind)
    first(2, across)
    keep().wait()
    yield
    line.take(0, rows_of(back), ahead)
    relay(3, ahead, back, 0, half)
    relay(4, across, back, half, half)
    share(1, back)
    line.take(1, rows_of(front), behind)
    relay(5, behind, front, half, half)
    relay(6, across, front, half, half)
    share(2, front)
    line.take(2, rows_of(pair), across)
    relay(7, ahead, pair, 0, half)
    relay(8, behind, pair, 0, half)
    share(3, pair)
    yield
    line.take(3, rows_of(far, 0, half), ahead)
    line.take(5, rows_of(far, half, half), behind)
    relay(9, across, far, half, half)
    share(4, far)
    line.take(7, rows_of(pair_back, 0, half), ahead)
    relay(10, ahead, pair_back, 0, quarter)
    line.take(8, rows_of(pair_front, 0, half), behind)
    relay(11, behind, pair_front, quarter, quarter)
    line.take(4, rows_of(pair_back, half, half), across)
    share(5, pair_back)
    line.take(6, rows_of(pair_front, half, half), across)
    share(6, pair_front)
    yield
    line.take(10, rows_of(pair_far, 0, quarter), ahead)
    line.take(11, rows_of(pair_far, quarter, quarter), behind)
    line.take(9, rows_of(pair_far, half, half), across)
    share(7, pair_far)
    yield
    if twin is not None and not twin_later:
        for index, which in enumerate(gather_order(axes)):
            line.take(12 + index, rows_of(which, other=True), twin)
    line.finish()


SUM_SEMS = 20
TOTAL_SEMS = 16


def total_parts(place, line, own, got, total, target, local_sem):
    rep = place.rep
    steps = range(1, REPS)
    peers = {step: (place.shard, place.others[step]) for step in steps}
    before = {step: place.others[REPS - step] for step in steps}

    def kept():
        return pltpu.make_async_copy(total, target(rep), local_sem)

    for step in steps:
        line.send(step, lambda p=place.others[step]: own(p), lambda: got.at[rep], peers[step])
    yield
    value = own(rep)[...].astype(f32)
    for step in steps:
        line.take(step, lambda b=before[step]: got.at[b], peers[step])
        value = value + got[before[step]].astype(f32)
    total[...] = value.astype(bf16)
    kept().start()
    for step in steps:
        line.send(8 + step, lambda: total, lambda: target(rep), peers[step])
    yield
    for step in steps:
        line.take(8 + step, lambda b=before[step]: target(b), peers[step])
    kept().wait()
    line.finish()


def spread_parts(place, line, own, got, total):
    rep = place.rep
    steps = range(1, REPS)
    for step in steps:
        peer = (place.shard, place.others[step])
        line.send(step, lambda: own, lambda: got.at[rep], peer)
    yield
    value = own[...].astype(f32)
    for step in steps:
        before = place.others[REPS - step]
        line.take(step, lambda: got.at[before], (place.shard, place.others[step]))
        value = value + got[before].astype(f32)
    total[...] = value
    line.finish()


def add_rows(target, source, rows):
    step = 16
    count = rows // step

    def body(index, carry):
        at = pl.ds(pl.multiple_of(index * step, step), step)
        target[at] = target[at] + source[at]
        return carry

    lax.fori_loop(0, count, body, 0)


def stage_rows(rows):
    return 7 * rows


def gather_order(axes):
    return [axes.at(*v) for v in ((0, 0), (0, -1), (0, 1), (1, 0), (0, 2), (1, -1), (1, 1), (1, 2))]


def sum_order(axes):
    return [axes.at(*v) for v in ((1, 2), (0, 2), (1, -1), (1, 1), (0, -1), (0, 1), (1, 0), (0, 0))]


def sum_parts(axes, line, part, stage, rows, result, twin=None, store=None):
    half, quarter = rows // 2, rows // 4
    mine, back, front, far = axes.at(0, 0), axes.at(0, -1), axes.at(0, 1), axes.at(0, 2)
    pair, pair_back, pair_front, pair_far = (axes.at(1, n) for n in (0, -1, 1, 2))
    ahead, behind, across = axes.ahead, axes.behind, axes.across
    order = sum_order(axes)
    offsets, used = {}, 0
    for name, size in (
        ("Y0", half), ("M0", quarter), ("P0", quarter), ("M1", half), ("Y1", half), ("Y2", half),
        ("P1", half), ("M2", half), ("P2", half), ("M3", rows), ("P3", rows), ("Y3", rows),
    ):
        offsets[name] = (used, size, len(offsets))
        used += size

    def landing(name):
        low, size, _ = offsets[name]
        return lambda: stage.at[pl.ds(low, size)]

    def send(name, which, low, device):
        _, size, index = offsets[name]
        line.send(index, lambda: part(which, low, size), landing(name), device)

    def add(name, which, low, device):
        _, size, index = offsets[name]
        line.take(index, landing(name), device)
        add_rows(part(which, low, size), landing(name)(), size)

    def join(*places):
        if twin is not None:
            for place in places:
                line.take(12 + place, lambda: twin[2](order[place]), twin[0])
                add_rows(part(order[place], 0, rows), twin[2](order[place]), rows)

    def hand(*places):
        if twin is not None:
            for place in places:
                which = order[place]
                line.send(
                    12 + place, lambda w=which: twin[1](w), lambda w=which: twin[2](w), twin[0]
                )

    hand(0, 1, 2, 3)
    yield
    join(0)
    send("Y0", pair_far, half, across)
    send("M0", pair_far, 0, behind)
    send("P0", pair_far, quarter, ahead)
    join(1)
    send("M1", far, 0, behind)
    join(2)
    send("Y1", pair_back, half, across)
    join(3)
    send("Y2", pair_front, half, across)
    yield
    hand(4, 5, 6, 7)
    yield
    add("M0", pair_back, 0, behind)
    send("M2", pair_back, 0, behind)
    add("P0", pair_front, quarter, ahead)
    send("P2", pair_front, 0, ahead)
    add("Y0", far, half, across)
    send("P1", far, half, ahead)
    yield
    join(4, 5, 6, 7)
    add("M1", back, 0, behind)
    add("Y1", back, half, across)
    send("M3", back, 0, behind)
    add("M2", pair, 0, behind)
    add("P2", pair, 0, ahead)
    send("Y3", pair, 0, across)
    add("P1", front, half, ahead)
    add("Y2", front, half, across)
    send("P3", front, 0, ahead)
    yield
    for name, device in (("M3", behind), ("P3", ahead), ("Y3", across)):
        line.take(offsets[name][2], landing(name), device)
    step = 16

    def body(index, carry):
        low = pl.multiple_of(index * step, step)
        total = part(mine, low, step)[...].astype(f32)
        for name in ("M3", "P3", "Y3"):
            total = total + stage[pl.ds(offsets[name][0] + low, step)].astype(f32)
        if store is None:
            result[pl.ds(low, step)] = total.astype(result.dtype)
        else:
            store(low, step, total)
        return carry

    lax.fori_loop(0, rows // step, body, 0)
    line.finish()


def sems(count):
    return [pltpu.SemaphoreType.DMA((count,)), pltpu.SemaphoreType.DMA((count,))]


ANY = pl.BlockSpec(memory_space=pl.ANY)
IN_VMEM = pl.BlockSpec(memory_space=pltpu.VMEM)


def params(collective_id):
    return pltpu.CompilerParams(
        collective_id=collective_id, has_side_effects=True, vmem_limit_bytes=VMEM_LIMIT
    )


def dot(a, b):
    return jnp.dot(a, b, preferred_element_type=f32)


def dot_nt(a, b):
    return lax.dot_general(a, b, (((1,), (1,)), ((), ())), preferred_element_type=f32)


def dot_tn(a, b):
    return lax.dot_general(a, b, (((0,), (0,)), ((), ())), preferred_element_type=f32)


def pick(index, values):
    chosen = values[-1]
    for at in range(len(values) - 2, -1, -1):
        chosen = jnp.where(index == at, values[at], chosen)
    return chosen


def moe_call(collective_id, sent, rows_first, grad_all, inner, outer):
    count, columns = sent.shape
    width = inner.shape[0]
    hidden_width = outer.shape[0]
    small = columns - width
    half = count // 2
    chips = GROUP // 2
    wide = 4
    rounds = GROUP // wide

    def kernel(
        sent_ref, first_ref, grad_ref, inner_ref, outer_ref,
        returned, expert_own, out_terms,
        rows_in, grads, hidden, back_gu, back, back_staged, back_stage, out_box,
        term_stage,
        gs, gr, bs0, br0, bs1, br1, ia, ja, ib, jb, ds_, dr, own_sem, load_sem, box_sem,
    ):
        place = Place()
        axes, core, shard = place.tokens, place.core, place.shard
        gather_line = Line(gs, gr)

        def chip_of(which):
            return which[0] * RING + which[1]

        def blocks(which, other=False):
            return chip_of(which) * 2 + ((1 - core) if other else core)

        gather = gather_parts(
            axes, gather_line, sent_ref.at[pl.ds(half, half)],
            lambda which, low, n, other=False: rows_in.at[1, blocks(which, other), pl.ds(low, n)],
            half, own_sem, place.twin, twin_later=True,
        )

        def sum_of(chunk, send_sem, recv_sem):
            return sum_parts(
                axes, Line(send_sem, recv_sem),
                lambda which, low, n: back.at[chunk, blocks(which), pl.ds(low, n)],
                back_stage.at[chunk], half, returned.at[pl.ds(chunk * half, half)],
                (place.twin, lambda which: back.at[chunk, blocks(which, True)],
                 lambda which: back_staged.at[chunk, chip_of(which)]),
            )

        sums = [sum_of(0, bs0, br0), sum_of(1, bs1, br1)]
        piece = hidden_width // REPS

        def inner_part(part):
            def rows(which, low, n):
                at = chip_of(which)
                return out_box.at[part, lax.div(at, 2), pl.ds(lax.rem(at, 2) * piece + low, n)]

            return rows

        def down_part(which, low, n):
            at = chip_of(which)
            return back_gu.at[0, lax.div(at, 2), pl.ds(lax.rem(at, 2) * piece + low, n)]

        inner_sums = [
            sum_parts(
                place.copies, Line(send_sem, recv_sem), inner_part(part), term_stage.at[part], piece,
                expert_own.at[pl.ds(part * piece, piece)],
            )
            for part, (send_sem, recv_sem) in enumerate(((ia, ja), (ib, jb)))
        ]
        down_sum = sum_parts(
            place.copies, Line(ds_, dr), down_part, term_stage.at[2], piece,
            expert_own.at[pl.ds(2 * piece, piece)],
        )

        def loads(t):
            at = pl.ds(t * wide, wide)
            return [
                pltpu.make_async_copy(first_ref.at[at], rows_in.at[0, at], load_sem.at[t, 0]),
                pltpu.make_async_copy(
                    grad_ref.at[at, pl.ds(0, half)], grads.at[0, at], load_sem.at[t, 1]
                ),
            ]

        second_grads = pltpu.make_async_copy(
            grad_ref.at[:, pl.ds(half, half)], grads.at[1], load_sem.at[rounds, 0]
        )

        def box_copy(chunk, first, slot):
            return pltpu.make_async_copy(
                out_box.at[slot],
                out_terms.at[pl.ds(first, wide), pl.ds(chunk * half, half)],
                box_sem.at[slot],
            )

        rows_count = wide * half
        lanes = lane_of((rows_count, small))
        is_high, is_rest = lanes == shard, lanes == shard + GROUP

        def tile(chunk, first, slot, wait_first):
            at = pl.ds(first, wide)
            row_block = rows_in[chunk, at].reshape(rows_count, columns)
            gate = jnp.sum(
                jnp.where(is_high | is_rest, row_block[:, width:].astype(f32), 0.0),
                axis=1, keepdims=True,
            )
            gate_up = dot(row_block[:, :width], inner_ref[...])
            gate_part, up_part = gate_up[:, :hidden_width], gate_up[:, hidden_width:]
            sigmoid = 1.0 / (1.0 + jnp.exp(-gate_part))
            active = gate_part * sigmoid
            product = active * up_part
            hidden_low = product.astype(bf16)
            hidden[chunk, at] = hidden_low.reshape(wide, half, hidden_width)
            out_rows = (gate * dot(hidden_low, outer_ref[...])).astype(bf16)

            @pl.when(wait_first)
            def _():
                box_copy(chunk, first, slot).wait()

            out_box[slot] = out_rows.reshape(wide, half, width)
            box_copy(chunk, first, slot).start()
            grad = grads[chunk, at].reshape(rows_count, width)
            grad_hidden = dot_nt(grad, outer_ref[...])
            grad_gate = jnp.sum(grad_hidden * product, axis=1, keepdims=True)
            grad_hidden = grad_hidden * gate
            grad_gate_up = jnp.concatenate(
                [
                    grad_hidden * up_part * sigmoid * (1.0 + gate_part * (1.0 - sigmoid)),
                    grad_hidden * active,
                ],
                axis=1,
            ).astype(bf16)
            back_gu[chunk, at] = grad_gate_up.reshape(wide, half, 2 * hidden_width)
            grads[chunk, at] = (gate * grad.astype(f32)).astype(bf16).reshape(wide, half, width)
            grad_rows = dot_nt(grad_gate_up, inner_ref[...]).astype(bf16)
            back[chunk, at, :, pl.ds(0, width)] = grad_rows.reshape(wide, half, width)
            high = grad_gate.astype(bf16).astype(f32)
            tail = jnp.where(is_high, high, jnp.where(is_rest, grad_gate - high, 0.0))
            back[chunk, at, :, pl.ds(width, small)] = tail.astype(bf16).reshape(wide, half, small)

        for t in range(rounds):
            for load in loads(t):
                load.start()
        second_grads.start()
        greet(axes.neighbours() + place.copies.neighbours() + [place.twin])
        next(gather)

        def first_tiles(t, carry):
            hooks(t, ((2, lambda: next(gather)),))
            for load in loads(t):
                load.wait()
            tile(0, t * wide, lax.rem(t, 2), t >= 2)
            return carry

        lax.fori_loop(0, rounds, first_tiles, 0)
        next(sums[0])
        next(gather)
        second_grads.wait()
        near, beyond = lax.div(axes.spot, 2), 1 - lax.div(axes.spot, 2)
        chips_per_round = wide // 2
        firsts = [
            (side * RING + part * chips_per_round) * 2
            for side, part in (
                (axes.side, beyond), (1 - axes.side, near), (1 - axes.side, beyond), (axes.side, near),
            )
        ]
        arrivals = gather_order(axes)

        def arrived(*numbers):
            for number in numbers:
                gather_line.take(
                    12 + number, lambda: rows_in.at[1, blocks(arrivals[number], True)], place.twin
                )

        def second_tiles(t, carry):
            hooks(
                t,
                (
                    (0, lambda: arrived(0, 1, 2, 4)),
                    (1, lambda: (next(sums[0]), next(sums[0]), arrived(3, 5, 6))[2]),
                    (2, lambda: (next(gather), arrived(7))[1]),
                    (3, lambda: (next(sums[1]), next(sums[0]))[0]),
                ),
            )
            tile(1, pick(t, firsts), lax.rem(t, 2), t >= 0)
            return carry

        lax.fori_loop(0, rounds, second_tiles, 0)
        next(sums[1])
        next(sums[1])

        every = 2 * GROUP * half
        for slot in range(2):
            box_copy(1, 0, slot).wait()

        def begin(part):
            for _ in range(3):
                next(part)

        def inner_terms(index, carry):
            hooks(
                index,
                (
                    (2, lambda: (begin(inner_sums[0]), next(sums[0]))[0]),
                    (3, lambda: next(sums[1])),
                ),
            )
            at = chunk_256(index)
            value = dot_tn(
                rows_in[:, :, :, at].reshape(every, 256),
                back_gu[...].reshape(every, 2 * hidden_width),
            )
            out_box[lax.div(index, 2), pl.ds(2 * lax.rem(index, 2), 2)] = value.astype(bf16).reshape(
                2, half, width
            )
            return carry

        lax.fori_loop(0, width // 256, inner_terms, 0)
        begin(inner_sums[1])

        def down_terms(index, carry):
            hooks(index, ((1, lambda: next(inner_sums[0])),))
            at = chunk_256(index)
            value = dot_tn(hidden[:, :, :, at].reshape(every, 256), grads[...].reshape(every, width))
            back_gu[0, pl.ds(2 * index, 2)] = value.astype(bf16).reshape(2, half, width)
            return carry

        lax.fori_loop(0, hidden_width // 256, down_terms, 0)
        begin(down_sum)
        drained(sums[0])
        next(inner_sums[1])
        next(inner_sums[0])
        next(sums[1])
        next(down_sum)
        next(inner_sums[1])
        drained(inner_sums[0])
        next(down_sum)
        drained(sums[1])
        drained(inner_sums[1])
        drained(down_sum)
        drained(gather)

    own_rows = (width + hidden_width) // REPS
    return pl.pallas_call(
        kernel,
        out_shape=[
            jax.ShapeDtypeStruct((count, columns), bf16),
            jax.ShapeDtypeStruct((own_rows, width), bf16),
            jax.ShapeDtypeStruct((GROUP, count, width), bf16),
        ],
        in_specs=[ANY, ANY, ANY, IN_VMEM, IN_VMEM],
        out_specs=[IN_VMEM, IN_VMEM, ANY],
        scratch_shapes=[
            pltpu.VMEM((2, GROUP, half, columns), bf16),
            pltpu.VMEM((2, GROUP, half, width), bf16),
            pltpu.VMEM((2, GROUP, half, hidden_width), bf16),
            pltpu.VMEM((2, GROUP, half, 2 * hidden_width), bf16),
            pltpu.VMEM((2, GROUP, half, columns), bf16),
            pltpu.VMEM((2, chips, half, columns), bf16),
            pltpu.VMEM((2, stage_rows(half), columns), bf16),
            pltpu.VMEM((2, wide, half, width), bf16),
            pltpu.VMEM((3, stage_rows(hidden_width // REPS), width), bf16),
        ]
        + sems(GATHER_SEMS)
        + sems(SUM_SEMS) * 5
        + [
            pltpu.SemaphoreType.DMA,
            pltpu.SemaphoreType.DMA((rounds + 1, 2)),
            pltpu.SemaphoreType.DMA((2,)),
        ],
        compiler_params=params(collective_id),
    )(sent, rows_first, grad_all, inner, outer)


WIDTH = 1024
QUERY = HEADS * HEAD_DIM
KEY = KV_HEADS * HEAD_DIM
EXPERTS = 16
SMALL = 128
LANES = 128
AT_K = QUERY
AT_V = AT_K + KEY
AT_S = AT_V + KEY
AT_O = AT_S + SMALL
PACKED = AT_O + WIDTH
ROWS_OWN = WIDTH // GROUP
KGAIN_OWN = KEY // GROUP
HEAD_PAIRS = KV_HEADS // 2
REST = 2 * KEY + SMALL
DENSE = QUERY + WIDTH + 2 * KEY


def drained(part):
    for _ in part:
        pass


def hooks(index, steps):
    for at, step in steps:
        pl.when(index == at)(step)


def chunk_256(index):
    return pl.ds(pl.multiple_of(index * 256, 256), 256)


def root_mean(values):
    return lax.rsqrt(jnp.mean(values * values, axis=1, keepdims=True) + norm_eps)


def lane_of(shape):
    return lax.broadcasted_iota(jnp.int32, shape, 1)


def turned(values, cosine, sine):
    first = (lane_of(values.shape) & (HEAD_DIM - 1)) < HEAD_DIM // 2
    swapped = jnp.where(
        first, pltpu.roll(values, LANES - HEAD_DIM // 2, 1), pltpu.roll(values, HEAD_DIM // 2, 1)
    )
    return values * cosine + swapped * sine


def gain_rows(small):
    rows = jnp.transpose(small.astype(f32))
    short = small.reshape(GROUP, ROWS_OWN, SMALL)[:, :KGAIN_OWN].reshape(KEY, SMALL)
    gain_k = jnp.transpose(short.astype(f32))[EXPERTS + 3 : EXPERTS + 4]
    return rows[EXPERTS : EXPERTS + 1], rows[EXPERTS + 1 : EXPERTS + 2], rows[EXPERTS + 2 : EXPERTS + 3], gain_k


def long_column(columns):
    cut = columns.reshape(GROUP, KGAIN_OWN, SMALL)
    return jnp.concatenate([cut, jnp.zeros_like(cut)], axis=1).reshape(WIDTH, SMALL)


def four_heads(chunk_a, chunk_b):
    low = lane_of(chunk_a.shape) < HEAD_DIM
    zero = jnp.zeros_like(chunk_a)
    return jnp.concatenate(
        [
            jnp.where(low, chunk_a, zero),
            jnp.where(low, pltpu.roll(chunk_a, HEAD_DIM, 1), zero),
            jnp.where(low, zero, pltpu.roll(chunk_b, HEAD_DIM, 1)),
            jnp.where(low, zero, chunk_b),
        ],
        axis=0,
    )


def two_chunks(blocks):
    rows = blocks.shape[0] // 4
    one, two, three, four = (blocks[n * rows : (n + 1) * rows] for n in range(4))
    low = lane_of(one.shape) < HEAD_DIM
    return (
        jnp.where(low, one, pltpu.roll(two, HEAD_DIM, 1)),
        jnp.where(low, pltpu.roll(three, HEAD_DIM, 1), four),
    )


def chunk_at(index, base=0):
    return pl.ds(pl.multiple_of(base + index * LANES, LANES), LANES)


def front_call(collective_id, tokens, cotangent, weights_own, gains, router, cosine, sine, routes, starts):
    count, width = tokens.shape
    seqs = starts.shape[0]
    positions = count // seqs
    length = REPS * positions
    score_scale = HEAD_DIM ** (-0.5)
    sent_width = width + SMALL

    def kernel(
        starts_ref, tokens_ref, grad_ref, query_w, key_w, value_w, output_w,
        gain_a_ref, gain_q_ref, gain_f_ref, gain_k_ref, router_ref, cos_ref, sin_ref, routes_ref,
        dense_out, grad_all, pairs_out, soft_out, rows_first,
        attn_in, query_raw, key_raw, query_low, mixed, middle, sent, gates_out,
        packed, small_box, dense, pairs, pair_own, soft_box, bias_box,
        ws0, wr0, ws1, wr1, ws2, wr2, gs0, gr0, gs1, gr1, ks0, kr0, ks1, kr1, rs, rr, own_sem, out_sem, soft_sem, pack_sem,
    ):
        place = Place()
        core = place.core
        packing = [
            pltpu.make_async_copy(
                source, packed.at[:, pl.ds(low, source.shape[1])], pack_sem.at[index]
            )
            for index, (source, low) in enumerate(
                ((key_w, AT_K), (value_w, AT_V), (query_w, 0), (output_w, AT_O))
            )
        ]
        for copy in packing:
            copy.start()
        small_box[...] = jnp.zeros_like(small_box)
        small_box[pl.ds(0, EXPERTS), pl.ds(0, ROWS_OWN)] = router_ref[...].astype(f32)
        for at, ref in enumerate((gain_a_ref, gain_q_ref, gain_f_ref, gain_k_ref)):
            size = ref.shape[0]
            small_box[pl.ds(EXPERTS + at, 1), pl.ds(0, size)] = (
                ref[...].astype(f32).reshape(1, size)
            )
        packed[:, pl.ds(AT_S, SMALL)] = jnp.transpose(small_box[...])[:ROWS_OWN].astype(bf16)

        def token_block(index, low, size):
            def block(which, row, n, other=False):
                at = (which[0] * RING + which[1]) * 2 + ((1 - core) if other else core)
                return dense.at[at, pl.ds(row, n), pl.ds(low, size)]

            return block

        def weight_gather(index, low, size, send_sem, recv_sem):
            return gather_parts(
                place.tokens, Line(send_sem, recv_sem), packed.at[:, pl.ds(low, size)],
                token_block(index, low, size), ROWS_OWN, own_sem.at[index], place.twin,
            )

        def rows_of(target):
            def block(which, row, n, other=False):
                at = (which[0] * RING + which[1]) * 2 + ((1 - core) if other else core)
                return target.at[at, pl.ds(row, n)]

            return block

        def pair_gather(seq, send_sem, recv_sem):
            def block(which, row, n, other=False):
                return pairs.at[seq, which[0] * RING + which[1], pl.ds(row, n)]

            return gather_parts(
                place.copies, Line(send_sem, recv_sem),
                pair_own.at[pl.ds(seq * positions, positions)], block, positions, own_sem.at[3 + seq],
            )

        def soft_copy(seq, index, slot):
            return pltpu.make_async_copy(
                soft_box.at[slot], soft_out.at[seq, index], soft_sem.at[slot]
            )

        rest_gather = weight_gather(0, AT_K, REST, ws0, wr0)
        query_gather = weight_gather(1, 0, QUERY, ws1, wr1)
        output_gather = weight_gather(2, AT_O, WIDTH, ws2, wr2)
        def grad_gather(seq, send_sem, recv_sem):
            base = seq * positions

            def block(which, row, n, other=False):
                at = (which[0] * RING + which[1]) * 2 + ((1 - core) if other else core)
                return grad_all.at[at, pl.ds(base + row, n)]

            return gather_parts(
                place.tokens, Line(send_sem, recv_sem), grad_ref.at[pl.ds(base, positions)], block,
                positions, own_sem.at[5 + seq], place.twin,
            )

        grads = [grad_gather(0, gs0, gr0), grad_gather(1, gs1, gr1)]
        first_rows = gather_parts(
            place.tokens, Line(rs, rr), sent.at[pl.ds(0, positions)], rows_of(rows_first), positions,
            own_sem.at[7], place.twin,
        )
        pair_gathers = [pair_gather(0, ks0, kr0), pair_gather(1, ks1, kr1)]

        greet(place.tokens.neighbours() + place.copies.neighbours() + [place.twin])
        for copy in packing:
            copy.wait()
        next(rest_gather)
        inputs = tokens_ref[...].astype(f32)
        middle[...] = inputs * root_mean(inputs)
        next(rest_gather)
        next(query_gather)
        query_at = place.rep * positions + lax.broadcasted_iota(jnp.int32, (positions, 1), 0)
        key_at = lax.broadcasted_iota(jnp.int32, (1, length), 1)
        for seq in range(seqs):
            allowed = key_at <= query_at
            for piece in range(starts_ref.shape[1]):
                start = starts_ref[seq, piece]
                query_inside = (query_at >= start) & (query_at < start + PIC)
                key_inside = (key_at >= start) & (key_at < start + PIC)
                allowed = allowed | (query_inside & key_inside)
            bias_box[seq] = jnp.where(allowed, 0.0, masked_score)
        next(rest_gather)
        next(query_gather)
        next(output_gather)
        drained(rest_gather)
        next(query_gather)
        next(output_gather)

        def weights(low, size):
            return dense[:, :, pl.ds(low, size)].reshape(width, size)

        small = weights(AT_S, SMALL)
        gain_a, gain_q, gain_f, gain_k = gain_rows(small)
        rows = (middle[...] * gain_a).astype(bf16)
        attn_in[...] = rows
        cos2 = jnp.concatenate([cos_ref[...]] * seqs, axis=0)
        sin2 = jnp.concatenate([sin_ref[...]] * seqs, axis=0)
        raw = dot(rows, weights(AT_K, KEY))
        key_raw[...] = raw
        scaled = raw * root_mean(raw) * gain_k
        for chunk in range(KEY // LANES):
            at = slice(chunk * LANES, (chunk + 1) * LANES)
            pair_own[:, at] = turned(scaled[:, at], cos2, sin2).astype(bf16)
        pair_own[:, KEY:] = dot(rows, weights(AT_V, KEY)).astype(bf16)
        next(pair_gathers[0])
        drained(query_gather)
        next(output_gather)
        next(grads[0])
        raw = dot(rows, weights(0, QUERY))
        query_raw[...] = raw
        scaled = raw * root_mean(raw) * gain_q
        for chunk in range(QUERY // LANES):
            at = slice(chunk * LANES, (chunk + 1) * LANES)
            query_low[:, at] = turned(scaled[:, at], cos2, sin2).astype(bf16)
        next(pair_gathers[0])
        next(pair_gathers[1])
        drained(output_gather)
        dense_copy = pltpu.make_async_copy(dense, dense_out, out_sem.at[0])
        dense_copy.start()
        next(grads[0])
        next(grads[1])
        next(pair_gathers[0])
        next(pair_gathers[1])
        next(grads[0])
        drained(pair_gathers[0])
        next(grads[1])

        def attend(seq, index, slot, wait_first):
            rows_at = pl.ds(seq * positions, positions)
            queries = four_heads(
                query_low[rows_at, chunk_at(2 * index)].astype(f32),
                query_low[rows_at, chunk_at(2 * index + 1)].astype(f32),
            )
            queries = (queries * score_scale).astype(bf16)
            keys = pairs[seq, :, :, chunk_at(index)].reshape(length, LANES)
            scores = dot_nt(queries, keys).reshape(4, positions, length) + bias_box[seq][None]
            scores = scores.reshape(4 * positions, length)
            raised = jnp.exp(scores - jnp.max(scores, axis=1, keepdims=True))
            soft = (raised * (1.0 / jnp.sum(raised, axis=1, keepdims=True))).astype(bf16)

            @pl.when(wait_first)
            def _():
                soft_copy(seq, index, slot).wait()

            soft_box[slot] = soft
            soft_copy(seq, index, slot).start()
            values = pairs[seq, :, :, chunk_at(index, KEY)].reshape(length, LANES)
            chunk_a, chunk_b = two_chunks(dot(soft, values))
            mixed[rows_at, chunk_at(2 * index)] = chunk_a.astype(bf16)
            mixed[rows_at, chunk_at(2 * index + 1)] = chunk_b.astype(bf16)

        def features(seq):
            at = pl.ds(seq * positions, positions)
            total = tokens_ref[at].astype(f32) + dot(mixed[at], weights(AT_O, WIDTH))
            middle[at] = total
            ffn_in = (total * root_mean(total) * gain_f).astype(bf16)
            sent[at, pl.ds(0, width)] = ffn_in
            lanes = lane_of((positions, SMALL))
            named = jnp.transpose(routes_ref[seq].astype(f32)).astype(jnp.int32)
            chosen = lanes == named[:, :1]
            for choice in range(1, named.shape[1]):
                chosen = chosen | (lanes == named[:, choice : choice + 1])
            logits = jnp.where(chosen, dot(ffn_in, small), masked_score)
            raised = jnp.exp(logits - jnp.max(logits, axis=1, keepdims=True))
            gates = raised * (1.0 / jnp.sum(raised, axis=1, keepdims=True))
            gates = jnp.where(chosen, gates, 0.0)
            gates_out[at] = gates
            high = gates.astype(bf16).astype(f32)
            tail = high + pltpu.roll(gates - high, EXPERTS, 1)
            sent[at, pl.ds(width, SMALL)] = tail.astype(bf16)

        def first_heads(index, carry):
            hooks(
                index,
                (
                    (1, lambda: next(grads[0])),
                    (2, lambda: next(pair_gathers[1])),
                    (3, lambda: next(grads[1])),
                ),
            )
            attend(0, index, lax.rem(index, 2), index >= 2)
            return carry

        lax.fori_loop(0, HEAD_PAIRS, first_heads, 0)
        features(0)
        next(first_rows)
        drained(pair_gathers[1])
        pairs_copy = pltpu.make_async_copy(pairs, pairs_out, out_sem.at[1])
        pairs_copy.start()

        def second_heads(index, carry):
            hooks(
                index,
                (
                    (1, lambda: next(grads[1])),
                    (3, lambda: next(first_rows)),
                ),
            )
            attend(1, index, lax.rem(index, 2), index >= 0)
            return carry

        lax.fori_loop(0, HEAD_PAIRS, second_heads, 0)
        features(1)
        next(first_rows)
        drained(grads[0])
        drained(grads[1])
        drained(first_rows)
        dense_copy.wait()
        pairs_copy.wait()
        for slot in range(2):
            soft_copy(1, 0, slot).wait()

    return pl.pallas_call(
        kernel,
        out_shape=[
            jax.ShapeDtypeStruct((GROUP, ROWS_OWN, PACKED), bf16),
            jax.ShapeDtypeStruct((GROUP, count, width), bf16),
            jax.ShapeDtypeStruct((seqs, REPS, positions, 2 * KEY), bf16),
            jax.ShapeDtypeStruct((seqs, HEAD_PAIRS, 4 * positions, length), bf16),
            jax.ShapeDtypeStruct((GROUP, positions, sent_width), bf16),
            jax.ShapeDtypeStruct((count, width), bf16),
            jax.ShapeDtypeStruct((count, QUERY), f32),
            jax.ShapeDtypeStruct((count, KEY), f32),
            jax.ShapeDtypeStruct((count, QUERY), bf16),
            jax.ShapeDtypeStruct((count, QUERY), bf16),
            jax.ShapeDtypeStruct((count, width), f32),
            jax.ShapeDtypeStruct((count, width + SMALL), bf16),
            jax.ShapeDtypeStruct((count, SMALL), f32),
        ],
        in_specs=[pl.BlockSpec(memory_space=pltpu.SMEM), IN_VMEM] + [ANY] * 5 + [IN_VMEM] * 8,
        out_specs=[ANY] * 5 + [IN_VMEM] * 8,
        scratch_shapes=[
            pltpu.VMEM((ROWS_OWN, PACKED), bf16),
            pltpu.VMEM((SMALL, LANES), f32),
            pltpu.VMEM((GROUP, ROWS_OWN, PACKED), bf16),
            pltpu.VMEM((seqs, REPS, positions, 2 * KEY), bf16),
            pltpu.VMEM((count, 2 * KEY), bf16),
            pltpu.VMEM((2, 4 * positions, length), bf16),
            pltpu.VMEM((seqs, positions, length), f32),
        ]
        + sems(GATHER_SEMS) * 8
        + [
            pltpu.SemaphoreType.DMA((8,)),
            pltpu.SemaphoreType.DMA((2,)),
            pltpu.SemaphoreType.DMA((2,)),
            pltpu.SemaphoreType.DMA((4,)),
        ],
        compiler_params=params(collective_id),
    )(starts, tokens, cotangent, *weights_own, *gains, router, cosine, sine, routes)


def key_chunk(index, base=0):
    low = lax.div(index, 2) * KEY + lax.rem(index, 2) * LANES + base
    return pl.ds(pl.multiple_of(low, LANES), LANES)


def norm_back(values, gain, grad):
    scale = root_mean(values)
    weighted = grad * gain
    mean = jnp.mean(values * weighted, axis=1, keepdims=True)
    inner = weighted * scale - values * (scale * scale * scale * mean)
    return inner, jnp.sum(grad * values * scale, axis=0, keepdims=True)


def back_call(
    collective_id, returned, gates, middle, sent, dense, cotangent, tokens, attn_in, query_raw, key_raw,
    query_low, mixed, pairs, soft, out_terms, expert_own, cosine, sine,
):
    count, width = tokens.shape
    seqs, _, positions, _ = pairs.shape
    length = REPS * positions
    expert_rows = expert_own.shape[0]
    score_scale = HEAD_DIM ** (-0.5)
    chips = GROUP // 2

    def kernel(
        returned_ref, gates_ref, middle_ref, sent_ref, dense_ref, grad_ref, tokens_ref, attn_ref,
        query_raw_ref, key_raw_ref, query_ref, mixed_ref, pairs_ref, soft_ref, out_ref, expert_ref,
        cos_ref, sin_ref,
        block_out, tokens_grad, small_out, dense_out, expert_all,
        weight_box, weight_rest, wide_terms, rest_terms, dense_own,
        wide_staged, rest_staged, wide_stage, rest_stage,
        out_held, out_staged, out_stage, small_terms, small_staged, small_stage, small_own,
        soft_box, key_box, value_box, pair_terms, pair_stage, pair_grads,
        grad_mixed, grad_query, grad_middle, grad_attn, grad_attn_in, gain_box,
        wide_got, rest_got, small_got, wide_total_box, rest_total_box,
        out_s, out_r, small_s, small_r, kv0_s, kv0_r, kva_s, kva_r, kvb_s, kvb_r, wide_s, wide_r, rest_s, rest_r,
        ge_s, ge_r, gwide_s, gwide_r, grest_s, grest_r, gsmall_s, gsmall_r,
        load_sem, held_sem, box_sem, own_sem, total_sem,
    ):
        place = Place()
        core = place.core
        token_axes, copy_axes = place.tokens, place.copies

        def chip_of(which):
            return which[0] * RING + which[1]

        def blocks(which, other=False):
            return chip_of(which) * 2 + ((1 - core) if other else core)

        def out_store(low, step, value):
            at = pl.ds(low, step)
            block_out[at] = (middle_ref[at] + value).astype(bf16)

        out_sum = sum_parts(
            token_axes, Line(out_s, out_r),
            lambda which, low, n: out_held.at[chip_of(which), pl.ds(low, n)],
            out_stage, count, None,
            (place.twin, lambda which: out_ref.at[blocks(which, True)],
             lambda which: out_staged.at[chip_of(which)]),
            store=out_store,
        )
        def pair_sum(seq, low, size, index, send_sem, recv_sem):
            columns = pl.ds(low, size)
            return sum_parts(
                copy_axes, Line(send_sem, recv_sem),
                lambda which, row, n: pair_terms.at[seq, chip_of(which), pl.ds(row, n), columns],
                pair_stage.at[index, :, columns], positions,
                pair_grads.at[pl.ds(seq * positions, positions), columns],
            )

        first_pairs = pair_sum(0, 0, 2 * KEY, 0, kv0_s, kv0_r)
        second_pairs = [
            pair_sum(1, 0, KEY, 1, kva_s, kva_r), pair_sum(1, KEY, KEY, 1, kvb_s, kvb_r)
        ]

        def rows_of_block(terms, index, low, n):
            return terms.at[pl.ds(index * ROWS_OWN + low, n)]

        def dense_sum(terms, staged, stage, own, send_sem, recv_sem):
            return sum_parts(
                token_axes, Line(send_sem, recv_sem),
                lambda which, row, n: rows_of_block(terms, blocks(which), row, n),
                stage, ROWS_OWN, own,
                (place.twin, lambda which: rows_of_block(terms, blocks(which, True), 0, ROWS_OWN),
                 lambda which: staged.at[chip_of(which)]),
            )

        wide_sum = dense_sum(
            wide_terms, wide_staged, wide_stage, dense_own.at[:, pl.ds(0, QUERY + width)], wide_s, wide_r
        )
        rest_sum = dense_sum(
            rest_terms, rest_staged, rest_stage, dense_own.at[:, pl.ds(QUERY + width, 2 * KEY)],
            rest_s, rest_r,
        )
        small_sum = dense_sum(small_terms, small_staged, small_stage, small_own, small_s, small_r)

        def dense_total(index, low, size, got, total, send_sem, recv_sem):
            share = size // REPS

            def columns(rep):
                return pl.ds(pl.multiple_of(low + rep * share, LANES), share)

            return total_parts(
                place, Line(send_sem, recv_sem), lambda rep: dense_own.at[:, columns(rep)], got, total,
                lambda rep: dense_out.at[:, columns(rep)], total_sem.at[index],
            )

        wide_total = dense_total(0, 0, QUERY + width, wide_got, wide_total_box, gwide_s, gwide_r)
        rest_total = dense_total(
            1, QUERY + width, 2 * KEY, rest_got, rest_total_box, grest_s, grest_r
        )
        small_total = spread_parts(place, Line(gsmall_s, gsmall_r), small_own, small_got, small_out)
        expert_gather = gather_parts(
            copy_axes, Line(ge_s, ge_r), expert_ref,
            lambda which, row, n, other=False: expert_all.at[chip_of(which), pl.ds(row, n)],
            expert_rows, own_sem,
        )

        def weight_load(low, index):
            return pltpu.make_async_copy(
                dense_ref.at[:, :, pl.ds(low, width)], weight_box, load_sem.at[index]
            )

        rest_load = pltpu.make_async_copy(
            dense_ref.at[:, :, pl.ds(AT_K, REST)], weight_rest, load_sem.at[1]
        )
        held_loads = [
            pltpu.make_async_copy(
                out_ref.at[2 * chip + core], out_held.at[chip], held_sem.at[chip]
            )
            for chip in range(chips)
        ]

        def box_loads(number, slot):
            seq, index = lax.div(number, HEAD_PAIRS), lax.rem(number, HEAD_PAIRS)
            return [
                pltpu.make_async_copy(
                    soft_ref.at[seq, index], soft_box.at[slot], box_sem.at[slot, 0]
                ),
                pltpu.make_async_copy(
                    pairs_ref.at[seq, :, :, chunk_at(index)], key_box.at[slot], box_sem.at[slot, 1]
                ),
                pltpu.make_async_copy(
                    pairs_ref.at[seq, :, :, chunk_at(index, KEY)],
                    value_box.at[slot],
                    box_sem.at[slot, 2],
                ),
            ]

        rest_load.start()
        weight_load(AT_O, 0).start()
        for load in held_loads + box_loads(0, 0):
            load.start()
        greet(
            token_axes.neighbours()
            + [place.twin]
            + [(place.shard, other) for other in place.others[1:]]
        )
        next(out_sum)
        rest_load.wait()

        small = weight_rest[:, :, pl.ds(2 * KEY, SMALL)].reshape(width, SMALL)
        gain_a, gain_q, gain_f, gain_k = gain_rows(small)
        gates = gates_ref[...]
        tail = returned_ref[:, pl.ds(width, SMALL)].astype(f32)
        grad_gates = tail + pltpu.roll(tail, SMALL - EXPERTS, 1)
        grad_logits = gates * (grad_gates - jnp.sum(gates * grad_gates, axis=1, keepdims=True))
        grad_logits = grad_logits.astype(bf16)
        grad_ffn = returned_ref[:, pl.ds(0, width)].astype(f32) + dot_nt(grad_logits, small)
        inner, gain_f_terms = norm_back(middle_ref[...], gain_f, grad_ffn)
        inner = grad_ref[...].astype(f32) + inner
        grad_middle[...] = inner
        grad_attn[...] = inner.astype(bf16)
        gain_box[...] = jnp.zeros_like(gain_box)
        gain_box[pl.ds(EXPERTS + 2, 1)] = gain_f_terms
        weight_load(AT_O, 0).wait()
        grad_mixed[...] = dot_nt(
            grad_attn[...], weight_box[...].reshape(QUERY, width)
        ).astype(bf16)
        weight_load(0, 3).start()

        def attend_back(seq, index):
            number = seq * HEAD_PAIRS + index
            slot = lax.rem(number, 2)
            for load in box_loads(number, slot):
                load.wait()

            @pl.when(number + 1 < seqs * HEAD_PAIRS)
            def _():
                for load in box_loads(number + 1, 1 - slot):
                    load.start()

            rows_at = pl.ds(seq * positions, positions)
            first, second = chunk_at(2 * index), chunk_at(2 * index + 1)
            queries = four_heads(
                query_ref[rows_at, first].astype(f32), query_ref[rows_at, second].astype(f32)
            )
            queries = (queries * score_scale).astype(bf16)
            grads = four_heads(
                grad_mixed[rows_at, first].astype(f32), grad_mixed[rows_at, second].astype(f32)
            ).astype(bf16)
            keys = key_box[slot].reshape(length, LANES)
            values = value_box[slot].reshape(length, LANES)
            soft_low = soft_box[slot]
            value_terms = dot_tn(soft_low, grads)
            pair_terms[seq, :, :, key_chunk(index, KEY // 2)] = value_terms.astype(bf16).reshape(
                REPS, positions, LANES
            )
            soft_full = soft_low.astype(f32)
            grad_soft = dot_nt(grads, values)
            weighted = soft_full * grad_soft
            grad_scores = (
                weighted - soft_full * jnp.sum(weighted, axis=1, keepdims=True)
            ).astype(bf16)
            key_terms = dot_tn(grad_scores, queries)
            pair_terms[seq, :, :, key_chunk(index)] = key_terms.astype(bf16).reshape(
                REPS, positions, LANES
            )
            chunk_a, chunk_b = two_chunks(dot(grad_scores, keys) * score_scale)
            grad_query[rows_at, first] = chunk_a.astype(bf16)
            grad_query[rows_at, second] = chunk_b.astype(bf16)

        def out_ready():
            for load in held_loads:
                load.wait()
            next(out_sum)
            next(out_sum)

        def begin(part):
            for _ in range(3):
                next(part)

        def first_heads(index, carry):
            hooks(index, ((2, out_ready),))
            attend_back(0, index)
            return carry

        lax.fori_loop(0, HEAD_PAIRS, first_heads, 0)
        begin(first_pairs)

        def second_heads(index, carry):
            hooks(
                index,
                (
                    (1, lambda: next(out_sum)),
                    (2, lambda: begin(second_pairs[0])),
                    (3, lambda: next(first_pairs)),
                ),
            )
            attend_back(1, index)
            return carry

        lax.fori_loop(0, HEAD_PAIRS, second_heads, 0)
        begin(second_pairs[1])
        next(second_pairs[0])
        router_terms = dot_tn(sent_ref[:, pl.ds(0, width)], grad_logits)

        cos2 = jnp.concatenate([cos_ref[...]] * seqs, axis=0)
        sin2 = -jnp.concatenate([sin_ref[...]] * seqs, axis=0)

        def turned_back(values):
            return jnp.concatenate(
                [
                    turned(values[:, low : low + LANES], cos2, sin2)
                    for low in range(0, values.shape[1], LANES)
                ],
                axis=1,
            )

        grad, gain_q_terms = norm_back(
            query_raw_ref[...], gain_q, turned_back(grad_query[...].astype(f32))
        )
        gain_box[pl.ds(EXPERTS + 1, 1)] = gain_q_terms
        grad_query_low = grad.astype(bf16)
        weight_load(0, 3).wait()
        grad_attn_in[...] = dot_nt(grad_query_low, weight_box[...].reshape(width, QUERY))

        next(second_pairs[1])
        next(first_pairs)
        next(second_pairs[0])

        def q_rows(index, carry):
            at = chunk_256(index)
            wide_terms[at, pl.ds(0, QUERY)] = dot_tn(attn_ref[:, at], grad_query_low).astype(bf16)
            wide_terms[at, pl.ds(QUERY, width)] = dot_tn(mixed_ref[:, at], grad_attn[...]).astype(bf16)
            return carry

        lax.fori_loop(0, width // 256, q_rows, 0)
        next(wide_sum)
        next(second_pairs[1])
        next(out_sum)
        next(wide_sum)
        next(wide_sum)
        drained(first_pairs)
        drained(second_pairs[0])
        drained(second_pairs[1])
        next(expert_gather)

        grads = pair_grads[...]
        half = KEY // 2
        key_grads = jnp.concatenate([grads[:, :half], grads[:, KEY : KEY + half]], axis=1)
        value_grads = jnp.concatenate([grads[:, half:KEY], grads[:, KEY + half :]], axis=1)
        grad, gain_k_terms = norm_back(
            key_raw_ref[...], gain_k, turned_back(key_grads.astype(bf16).astype(f32))
        )
        grad_pairs = jnp.concatenate([grad.astype(bf16), value_grads.astype(bf16)], axis=1)

        def rest_rows(index, carry):
            at = chunk_256(index)
            rest_terms[at] = dot_tn(attn_ref[:, at], grad_pairs).astype(bf16)
            return carry

        lax.fori_loop(0, width // 256, rest_rows, 0)
        next(rest_sum)
        grad = grad_attn_in[...] + dot_nt(
            grad_pairs, weight_rest[:, :, pl.ds(0, 2 * KEY)].reshape(width, 2 * KEY)
        )
        next(rest_sum)
        next(rest_sum)
        values = tokens_ref[...].astype(f32)
        inner, gain_a_terms = norm_back(values, gain_a, grad)
        gain_box[pl.ds(EXPERTS, 1)] = gain_a_terms
        lanes = lane_of((KEY, SMALL))
        gain_k_column = jnp.where(
            lanes == EXPERTS + 3,
            jnp.transpose(jnp.broadcast_to(gain_k_terms, (SMALL, KEY))),
            0.0,
        )
        small_terms[...] = (
            router_terms + jnp.transpose(gain_box[...]) + long_column(gain_k_column)
        ).astype(bf16)
        next(small_sum)
        tokens_grad[...] = (grad_middle[...] + inner).astype(bf16)
        next(small_sum)
        next(small_sum)
        next(wide_sum)
        next(rest_sum)
        next(expert_gather)
        next(small_sum)
        next(wide_sum)
        next(small_sum)
        next(rest_sum)
        drained(out_sum)
        drained(wide_sum)
        next(wide_total)
        drained(small_sum)
        next(small_total)
        next(expert_gather)
        drained(rest_sum)
        next(rest_total)
        next(wide_total)
        next(expert_gather)
        drained(small_total)
        next(rest_total)
        drained(expert_gather)
        drained(wide_total)
        drained(rest_total)

    block = pltpu.VMEM((GROUP, ROWS_OWN, width), bf16)
    scratch = [
        block,
        pltpu.VMEM((GROUP, ROWS_OWN, REST), bf16),
        pltpu.VMEM((width, QUERY + width), bf16),
        pltpu.VMEM((width, 2 * KEY), bf16),
        pltpu.VMEM((ROWS_OWN, DENSE), bf16),
        pltpu.VMEM((chips, ROWS_OWN, QUERY + width), bf16),
        pltpu.VMEM((chips, ROWS_OWN, 2 * KEY), bf16),
        pltpu.VMEM((stage_rows(ROWS_OWN), QUERY + width), bf16),
        pltpu.VMEM((stage_rows(ROWS_OWN), 2 * KEY), bf16),
        pltpu.VMEM((chips, count, width), bf16),
        pltpu.VMEM((chips, count, width), bf16),
        pltpu.VMEM((stage_rows(count), width), bf16),
        pltpu.VMEM((width, SMALL), bf16),
        pltpu.VMEM((chips, ROWS_OWN, SMALL), bf16),
        pltpu.VMEM((stage_rows(ROWS_OWN), SMALL), bf16),
        pltpu.VMEM((ROWS_OWN, SMALL), bf16),
        pltpu.VMEM((2, 4 * positions, length), bf16),
        pltpu.VMEM((2, REPS, positions, LANES), bf16),
        pltpu.VMEM((2, REPS, positions, LANES), bf16),
        pltpu.VMEM((seqs, REPS, positions, 2 * KEY), bf16),
        pltpu.VMEM((seqs, stage_rows(positions), 2 * KEY), bf16),
        pltpu.VMEM((count, 2 * KEY), f32),
        pltpu.VMEM((count, QUERY), bf16),
        pltpu.VMEM((count, QUERY), bf16),
        pltpu.VMEM((count, width), f32),
        pltpu.VMEM((count, width), bf16),
        pltpu.VMEM((count, width), f32),
        pltpu.VMEM((SMALL, width), f32),
    ]
    wide_share, rest_share = (QUERY + width) // REPS, 2 * KEY // REPS
    scratch += [
        pltpu.VMEM((REPS, ROWS_OWN, wide_share), bf16),
        pltpu.VMEM((REPS, ROWS_OWN, rest_share), bf16),
        pltpu.VMEM((REPS, ROWS_OWN, SMALL), bf16),
        pltpu.VMEM((ROWS_OWN, wide_share), bf16),
        pltpu.VMEM((ROWS_OWN, rest_share), bf16),
    ]
    return pl.pallas_call(
        kernel,
        out_shape=[
            jax.ShapeDtypeStruct((count, width), bf16),
            jax.ShapeDtypeStruct((count, width), bf16),
            jax.ShapeDtypeStruct((ROWS_OWN, SMALL), f32),
            jax.ShapeDtypeStruct((ROWS_OWN, DENSE), bf16),
            jax.ShapeDtypeStruct((REPS, expert_rows, width), bf16),
        ],
        in_specs=[IN_VMEM] * 4 + [ANY] + [IN_VMEM] * 7 + [ANY] * 4 + [IN_VMEM] * 2,
        out_specs=[IN_VMEM, IN_VMEM, IN_VMEM, ANY, ANY],
        scratch_shapes=scratch
        + sems(SUM_SEMS) * 7
        + sems(GATHER_SEMS)
        + sems(TOTAL_SEMS) * 3
        + [
            pltpu.SemaphoreType.DMA((4,)),
            pltpu.SemaphoreType.DMA((chips,)),
            pltpu.SemaphoreType.DMA((2, 3)),
            pltpu.SemaphoreType.DMA,
            pltpu.SemaphoreType.DMA((2,)),
        ],
        compiler_params=params(collective_id),
    )(
        returned, gates, middle, sent, dense, cotangent, tokens, attn_in, query_raw, key_raw,
        query_low, mixed, pairs, soft, out_terms, expert_own, cosine, sine,
    )


def finish_call(block_out, tokens_grad, small_sum, dense_own, expert_all):
    reps, expert_rows, width = expert_all.shape
    piece = expert_rows // 3
    rows = block_out.shape[0] // reps

    def kernel(
        block_ref, tokens_ref, small_ref, dense_ref, expert_ref,
        block, tokens, inner, outer, query, key, value, output, router, gain_a, gain_q, gain_f, gain_k,
    ):
        block[...] = block_ref[...]
        tokens[...] = tokens_ref[...]
        inner[0] = expert_ref[0, :piece].astype(f32)
        inner[1] = expert_ref[0, piece : 2 * piece].astype(f32)
        outer[...] = expert_ref[0, 2 * piece :].astype(f32)

        @pl.when(pl.program_id(0) == 1)
        def _():
            at_k = QUERY + WIDTH
            for low, target in ((0, query), (at_k, key), (at_k + KEY, value), (QUERY, output)):
                target[...] = dense_ref[:, pl.ds(low, target.shape[1])].astype(f32)
            turned_small = jnp.transpose(small_ref[...])
            router[...] = turned_small[:EXPERTS, :ROWS_OWN]
            for at, target in enumerate((gain_a, gain_q, gain_f, gain_k)):
                size = target.shape[0]
                target[...] = turned_small[EXPERTS + at, :size].reshape(size)

    def whole(*shape):
        return pl.BlockSpec(shape, lambda i: (0,) * len(shape))

    by_rows = pl.BlockSpec((rows, width), lambda i: (i, 0))
    shapes = [(ROWS_OWN, QUERY), (ROWS_OWN, KEY), (ROWS_OWN, KEY), (ROWS_OWN, WIDTH)]
    shapes += [(EXPERTS, ROWS_OWN), (ROWS_OWN,), (ROWS_OWN,), (ROWS_OWN,), (KGAIN_OWN,)]
    return pl.pallas_call(
        kernel,
        grid=(reps,),
        out_shape=[
            jax.ShapeDtypeStruct(block_out.shape, bf16),
            jax.ShapeDtypeStruct(tokens_grad.shape, bf16),
            jax.ShapeDtypeStruct((2, reps * piece, width), f32),
            jax.ShapeDtypeStruct((reps * piece, width), f32),
        ]
        + [jax.ShapeDtypeStruct(shape, f32) for shape in shapes],
        in_specs=[
            by_rows,
            by_rows,
            whole(*small_sum.shape),
            whole(*dense_own.shape),
            pl.BlockSpec((1, expert_rows, width), lambda i: (i, 0, 0)),
        ],
        out_specs=[
            by_rows,
            by_rows,
            pl.BlockSpec((2, piece, width), lambda i: (0, i, 0)),
            pl.BlockSpec((piece, width), lambda i: (i, 0)),
        ]
        + [whole(*shape) for shape in shapes],
        compiler_params=pltpu.CompilerParams(vmem_limit_bytes=VMEM_LIMIT),
    )(block_out, tokens_grad, small_sum, dense_own, expert_all)


def rotary_tables(positions):
    lane = jnp.arange(LANES, dtype=jnp.int32)
    half = HEAD_DIM // 2
    exponent = (lane % half).astype(f32) * (2.0 / HEAD_DIM)
    frequency = rope_base ** (-exponent)
    angles = positions.astype(f32)[:, None] * frequency[None, :]
    sign = jnp.where(lane % HEAD_DIM < half, -1.0, 1.0).astype(f32)
    return jnp.cos(angles), jnp.sin(angles) * sign[None, :]


def shards(
    tokens,
    cotangent,
    routes,
    picture_starts,
    attn_gain,
    query_weight,
    key_weight,
    value_weight,
    query_gain,
    key_gain,
    output_weight,
    ffn_gain,
    router_weight,
    expert_in,
    expert_down,
):
    seqs, positions, width = tokens.shape
    count = seqs * positions
    query_pos = lax.axis_index("rep") * positions + jnp.arange(positions, dtype=jnp.int32)
    cosine, sine = rotary_tables(query_pos)
    rows = tokens.reshape(count, width)
    grad_rows = cotangent.reshape(count, width)
    (
        dense, grad_all, pairs, soft, rows_first,
        attn_in, query_raw, key_raw, query_low, mixed, middle, sent, gates,
    ) = front_call(
        1, rows, grad_rows, (query_weight, key_weight, value_weight, output_weight),
        (attn_gain, query_gain, ffn_gain, key_gain), router_weight.T,
        cosine, sine, jnp.transpose(routes, (0, 2, 1)), picture_starts,
    )
    returned, expert_own, out_terms = moe_call(
        2, sent, rows_first, grad_all, expert_in[0], expert_down[0]
    )
    block_out, tokens_grad, small_sum, dense_out, expert_all = back_call(
        3, returned, gates, middle, sent, dense, grad_rows, rows, attn_in,
        query_raw, key_raw, query_low, mixed, pairs, soft, out_terms, expert_own, cosine, sine,
    )
    (
        block_out, tokens_grad, inner, outer, query, key, value, output, router, gain_a, gain_q, gain_f, gain_k,
    ) = finish_call(block_out, tokens_grad, small_sum, dense_out, expert_all)
    return (
        block_out.reshape(tokens.shape),
        tokens_grad.reshape(tokens.shape),
        gain_a,
        query,
        key,
        value,
        gain_q,
        gain_k,
        output,
        gain_f,
        router.T,
        inner.reshape(expert_in.shape),
        outer[None],
    )


def solution(mesh):
    by_tokens = P("shard", "rep", None)
    rows, line, block = P("shard", None), P("shard"), P("shard", None, None)
    in_specs = (
        by_tokens, by_tokens, by_tokens, rows, line, rows, rows, rows, line, line, rows, line, rows, block, block,
    )
    out_specs = (
        by_tokens, by_tokens, line, rows, rows, rows, line, line, rows, line, rows, block, block,
    )
    return jax.shard_map(shards, mesh=mesh, in_specs=in_specs, out_specs=out_specs, check_vma=False)
```

```python
import jax
import jax.numpy as jnp
from jax import lax
from jax.experimental import pallas as pl
from jax.experimental.pallas import tpu as pltpu
from jax.sharding import PartitionSpec as P

HEADS = 16
KV_HEADS = 8
HEAD_DIM = 64
PIC = 256
RING = 4
GROUP = 16
REPS = 8
VMEM_LIMIT = 63 << 20

norm_eps = 1e-06
rope_base = 10000.0
masked_score = -1e30

bf16 = jnp.bfloat16
f32 = jnp.float32


class Place:
    def __init__(self):
        shard = lax.axis_index("shard")
        rep = lax.axis_index("rep")
        self.shard, self.rep = shard, rep
        core = lax.rem(shard, 2)
        ring_z = lax.rem(lax.div(shard, 2), RING)
        y_hi = lax.div(shard, 8)
        ring_x = lax.rem(rep, RING)
        y_lo = lax.div(rep, RING)
        self.core = core

        def shard_of(hi, z, c):
            return (hi * RING + z) * 2 + c

        def rep_of(lo, x):
            return lo * RING + x

        def up(v):
            return lax.rem(v + 1, RING)

        def down(v):
            return lax.rem(v + RING - 1, RING)

        self.twin = (shard_of(y_hi, ring_z, 1 - core), rep)
        self.others = [lax.rem(rep + step, REPS) for step in range(REPS)]
        self.tokens = Axes(
            y_hi,
            ring_z,
            (shard_of(y_hi, up(ring_z), core), rep),
            (shard_of(y_hi, down(ring_z), core), rep),
            (shard_of(1 - y_hi, ring_z, core), rep_of(1 - y_lo, ring_x)),
        )
        self.copies = Axes(
            y_lo,
            ring_x,
            (shard, rep_of(y_lo, up(ring_x))),
            (shard, rep_of(y_lo, down(ring_x))),
            (shard, rep_of(1 - y_lo, ring_x)),
        )


class Axes:
    def __init__(self, side, spot, ahead, behind, across):
        self.side, self.spot = side, spot
        self.ahead, self.behind, self.across = ahead, behind, across
        sides = (side, 1 - side)
        spots = [lax.rem(spot + step, RING) for step in range(RING)]
        self.places = [[(sides[flip], spots[step]) for step in range(RING)] for flip in range(2)]

    def at(self, flip, step):
        return self.places[flip][step % RING]

    def neighbours(self):
        return [self.ahead, self.behind, self.across]


def greet(devices):
    barrier = pltpu.get_barrier_semaphore()
    for device in devices:
        pl.semaphore_signal(barrier, inc=1, device_id=device, device_id_type=pl.DeviceIdType.MESH)
    pl.semaphore_wait(barrier, len(devices))


class Line:
    def __init__(self, send_sem, recv_sem):
        self.send_sem, self.recv_sem = send_sem, recv_sem
        self.sent = []

    def copy(self, index, source, target, device):
        return pltpu.make_async_remote_copy(
            src_ref=source(),
            dst_ref=target(),
            send_sem=self.send_sem.at[index],
            recv_sem=self.recv_sem.at[index],
            device_id=device,
            device_id_type=pl.DeviceIdType.MESH,
        )

    def send(self, index, source, target, device):
        self.copy(index, source, target, device).start()
        self.sent.append((index, source, target, device))

    def take(self, index, target, device):
        self.copy(index, target, target, device).wait_recv()

    def finish(self):
        for sent in self.sent:
            self.copy(*sent).wait_send()


def abreast(*parts):
    running = list(parts)
    while running:
        for part in list(running):
            try:
                next(part)
            except StopIteration:
                running.remove(part)


GATHER_SEMS = 20


def gather_parts(axes, line, own, block, rows, local_sem, twin=None, twin_later=False):
    half, quarter = rows // 2, rows // 4
    mine, back, front, far = axes.at(0, 0), axes.at(0, -1), axes.at(0, 1), axes.at(0, 2)
    pair, pair_back, pair_front, pair_far = (axes.at(1, n) for n in (0, -1, 1, 2))
    ahead, behind, across = axes.ahead, axes.behind, axes.across

    def rows_of(which, low=0, count=rows, other=False):
        return lambda: block(which, low, count, other)

    def first(index, device):
        line.send(index, lambda: own, rows_of(mine), device)

    def relay(index, device, which, low=0, count=rows):
        line.send(index, rows_of(which, low, count), rows_of(which, low, count), device)

    def share(index, which):
        if twin is not None:
            relay(12 + index, twin, which)

    def keep():
        return pltpu.make_async_copy(own, block(mine, 0, rows), local_sem)

    keep().start()
    if twin is not None:
        first(12, twin)
    first(0, ahead)
    first(1, behind)
    first(2, across)
    keep().wait()
    yield
    line.take(0, rows_of(back), ahead)
    relay(3, ahead, back, 0, half)
    relay(4, across, back, half, half)
    share(1, back)
    line.take(1, rows_of(front), behind)
    relay(5, behind, front, half, half)
    relay(6, across, front, half, half)
    share(2, front)
    line.take(2, rows_of(pair), across)
    relay(7, ahead, pair, 0, half)
    relay(8, behind, pair, 0, half)
    share(3, pair)
    yield
    line.take(3, rows_of(far, 0, half), ahead)
    line.take(5, rows_of(far, half, half), behind)
    relay(9, across, far, half, half)
    share(4, far)
    line.take(7, rows_of(pair_back, 0, half), ahead)
    relay(10, ahead, pair_back, 0, quarter)
    line.take(8, rows_of(pair_front, 0, half), behind)
    relay(11, behind, pair_front, quarter, quarter)
    line.take(4, rows_of(pair_back, half, half), across)
    share(5, pair_back)
    line.take(6, rows_of(pair_front, half, half), across)
    share(6, pair_front)
    yield
    line.take(10, rows_of(pair_far, 0, quarter), ahead)
    line.take(11, rows_of(pair_far, quarter, quarter), behind)
    line.take(9, rows_of(pair_far, half, half), across)
    share(7, pair_far)
    yield
    if twin is not None and not twin_later:
        for index, which in enumerate(gather_order(axes)):
            line.take(12 + index, rows_of(which, other=True), twin)
    line.finish()


SUM_SEMS = 20
TOTAL_SEMS = 24


def total_parts(place, line, own, got, total, target, local_sem, tail=None):
    rep = place.rep
    steps = range(1, REPS)
    peers = {step: (place.shard, place.others[step]) for step in steps}
    before = {step: place.others[REPS - step] for step in steps}

    def added(mine, received):
        value = mine[...].astype(f32)
        for step in steps:
            value = value + received[before[step]].astype(f32)
        return value.astype(bf16)

    def kept(index, source, place_of):
        return pltpu.make_async_copy(source, place_of, local_sem.at[index])

    for step in steps:
        line.send(
            step, lambda p=place.others[step]: own(p), lambda: got.at[rep], peers[step]
        )
        if tail is not None:
            line.send(16 + step, lambda: tail[0], lambda: tail[1].at[rep], peers[step])
    yield
    for step in steps:
        line.take(step, lambda b=before[step]: got.at[b], peers[step])
    total[...] = added(own(rep), got)
    kept(0, total, target(rep)).start()
    for step in steps:
        line.send(8 + step, lambda: total, lambda: target(rep), peers[step])
    if tail is not None:
        for step in steps:
            line.take(16 + step, lambda b=before[step]: tail[1].at[b], peers[step])
        tail[2][...] = added(tail[0], tail[1])
        kept(1, tail[2], tail[3]).start()
    yield
    for step in steps:
        line.take(8 + step, lambda b=before[step]: target(b), peers[step])
    kept(0, total, target(rep)).wait()
    if tail is not None:
        kept(1, tail[2], tail[3]).wait()
    line.finish()


def add_rows(target, source, rows):
    step = 16
    count = rows // step

    def body(index, carry):
        at = pl.ds(pl.multiple_of(index * step, step), step)
        target[at] = target[at] + source[at]
        return carry

    lax.fori_loop(0, count, body, 0)


def stage_rows(rows):
    return 7 * rows


def gather_order(axes):
    return [axes.at(*v) for v in ((0, 0), (0, -1), (0, 1), (1, 0), (0, 2), (1, -1), (1, 1), (1, 2))]


def sum_order(axes):
    return [axes.at(*v) for v in ((1, 2), (0, 2), (1, -1), (1, 1), (0, -1), (0, 1), (1, 0), (0, 0))]


def sum_parts(axes, line, part, stage, rows, result, twin=None, store=None):
    half, quarter = rows // 2, rows // 4
    mine, back, front, far = axes.at(0, 0), axes.at(0, -1), axes.at(0, 1), axes.at(0, 2)
    pair, pair_back, pair_front, pair_far = (axes.at(1, n) for n in (0, -1, 1, 2))
    ahead, behind, across = axes.ahead, axes.behind, axes.across
    order = sum_order(axes)
    offsets, used = {}, 0
    for name, size in (
        ("Y0", half), ("M0", quarter), ("P0", quarter), ("M1", half), ("Y1", half), ("Y2", half),
        ("P1", half), ("M2", half), ("P2", half), ("M3", rows), ("P3", rows), ("Y3", rows),
    ):
        offsets[name] = (used, size, len(offsets))
        used += size

    def landing(name):
        low, size, _ = offsets[name]
        return lambda: stage.at[pl.ds(low, size)]

    def send(name, which, low, device):
        _, size, index = offsets[name]
        line.send(index, lambda: part(which, low, size), landing(name), device)

    def add(name, which, low, device):
        _, size, index = offsets[name]
        line.take(index, landing(name), device)
        add_rows(part(which, low, size), landing(name)(), size)

    def join(*places):
        if twin is not None:
            for place in places:
                line.take(12 + place, lambda: twin[2](order[place]), twin[0])
                add_rows(part(order[place], 0, rows), twin[2](order[place]), rows)

    def hand(*places):
        if twin is not None:
            for place in places:
                which = order[place]
                line.send(
                    12 + place, lambda w=which: twin[1](w), lambda w=which: twin[2](w), twin[0]
                )

    hand(0, 1, 2, 3)
    yield
    join(0)
    send("Y0", pair_far, half, across)
    send("M0", pair_far, 0, behind)
    send("P0", pair_far, quarter, ahead)
    join(1)
    send("M1", far, 0, behind)
    join(2)
    send("Y1", pair_back, half, across)
    join(3)
    send("Y2", pair_front, half, across)
    yield
    hand(4, 5, 6, 7)
    yield
    add("M0", pair_back, 0, behind)
    send("M2", pair_back, 0, behind)
    add("P0", pair_front, quarter, ahead)
    send("P2", pair_front, 0, ahead)
    add("Y0", far, half, across)
    send("P1", far, half, ahead)
    yield
    join(4, 5, 6, 7)
    add("M1", back, 0, behind)
    add("Y1", back, half, across)
    send("M3", back, 0, behind)
    add("M2", pair, 0, behind)
    add("P2", pair, 0, ahead)
    send("Y3", pair, 0, across)
    add("P1", front, half, ahead)
    add("Y2", front, half, across)
    send("P3", front, 0, ahead)
    yield
    for name, device in (("M3", behind), ("P3", ahead), ("Y3", across)):
        line.take(offsets[name][2], landing(name), device)
    step = 16

    def body(index, carry):
        low = pl.multiple_of(index * step, step)
        total = part(mine, low, step)[...].astype(f32)
        for name in ("M3", "P3", "Y3"):
            total = total + stage[pl.ds(offsets[name][0] + low, step)].astype(f32)
        if store is None:
            result[pl.ds(low, step)] = total.astype(result.dtype)
        else:
            store(low, step, total)
        return carry

    lax.fori_loop(0, rows // step, body, 0)
    line.finish()


def sems(count):
    return [pltpu.SemaphoreType.DMA((count,)), pltpu.SemaphoreType.DMA((count,))]


ANY = pl.BlockSpec(memory_space=pl.ANY)
IN_VMEM = pl.BlockSpec(memory_space=pltpu.VMEM)


def params(collective_id):
    return pltpu.CompilerParams(
        collective_id=collective_id, has_side_effects=True, vmem_limit_bytes=VMEM_LIMIT
    )


def dot(a, b):
    return jnp.dot(a, b, preferred_element_type=f32)


def dot_nt(a, b):
    return lax.dot_general(a, b, (((1,), (1,)), ((), ())), preferred_element_type=f32)


def dot_tn(a, b):
    return lax.dot_general(a, b, (((0,), (0,)), ((), ())), preferred_element_type=f32)


def pick(index, values):
    chosen = values[-1]
    for at in range(len(values) - 2, -1, -1):
        chosen = jnp.where(index == at, values[at], chosen)
    return chosen


def moe_call(collective_id, sent, rows_first, grad_all, inner, outer):
    count, columns = sent.shape
    width = inner.shape[0]
    hidden_width = outer.shape[0]
    small = columns - width
    half = count // 2
    chips = GROUP // 2
    wide = 4
    rounds = GROUP // wide

    def kernel(
        sent_ref, first_ref, grad_ref, inner_ref, outer_ref,
        returned, out_terms, terms,
        rows_in, grads, hidden, back_gu, back, back_staged, back_stage, out_box, term_box,
        gs, gr, bs0, br0, bs1, br1, own_sem, load_sem, box_sem, term_sem,
    ):
        place = Place()
        axes, core, shard = place.tokens, place.core, place.shard
        gather_line = Line(gs, gr)

        def chip_of(which):
            return which[0] * RING + which[1]

        def blocks(which, other=False):
            return chip_of(which) * 2 + ((1 - core) if other else core)

        gather = gather_parts(
            axes, gather_line, sent_ref.at[pl.ds(half, half)],
            lambda which, low, n, other=False: rows_in.at[1, blocks(which, other), pl.ds(low, n)],
            half, own_sem, place.twin, twin_later=True,
        )

        def sum_of(chunk, send_sem, recv_sem):
            return sum_parts(
                axes, Line(send_sem, recv_sem),
                lambda which, low, n: back.at[chunk, blocks(which), pl.ds(low, n)],
                back_stage.at[chunk], half, returned.at[pl.ds(chunk * half, half)],
                (place.twin, lambda which: back.at[chunk, blocks(which, True)],
                 lambda which: back_staged.at[chunk, chip_of(which)]),
            )

        sums = [sum_of(0, bs0, br0), sum_of(1, bs1, br1)]

        def loads(t):
            at = pl.ds(t * wide, wide)
            return [
                pltpu.make_async_copy(first_ref.at[at], rows_in.at[0, at], load_sem.at[t, 0]),
                pltpu.make_async_copy(
                    grad_ref.at[at, pl.ds(0, half)], grads.at[0, at], load_sem.at[t, 1]
                ),
            ]

        second_grads = pltpu.make_async_copy(
            grad_ref.at[:, pl.ds(half, half)], grads.at[1], load_sem.at[rounds, 0]
        )

        def box_copy(chunk, first, slot):
            return pltpu.make_async_copy(
                out_box.at[slot],
                out_terms.at[pl.ds(first, wide), pl.ds(chunk * half, half)],
                box_sem.at[slot],
            )

        rows_count = wide * half
        lanes = lane_of((rows_count, small))
        is_high, is_rest = lanes == shard, lanes == shard + GROUP

        def tile(chunk, first, slot, wait_first):
            at = pl.ds(first, wide)
            row_block = rows_in[chunk, at].reshape(rows_count, columns)
            gate = jnp.sum(
                jnp.where(is_high | is_rest, row_block[:, width:].astype(f32), 0.0),
                axis=1, keepdims=True,
            )
            gate_up = dot(row_block[:, :width], inner_ref[...])
            gate_part, up_part = gate_up[:, :hidden_width], gate_up[:, hidden_width:]
            sigmoid = 1.0 / (1.0 + jnp.exp(-gate_part))
            active = gate_part * sigmoid
            product = active * up_part
            hidden_low = product.astype(bf16)
            hidden[chunk, at] = hidden_low.reshape(wide, half, hidden_width)
            out_rows = (gate * dot(hidden_low, outer_ref[...])).astype(bf16)

            @pl.when(wait_first)
            def _():
                box_copy(chunk, first, slot).wait()

            out_box[slot] = out_rows.reshape(wide, half, width)
            box_copy(chunk, first, slot).start()
            grad = grads[chunk, at].reshape(rows_count, width)
            grad_hidden = dot_nt(grad, outer_ref[...])
            grad_gate = jnp.sum(grad_hidden * product, axis=1, keepdims=True)
            grad_hidden = grad_hidden * gate
            grad_gate_up = jnp.concatenate(
                [
                    grad_hidden * up_part * sigmoid * (1.0 + gate_part * (1.0 - sigmoid)),
                    grad_hidden * active,
                ],
                axis=1,
            ).astype(bf16)
            back_gu[chunk, at] = grad_gate_up.reshape(wide, half, 2 * hidden_width)
            grads[chunk, at] = (gate * grad.astype(f32)).astype(bf16).reshape(wide, half, width)
            grad_rows = dot_nt(grad_gate_up, inner_ref[...]).astype(bf16)
            back[chunk, at, :, pl.ds(0, width)] = grad_rows.reshape(wide, half, width)
            high = grad_gate.astype(bf16).astype(f32)
            tail = jnp.where(is_high, high, jnp.where(is_rest, grad_gate - high, 0.0))
            back[chunk, at, :, pl.ds(width, small)] = tail.astype(bf16).reshape(wide, half, small)

        for t in range(rounds):
            for load in loads(t):
                load.start()
        second_grads.start()
        greet(axes.neighbours() + [place.twin])
        next(gather)

        def first_tiles(t, carry):
            hooks(t, ((2, lambda: next(gather)),))
            for load in loads(t):
                load.wait()
            tile(0, t * wide, lax.rem(t, 2), t >= 2)
            return carry

        lax.fori_loop(0, rounds, first_tiles, 0)
        next(sums[0])
        next(gather)
        second_grads.wait()
        near, beyond = lax.div(axes.spot, 2), 1 - lax.div(axes.spot, 2)
        chips_per_round = wide // 2
        firsts = [
            (side * RING + part * chips_per_round) * 2
            for side, part in (
                (axes.side, beyond), (1 - axes.side, near), (1 - axes.side, beyond), (axes.side, near),
            )
        ]
        arrivals = gather_order(axes)

        def arrived(*numbers):
            for number in numbers:
                gather_line.take(
                    12 + number, lambda: rows_in.at[1, blocks(arrivals[number], True)], place.twin
                )

        def second_tiles(t, carry):
            hooks(
                t,
                (
                    (0, lambda: arrived(0, 1, 2, 4)),
                    (1, lambda: (next(sums[0]), next(sums[0]), arrived(3, 5, 6))[2]),
                    (2, lambda: (next(gather), arrived(7))[1]),
                    (3, lambda: (next(sums[1]), next(sums[0]))[0]),
                ),
            )
            tile(1, pick(t, firsts), lax.rem(t, 2), t >= 0)
            return carry

        lax.fori_loop(0, rounds, second_tiles, 0)
        next(sums[1])
        next(sums[1])

        def term_copy(low, slot):
            return pltpu.make_async_copy(
                term_box.at[slot], terms.at[pl.ds(low, 256)], term_sem.at[slot]
            )

        every = 2 * GROUP * half

        def keep(index, low, value):
            slot = lax.rem(index, 2)

            @pl.when(index >= 2)
            def _():
                term_copy(low, slot).wait()

            term_box[slot] = value.astype(bf16)
            term_copy(low, slot).start()

        downs = hidden_width // 256

        def down_terms(index, carry):
            at = chunk_256(index)
            value = dot_tn(hidden[:, :, :, at].reshape(every, 256), grads[...].reshape(every, width))
            keep(index, pl.multiple_of(width + index * 256, 256), value)
            return carry

        lax.fori_loop(0, downs, down_terms, 0)

        def inner_terms(index, carry):
            hooks(
                index,
                (
                    (0, lambda: next(sums[0])),
                    (1, lambda: next(sums[1])),
                ),
            )
            at = chunk_256(index)
            value = dot_tn(
                rows_in[:, :, :, at].reshape(every, 256),
                back_gu[...].reshape(every, 2 * hidden_width),
            )
            keep(index + downs, pl.multiple_of(index * 256, 256), value)
            return carry

        lax.fori_loop(0, width // 256, inner_terms, 0)
        drained(sums[0])
        drained(sums[1])
        drained(gather)
        for slot in range(2):
            box_copy(1, 0, slot).wait()
            term_copy(0, slot).wait()

    term_rows = width + hidden_width
    return pl.pallas_call(
        kernel,
        out_shape=[
            jax.ShapeDtypeStruct((count, columns), f32),
            jax.ShapeDtypeStruct((GROUP, count, width), bf16),
            jax.ShapeDtypeStruct((term_rows, width), bf16),
        ],
        in_specs=[ANY, ANY, ANY, IN_VMEM, IN_VMEM],
        out_specs=[IN_VMEM, ANY, ANY],
        scratch_shapes=[
            pltpu.VMEM((2, GROUP, half, columns), bf16),
            pltpu.VMEM((2, GROUP, half, width), bf16),
            pltpu.VMEM((2, GROUP, half, hidden_width), bf16),
            pltpu.VMEM((2, GROUP, half, 2 * hidden_width), bf16),
            pltpu.VMEM((2, GROUP, half, columns), bf16),
            pltpu.VMEM((2, chips, half, columns), bf16),
            pltpu.VMEM((2, stage_rows(half), columns), bf16),
            pltpu.VMEM((2, wide, half, width), bf16),
            pltpu.VMEM((2, 256, width), bf16),
        ]
        + sems(GATHER_SEMS)
        + sems(SUM_SEMS) * 2
        + [
            pltpu.SemaphoreType.DMA,
            pltpu.SemaphoreType.DMA((rounds + 1, 2)),
            pltpu.SemaphoreType.DMA((2,)),
            pltpu.SemaphoreType.DMA((2,)),
        ],
        compiler_params=params(collective_id),
    )(sent, rows_first, grad_all, inner, outer)


WIDTH = 1024
QUERY = HEADS * HEAD_DIM
KEY = KV_HEADS * HEAD_DIM
EXPERTS = 16
SMALL = 128
LANES = 128
AT_K = QUERY
AT_V = AT_K + KEY
AT_S = AT_V + KEY
AT_O = AT_S + SMALL
PACKED = AT_O + WIDTH
ROWS_OWN = WIDTH // GROUP
KGAIN_OWN = KEY // GROUP
HEAD_PAIRS = KV_HEADS // 2
REST = 2 * KEY + SMALL


def drained(part):
    for _ in part:
        pass


def hooks(index, steps):
    for at, step in steps:
        pl.when(index == at)(step)


def chunk_256(index):
    return pl.ds(pl.multiple_of(index * 256, 256), 256)


def root_mean(values):
    return lax.rsqrt(jnp.mean(values * values, axis=1, keepdims=True) + norm_eps)


def lane_of(shape):
    return lax.broadcasted_iota(jnp.int32, shape, 1)


def turned(values, cosine, sine):
    first = (lane_of(values.shape) & (HEAD_DIM - 1)) < HEAD_DIM // 2
    swapped = jnp.where(
        first, pltpu.roll(values, LANES - HEAD_DIM // 2, 1), pltpu.roll(values, HEAD_DIM // 2, 1)
    )
    return values * cosine + swapped * sine


def gain_rows(small):
    rows = jnp.transpose(small.astype(f32))
    short = small.reshape(GROUP, ROWS_OWN, SMALL)[:, :KGAIN_OWN].reshape(KEY, SMALL)
    gain_k = jnp.transpose(short.astype(f32))[EXPERTS + 3 : EXPERTS + 4]
    return rows[EXPERTS : EXPERTS + 1], rows[EXPERTS + 1 : EXPERTS + 2], rows[EXPERTS + 2 : EXPERTS + 3], gain_k


def long_column(columns):
    cut = columns.reshape(GROUP, KGAIN_OWN, SMALL)
    return jnp.concatenate([cut, jnp.zeros_like(cut)], axis=1).reshape(WIDTH, SMALL)


def four_heads(chunk_a, chunk_b):
    low = lane_of(chunk_a.shape) < HEAD_DIM
    zero = jnp.zeros_like(chunk_a)
    return jnp.concatenate(
        [
            jnp.where(low, chunk_a, zero),
            jnp.where(low, pltpu.roll(chunk_a, HEAD_DIM, 1), zero),
            jnp.where(low, zero, pltpu.roll(chunk_b, HEAD_DIM, 1)),
            jnp.where(low, zero, chunk_b),
        ],
        axis=0,
    )


def two_chunks(blocks):
    rows = blocks.shape[0] // 4
    one, two, three, four = (blocks[n * rows : (n + 1) * rows] for n in range(4))
    low = lane_of(one.shape) < HEAD_DIM
    return (
        jnp.where(low, one, pltpu.roll(two, HEAD_DIM, 1)),
        jnp.where(low, pltpu.roll(three, HEAD_DIM, 1), four),
    )


def chunk_at(index, base=0):
    return pl.ds(pl.multiple_of(base + index * LANES, LANES), LANES)


def front_call(collective_id, tokens, cotangent, weights_own, gains, router, cosine, sine, routes, starts):
    count, width = tokens.shape
    seqs = starts.shape[0]
    positions = count // seqs
    length = REPS * positions
    score_scale = HEAD_DIM ** (-0.5)
    sent_width = width + SMALL

    def kernel(
        starts_ref, tokens_ref, grad_ref, query_w, key_w, value_w, output_w,
        gain_a_ref, gain_q_ref, gain_f_ref, gain_k_ref, router_ref, cos_ref, sin_ref, routes_ref,
        dense_out, grad_all, pairs_out, soft_out, rows_first,
        attn_in, query_raw, key_raw, query_low, mixed, middle, sent, gates_out,
        packed, small_box, dense, pairs, pair_own, soft_box, bias_box,
        ws0, wr0, ws1, wr1, ws2, wr2, gs0, gr0, gs1, gr1, ks0, kr0, ks1, kr1, rs, rr, own_sem, out_sem, soft_sem, pack_sem,
    ):
        place = Place()
        core = place.core
        packing = [
            pltpu.make_async_copy(
                source, packed.at[:, pl.ds(low, source.shape[1])], pack_sem.at[index]
            )
            for index, (source, low) in enumerate(
                ((key_w, AT_K), (value_w, AT_V), (query_w, 0), (output_w, AT_O))
            )
        ]
        for copy in packing:
            copy.start()
        small_box[...] = jnp.zeros_like(small_box)
        small_box[pl.ds(0, EXPERTS), pl.ds(0, ROWS_OWN)] = router_ref[...].astype(f32)
        for at, ref in enumerate((gain_a_ref, gain_q_ref, gain_f_ref, gain_k_ref)):
            size = ref.shape[0]
            small_box[pl.ds(EXPERTS + at, 1), pl.ds(0, size)] = (
                ref[...].astype(f32).reshape(1, size)
            )
        packed[:, pl.ds(AT_S, SMALL)] = jnp.transpose(small_box[...])[:ROWS_OWN].astype(bf16)

        def token_block(index, low, size):
            def block(which, row, n, other=False):
                at = (which[0] * RING + which[1]) * 2 + ((1 - core) if other else core)
                return dense.at[at, pl.ds(row, n), pl.ds(low, size)]

            return block

        def weight_gather(index, low, size, send_sem, recv_sem):
            return gather_parts(
                place.tokens, Line(send_sem, recv_sem), packed.at[:, pl.ds(low, size)],
                token_block(index, low, size), ROWS_OWN, own_sem.at[index], place.twin,
            )

        def rows_of(target):
            def block(which, row, n, other=False):
                at = (which[0] * RING + which[1]) * 2 + ((1 - core) if other else core)
                return target.at[at, pl.ds(row, n)]

            return block

        def pair_gather(seq, send_sem, recv_sem):
            def block(which, row, n, other=False):
                return pairs.at[seq, which[0] * RING + which[1], pl.ds(row, n)]

            return gather_parts(
                place.copies, Line(send_sem, recv_sem),
                pair_own.at[pl.ds(seq * positions, positions)], block, positions, own_sem.at[3 + seq],
            )

        def soft_copy(seq, index, slot):
            return pltpu.make_async_copy(
                soft_box.at[slot], soft_out.at[seq, index], soft_sem.at[slot]
            )

        rest_gather = weight_gather(0, AT_K, REST, ws0, wr0)
        query_gather = weight_gather(1, 0, QUERY, ws1, wr1)
        output_gather = weight_gather(2, AT_O, WIDTH, ws2, wr2)
        def grad_gather(seq, send_sem, recv_sem):
            base = seq * positions

            def block(which, row, n, other=False):
                at = (which[0] * RING + which[1]) * 2 + ((1 - core) if other else core)
                return grad_all.at[at, pl.ds(base + row, n)]

            return gather_parts(
                place.tokens, Line(send_sem, recv_sem), grad_ref.at[pl.ds(base, positions)], block,
                positions, own_sem.at[5 + seq], place.twin,
            )

        grads = [grad_gather(0, gs0, gr0), grad_gather(1, gs1, gr1)]
        first_rows = gather_parts(
            place.tokens, Line(rs, rr), sent.at[pl.ds(0, positions)], rows_of(rows_first), positions,
            own_sem.at[7], place.twin,
        )
        pair_gathers = [pair_gather(0, ks0, kr0), pair_gather(1, ks1, kr1)]

        greet(place.tokens.neighbours() + place.copies.neighbours() + [place.twin])
        for copy in packing:
            copy.wait()
        next(rest_gather)
        inputs = tokens_ref[...].astype(f32)
        middle[...] = inputs * root_mean(inputs)
        next(rest_gather)
        next(query_gather)
        query_at = place.rep * positions + lax.broadcasted_iota(jnp.int32, (positions, 1), 0)
        key_at = lax.broadcasted_iota(jnp.int32, (1, length), 1)
        for seq in range(seqs):
            allowed = key_at <= query_at
            for piece in range(starts_ref.shape[1]):
                start = starts_ref[seq, piece]
                query_inside = (query_at >= start) & (query_at < start + PIC)
                key_inside = (key_at >= start) & (key_at < start + PIC)
                allowed = allowed | (query_inside & key_inside)
            bias_box[seq] = jnp.where(allowed, 0.0, masked_score)
        next(rest_gather)
        next(query_gather)
        next(output_gather)
        drained(rest_gather)
        next(query_gather)
        next(output_gather)

        def weights(low, size):
            return dense[:, :, pl.ds(low, size)].reshape(width, size)

        small = weights(AT_S, SMALL)
        gain_a, gain_q, gain_f, gain_k = gain_rows(small)
        rows = (middle[...] * gain_a).astype(bf16)
        attn_in[...] = rows
        cos2 = jnp.concatenate([cos_ref[...]] * seqs, axis=0)
        sin2 = jnp.concatenate([sin_ref[...]] * seqs, axis=0)
        raw = dot(rows, weights(AT_K, KEY))
        key_raw[...] = raw
        scaled = raw * root_mean(raw) * gain_k
        for chunk in range(KEY // LANES):
            at = slice(chunk * LANES, (chunk + 1) * LANES)
            pair_own[:, at] = turned(scaled[:, at], cos2, sin2).astype(bf16)
        pair_own[:, KEY:] = dot(rows, weights(AT_V, KEY)).astype(bf16)
        next(pair_gathers[0])
        drained(query_gather)
        next(output_gather)
        next(grads[0])
        raw = dot(rows, weights(0, QUERY))
        query_raw[...] = raw
        scaled = raw * root_mean(raw) * gain_q
        for chunk in range(QUERY // LANES):
            at = slice(chunk * LANES, (chunk + 1) * LANES)
            query_low[:, at] = turned(scaled[:, at], cos2, sin2).astype(bf16)
        next(pair_gathers[0])
        next(pair_gathers[1])
        drained(output_gather)
        dense_copy = pltpu.make_async_copy(dense, dense_out, out_sem.at[0])
        dense_copy.start()
        next(grads[0])
        next(grads[1])
        next(pair_gathers[0])
        next(pair_gathers[1])
        next(grads[0])
        drained(pair_gathers[0])
        next(grads[1])

        def attend(seq, index, slot, wait_first):
            rows_at = pl.ds(seq * positions, positions)
            queries = four_heads(
                query_low[rows_at, chunk_at(2 * index)].astype(f32),
                query_low[rows_at, chunk_at(2 * index + 1)].astype(f32),
            )
            queries = (queries * score_scale).astype(bf16)
            keys = pairs[seq, :, :, chunk_at(index)].reshape(length, LANES)
            scores = dot_nt(queries, keys).reshape(4, positions, length) + bias_box[seq][None]
            scores = scores.reshape(4 * positions, length)
            raised = jnp.exp(scores - jnp.max(scores, axis=1, keepdims=True))
            soft = (raised * (1.0 / jnp.sum(raised, axis=1, keepdims=True))).astype(bf16)

            @pl.when(wait_first)
            def _():
                soft_copy(seq, index, slot).wait()

            soft_box[slot] = soft
            soft_copy(seq, index, slot).start()
            values = pairs[seq, :, :, chunk_at(index, KEY)].reshape(length, LANES)
            chunk_a, chunk_b = two_chunks(dot(soft, values))
            mixed[rows_at, chunk_at(2 * index)] = chunk_a.astype(bf16)
            mixed[rows_at, chunk_at(2 * index + 1)] = chunk_b.astype(bf16)

        def features(seq):
            at = pl.ds(seq * positions, positions)
            total = tokens_ref[at].astype(f32) + dot(mixed[at], weights(AT_O, WIDTH))
            middle[at] = total
            ffn_in = (total * root_mean(total) * gain_f).astype(bf16)
            sent[at, pl.ds(0, width)] = ffn_in
            lanes = lane_of((positions, SMALL))
            named = jnp.transpose(routes_ref[seq].astype(f32)).astype(jnp.int32)
            chosen = lanes == named[:, :1]
            for choice in range(1, named.shape[1]):
                chosen = chosen | (lanes == named[:, choice : choice + 1])
            logits = jnp.where(chosen, dot(ffn_in, small), masked_score)
            raised = jnp.exp(logits - jnp.max(logits, axis=1, keepdims=True))
            gates = raised * (1.0 / jnp.sum(raised, axis=1, keepdims=True))
            gates = jnp.where(chosen, gates, 0.0)
            gates_out[at] = gates
            high = gates.astype(bf16).astype(f32)
            tail = high + pltpu.roll(gates - high, EXPERTS, 1)
            sent[at, pl.ds(width, SMALL)] = tail.astype(bf16)

        def first_heads(index, carry):
            hooks(
                index,
                (
                    (1, lambda: next(grads[0])),
                    (2, lambda: next(pair_gathers[1])),
                    (3, lambda: next(grads[1])),
                ),
            )
            attend(0, index, lax.rem(index, 2), index >= 2)
            return carry

        lax.fori_loop(0, HEAD_PAIRS, first_heads, 0)
        features(0)
        next(first_rows)
        drained(pair_gathers[1])
        pairs_copy = pltpu.make_async_copy(pairs, pairs_out, out_sem.at[1])
        pairs_copy.start()

        def second_heads(index, carry):
            hooks(
                index,
                (
                    (1, lambda: next(grads[1])),
                    (3, lambda: next(first_rows)),
                ),
            )
            attend(1, index, lax.rem(index, 2), index >= 0)
            return carry

        lax.fori_loop(0, HEAD_PAIRS, second_heads, 0)
        features(1)
        next(first_rows)
        drained(grads[0])
        drained(grads[1])
        drained(first_rows)
        dense_copy.wait()
        pairs_copy.wait()
        for slot in range(2):
            soft_copy(1, 0, slot).wait()

    return pl.pallas_call(
        kernel,
        out_shape=[
            jax.ShapeDtypeStruct((GROUP, ROWS_OWN, PACKED), bf16),
            jax.ShapeDtypeStruct((GROUP, count, width), bf16),
            jax.ShapeDtypeStruct((seqs, REPS, positions, 2 * KEY), bf16),
            jax.ShapeDtypeStruct((seqs, HEAD_PAIRS, 4 * positions, length), bf16),
            jax.ShapeDtypeStruct((GROUP, positions, sent_width), bf16),
            jax.ShapeDtypeStruct((count, width), bf16),
            jax.ShapeDtypeStruct((count, QUERY), f32),
            jax.ShapeDtypeStruct((count, KEY), f32),
            jax.ShapeDtypeStruct((count, QUERY), bf16),
            jax.ShapeDtypeStruct((count, QUERY), bf16),
            jax.ShapeDtypeStruct((count, width), f32),
            jax.ShapeDtypeStruct((count, width + SMALL), bf16),
            jax.ShapeDtypeStruct((count, SMALL), f32),
        ],
        in_specs=[pl.BlockSpec(memory_space=pltpu.SMEM), IN_VMEM] + [ANY] * 5 + [IN_VMEM] * 8,
        out_specs=[ANY] * 5 + [IN_VMEM] * 8,
        scratch_shapes=[
            pltpu.VMEM((ROWS_OWN, PACKED), bf16),
            pltpu.VMEM((SMALL, LANES), f32),
            pltpu.VMEM((GROUP, ROWS_OWN, PACKED), bf16),
            pltpu.VMEM((seqs, REPS, positions, 2 * KEY), bf16),
            pltpu.VMEM((count, 2 * KEY), bf16),
            pltpu.VMEM((2, 4 * positions, length), bf16),
            pltpu.VMEM((seqs, positions, length), f32),
        ]
        + sems(GATHER_SEMS) * 8
        + [
            pltpu.SemaphoreType.DMA((8,)),
            pltpu.SemaphoreType.DMA((2,)),
            pltpu.SemaphoreType.DMA((2,)),
            pltpu.SemaphoreType.DMA((4,)),
        ],
        compiler_params=params(collective_id),
    )(starts, tokens, cotangent, *weights_own, *gains, router, cosine, sine, routes)


def key_chunk(index, base=0):
    low = lax.div(index, 2) * KEY + lax.rem(index, 2) * LANES + base
    return pl.ds(pl.multiple_of(low, LANES), LANES)


def norm_back(values, gain, grad):
    scale = root_mean(values)
    weighted = grad * gain
    mean = jnp.mean(values * weighted, axis=1, keepdims=True)
    inner = weighted * scale - values * (scale * scale * scale * mean)
    return inner, jnp.sum(grad * values * scale, axis=0, keepdims=True)


def back_call(
    collective_id, returned, gates, middle, sent, dense, cotangent, tokens, attn_in, query_raw, key_raw,
    query_low, mixed, pairs, soft, out_terms, expert_terms, cosine, sine,
):
    count, width = tokens.shape
    seqs, _, positions, _ = pairs.shape
    length = REPS * positions
    expert_rows = expert_terms.shape[0] // REPS
    score_scale = HEAD_DIM ** (-0.5)
    chips = GROUP // 2

    def kernel(
        returned_ref, gates_ref, middle_ref, sent_ref, dense_ref, grad_ref, tokens_ref, attn_ref,
        query_raw_ref, key_raw_ref, query_ref, mixed_ref, pairs_ref, soft_ref, out_ref, expert_ref,
        cos_ref, sin_ref,
        block_out, tokens_grad, dense_out, expert_all,
        weight_box, weight_rest, rest_terms, dense_own,
        o_staged, q_staged, rest_staged, o_stage, q_stage, rest_stage,
        out_held, out_staged, out_stage, expert_held, expert_stage, expert_own,
        soft_box, key_box, value_box, pair_terms, pair_stage, pair_grads,
        grad_mixed, grad_query, grad_middle, grad_attn, grad_attn_in, gain_box,
        o_got, q_got, rest_got, small_got, totals,
        out_s, out_r, exp_s, exp_r, kv0_s, kv0_r, kva_s, kva_r, kvb_s, kvb_r, o_s, o_r, q_s, q_r, rest_s, rest_r,
        ge_s, ge_r, go_s, go_r, gq_s, gq_r, grest_s, grest_r,
        load_sem, held_sem, box_sem, own_sem, total_sem,
    ):
        place = Place()
        core = place.core
        token_axes, copy_axes = place.tokens, place.copies
        q_terms = expert_held

        def chip_of(which):
            return which[0] * RING + which[1]

        def blocks(which, other=False):
            return chip_of(which) * 2 + ((1 - core) if other else core)

        def out_store(low, step, value):
            at = pl.ds(low, step)
            block_out[at] = (middle_ref[at] + value).astype(bf16)

        out_sum = sum_parts(
            token_axes, Line(out_s, out_r),
            lambda which, low, n: out_held.at[chip_of(which), pl.ds(low, n)],
            out_stage, count, None,
            (place.twin, lambda which: out_ref.at[blocks(which, True)],
             lambda which: out_staged.at[chip_of(which)]),
            store=out_store,
        )
        expert_sum = sum_parts(
            copy_axes, Line(exp_s, exp_r),
            lambda which, low, n: expert_held.at[pl.ds(chip_of(which) * expert_rows + low, n)],
            expert_stage, expert_rows, expert_own,
        )

        def pair_sum(seq, low, size, send_sem, recv_sem):
            columns = pl.ds(low, size)
            return sum_parts(
                copy_axes, Line(send_sem, recv_sem),
                lambda which, row, n: pair_terms.at[seq, chip_of(which), pl.ds(row, n), columns],
                pair_stage.at[seq, :, columns], positions,
                pair_grads.at[pl.ds(seq * positions, positions), columns],
            )

        first_pairs = pair_sum(0, 0, 2 * KEY, kv0_s, kv0_r)
        second_pairs = [pair_sum(1, 0, KEY, kva_s, kva_r), pair_sum(1, KEY, KEY, kvb_s, kvb_r)]

        def rows_of_block(terms, index, low, n):
            return terms.at[pl.ds(index * ROWS_OWN + low, n)]

        def rows_of_pairs(terms, index, low, n):
            at = lax.rem(index, 2) * ROWS_OWN + low
            return terms.at[0, lax.div(index, 2), pl.ds(at, n)]

        def dense_sum(rows_of, terms, staged, stage, low, size, send_sem, recv_sem):
            return sum_parts(
                token_axes, Line(send_sem, recv_sem),
                lambda which, row, n: rows_of(terms, blocks(which), row, n),
                stage, ROWS_OWN, dense_own.at[:, pl.ds(low, size)],
                (place.twin, lambda which: rows_of(terms, blocks(which, True), 0, ROWS_OWN),
                 lambda which: staged.at[chip_of(which)]),
            )

        o_sum = dense_sum(rows_of_pairs, pair_terms, o_staged, o_stage, AT_O, width, o_s, o_r)
        q_sum = dense_sum(rows_of_block, q_terms, q_staged, q_stage, 0, QUERY, q_s, q_r)
        rest_sum = dense_sum(rows_of_block, rest_terms, rest_staged, rest_stage, AT_K, REST, rest_s, rest_r)

        def dense_total(index, low, got, send_sem, recv_sem, tail=None):
            def own(rep):
                return dense_own.at[:, chunk_at(rep, low)]

            def target(rep):
                return dense_out.at[:, chunk_at(rep, low)]

            return total_parts(
                place, Line(send_sem, recv_sem), own, got, totals.at[index], target,
                total_sem.at[index], tail,
            )

        o_total = dense_total(0, AT_O, o_got, go_s, go_r)
        q_total = dense_total(1, 0, q_got, gq_s, gq_r)
        small_at = pl.ds(AT_S, SMALL)
        rest_total = dense_total(
            2, AT_K, rest_got, grest_s, grest_r,
            (dense_own.at[:, small_at], small_got, totals.at[3], dense_out.at[:, small_at]),
        )
        expert_gather = gather_parts(
            copy_axes, Line(ge_s, ge_r), expert_own,
            lambda which, row, n, other=False: expert_all.at[chip_of(which), pl.ds(row, n)],
            expert_rows, own_sem,
        )

        def weight_load(low, index):
            return pltpu.make_async_copy(
                dense_ref.at[:, :, pl.ds(low, width)], weight_box, load_sem.at[index]
            )

        rest_load = pltpu.make_async_copy(
            dense_ref.at[:, :, pl.ds(AT_K, REST)], weight_rest, load_sem.at[1]
        )
        expert_load = pltpu.make_async_copy(expert_ref, expert_held, load_sem.at[2])
        held_loads = [
            pltpu.make_async_copy(
                out_ref.at[2 * chip + core], out_held.at[chip], held_sem.at[chip]
            )
            for chip in range(chips)
        ]

        def box_loads(number, slot):
            seq, index = lax.div(number, HEAD_PAIRS), lax.rem(number, HEAD_PAIRS)
            return [
                pltpu.make_async_copy(
                    soft_ref.at[seq, index], soft_box.at[slot], box_sem.at[slot, 0]
                ),
                pltpu.make_async_copy(
                    pairs_ref.at[seq, :, :, chunk_at(index)], key_box.at[slot], box_sem.at[slot, 1]
                ),
                pltpu.make_async_copy(
                    pairs_ref.at[seq, :, :, chunk_at(index, KEY)],
                    value_box.at[slot],
                    box_sem.at[slot, 2],
                ),
            ]

        expert_load.start()
        rest_load.start()
        weight_load(AT_O, 0).start()
        for load in held_loads + box_loads(0, 0):
            load.start()
        greet(
            token_axes.neighbours()
            + [place.twin]
            + [(place.shard, other) for other in place.others[1:]]
        )
        next(out_sum)
        expert_load.wait()
        next(expert_sum)
        next(expert_sum)
        next(expert_sum)
        rest_load.wait()

        small = weight_rest[:, :, pl.ds(2 * KEY, SMALL)].reshape(width, SMALL)
        gain_a, gain_q, gain_f, gain_k = gain_rows(small)
        gates = gates_ref[...]
        tail = returned_ref[:, pl.ds(width, SMALL)]
        grad_gates = tail + pltpu.roll(tail, SMALL - EXPERTS, 1)
        grad_logits = gates * (grad_gates - jnp.sum(gates * grad_gates, axis=1, keepdims=True))
        grad_logits = grad_logits.astype(bf16)
        grad_ffn = returned_ref[:, pl.ds(0, width)] + dot_nt(grad_logits, small)
        inner, gain_f_terms = norm_back(middle_ref[...], gain_f, grad_ffn)
        inner = grad_ref[...].astype(f32) + inner
        grad_middle[...] = inner
        grad_attn[...] = inner.astype(bf16)
        gain_box[...] = jnp.zeros_like(gain_box)
        gain_box[pl.ds(EXPERTS + 2, 1)] = gain_f_terms
        weight_load(AT_O, 0).wait()
        grad_mixed[...] = dot_nt(
            grad_attn[...], weight_box[...].reshape(QUERY, width)
        ).astype(bf16)
        weight_load(0, 3).start()

        def attend_back(seq, index):
            number = seq * HEAD_PAIRS + index
            slot = lax.rem(number, 2)
            for load in box_loads(number, slot):
                load.wait()

            @pl.when(number + 1 < seqs * HEAD_PAIRS)
            def _():
                for load in box_loads(number + 1, 1 - slot):
                    load.start()

            rows_at = pl.ds(seq * positions, positions)
            first, second = chunk_at(2 * index), chunk_at(2 * index + 1)
            queries = four_heads(
                query_ref[rows_at, first].astype(f32), query_ref[rows_at, second].astype(f32)
            )
            queries = (queries * score_scale).astype(bf16)
            grads = four_heads(
                grad_mixed[rows_at, first].astype(f32), grad_mixed[rows_at, second].astype(f32)
            ).astype(bf16)
            keys = key_box[slot].reshape(length, LANES)
            values = value_box[slot].reshape(length, LANES)
            soft_low = soft_box[slot]
            value_terms = dot_tn(soft_low, grads)
            pair_terms[seq, :, :, key_chunk(index, KEY // 2)] = value_terms.astype(bf16).reshape(
                REPS, positions, LANES
            )
            soft_full = soft_low.astype(f32)
            grad_soft = dot_nt(grads, values)
            weighted = soft_full * grad_soft
            grad_scores = (
                weighted - soft_full * jnp.sum(weighted, axis=1, keepdims=True)
            ).astype(bf16)
            key_terms = dot_tn(grad_scores, queries)
            pair_terms[seq, :, :, key_chunk(index)] = key_terms.astype(bf16).reshape(
                REPS, positions, LANES
            )
            chunk_a, chunk_b = two_chunks(dot(grad_scores, keys) * score_scale)
            grad_query[rows_at, first] = chunk_a.astype(bf16)
            grad_query[rows_at, second] = chunk_b.astype(bf16)

        def out_ready():
            for load in held_loads:
                load.wait()
            next(out_sum)
            next(out_sum)

        def first_heads(index, carry):
            hooks(index, ((2, lambda: next(expert_sum)), (3, out_ready)))
            attend_back(0, index)
            return carry

        lax.fori_loop(0, HEAD_PAIRS, first_heads, 0)
        for _ in range(3):
            next(first_pairs)

        def begin_second():
            for _ in range(3):
                next(second_pairs[0])

        def second_heads(index, carry):
            hooks(index, ((2, begin_second), (3, lambda: next(out_sum))))
            attend_back(1, index)
            return carry

        lax.fori_loop(0, HEAD_PAIRS, second_heads, 0)
        for _ in range(3):
            next(second_pairs[1])
        next(first_pairs)
        next(second_pairs[0])
        router_terms = dot_tn(sent_ref[:, pl.ds(0, width)], grad_logits)

        cos2 = jnp.concatenate([cos_ref[...]] * seqs, axis=0)
        sin2 = -jnp.concatenate([sin_ref[...]] * seqs, axis=0)

        def turned_back(values):
            return jnp.concatenate(
                [
                    turned(values[:, low : low + LANES], cos2, sin2)
                    for low in range(0, values.shape[1], LANES)
                ],
                axis=1,
            )

        grad, gain_q_terms = norm_back(
            query_raw_ref[...], gain_q, turned_back(grad_query[...].astype(f32))
        )
        gain_box[pl.ds(EXPERTS + 1, 1)] = gain_q_terms
        grad_query_low = grad.astype(bf16)
        weight_load(0, 3).wait()
        grad_attn_in[...] = dot_nt(grad_query_low, weight_box[...].reshape(width, QUERY))

        next(second_pairs[1])
        next(first_pairs)
        next(second_pairs[0])
        next(second_pairs[1])
        next(expert_sum)
        next(out_sum)
        drained(first_pairs)

        def o_rows(index, carry):
            at = chunk_256(index)
            value = dot_tn(mixed_ref[:, at], grad_attn[...]).astype(bf16)
            pair_terms[0, pl.ds(2 * index, 2)] = value.reshape(2, positions, width)
            return carry

        lax.fori_loop(0, QUERY // 256, o_rows, 0)
        next(o_sum)
        drained(expert_sum)
        next(expert_gather)

        def q_rows(index, carry):
            at = chunk_256(index)
            q_terms[at] = dot_tn(attn_ref[:, at], grad_query_low).astype(bf16)
            return carry

        lax.fori_loop(0, width // 256, q_rows, 0)
        next(q_sum)
        next(o_sum)
        next(o_sum)
        drained(out_sum)
        next(q_sum)
        next(q_sum)
        next(o_sum)
        drained(second_pairs[0])
        drained(second_pairs[1])

        grads = pair_grads[...]
        half = KEY // 2
        key_grads = jnp.concatenate([grads[:, :half], grads[:, KEY : KEY + half]], axis=1)
        value_grads = jnp.concatenate([grads[:, half:KEY], grads[:, KEY + half :]], axis=1)
        grad, gain_k_terms = norm_back(
            key_raw_ref[...], gain_k, turned_back(key_grads.astype(bf16).astype(f32))
        )
        grad_pairs = jnp.concatenate([grad.astype(bf16), value_grads.astype(bf16)], axis=1)
        gain_k_column = jnp.where(
            lane_of((KEY, SMALL)) == EXPERTS + 3,
            jnp.transpose(jnp.broadcast_to(gain_k_terms, (SMALL, KEY))),
            0.0,
        )
        grad = grad_attn_in[...] + dot_nt(
            grad_pairs, weight_rest[:, :, pl.ds(0, 2 * KEY)].reshape(width, 2 * KEY)
        )
        values = tokens_ref[...].astype(f32)
        inner, gain_a_terms = norm_back(values, gain_a, grad)
        tokens_grad[...] = (grad_middle[...] + inner).astype(bf16)
        gain_box[pl.ds(EXPERTS, 1)] = gain_a_terms
        rest_terms[:, pl.ds(2 * KEY, SMALL)] = (
            router_terms + jnp.transpose(gain_box[...]) + long_column(gain_k_column)
        ).astype(bf16)

        def rest_rows(index, carry):
            at = chunk_256(index)
            rest_terms[at, pl.ds(0, 2 * KEY)] = dot_tn(attn_ref[:, at], grad_pairs).astype(bf16)
            return carry

        lax.fori_loop(0, width // 256, rest_rows, 0)
        next(rest_sum)
        next(rest_sum)
        next(rest_sum)
        next(q_sum)
        next(o_sum)
        next(expert_gather)
        next(rest_sum)
        drained(o_sum)
        next(o_total)
        next(q_sum)
        next(expert_gather)
        next(rest_sum)
        next(o_total)
        drained(q_sum)
        next(q_total)
        drained(rest_sum)
        next(rest_total)
        next(q_total)
        next(rest_total)
        drained(o_total)
        drained(q_total)
        drained(expert_gather)
        drained(rest_total)

    block = pltpu.VMEM((GROUP, ROWS_OWN, width), bf16)
    scratch = [
        block,
        pltpu.VMEM((GROUP, ROWS_OWN, REST), bf16),
        pltpu.VMEM((width, REST), bf16),
        pltpu.VMEM((ROWS_OWN, PACKED), bf16),
        pltpu.VMEM((chips, ROWS_OWN, width), bf16),
        pltpu.VMEM((chips, ROWS_OWN, QUERY), bf16),
        pltpu.VMEM((chips, ROWS_OWN, REST), bf16),
        pltpu.VMEM((stage_rows(ROWS_OWN), width), bf16),
        pltpu.VMEM((stage_rows(ROWS_OWN), QUERY), bf16),
        pltpu.VMEM((stage_rows(ROWS_OWN), REST), bf16),
        pltpu.VMEM((chips, count, width), bf16),
        pltpu.VMEM((chips, count, width), bf16),
        pltpu.VMEM((stage_rows(count), width), bf16),
        pltpu.VMEM(expert_terms.shape, bf16),
        pltpu.VMEM((stage_rows(expert_rows), width), bf16),
        pltpu.VMEM((expert_rows, width), bf16),
        pltpu.VMEM((2, 4 * positions, length), bf16),
        pltpu.VMEM((2, REPS, positions, LANES), bf16),
        pltpu.VMEM((2, REPS, positions, LANES), bf16),
        pltpu.VMEM((seqs, REPS, positions, 2 * KEY), bf16),
        pltpu.VMEM((seqs, stage_rows(positions), 2 * KEY), bf16),
        pltpu.VMEM((count, 2 * KEY), f32),
        pltpu.VMEM((count, QUERY), bf16),
        pltpu.VMEM((count, QUERY), bf16),
        pltpu.VMEM((count, width), f32),
        pltpu.VMEM((count, width), bf16),
        pltpu.VMEM((count, width), f32),
        pltpu.VMEM((SMALL, width), f32),
    ]
    scratch += [pltpu.VMEM((REPS, ROWS_OWN, LANES), bf16)] * 4
    scratch += [pltpu.VMEM((4, ROWS_OWN, LANES), bf16)]
    return pl.pallas_call(
        kernel,
        out_shape=[
            jax.ShapeDtypeStruct((count, width), bf16),
            jax.ShapeDtypeStruct((count, width), bf16),
            jax.ShapeDtypeStruct((ROWS_OWN, PACKED), bf16),
            jax.ShapeDtypeStruct((REPS, expert_rows, width), bf16),
        ],
        in_specs=[IN_VMEM] * 4 + [ANY] + [IN_VMEM] * 7 + [ANY] * 4 + [IN_VMEM] * 2,
        out_specs=[IN_VMEM, IN_VMEM, ANY, ANY],
        scratch_shapes=scratch
        + sems(SUM_SEMS) * 8
        + sems(GATHER_SEMS)
        + sems(TOTAL_SEMS) * 3
        + [
            pltpu.SemaphoreType.DMA((4,)),
            pltpu.SemaphoreType.DMA((chips,)),
            pltpu.SemaphoreType.DMA((2, 3)),
            pltpu.SemaphoreType.DMA,
            pltpu.SemaphoreType.DMA((3, 2)),
        ],
        compiler_params=params(collective_id),
    )(
        returned, gates, middle, sent, dense, cotangent, tokens, attn_in, query_raw, key_raw,
        query_low, mixed, pairs, soft, out_terms, expert_terms, cosine, sine,
    )


def finish_call(block_out, tokens_grad, dense_own, expert_all, inner_rows):
    total_rows, width = expert_all.shape
    step = 256
    inner_steps, steps = inner_rows // step, total_rows // step
    rows = block_out.shape[0] // inner_steps

    def kernel(
        block_ref, tokens_ref, dense_ref, expert_ref,
        block, tokens, inner, outer, query, key, value, output, router, gain_a, gain_q, gain_f, gain_k,
    ):
        at = pl.program_id(0)

        @pl.when(at < inner_steps)
        def _():
            block[...] = block_ref[...]
            tokens[...] = tokens_ref[...]
            inner[...] = expert_ref[...].astype(f32)

        @pl.when(at >= inner_steps)
        def _():
            outer[...] = expert_ref[...].astype(f32)

        @pl.when(at == 1)
        def _():
            for low, target in ((0, query), (AT_K, key), (AT_V, value), (AT_O, output)):
                target[...] = dense_ref[:, pl.ds(low, target.shape[1])].astype(f32)
            turned_small = jnp.transpose(dense_ref[:, pl.ds(AT_S, SMALL)].astype(f32))
            router[...] = turned_small[:EXPERTS, :ROWS_OWN]
            for index, target in enumerate((gain_a, gain_q, gain_f, gain_k)):
                size = target.shape[0]
                target[...] = turned_small[EXPERTS + index, :size].reshape(size)

    def whole(*shape):
        return pl.BlockSpec(shape, lambda i: (0,) * len(shape))

    def by_rows(size):
        return pl.BlockSpec((size, width), lambda i: (jnp.minimum(i, inner_steps - 1), 0))

    shapes = [(ROWS_OWN, QUERY), (ROWS_OWN, KEY), (ROWS_OWN, KEY), (ROWS_OWN, WIDTH)]
    shapes += [(EXPERTS, ROWS_OWN), (ROWS_OWN,), (ROWS_OWN,), (ROWS_OWN,), (KGAIN_OWN,)]
    return pl.pallas_call(
        kernel,
        grid=(steps,),
        out_shape=[
            jax.ShapeDtypeStruct(block_out.shape, bf16),
            jax.ShapeDtypeStruct(tokens_grad.shape, bf16),
            jax.ShapeDtypeStruct((inner_rows, width), f32),
            jax.ShapeDtypeStruct((total_rows - inner_rows, width), f32),
        ]
        + [jax.ShapeDtypeStruct(shape, f32) for shape in shapes],
        in_specs=[
            by_rows(rows),
            by_rows(rows),
            whole(*dense_own.shape),
            pl.BlockSpec((step, width), lambda i: (i, 0)),
        ],
        out_specs=[
            by_rows(rows),
            by_rows(rows),
            by_rows(step),
            pl.BlockSpec((step, width), lambda i: (jnp.maximum(i - inner_steps, 0), 0)),
        ]
        + [whole(*shape) for shape in shapes],
        compiler_params=pltpu.CompilerParams(vmem_limit_bytes=VMEM_LIMIT),
    )(block_out, tokens_grad, dense_own, expert_all)


def rotary_tables(positions):
    lane = jnp.arange(LANES, dtype=jnp.int32)
    half = HEAD_DIM // 2
    exponent = (lane % half).astype(f32) * (2.0 / HEAD_DIM)
    frequency = rope_base ** (-exponent)
    angles = positions.astype(f32)[:, None] * frequency[None, :]
    sign = jnp.where(lane % HEAD_DIM < half, -1.0, 1.0).astype(f32)
    return jnp.cos(angles), jnp.sin(angles) * sign[None, :]


def shards(
    tokens,
    cotangent,
    routes,
    picture_starts,
    attn_gain,
    query_weight,
    key_weight,
    value_weight,
    query_gain,
    key_gain,
    output_weight,
    ffn_gain,
    router_weight,
    expert_in,
    expert_down,
):
    seqs, positions, width = tokens.shape
    count = seqs * positions
    query_pos = lax.axis_index("rep") * positions + jnp.arange(positions, dtype=jnp.int32)
    cosine, sine = rotary_tables(query_pos)
    rows = tokens.reshape(count, width)
    grad_rows = cotangent.reshape(count, width)
    (
        dense, grad_all, pairs, soft, rows_first,
        attn_in, query_raw, key_raw, query_low, mixed, middle, sent, gates,
    ) = front_call(
        1, rows, grad_rows, (query_weight, key_weight, value_weight, output_weight),
        (attn_gain, query_gain, ffn_gain, key_gain), router_weight.T,
        cosine, sine, jnp.transpose(routes, (0, 2, 1)), picture_starts,
    )
    returned, out_terms, expert_terms = moe_call(
        2, sent, rows_first, grad_all, expert_in[0], expert_down[0]
    )
    block_out, tokens_grad, dense_out, expert_all = back_call(
        3, returned, gates, middle, sent, dense, grad_rows, rows, attn_in,
        query_raw, key_raw, query_low, mixed, pairs, soft, out_terms, expert_terms, cosine, sine,
    )
    (
        block_out, tokens_grad, inner, outer, query, key, value, output, router, gain_a, gain_q, gain_f, gain_k,
    ) = finish_call(
        block_out, tokens_grad, dense_out, expert_all.reshape(-1, width), expert_in.shape[1]
    )
    return (
        block_out.reshape(tokens.shape),
        tokens_grad.reshape(tokens.shape),
        gain_a,
        query,
        key,
        value,
        gain_q,
        gain_k,
        output,
        gain_f,
        router.T,
        inner[None],
        outer[None],
    )


def solution(mesh):
    by_tokens = P("shard", "rep", None)
    rows, line, block = P("shard", None), P("shard"), P("shard", None, None)
    in_specs = (
        by_tokens, by_tokens, by_tokens, rows, line, rows, rows, rows, line, line, rows, line, rows, block, block,
    )
    out_specs = (
        by_tokens, by_tokens, line, rows, rows, rows, line, line, rows, line, rows, block, block,
    )
    return jax.shard_map(shards, mesh=mesh, in_specs=in_specs, out_specs=out_specs, check_vma=False)
```

```python
import jax
import jax.numpy as jnp
from jax import lax
from jax.experimental import pallas as pl
from jax.experimental.pallas import tpu as pltpu
from jax.sharding import PartitionSpec as P

HEADS = 16
KV_HEADS = 8
HEAD_DIM = 64
PIC = 256
RING = 4
GROUP = 16
REPS = 8
VMEM_LIMIT = 63 << 20

norm_eps = 1e-06
rope_base = 10000.0
masked_score = -1e30

bf16 = jnp.bfloat16
f32 = jnp.float32


class Place:
    def __init__(self):
        shard = lax.axis_index("shard")
        rep = lax.axis_index("rep")
        self.shard, self.rep = shard, rep
        core = lax.rem(shard, 2)
        ring_z = lax.rem(lax.div(shard, 2), RING)
        y_hi = lax.div(shard, 8)
        ring_x = lax.rem(rep, RING)
        y_lo = lax.div(rep, RING)
        self.core = core

        def shard_of(hi, z, c):
            return (hi * RING + z) * 2 + c

        def rep_of(lo, x):
            return lo * RING + x

        def up(v):
            return lax.rem(v + 1, RING)

        def down(v):
            return lax.rem(v + RING - 1, RING)

        self.twin = (shard_of(y_hi, ring_z, 1 - core), rep)
        self.others = [lax.rem(rep + step, REPS) for step in range(REPS)]
        self.tokens = Axes(
            y_hi,
            ring_z,
            (shard_of(y_hi, up(ring_z), core), rep),
            (shard_of(y_hi, down(ring_z), core), rep),
            (shard_of(1 - y_hi, ring_z, core), rep_of(1 - y_lo, ring_x)),
        )
        self.copies = Axes(
            y_lo,
            ring_x,
            (shard, rep_of(y_lo, up(ring_x))),
            (shard, rep_of(y_lo, down(ring_x))),
            (shard, rep_of(1 - y_lo, ring_x)),
        )


class Axes:
    def __init__(self, side, spot, ahead, behind, across):
        self.side, self.spot = side, spot
        self.ahead, self.behind, self.across = ahead, behind, across
        sides = (side, 1 - side)
        spots = [lax.rem(spot + step, RING) for step in range(RING)]
        self.places = [[(sides[flip], spots[step]) for step in range(RING)] for flip in range(2)]

    def at(self, flip, step):
        return self.places[flip][step % RING]

    def neighbours(self):
        return [self.ahead, self.behind, self.across]


def greet(devices):
    barrier = pltpu.get_barrier_semaphore()
    for device in devices:
        pl.semaphore_signal(barrier, inc=1, device_id=device, device_id_type=pl.DeviceIdType.MESH)
    pl.semaphore_wait(barrier, len(devices))


class Line:
    def __init__(self, send_sem, recv_sem):
        self.send_sem, self.recv_sem = send_sem, recv_sem
        self.sent = []

    def copy(self, index, source, target, device):
        return pltpu.make_async_remote_copy(
            src_ref=source(),
            dst_ref=target(),
            send_sem=self.send_sem.at[index],
            recv_sem=self.recv_sem.at[index],
            device_id=device,
            device_id_type=pl.DeviceIdType.MESH,
        )

    def send(self, index, source, target, device):
        self.copy(index, source, target, device).start()
        self.sent.append((index, source, target, device))

    def take(self, index, target, device):
        self.copy(index, target, target, device).wait_recv()

    def finish(self):
        for sent in self.sent:
            self.copy(*sent).wait_send()


def abreast(*parts):
    running = list(parts)
    while running:
        for part in list(running):
            try:
                next(part)
            except StopIteration:
                running.remove(part)


GATHER_SEMS = 20


def gather_parts(axes, line, own, block, rows, local_sem, twin=None, twin_later=False):
    half, quarter = rows // 2, rows // 4
    mine, back, front, far = axes.at(0, 0), axes.at(0, -1), axes.at(0, 1), axes.at(0, 2)
    pair, pair_back, pair_front, pair_far = (axes.at(1, n) for n in (0, -1, 1, 2))
    ahead, behind, across = axes.ahead, axes.behind, axes.across

    def rows_of(which, low=0, count=rows, other=False):
        return lambda: block(which, low, count, other)

    def first(index, device):
        line.send(index, lambda: own, rows_of(mine), device)

    def relay(index, device, which, low=0, count=rows):
        line.send(index, rows_of(which, low, count), rows_of(which, low, count), device)

    def share(index, which):
        if twin is not None:
            relay(12 + index, twin, which)

    def keep():
        return pltpu.make_async_copy(own, block(mine, 0, rows), local_sem)

    keep().start()
    if twin is not None:
        first(12, twin)
    first(0, ahead)
    first(1, behind)
    first(2, across)
    keep().wait()
    yield
    line.take(0, rows_of(back), ahead)
    relay(3, ahead, back, 0, half)
    relay(4, across, back, half, half)
    share(1, back)
    line.take(1, rows_of(front), behind)
    relay(5, behind, front, half, half)
    relay(6, across, front, half, half)
    share(2, front)
    line.take(2, rows_of(pair), across)
    relay(7, ahead, pair, 0, half)
    relay(8, behind, pair, 0, half)
    share(3, pair)
    yield
    line.take(3, rows_of(far, 0, half), ahead)
    line.take(5, rows_of(far, half, half), behind)
    relay(9, across, far, half, half)
    share(4, far)
    line.take(7, rows_of(pair_back, 0, half), ahead)
    relay(10, ahead, pair_back, 0, quarter)
    line.take(8, rows_of(pair_front, 0, half), behind)
    relay(11, behind, pair_front, quarter, quarter)
    line.take(4, rows_of(pair_back, half, half), across)
    share(5, pair_back)
    line.take(6, rows_of(pair_front, half, half), across)
    share(6, pair_front)
    yield
    line.take(10, rows_of(pair_far, 0, quarter), ahead)
    line.take(11, rows_of(pair_far, quarter, quarter), behind)
    line.take(9, rows_of(pair_far, half, half), across)
    share(7, pair_far)
    yield
    if twin is not None and not twin_later:
        for index, which in enumerate(gather_order(axes)):
            line.take(12 + index, rows_of(which, other=True), twin)
    line.finish()


SUM_SEMS = 20
TOTAL_SEMS = 16


def total_parts(place, line, own, got, total, target, local_sem):
    rep = place.rep
    steps = range(1, REPS)
    peers = {step: (place.shard, place.others[step]) for step in steps}
    before = {step: place.others[REPS - step] for step in steps}

    def kept():
        return pltpu.make_async_copy(total, target(rep), local_sem)

    for step in steps:
        line.send(step, lambda p=place.others[step]: own(p), lambda: got.at[rep], peers[step])
    yield
    value = own(rep)[...].astype(f32)
    for step in steps:
        line.take(step, lambda b=before[step]: got.at[b], peers[step])
        value = value + got[before[step]].astype(f32)
    total[...] = value.astype(bf16)
    kept().start()
    for step in steps:
        line.send(8 + step, lambda: total, lambda: target(rep), peers[step])
    yield
    for step in steps:
        line.take(8 + step, lambda b=before[step]: target(b), peers[step])
    kept().wait()
    line.finish()


def spread_parts(place, line, own, got, total):
    rep = place.rep
    steps = range(1, REPS)
    for step in steps:
        peer = (place.shard, place.others[step])
        line.send(step, lambda: own, lambda: got.at[rep], peer)
    yield
    value = own[...].astype(f32)
    for step in steps:
        before = place.others[REPS - step]
        line.take(step, lambda: got.at[before], (place.shard, place.others[step]))
        value = value + got[before].astype(f32)
    total[...] = value
    line.finish()


def add_rows(target, source, rows):
    step = 16
    count = rows // step

    def body(index, carry):
        at = pl.ds(pl.multiple_of(index * step, step), step)
        target[at] = target[at] + source[at]
        return carry

    lax.fori_loop(0, count, body, 0)


def stage_rows(rows):
    return 7 * rows


def gather_order(axes):
    return [axes.at(*v) for v in ((0, 0), (0, -1), (0, 1), (1, 0), (0, 2), (1, -1), (1, 1), (1, 2))]


def sum_order(axes):
    return [axes.at(*v) for v in ((1, 2), (0, 2), (1, -1), (1, 1), (0, -1), (0, 1), (1, 0), (0, 0))]


def sum_parts(axes, line, part, stage, rows, result, twin=None, store=None):
    half, quarter = rows // 2, rows // 4
    mine, back, front, far = axes.at(0, 0), axes.at(0, -1), axes.at(0, 1), axes.at(0, 2)
    pair, pair_back, pair_front, pair_far = (axes.at(1, n) for n in (0, -1, 1, 2))
    ahead, behind, across = axes.ahead, axes.behind, axes.across
    order = sum_order(axes)
    offsets, used = {}, 0
    for name, size in (
        ("Y0", half), ("M0", quarter), ("P0", quarter), ("M1", half), ("Y1", half), ("Y2", half),
        ("P1", half), ("M2", half), ("P2", half), ("M3", rows), ("P3", rows), ("Y3", rows),
    ):
        offsets[name] = (used, size, len(offsets))
        used += size

    def landing(name):
        low, size, _ = offsets[name]
        return lambda: stage.at[pl.ds(low, size)]

    def send(name, which, low, device):
        _, size, index = offsets[name]
        line.send(index, lambda: part(which, low, size), landing(name), device)

    def add(name, which, low, device):
        _, size, index = offsets[name]
        line.take(index, landing(name), device)
        add_rows(part(which, low, size), landing(name)(), size)

    def join(*places):
        if twin is not None:
            for place in places:
                line.take(12 + place, lambda: twin[2](order[place]), twin[0])
                add_rows(part(order[place], 0, rows), twin[2](order[place]), rows)

    def hand(*places):
        if twin is not None:
            for place in places:
                which = order[place]
                line.send(
                    12 + place, lambda w=which: twin[1](w), lambda w=which: twin[2](w), twin[0]
                )

    hand(0, 1, 2, 3)
    yield
    join(0)
    send("Y0", pair_far, half, across)
    send("M0", pair_far, 0, behind)
    send("P0", pair_far, quarter, ahead)
    join(1)
    send("M1", far, 0, behind)
    join(2)
    send("Y1", pair_back, half, across)
    join(3)
    send("Y2", pair_front, half, across)
    yield
    hand(4, 5, 6, 7)
    yield
    add("M0", pair_back, 0, behind)
    send("M2", pair_back, 0, behind)
    add("P0", pair_front, quarter, ahead)
    send("P2", pair_front, 0, ahead)
    add("Y0", far, half, across)
    send("P1", far, half, ahead)
    yield
    join(4, 5, 6, 7)
    add("M1", back, 0, behind)
    add("Y1", back, half, across)
    send("M3", back, 0, behind)
    add("M2", pair, 0, behind)
    add("P2", pair, 0, ahead)
    send("Y3", pair, 0, across)
    add("P1", front, half, ahead)
    add("Y2", front, half, across)
    send("P3", front, 0, ahead)
    yield
    for name, device in (("M3", behind), ("P3", ahead), ("Y3", across)):
        line.take(offsets[name][2], landing(name), device)
    step = 16

    def body(index, carry):
        low = pl.multiple_of(index * step, step)
        total = part(mine, low, step)[...].astype(f32)
        for name in ("M3", "P3", "Y3"):
            total = total + stage[pl.ds(offsets[name][0] + low, step)].astype(f32)
        if store is None:
            result[pl.ds(low, step)] = total.astype(result.dtype)
        else:
            store(low, step, total)
        return carry

    lax.fori_loop(0, rows // step, body, 0)
    line.finish()


def sems(count):
    return [pltpu.SemaphoreType.DMA((count,)), pltpu.SemaphoreType.DMA((count,))]


ANY = pl.BlockSpec(memory_space=pl.ANY)
IN_VMEM = pl.BlockSpec(memory_space=pltpu.VMEM)


def params(collective_id):
    return pltpu.CompilerParams(
        collective_id=collective_id, has_side_effects=True, vmem_limit_bytes=VMEM_LIMIT
    )


def dot(a, b):
    return jnp.dot(a, b, preferred_element_type=f32)


def dot_nt(a, b):
    return lax.dot_general(a, b, (((1,), (1,)), ((), ())), preferred_element_type=f32)


def dot_tn(a, b):
    return lax.dot_general(a, b, (((0,), (0,)), ((), ())), preferred_element_type=f32)


def pick(index, values):
    chosen = values[-1]
    for at in range(len(values) - 2, -1, -1):
        chosen = jnp.where(index == at, values[at], chosen)
    return chosen


def moe_call(collective_id, sent, rows_first, grad_all, inner, outer):
    count, columns = sent.shape
    width = inner.shape[0]
    hidden_width = outer.shape[0]
    small = columns - width
    half = count // 2
    chips = GROUP // 2
    wide = 4
    rounds = GROUP // wide

    def kernel(
        sent_ref, first_ref, grad_ref, inner_ref, outer_ref,
        returned, out_terms, terms,
        rows_in, grads, hidden, back_gu, back, back_staged, back_stage, out_box, term_box,
        gs, gr, bs0, br0, bs1, br1, own_sem, load_sem, box_sem, term_sem,
    ):
        place = Place()
        axes, core, shard = place.tokens, place.core, place.shard
        gather_line = Line(gs, gr)

        def chip_of(which):
            return which[0] * RING + which[1]

        def blocks(which, other=False):
            return chip_of(which) * 2 + ((1 - core) if other else core)

        gather = gather_parts(
            axes, gather_line, sent_ref.at[pl.ds(half, half)],
            lambda which, low, n, other=False: rows_in.at[1, blocks(which, other), pl.ds(low, n)],
            half, own_sem, place.twin, twin_later=True,
        )

        def sum_of(chunk, send_sem, recv_sem):
            return sum_parts(
                axes, Line(send_sem, recv_sem),
                lambda which, low, n: back.at[chunk, blocks(which), pl.ds(low, n)],
                back_stage.at[chunk], half, returned.at[pl.ds(chunk * half, half)],
                (place.twin, lambda which: back.at[chunk, blocks(which, True)],
                 lambda which: back_staged.at[chunk, chip_of(which)]),
            )

        sums = [sum_of(0, bs0, br0), sum_of(1, bs1, br1)]

        def loads(t):
            at = pl.ds(t * wide, wide)
            return [
                pltpu.make_async_copy(first_ref.at[at], rows_in.at[0, at], load_sem.at[t, 0]),
                pltpu.make_async_copy(
                    grad_ref.at[at, pl.ds(0, half)], grads.at[0, at], load_sem.at[t, 1]
                ),
            ]

        second_grads = pltpu.make_async_copy(
            grad_ref.at[:, pl.ds(half, half)], grads.at[1], load_sem.at[rounds, 0]
        )

        def box_copy(chunk, first, slot):
            return pltpu.make_async_copy(
                out_box.at[slot],
                out_terms.at[pl.ds(first, wide), pl.ds(chunk * half, half)],
                box_sem.at[slot],
            )

        rows_count = wide * half
        lanes = lane_of((rows_count, small))
        is_high, is_rest = lanes == shard, lanes == shard + GROUP

        def tile(chunk, first, slot, wait_first):
            at = pl.ds(first, wide)
            row_block = rows_in[chunk, at].reshape(rows_count, columns)
            gate = jnp.sum(
                jnp.where(is_high | is_rest, row_block[:, width:].astype(f32), 0.0),
                axis=1, keepdims=True,
            )
            gate_up = dot(row_block[:, :width], inner_ref[...])
            gate_part, up_part = gate_up[:, :hidden_width], gate_up[:, hidden_width:]
            sigmoid = 1.0 / (1.0 + jnp.exp(-gate_part))
            active = gate_part * sigmoid
            product = active * up_part
            hidden_low = product.astype(bf16)
            hidden[chunk, at] = hidden_low.reshape(wide, half, hidden_width)
            out_rows = (gate * dot(hidden_low, outer_ref[...])).astype(bf16)

            @pl.when(wait_first)
            def _():
                box_copy(chunk, first, slot).wait()

            out_box[slot] = out_rows.reshape(wide, half, width)
            box_copy(chunk, first, slot).start()
            grad = grads[chunk, at].reshape(rows_count, width)
            grad_hidden = dot_nt(grad, outer_ref[...])
            grad_gate = jnp.sum(grad_hidden * product, axis=1, keepdims=True)
            grad_hidden = grad_hidden * gate
            grad_gate_up = jnp.concatenate(
                [
                    grad_hidden * up_part * sigmoid * (1.0 + gate_part * (1.0 - sigmoid)),
                    grad_hidden * active,
                ],
                axis=1,
            ).astype(bf16)
            back_gu[chunk, at] = grad_gate_up.reshape(wide, half, 2 * hidden_width)
            grads[chunk, at] = (gate * grad.astype(f32)).astype(bf16).reshape(wide, half, width)
            grad_rows = dot_nt(grad_gate_up, inner_ref[...]).astype(bf16)
            back[chunk, at, :, pl.ds(0, width)] = grad_rows.reshape(wide, half, width)
            high = grad_gate.astype(bf16).astype(f32)
            tail = jnp.where(is_high, high, jnp.where(is_rest, grad_gate - high, 0.0))
            back[chunk, at, :, pl.ds(width, small)] = tail.astype(bf16).reshape(wide, half, small)

        for t in range(rounds):
            for load in loads(t):
                load.start()
        second_grads.start()
        greet(axes.neighbours() + [place.twin])
        next(gather)

        def first_tiles(t, carry):
            hooks(t, ((2, lambda: next(gather)),))
            for load in loads(t):
                load.wait()
            tile(0, t * wide, lax.rem(t, 2), t >= 2)
            return carry

        lax.fori_loop(0, rounds, first_tiles, 0)
        next(sums[0])
        next(gather)
        second_grads.wait()
        near, beyond = lax.div(axes.spot, 2), 1 - lax.div(axes.spot, 2)
        chips_per_round = wide // 2
        firsts = [
            (side * RING + part * chips_per_round) * 2
            for side, part in (
                (axes.side, beyond), (1 - axes.side, near), (1 - axes.side, beyond), (axes.side, near),
            )
        ]
        arrivals = gather_order(axes)

        def arrived(*numbers):
            for number in numbers:
                gather_line.take(
                    12 + number, lambda: rows_in.at[1, blocks(arrivals[number], True)], place.twin
                )

        def second_tiles(t, carry):
            hooks(
                t,
                (
                    (0, lambda: arrived(0, 1, 2, 4)),
                    (1, lambda: (next(sums[0]), next(sums[0]), arrived(3, 5, 6))[2]),
                    (2, lambda: (next(gather), arrived(7))[1]),
                    (3, lambda: (next(sums[1]), next(sums[0]))[0]),
                ),
            )
            tile(1, pick(t, firsts), lax.rem(t, 2), t >= 0)
            return carry

        lax.fori_loop(0, rounds, second_tiles, 0)
        next(sums[1])
        next(sums[1])

        def term_copy(low, slot):
            return pltpu.make_async_copy(
                term_box.at[slot], terms.at[pl.ds(low, 256)], term_sem.at[slot]
            )

        every = 2 * GROUP * half

        def keep(index, low, value):
            slot = lax.rem(index, 2)

            @pl.when(index >= 2)
            def _():
                term_copy(low, slot).wait()

            term_box[slot] = value.astype(bf16)
            term_copy(low, slot).start()

        downs = hidden_width // 256

        def down_terms(index, carry):
            at = chunk_256(index)
            value = dot_tn(hidden[:, :, :, at].reshape(every, 256), grads[...].reshape(every, width))
            keep(index, pl.multiple_of(width + index * 256, 256), value)
            return carry

        lax.fori_loop(0, downs, down_terms, 0)

        def inner_terms(index, carry):
            hooks(
                index,
                (
                    (0, lambda: next(sums[0])),
                    (1, lambda: next(sums[1])),
                ),
            )
            at = chunk_256(index)
            value = dot_tn(
                rows_in[:, :, :, at].reshape(every, 256),
                back_gu[...].reshape(every, 2 * hidden_width),
            )
            keep(index + downs, pl.multiple_of(index * 256, 256), value)
            return carry

        lax.fori_loop(0, width // 256, inner_terms, 0)
        drained(sums[0])
        drained(sums[1])
        drained(gather)
        for slot in range(2):
            box_copy(1, 0, slot).wait()
            term_copy(0, slot).wait()

    term_rows = width + hidden_width
    return pl.pallas_call(
        kernel,
        out_shape=[
            jax.ShapeDtypeStruct((count, columns), f32),
            jax.ShapeDtypeStruct((GROUP, count, width), bf16),
            jax.ShapeDtypeStruct((term_rows, width), bf16),
        ],
        in_specs=[ANY, ANY, ANY, IN_VMEM, IN_VMEM],
        out_specs=[IN_VMEM, ANY, ANY],
        scratch_shapes=[
            pltpu.VMEM((2, GROUP, half, columns), bf16),
            pltpu.VMEM((2, GROUP, half, width), bf16),
            pltpu.VMEM((2, GROUP, half, hidden_width), bf16),
            pltpu.VMEM((2, GROUP, half, 2 * hidden_width), bf16),
            pltpu.VMEM((2, GROUP, half, columns), bf16),
            pltpu.VMEM((2, chips, half, columns), bf16),
            pltpu.VMEM((2, stage_rows(half), columns), bf16),
            pltpu.VMEM((2, wide, half, width), bf16),
            pltpu.VMEM((2, 256, width), bf16),
        ]
        + sems(GATHER_SEMS)
        + sems(SUM_SEMS) * 2
        + [
            pltpu.SemaphoreType.DMA,
            pltpu.SemaphoreType.DMA((rounds + 1, 2)),
            pltpu.SemaphoreType.DMA((2,)),
            pltpu.SemaphoreType.DMA((2,)),
        ],
        compiler_params=params(collective_id),
    )(sent, rows_first, grad_all, inner, outer)


WIDTH = 1024
QUERY = HEADS * HEAD_DIM
KEY = KV_HEADS * HEAD_DIM
EXPERTS = 16
SMALL = 128
LANES = 128
AT_K = QUERY
AT_V = AT_K + KEY
AT_S = AT_V + KEY
AT_O = AT_S + SMALL
PACKED = AT_O + WIDTH
ROWS_OWN = WIDTH // GROUP
KGAIN_OWN = KEY // GROUP
HEAD_PAIRS = KV_HEADS // 2
REST = 2 * KEY + SMALL
DENSE = QUERY + WIDTH + 2 * KEY


def drained(part):
    for _ in part:
        pass


def hooks(index, steps):
    for at, step in steps:
        pl.when(index == at)(step)


def chunk_256(index):
    return pl.ds(pl.multiple_of(index * 256, 256), 256)


def root_mean(values):
    return lax.rsqrt(jnp.mean(values * values, axis=1, keepdims=True) + norm_eps)


def lane_of(shape):
    return lax.broadcasted_iota(jnp.int32, shape, 1)


def turned(values, cosine, sine):
    first = (lane_of(values.shape) & (HEAD_DIM - 1)) < HEAD_DIM // 2
    swapped = jnp.where(
        first, pltpu.roll(values, LANES - HEAD_DIM // 2, 1), pltpu.roll(values, HEAD_DIM // 2, 1)
    )
    return values * cosine + swapped * sine


def gain_rows(small):
    rows = jnp.transpose(small.astype(f32))
    short = small.reshape(GROUP, ROWS_OWN, SMALL)[:, :KGAIN_OWN].reshape(KEY, SMALL)
    gain_k = jnp.transpose(short.astype(f32))[EXPERTS + 3 : EXPERTS + 4]
    return rows[EXPERTS : EXPERTS + 1], rows[EXPERTS + 1 : EXPERTS + 2], rows[EXPERTS + 2 : EXPERTS + 3], gain_k


def long_column(columns):
    cut = columns.reshape(GROUP, KGAIN_OWN, SMALL)
    return jnp.concatenate([cut, jnp.zeros_like(cut)], axis=1).reshape(WIDTH, SMALL)


def four_heads(chunk_a, chunk_b):
    low = lane_of(chunk_a.shape) < HEAD_DIM
    zero = jnp.zeros_like(chunk_a)
    return jnp.concatenate(
        [
            jnp.where(low, chunk_a, zero),
            jnp.where(low, pltpu.roll(chunk_a, HEAD_DIM, 1), zero),
            jnp.where(low, zero, pltpu.roll(chunk_b, HEAD_DIM, 1)),
            jnp.where(low, zero, chunk_b),
        ],
        axis=0,
    )


def two_chunks(blocks):
    rows = blocks.shape[0] // 4
    one, two, three, four = (blocks[n * rows : (n + 1) * rows] for n in range(4))
    low = lane_of(one.shape) < HEAD_DIM
    return (
        jnp.where(low, one, pltpu.roll(two, HEAD_DIM, 1)),
        jnp.where(low, pltpu.roll(three, HEAD_DIM, 1), four),
    )


def chunk_at(index, base=0):
    return pl.ds(pl.multiple_of(base + index * LANES, LANES), LANES)


def front_call(collective_id, tokens, cotangent, weights_own, gains, router, cosine, sine, routes, starts):
    count, width = tokens.shape
    seqs = starts.shape[0]
    positions = count // seqs
    length = REPS * positions
    score_scale = HEAD_DIM ** (-0.5)
    sent_width = width + SMALL

    def kernel(
        starts_ref, tokens_ref, grad_ref, query_w, key_w, value_w, output_w,
        gain_a_ref, gain_q_ref, gain_f_ref, gain_k_ref, router_ref, cos_ref, sin_ref, routes_ref,
        dense_out, grad_all, pairs_out, soft_out, rows_first,
        attn_in, query_raw, key_raw, query_low, mixed, middle, sent, gates_out,
        packed, small_box, dense, pairs, pair_own, soft_box, bias_box,
        ws0, wr0, ws1, wr1, ws2, wr2, gs0, gr0, gs1, gr1, ks0, kr0, ks1, kr1, rs, rr, own_sem, out_sem, soft_sem, pack_sem,
    ):
        place = Place()
        core = place.core
        packing = [
            pltpu.make_async_copy(
                source, packed.at[:, pl.ds(low, source.shape[1])], pack_sem.at[index]
            )
            for index, (source, low) in enumerate(
                ((key_w, AT_K), (value_w, AT_V), (query_w, 0), (output_w, AT_O))
            )
        ]
        for copy in packing:
            copy.start()
        small_box[...] = jnp.zeros_like(small_box)
        small_box[pl.ds(0, EXPERTS), pl.ds(0, ROWS_OWN)] = router_ref[...].astype(f32)
        for at, ref in enumerate((gain_a_ref, gain_q_ref, gain_f_ref, gain_k_ref)):
            size = ref.shape[0]
            small_box[pl.ds(EXPERTS + at, 1), pl.ds(0, size)] = (
                ref[...].astype(f32).reshape(1, size)
            )
        packed[:, pl.ds(AT_S, SMALL)] = jnp.transpose(small_box[...])[:ROWS_OWN].astype(bf16)

        def token_block(index, low, size):
            def block(which, row, n, other=False):
                at = (which[0] * RING + which[1]) * 2 + ((1 - core) if other else core)
                return dense.at[at, pl.ds(row, n), pl.ds(low, size)]

            return block

        def weight_gather(index, low, size, send_sem, recv_sem):
            return gather_parts(
                place.tokens, Line(send_sem, recv_sem), packed.at[:, pl.ds(low, size)],
                token_block(index, low, size), ROWS_OWN, own_sem.at[index], place.twin,
            )

        def rows_of(target):
            def block(which, row, n, other=False):
                at = (which[0] * RING + which[1]) * 2 + ((1 - core) if other else core)
                return target.at[at, pl.ds(row, n)]

            return block

        def pair_gather(seq, send_sem, recv_sem):
            def block(which, row, n, other=False):
                return pairs.at[seq, which[0] * RING + which[1], pl.ds(row, n)]

            return gather_parts(
                place.copies, Line(send_sem, recv_sem),
                pair_own.at[pl.ds(seq * positions, positions)], block, positions, own_sem.at[3 + seq],
            )

        def soft_copy(seq, index, slot):
            return pltpu.make_async_copy(
                soft_box.at[slot], soft_out.at[seq, index], soft_sem.at[slot]
            )

        rest_gather = weight_gather(0, AT_K, REST, ws0, wr0)
        query_gather = weight_gather(1, 0, QUERY, ws1, wr1)
        output_gather = weight_gather(2, AT_O, WIDTH, ws2, wr2)
        def grad_gather(seq, send_sem, recv_sem):
            base = seq * positions

            def block(which, row, n, other=False):
                at = (which[0] * RING + which[1]) * 2 + ((1 - core) if other else core)
                return grad_all.at[at, pl.ds(base + row, n)]

            return gather_parts(
                place.tokens, Line(send_sem, recv_sem), grad_ref.at[pl.ds(base, positions)], block,
                positions, own_sem.at[5 + seq], place.twin,
            )

        grads = [grad_gather(0, gs0, gr0), grad_gather(1, gs1, gr1)]
        first_rows = gather_parts(
            place.tokens, Line(rs, rr), sent.at[pl.ds(0, positions)], rows_of(rows_first), positions,
            own_sem.at[7], place.twin,
        )
        pair_gathers = [pair_gather(0, ks0, kr0), pair_gather(1, ks1, kr1)]

        greet(place.tokens.neighbours() + place.copies.neighbours() + [place.twin])
        for copy in packing:
            copy.wait()
        next(rest_gather)
        inputs = tokens_ref[...].astype(f32)
        middle[...] = inputs * root_mean(inputs)
        next(rest_gather)
        next(query_gather)
        query_at = place.rep * positions + lax.broadcasted_iota(jnp.int32, (positions, 1), 0)
        key_at = lax.broadcasted_iota(jnp.int32, (1, length), 1)
        for seq in range(seqs):
            allowed = key_at <= query_at
            for piece in range(starts_ref.shape[1]):
                start = starts_ref[seq, piece]
                query_inside = (query_at >= start) & (query_at < start + PIC)
                key_inside = (key_at >= start) & (key_at < start + PIC)
                allowed = allowed | (query_inside & key_inside)
            bias_box[seq] = jnp.where(allowed, 0.0, masked_score)
        next(rest_gather)
        next(query_gather)
        next(output_gather)
        drained(rest_gather)
        next(query_gather)
        next(output_gather)

        def weights(low, size):
            return dense[:, :, pl.ds(low, size)].reshape(width, size)

        small = weights(AT_S, SMALL)
        gain_a, gain_q, gain_f, gain_k = gain_rows(small)
        rows = (middle[...] * gain_a).astype(bf16)
        attn_in[...] = rows
        cos2 = jnp.concatenate([cos_ref[...]] * seqs, axis=0)
        sin2 = jnp.concatenate([sin_ref[...]] * seqs, axis=0)
        raw = dot(rows, weights(AT_K, KEY))
        key_raw[...] = raw
        scaled = raw * root_mean(raw) * gain_k
        for chunk in range(KEY // LANES):
            at = slice(chunk * LANES, (chunk + 1) * LANES)
            pair_own[:, at] = turned(scaled[:, at], cos2, sin2).astype(bf16)
        pair_own[:, KEY:] = dot(rows, weights(AT_V, KEY)).astype(bf16)
        next(pair_gathers[0])
        drained(query_gather)
        next(output_gather)
        next(grads[0])
        raw = dot(rows, weights(0, QUERY))
        query_raw[...] = raw
        scaled = raw * root_mean(raw) * gain_q
        for chunk in range(QUERY // LANES):
            at = slice(chunk * LANES, (chunk + 1) * LANES)
            query_low[:, at] = turned(scaled[:, at], cos2, sin2).astype(bf16)
        next(pair_gathers[0])
        next(pair_gathers[1])
        drained(output_gather)
        dense_copy = pltpu.make_async_copy(dense, dense_out, out_sem.at[0])
        dense_copy.start()
        next(grads[0])
        next(grads[1])
        next(pair_gathers[0])
        next(pair_gathers[1])
        next(grads[0])
        drained(pair_gathers[0])
        next(grads[1])

        def attend(seq, index, slot, wait_first):
            rows_at = pl.ds(seq * positions, positions)
            queries = four_heads(
                query_low[rows_at, chunk_at(2 * index)].astype(f32),
                query_low[rows_at, chunk_at(2 * index + 1)].astype(f32),
            )
            queries = (queries * score_scale).astype(bf16)
            keys = pairs[seq, :, :, chunk_at(index)].reshape(length, LANES)
            scores = dot_nt(queries, keys).reshape(4, positions, length) + bias_box[seq][None]
            scores = scores.reshape(4 * positions, length)
            raised = jnp.exp(scores - jnp.max(scores, axis=1, keepdims=True))
            soft = (raised * (1.0 / jnp.sum(raised, axis=1, keepdims=True))).astype(bf16)

            @pl.when(wait_first)
            def _():
                soft_copy(seq, index, slot).wait()

            soft_box[slot] = soft
            soft_copy(seq, index, slot).start()
            values = pairs[seq, :, :, chunk_at(index, KEY)].reshape(length, LANES)
            chunk_a, chunk_b = two_chunks(dot(soft, values))
            mixed[rows_at, chunk_at(2 * index)] = chunk_a.astype(bf16)
            mixed[rows_at, chunk_at(2 * index + 1)] = chunk_b.astype(bf16)

        def features(seq):
            at = pl.ds(seq * positions, positions)
            total = tokens_ref[at].astype(f32) + dot(mixed[at], weights(AT_O, WIDTH))
            middle[at] = total
            ffn_in = (total * root_mean(total) * gain_f).astype(bf16)
            sent[at, pl.ds(0, width)] = ffn_in
            lanes = lane_of((positions, SMALL))
            named = jnp.transpose(routes_ref[seq].astype(f32)).astype(jnp.int32)
            chosen = lanes == named[:, :1]
            for choice in range(1, named.shape[1]):
                chosen = chosen | (lanes == named[:, choice : choice + 1])
            logits = jnp.where(chosen, dot(ffn_in, small), masked_score)
            raised = jnp.exp(logits - jnp.max(logits, axis=1, keepdims=True))
            gates = raised * (1.0 / jnp.sum(raised, axis=1, keepdims=True))
            gates = jnp.where(chosen, gates, 0.0)
            gates_out[at] = gates
            high = gates.astype(bf16).astype(f32)
            tail = high + pltpu.roll(gates - high, EXPERTS, 1)
            sent[at, pl.ds(width, SMALL)] = tail.astype(bf16)

        def first_heads(index, carry):
            hooks(
                index,
                (
                    (1, lambda: next(grads[0])),
                    (2, lambda: next(pair_gathers[1])),
                    (3, lambda: next(grads[1])),
                ),
            )
            attend(0, index, lax.rem(index, 2), index >= 2)
            return carry

        lax.fori_loop(0, HEAD_PAIRS, first_heads, 0)
        features(0)
        next(first_rows)
        drained(pair_gathers[1])
        pairs_copy = pltpu.make_async_copy(pairs, pairs_out, out_sem.at[1])
        pairs_copy.start()

        def second_heads(index, carry):
            hooks(
                index,
                (
                    (1, lambda: next(grads[1])),
                    (3, lambda: next(first_rows)),
                ),
            )
            attend(1, index, lax.rem(index, 2), index >= 0)
            return carry

        lax.fori_loop(0, HEAD_PAIRS, second_heads, 0)
        features(1)
        next(first_rows)
        drained(grads[0])
        drained(grads[1])
        drained(first_rows)
        dense_copy.wait()
        pairs_copy.wait()
        for slot in range(2):
            soft_copy(1, 0, slot).wait()

    return pl.pallas_call(
        kernel,
        out_shape=[
            jax.ShapeDtypeStruct((GROUP, ROWS_OWN, PACKED), bf16),
            jax.ShapeDtypeStruct((GROUP, count, width), bf16),
            jax.ShapeDtypeStruct((seqs, REPS, positions, 2 * KEY), bf16),
            jax.ShapeDtypeStruct((seqs, HEAD_PAIRS, 4 * positions, length), bf16),
            jax.ShapeDtypeStruct((GROUP, positions, sent_width), bf16),
            jax.ShapeDtypeStruct((count, width), bf16),
            jax.ShapeDtypeStruct((count, QUERY), f32),
            jax.ShapeDtypeStruct((count, KEY), f32),
            jax.ShapeDtypeStruct((count, QUERY), bf16),
            jax.ShapeDtypeStruct((count, QUERY), bf16),
            jax.ShapeDtypeStruct((count, width), f32),
            jax.ShapeDtypeStruct((count, width + SMALL), bf16),
            jax.ShapeDtypeStruct((count, SMALL), f32),
        ],
        in_specs=[pl.BlockSpec(memory_space=pltpu.SMEM), IN_VMEM] + [ANY] * 5 + [IN_VMEM] * 8,
        out_specs=[ANY] * 5 + [IN_VMEM] * 8,
        scratch_shapes=[
            pltpu.VMEM((ROWS_OWN, PACKED), bf16),
            pltpu.VMEM((SMALL, LANES), f32),
            pltpu.VMEM((GROUP, ROWS_OWN, PACKED), bf16),
            pltpu.VMEM((seqs, REPS, positions, 2 * KEY), bf16),
            pltpu.VMEM((count, 2 * KEY), bf16),
            pltpu.VMEM((2, 4 * positions, length), bf16),
            pltpu.VMEM((seqs, positions, length), f32),
        ]
        + sems(GATHER_SEMS) * 8
        + [
            pltpu.SemaphoreType.DMA((8,)),
            pltpu.SemaphoreType.DMA((2,)),
            pltpu.SemaphoreType.DMA((2,)),
            pltpu.SemaphoreType.DMA((4,)),
        ],
        compiler_params=params(collective_id),
    )(starts, tokens, cotangent, *weights_own, *gains, router, cosine, sine, routes)


def key_chunk(index, base=0):
    low = lax.div(index, 2) * KEY + lax.rem(index, 2) * LANES + base
    return pl.ds(pl.multiple_of(low, LANES), LANES)


def norm_back(values, gain, grad):
    scale = root_mean(values)
    weighted = grad * gain
    mean = jnp.mean(values * weighted, axis=1, keepdims=True)
    inner = weighted * scale - values * (scale * scale * scale * mean)
    return inner, jnp.sum(grad * values * scale, axis=0, keepdims=True)


def back_call(
    collective_id, returned, gates, middle, sent, dense, cotangent, tokens, attn_in, query_raw, key_raw,
    query_low, mixed, pairs, soft, out_terms, expert_terms, cosine, sine,
):
    count, width = tokens.shape
    seqs, _, positions, _ = pairs.shape
    length = REPS * positions
    expert_rows = expert_terms.shape[0] // REPS
    side_rows = RING * expert_rows
    score_scale = HEAD_DIM ** (-0.5)
    chips = GROUP // 2

    def kernel(
        returned_ref, gates_ref, middle_ref, sent_ref, dense_ref, grad_ref, tokens_ref, attn_ref,
        query_raw_ref, key_raw_ref, query_ref, mixed_ref, pairs_ref, soft_ref, out_ref, expert_ref,
        cos_ref, sin_ref,
        block_out, tokens_grad, small_out, dense_out, expert_all,
        weight_box, weight_rest, wide_terms, rest_terms, dense_own,
        wide_staged, rest_staged, wide_stage, rest_stage,
        out_held, out_staged, out_stage, small_terms, small_staged, small_stage, small_own,
        expert_stage, expert_own,
        soft_box, key_box, value_box, pair_terms, pair_stage, pair_grads,
        grad_mixed, grad_query, grad_middle, grad_attn, grad_attn_in, gain_box,
        wide_got, rest_got, small_got, wide_total_box, rest_total_box,
        out_s, out_r, exp_s, exp_r, small_s, small_r, kv0_s, kv0_r, kva_s, kva_r, kvb_s, kvb_r, wide_s, wide_r, rest_s, rest_r,
        ge_s, ge_r, gwide_s, gwide_r, grest_s, grest_r, gsmall_s, gsmall_r,
        load_sem, held_sem, box_sem, own_sem, total_sem,
    ):
        place = Place()
        core = place.core
        token_axes, copy_axes = place.tokens, place.copies

        def chip_of(which):
            return which[0] * RING + which[1]

        def blocks(which, other=False):
            return chip_of(which) * 2 + ((1 - core) if other else core)

        def out_store(low, step, value):
            at = pl.ds(low, step)
            block_out[at] = (middle_ref[at] + value).astype(bf16)

        out_sum = sum_parts(
            token_axes, Line(out_s, out_r),
            lambda which, low, n: out_held.at[chip_of(which), pl.ds(low, n)],
            out_stage, count, None,
            (place.twin, lambda which: out_ref.at[blocks(which, True)],
             lambda which: out_staged.at[chip_of(which)]),
            store=out_store,
        )
        def expert_part(which, low, n):
            columns = pl.ds(pl.multiple_of(which[0] * width, width), width)
            return wide_terms.at[pl.ds(which[1] * expert_rows + low, n), columns]

        expert_sum = sum_parts(
            copy_axes, Line(exp_s, exp_r), expert_part, expert_stage, expert_rows, expert_own
        )

        def pair_sum(seq, low, size, index, send_sem, recv_sem):
            columns = pl.ds(low, size)
            return sum_parts(
                copy_axes, Line(send_sem, recv_sem),
                lambda which, row, n: pair_terms.at[seq, chip_of(which), pl.ds(row, n), columns],
                pair_stage.at[index, :, columns], positions,
                pair_grads.at[pl.ds(seq * positions, positions), columns],
            )

        first_pairs = pair_sum(0, 0, 2 * KEY, 0, kv0_s, kv0_r)
        second_pairs = [
            pair_sum(1, 0, KEY, 1, kva_s, kva_r), pair_sum(1, KEY, KEY, 1, kvb_s, kvb_r)
        ]

        def rows_of_block(terms, index, low, n):
            return terms.at[pl.ds(index * ROWS_OWN + low, n)]

        def dense_sum(terms, staged, stage, own, send_sem, recv_sem):
            return sum_parts(
                token_axes, Line(send_sem, recv_sem),
                lambda which, row, n: rows_of_block(terms, blocks(which), row, n),
                stage, ROWS_OWN, own,
                (place.twin, lambda which: rows_of_block(terms, blocks(which, True), 0, ROWS_OWN),
                 lambda which: staged.at[chip_of(which)]),
            )

        wide_sum = dense_sum(
            wide_terms, wide_staged, wide_stage, dense_own.at[:, pl.ds(0, QUERY + width)], wide_s, wide_r
        )
        rest_sum = dense_sum(
            rest_terms, rest_staged, rest_stage, dense_own.at[:, pl.ds(QUERY + width, 2 * KEY)],
            rest_s, rest_r,
        )
        small_sum = dense_sum(small_terms, small_staged, small_stage, small_own, small_s, small_r)

        def dense_total(index, low, size, got, total, send_sem, recv_sem):
            share = size // REPS

            def columns(rep):
                return pl.ds(pl.multiple_of(low + rep * share, LANES), share)

            return total_parts(
                place, Line(send_sem, recv_sem), lambda rep: dense_own.at[:, columns(rep)], got, total,
                lambda rep: dense_out.at[:, columns(rep)], total_sem.at[index],
            )

        wide_total = dense_total(0, 0, QUERY + width, wide_got, wide_total_box, gwide_s, gwide_r)
        rest_total = dense_total(
            1, QUERY + width, 2 * KEY, rest_got, rest_total_box, grest_s, grest_r
        )
        small_total = spread_parts(place, Line(gsmall_s, gsmall_r), small_own, small_got, small_out)
        expert_gather = gather_parts(
            copy_axes, Line(ge_s, ge_r), expert_own,
            lambda which, row, n, other=False: expert_all.at[chip_of(which), pl.ds(row, n)],
            expert_rows, own_sem,
        )

        def begin(part):
            for _ in range(3):
                next(part)

        def weight_load(low, index):
            return pltpu.make_async_copy(
                dense_ref.at[:, :, pl.ds(low, width)], weight_box, load_sem.at[index]
            )

        rest_load = pltpu.make_async_copy(
            dense_ref.at[:, :, pl.ds(AT_K, REST)], weight_rest, load_sem.at[1]
        )
        expert_loads = [
            pltpu.make_async_copy(
                expert_ref.at[pl.ds(side * side_rows, side_rows)],
                wide_terms.at[pl.ds(0, side_rows), pl.ds(side * width, width)],
                load_sem.at[(2, 4)[side]],
            )
            for side in range(2)
        ]
        held_loads = [
            pltpu.make_async_copy(
                out_ref.at[2 * chip + core], out_held.at[chip], held_sem.at[chip]
            )
            for chip in range(chips)
        ]

        def box_loads(number, slot):
            seq, index = lax.div(number, HEAD_PAIRS), lax.rem(number, HEAD_PAIRS)
            return [
                pltpu.make_async_copy(
                    soft_ref.at[seq, index], soft_box.at[slot], box_sem.at[slot, 0]
                ),
                pltpu.make_async_copy(
                    pairs_ref.at[seq, :, :, chunk_at(index)], key_box.at[slot], box_sem.at[slot, 1]
                ),
                pltpu.make_async_copy(
                    pairs_ref.at[seq, :, :, chunk_at(index, KEY)],
                    value_box.at[slot],
                    box_sem.at[slot, 2],
                ),
            ]

        for load in expert_loads:
            load.start()
        rest_load.start()
        weight_load(AT_O, 0).start()
        for load in held_loads + box_loads(0, 0):
            load.start()
        greet(
            token_axes.neighbours()
            + [place.twin]
            + [(place.shard, other) for other in place.others[1:]]
        )
        next(out_sum)
        for load in expert_loads:
            load.wait()
        begin(expert_sum)
        rest_load.wait()

        small = weight_rest[:, :, pl.ds(2 * KEY, SMALL)].reshape(width, SMALL)
        gain_a, gain_q, gain_f, gain_k = gain_rows(small)
        gates = gates_ref[...]
        tail = returned_ref[:, pl.ds(width, SMALL)].astype(f32)
        grad_gates = tail + pltpu.roll(tail, SMALL - EXPERTS, 1)
        grad_logits = gates * (grad_gates - jnp.sum(gates * grad_gates, axis=1, keepdims=True))
        grad_logits = grad_logits.astype(bf16)
        grad_ffn = returned_ref[:, pl.ds(0, width)].astype(f32) + dot_nt(grad_logits, small)
        inner, gain_f_terms = norm_back(middle_ref[...], gain_f, grad_ffn)
        inner = grad_ref[...].astype(f32) + inner
        grad_middle[...] = inner
        grad_attn[...] = inner.astype(bf16)
        gain_box[...] = jnp.zeros_like(gain_box)
        gain_box[pl.ds(EXPERTS + 2, 1)] = gain_f_terms
        weight_load(AT_O, 0).wait()
        grad_mixed[...] = dot_nt(
            grad_attn[...], weight_box[...].reshape(QUERY, width)
        ).astype(bf16)
        weight_load(0, 3).start()

        def attend_back(seq, index):
            number = seq * HEAD_PAIRS + index
            slot = lax.rem(number, 2)
            for load in box_loads(number, slot):
                load.wait()

            @pl.when(number + 1 < seqs * HEAD_PAIRS)
            def _():
                for load in box_loads(number + 1, 1 - slot):
                    load.start()

            rows_at = pl.ds(seq * positions, positions)
            first, second = chunk_at(2 * index), chunk_at(2 * index + 1)
            queries = four_heads(
                query_ref[rows_at, first].astype(f32), query_ref[rows_at, second].astype(f32)
            )
            queries = (queries * score_scale).astype(bf16)
            grads = four_heads(
                grad_mixed[rows_at, first].astype(f32), grad_mixed[rows_at, second].astype(f32)
            ).astype(bf16)
            keys = key_box[slot].reshape(length, LANES)
            values = value_box[slot].reshape(length, LANES)
            soft_low = soft_box[slot]
            value_terms = dot_tn(soft_low, grads)
            pair_terms[seq, :, :, key_chunk(index, KEY // 2)] = value_terms.astype(bf16).reshape(
                REPS, positions, LANES
            )
            soft_full = soft_low.astype(f32)
            grad_soft = dot_nt(grads, values)
            weighted = soft_full * grad_soft
            grad_scores = (
                weighted - soft_full * jnp.sum(weighted, axis=1, keepdims=True)
            ).astype(bf16)
            key_terms = dot_tn(grad_scores, queries)
            pair_terms[seq, :, :, key_chunk(index)] = key_terms.astype(bf16).reshape(
                REPS, positions, LANES
            )
            chunk_a, chunk_b = two_chunks(dot(grad_scores, keys) * score_scale)
            grad_query[rows_at, first] = chunk_a.astype(bf16)
            grad_query[rows_at, second] = chunk_b.astype(bf16)

        def out_ready():
            for load in held_loads:
                load.wait()
            next(out_sum)
            next(out_sum)

        def first_heads(index, carry):
            hooks(index, ((2, lambda: next(expert_sum)), (3, out_ready)))
            attend_back(0, index)
            return carry

        lax.fori_loop(0, HEAD_PAIRS, first_heads, 0)
        begin(first_pairs)

        def second_heads(index, carry):
            hooks(
                index,
                (
                    (2, lambda: begin(second_pairs[0])),
                    (3, lambda: (next(out_sum), next(expert_sum))[0]),
                ),
            )
            attend_back(1, index)
            return carry

        lax.fori_loop(0, HEAD_PAIRS, second_heads, 0)
        begin(second_pairs[1])
        next(second_pairs[0])
        router_terms = dot_tn(sent_ref[:, pl.ds(0, width)], grad_logits)

        cos2 = jnp.concatenate([cos_ref[...]] * seqs, axis=0)
        sin2 = -jnp.concatenate([sin_ref[...]] * seqs, axis=0)

        def turned_back(values):
            return jnp.concatenate(
                [
                    turned(values[:, low : low + LANES], cos2, sin2)
                    for low in range(0, values.shape[1], LANES)
                ],
                axis=1,
            )

        grad, gain_q_terms = norm_back(
            query_raw_ref[...], gain_q, turned_back(grad_query[...].astype(f32))
        )
        gain_box[pl.ds(EXPERTS + 1, 1)] = gain_q_terms
        grad_query_low = grad.astype(bf16)
        weight_load(0, 3).wait()
        grad_attn_in[...] = dot_nt(grad_query_low, weight_box[...].reshape(width, QUERY))

        next(first_pairs)
        next(second_pairs[1])
        next(first_pairs)
        next(second_pairs[0])

        drained(expert_sum)

        def q_rows(index, carry):
            at = chunk_256(index)
            wide_terms[at, pl.ds(0, QUERY)] = dot_tn(attn_ref[:, at], grad_query_low).astype(bf16)
            wide_terms[at, pl.ds(QUERY, width)] = dot_tn(mixed_ref[:, at], grad_attn[...]).astype(bf16)
            return carry

        lax.fori_loop(0, width // 256, q_rows, 0)
        next(wide_sum)
        next(second_pairs[1])
        next(out_sum)
        next(wide_sum)
        next(wide_sum)
        drained(first_pairs)
        drained(second_pairs[0])
        drained(second_pairs[1])
        next(expert_gather)

        grads = pair_grads[...]
        half = KEY // 2
        key_grads = jnp.concatenate([grads[:, :half], grads[:, KEY : KEY + half]], axis=1)
        value_grads = jnp.concatenate([grads[:, half:KEY], grads[:, KEY + half :]], axis=1)
        grad, gain_k_terms = norm_back(
            key_raw_ref[...], gain_k, turned_back(key_grads.astype(bf16).astype(f32))
        )
        grad_pairs = jnp.concatenate([grad.astype(bf16), value_grads.astype(bf16)], axis=1)

        def rest_rows(index, carry):
            at = chunk_256(index)
            rest_terms[at] = dot_tn(attn_ref[:, at], grad_pairs).astype(bf16)
            return carry

        lax.fori_loop(0, width // 256, rest_rows, 0)
        next(rest_sum)
        grad = grad_attn_in[...] + dot_nt(
            grad_pairs, weight_rest[:, :, pl.ds(0, 2 * KEY)].reshape(width, 2 * KEY)
        )
        next(rest_sum)
        next(rest_sum)
        values = tokens_ref[...].astype(f32)
        inner, gain_a_terms = norm_back(values, gain_a, grad)
        gain_box[pl.ds(EXPERTS, 1)] = gain_a_terms
        lanes = lane_of((KEY, SMALL))
        gain_k_column = jnp.where(
            lanes == EXPERTS + 3,
            jnp.transpose(jnp.broadcast_to(gain_k_terms, (SMALL, KEY))),
            0.0,
        )
        small_terms[...] = (
            router_terms + jnp.transpose(gain_box[...]) + long_column(gain_k_column)
        ).astype(bf16)
        next(small_sum)
        tokens_grad[...] = (grad_middle[...] + inner).astype(bf16)
        next(small_sum)
        next(small_sum)
        next(wide_sum)
        next(rest_sum)
        next(expert_gather)
        next(small_sum)
        next(wide_sum)
        next(small_sum)
        next(rest_sum)
        drained(out_sum)
        drained(wide_sum)
        next(wide_total)
        drained(small_sum)
        next(small_total)
        next(expert_gather)
        drained(rest_sum)
        next(rest_total)
        next(wide_total)
        next(expert_gather)
        drained(small_total)
        next(rest_total)
        drained(expert_gather)
        drained(wide_total)
        drained(rest_total)

    block = pltpu.VMEM((GROUP, ROWS_OWN, width), bf16)
    scratch = [
        block,
        pltpu.VMEM((GROUP, ROWS_OWN, REST), bf16),
        pltpu.VMEM((width, QUERY + width), bf16),
        pltpu.VMEM((width, 2 * KEY), bf16),
        pltpu.VMEM((ROWS_OWN, DENSE), bf16),
        pltpu.VMEM((chips, ROWS_OWN, QUERY + width), bf16),
        pltpu.VMEM((chips, ROWS_OWN, 2 * KEY), bf16),
        pltpu.VMEM((stage_rows(ROWS_OWN), QUERY + width), bf16),
        pltpu.VMEM((stage_rows(ROWS_OWN), 2 * KEY), bf16),
        pltpu.VMEM((chips, count, width), bf16),
        pltpu.VMEM((chips, count, width), bf16),
        pltpu.VMEM((stage_rows(count), width), bf16),
        pltpu.VMEM((width, SMALL), bf16),
        pltpu.VMEM((chips, ROWS_OWN, SMALL), bf16),
        pltpu.VMEM((stage_rows(ROWS_OWN), SMALL), bf16),
        pltpu.VMEM((ROWS_OWN, SMALL), bf16),
        pltpu.VMEM((stage_rows(expert_rows), width), bf16),
        pltpu.VMEM((expert_rows, width), bf16),
        pltpu.VMEM((2, 4 * positions, length), bf16),
        pltpu.VMEM((2, REPS, positions, LANES), bf16),
        pltpu.VMEM((2, REPS, positions, LANES), bf16),
        pltpu.VMEM((seqs, REPS, positions, 2 * KEY), bf16),
        pltpu.VMEM((seqs, stage_rows(positions), 2 * KEY), bf16),
        pltpu.VMEM((count, 2 * KEY), f32),
        pltpu.VMEM((count, QUERY), bf16),
        pltpu.VMEM((count, QUERY), bf16),
        pltpu.VMEM((count, width), f32),
        pltpu.VMEM((count, width), bf16),
        pltpu.VMEM((count, width), f32),
        pltpu.VMEM((SMALL, width), f32),
    ]
    wide_share, rest_share = (QUERY + width) // REPS, 2 * KEY // REPS
    scratch += [
        pltpu.VMEM((REPS, ROWS_OWN, wide_share), bf16),
        pltpu.VMEM((REPS, ROWS_OWN, rest_share), bf16),
        pltpu.VMEM((REPS, ROWS_OWN, SMALL), bf16),
        pltpu.VMEM((ROWS_OWN, wide_share), bf16),
        pltpu.VMEM((ROWS_OWN, rest_share), bf16),
    ]
    return pl.pallas_call(
        kernel,
        out_shape=[
            jax.ShapeDtypeStruct((count, width), bf16),
            jax.ShapeDtypeStruct((count, width), bf16),
            jax.ShapeDtypeStruct((ROWS_OWN, SMALL), f32),
            jax.ShapeDtypeStruct((ROWS_OWN, DENSE), bf16),
            jax.ShapeDtypeStruct((REPS, expert_rows, width), bf16),
        ],
        in_specs=[IN_VMEM] * 4 + [ANY] + [IN_VMEM] * 7 + [ANY] * 4 + [IN_VMEM] * 2,
        out_specs=[IN_VMEM, IN_VMEM, IN_VMEM, ANY, ANY],
        scratch_shapes=scratch
        + sems(SUM_SEMS) * 8
        + sems(GATHER_SEMS)
        + sems(TOTAL_SEMS) * 3
        + [
            pltpu.SemaphoreType.DMA((5,)),
            pltpu.SemaphoreType.DMA((chips,)),
            pltpu.SemaphoreType.DMA((2, 3)),
            pltpu.SemaphoreType.DMA,
            pltpu.SemaphoreType.DMA((2,)),
        ],
        compiler_params=params(collective_id),
    )(
        returned, gates, middle, sent, dense, cotangent, tokens, attn_in, query_raw, key_raw,
        query_low, mixed, pairs, soft, out_terms, expert_terms, cosine, sine,
    )


def finish_call(block_out, tokens_grad, small_sum, dense_own, expert_all, inner_rows):
    total_rows, width = expert_all.shape
    step = 256
    inner_steps, steps = inner_rows // step, total_rows // step
    rows = block_out.shape[0] // inner_steps

    def kernel(
        block_ref, tokens_ref, small_ref, dense_ref, expert_ref,
        block, tokens, inner, outer, query, key, value, output, router, gain_a, gain_q, gain_f, gain_k,
    ):
        at = pl.program_id(0)

        @pl.when(at < inner_steps)
        def _():
            block[...] = block_ref[...]
            tokens[...] = tokens_ref[...]
            inner[...] = expert_ref[...].astype(f32)

        @pl.when(at >= inner_steps)
        def _():
            outer[...] = expert_ref[...].astype(f32)

        @pl.when(at == 1)
        def _():
            at_k = QUERY + WIDTH
            for low, target in ((0, query), (at_k, key), (at_k + KEY, value), (QUERY, output)):
                target[...] = dense_ref[:, pl.ds(low, target.shape[1])].astype(f32)
            turned_small = jnp.transpose(small_ref[...])
            router[...] = turned_small[:EXPERTS, :ROWS_OWN]
            for index, target in enumerate((gain_a, gain_q, gain_f, gain_k)):
                size = target.shape[0]
                target[...] = turned_small[EXPERTS + index, :size].reshape(size)

    def whole(*shape):
        return pl.BlockSpec(shape, lambda i: (0,) * len(shape))

    def by_rows(size):
        return pl.BlockSpec((size, width), lambda i: (jnp.minimum(i, inner_steps - 1), 0))

    shapes = [(ROWS_OWN, QUERY), (ROWS_OWN, KEY), (ROWS_OWN, KEY), (ROWS_OWN, WIDTH)]
    shapes += [(EXPERTS, ROWS_OWN), (ROWS_OWN,), (ROWS_OWN,), (ROWS_OWN,), (KGAIN_OWN,)]
    return pl.pallas_call(
        kernel,
        grid=(steps,),
        out_shape=[
            jax.ShapeDtypeStruct(block_out.shape, bf16),
            jax.ShapeDtypeStruct(tokens_grad.shape, bf16),
            jax.ShapeDtypeStruct((inner_rows, width), f32),
            jax.ShapeDtypeStruct((total_rows - inner_rows, width), f32),
        ]
        + [jax.ShapeDtypeStruct(shape, f32) for shape in shapes],
        in_specs=[
            by_rows(rows),
            by_rows(rows),
            whole(*small_sum.shape),
            whole(*dense_own.shape),
            pl.BlockSpec((step, width), lambda i: (i, 0)),
        ],
        out_specs=[
            by_rows(rows),
            by_rows(rows),
            by_rows(step),
            pl.BlockSpec((step, width), lambda i: (jnp.maximum(i - inner_steps, 0), 0)),
        ]
        + [whole(*shape) for shape in shapes],
        compiler_params=pltpu.CompilerParams(vmem_limit_bytes=VMEM_LIMIT),
    )(block_out, tokens_grad, small_sum, dense_own, expert_all)


def rotary_tables(positions):
    lane = jnp.arange(LANES, dtype=jnp.int32)
    half = HEAD_DIM // 2
    exponent = (lane % half).astype(f32) * (2.0 / HEAD_DIM)
    frequency = rope_base ** (-exponent)
    angles = positions.astype(f32)[:, None] * frequency[None, :]
    sign = jnp.where(lane % HEAD_DIM < half, -1.0, 1.0).astype(f32)
    return jnp.cos(angles), jnp.sin(angles) * sign[None, :]


def shards(
    tokens,
    cotangent,
    routes,
    picture_starts,
    attn_gain,
    query_weight,
    key_weight,
    value_weight,
    query_gain,
    key_gain,
    output_weight,
    ffn_gain,
    router_weight,
    expert_in,
    expert_down,
):
    seqs, positions, width = tokens.shape
    count = seqs * positions
    query_pos = lax.axis_index("rep") * positions + jnp.arange(positions, dtype=jnp.int32)
    cosine, sine = rotary_tables(query_pos)
    rows = tokens.reshape(count, width)
    grad_rows = cotangent.reshape(count, width)
    (
        dense, grad_all, pairs, soft, rows_first,
        attn_in, query_raw, key_raw, query_low, mixed, middle, sent, gates,
    ) = front_call(
        1, rows, grad_rows, (query_weight, key_weight, value_weight, output_weight),
        (attn_gain, query_gain, ffn_gain, key_gain), router_weight.T,
        cosine, sine, jnp.transpose(routes, (0, 2, 1)), picture_starts,
    )
    returned, out_terms, expert_terms = moe_call(
        2, sent, rows_first, grad_all, expert_in[0], expert_down[0]
    )
    block_out, tokens_grad, small_sum, dense_out, expert_all = back_call(
        3, returned, gates, middle, sent, dense, grad_rows, rows, attn_in,
        query_raw, key_raw, query_low, mixed, pairs, soft, out_terms, expert_terms, cosine, sine,
    )
    (
        block_out, tokens_grad, inner, outer, query, key, value, output, router, gain_a, gain_q, gain_f, gain_k,
    ) = finish_call(
        block_out, tokens_grad, small_sum, dense_out, expert_all.reshape(-1, width), expert_in.shape[1]
    )
    return (
        block_out.reshape(tokens.shape),
        tokens_grad.reshape(tokens.shape),
        gain_a,
        query,
        key,
        value,
        gain_q,
        gain_k,
        output,
        gain_f,
        router.T,
        inner[None],
        outer[None],
    )


def solution(mesh):
    by_tokens = P("shard", "rep", None)
    rows, line, block = P("shard", None), P("shard"), P("shard", None, None)
    in_specs = (
        by_tokens, by_tokens, by_tokens, rows, line, rows, rows, rows, line, line, rows, line, rows, block, block,
    )
    out_specs = (
        by_tokens, by_tokens, line, rows, rows, rows, line, line, rows, line, rows, block, block,
    )
    return jax.shard_map(shards, mesh=mesh, in_specs=in_specs, out_specs=out_specs, check_vma=False)
```

```python
import jax
import jax.numpy as jnp
from jax import lax
from jax.experimental import pallas as pl
from jax.experimental.pallas import tpu as pltpu
from jax.sharding import PartitionSpec as P

HEADS = 16
KV_HEADS = 8
HEAD_DIM = 64
PIC = 256
RING = 4
GROUP = 16
REPS = 8
VMEM_LIMIT = 63 << 20

norm_eps = 1e-06
rope_base = 10000.0
masked_score = -1e30

bf16 = jnp.bfloat16
f32 = jnp.float32


class Place:
    def __init__(self):
        shard = lax.axis_index("shard")
        rep = lax.axis_index("rep")
        self.shard, self.rep = shard, rep
        core = lax.rem(shard, 2)
        ring_z = lax.rem(lax.div(shard, 2), RING)
        y_hi = lax.div(shard, 8)
        ring_x = lax.rem(rep, RING)
        y_lo = lax.div(rep, RING)
        self.core = core

        def shard_of(hi, z, c):
            return (hi * RING + z) * 2 + c

        def rep_of(lo, x):
            return lo * RING + x

        def up(v):
            return lax.rem(v + 1, RING)

        def down(v):
            return lax.rem(v + RING - 1, RING)

        self.twin = (shard_of(y_hi, ring_z, 1 - core), rep)
        self.others = [lax.rem(rep + step, REPS) for step in range(REPS)]
        self.tokens = Axes(
            y_hi,
            ring_z,
            (shard_of(y_hi, up(ring_z), core), rep),
            (shard_of(y_hi, down(ring_z), core), rep),
            (shard_of(1 - y_hi, ring_z, core), rep_of(1 - y_lo, ring_x)),
        )
        self.copies = Axes(
            y_lo,
            ring_x,
            (shard, rep_of(y_lo, up(ring_x))),
            (shard, rep_of(y_lo, down(ring_x))),
            (shard, rep_of(1 - y_lo, ring_x)),
        )


class Axes:
    def __init__(self, side, spot, ahead, behind, across):
        self.side, self.spot = side, spot
        self.ahead, self.behind, self.across = ahead, behind, across
        sides = (side, 1 - side)
        spots = [lax.rem(spot + step, RING) for step in range(RING)]
        self.places = [[(sides[flip], spots[step]) for step in range(RING)] for flip in range(2)]

    def at(self, flip, step):
        return self.places[flip][step % RING]

    def neighbours(self):
        return [self.ahead, self.behind, self.across]


def greet(devices):
    barrier = pltpu.get_barrier_semaphore()
    for device in devices:
        pl.semaphore_signal(barrier, inc=1, device_id=device, device_id_type=pl.DeviceIdType.MESH)
    pl.semaphore_wait(barrier, len(devices))


class Line:
    def __init__(self, send_sem, recv_sem):
        self.send_sem, self.recv_sem = send_sem, recv_sem
        self.sent = []

    def copy(self, index, source, target, device):
        return pltpu.make_async_remote_copy(
            src_ref=source(),
            dst_ref=target(),
            send_sem=self.send_sem.at[index],
            recv_sem=self.recv_sem.at[index],
            device_id=device,
            device_id_type=pl.DeviceIdType.MESH,
        )

    def send(self, index, source, target, device):
        self.copy(index, source, target, device).start()
        self.sent.append((index, source, target, device))

    def take(self, index, target, device):
        self.copy(index, target, target, device).wait_recv()

    def finish(self):
        for sent in self.sent:
            self.copy(*sent).wait_send()


def abreast(*parts):
    running = list(parts)
    while running:
        for part in list(running):
            try:
                next(part)
            except StopIteration:
                running.remove(part)


GATHER_SEMS = 20


def gather_parts(axes, line, own, block, rows, local_sem, twin=None, twin_later=False):
    half, quarter = rows // 2, rows // 4
    mine, back, front, far = axes.at(0, 0), axes.at(0, -1), axes.at(0, 1), axes.at(0, 2)
    pair, pair_back, pair_front, pair_far = (axes.at(1, n) for n in (0, -1, 1, 2))
    ahead, behind, across = axes.ahead, axes.behind, axes.across

    def rows_of(which, low=0, count=rows, other=False):
        return lambda: block(which, low, count, other)

    def first(index, device):
        line.send(index, lambda: own, rows_of(mine), device)

    def relay(index, device, which, low=0, count=rows):
        line.send(index, rows_of(which, low, count), rows_of(which, low, count), device)

    def share(index, which):
        if twin is not None:
            relay(12 + index, twin, which)

    def keep():
        return pltpu.make_async_copy(own, block(mine, 0, rows), local_sem)

    keep().start()
    if twin is not None:
        first(12, twin)
    first(0, ahead)
    first(1, behind)
    first(2, across)
    keep().wait()
    yield
    line.take(0, rows_of(back), ahead)
    relay(3, ahead, back, 0, half)
    relay(4, across, back, half, half)
    share(1, back)
    line.take(1, rows_of(front), behind)
    relay(5, behind, front, half, half)
    relay(6, across, front, half, half)
    share(2, front)
    line.take(2, rows_of(pair), across)
    relay(7, ahead, pair, 0, half)
    relay(8, behind, pair, 0, half)
    share(3, pair)
    yield
    line.take(3, rows_of(far, 0, half), ahead)
    line.take(5, rows_of(far, half, half), behind)
    relay(9, across, far, half, half)
    share(4, far)
    line.take(7, rows_of(pair_back, 0, half), ahead)
    relay(10, ahead, pair_back, 0, quarter)
    line.take(8, rows_of(pair_front, 0, half), behind)
    relay(11, behind, pair_front, quarter, quarter)
    line.take(4, rows_of(pair_back, half, half), across)
    share(5, pair_back)
    line.take(6, rows_of(pair_front, half, half), across)
    share(6, pair_front)
    yield
    line.take(10, rows_of(pair_far, 0, quarter), ahead)
    line.take(11, rows_of(pair_far, quarter, quarter), behind)
    line.take(9, rows_of(pair_far, half, half), across)
    share(7, pair_far)
    yield
    if twin is not None and not twin_later:
        for index, which in enumerate(gather_order(axes)):
            line.take(12 + index, rows_of(which, other=True), twin)
    line.finish()


SUM_SEMS = 20
TOTAL_SEMS = 16


def total_parts(place, line, own, got, total, target, local_sem):
    rep = place.rep
    steps = range(1, REPS)
    peers = {step: (place.shard, place.others[step]) for step in steps}
    before = {step: place.others[REPS - step] for step in steps}

    def kept():
        return pltpu.make_async_copy(total, target(rep), local_sem)

    for step in steps:
        line.send(step, lambda p=place.others[step]: own(p), lambda: got.at[rep], peers[step])
    yield
    value = own(rep)[...].astype(f32)
    for step in steps:
        line.take(step, lambda b=before[step]: got.at[b], peers[step])
        value = value + got[before[step]].astype(f32)
    total[...] = value.astype(bf16)
    kept().start()
    for step in steps:
        line.send(8 + step, lambda: total, lambda: target(rep), peers[step])
    yield
    for step in steps:
        line.take(8 + step, lambda b=before[step]: target(b), peers[step])
    kept().wait()
    line.finish()


def spread_parts(place, line, own, got, total):
    rep = place.rep
    steps = range(1, REPS)
    for step in steps:
        peer = (place.shard, place.others[step])
        line.send(step, lambda: own, lambda: got.at[rep], peer)
    yield
    value = own[...].astype(f32)
    for step in steps:
        before = place.others[REPS - step]
        line.take(step, lambda: got.at[before], (place.shard, place.others[step]))
        value = value + got[before].astype(f32)
    total[...] = value
    line.finish()


def add_rows(target, source, rows):
    step = 16
    count = rows // step

    def body(index, carry):
        at = pl.ds(pl.multiple_of(index * step, step), step)
        target[at] = target[at] + source[at]
        return carry

    lax.fori_loop(0, count, body, 0)


def stage_rows(rows):
    return 7 * rows


def gather_order(axes):
    return [axes.at(*v) for v in ((0, 0), (0, -1), (0, 1), (1, 0), (0, 2), (1, -1), (1, 1), (1, 2))]


def sum_order(axes):
    return [axes.at(*v) for v in ((1, 2), (0, 2), (1, -1), (1, 1), (0, -1), (0, 1), (1, 0), (0, 0))]


def sum_parts(axes, line, part, stage, rows, result, twin=None, store=None):
    half, quarter = rows // 2, rows // 4
    mine, back, front, far = axes.at(0, 0), axes.at(0, -1), axes.at(0, 1), axes.at(0, 2)
    pair, pair_back, pair_front, pair_far = (axes.at(1, n) for n in (0, -1, 1, 2))
    ahead, behind, across = axes.ahead, axes.behind, axes.across
    order = sum_order(axes)
    offsets, used = {}, 0
    for name, size in (
        ("Y0", half), ("M0", quarter), ("P0", quarter), ("M1", half), ("Y1", half), ("Y2", half),
        ("P1", half), ("M2", half), ("P2", half), ("M3", rows), ("P3", rows), ("Y3", rows),
    ):
        offsets[name] = (used, size, len(offsets))
        used += size

    def landing(name):
        low, size, _ = offsets[name]
        return lambda: stage.at[pl.ds(low, size)]

    def send(name, which, low, device):
        _, size, index = offsets[name]
        line.send(index, lambda: part(which, low, size), landing(name), device)

    def add(name, which, low, device):
        _, size, index = offsets[name]
        line.take(index, landing(name), device)
        add_rows(part(which, low, size), landing(name)(), size)

    def join(*places):
        if twin is not None:
            for place in places:
                line.take(12 + place, lambda: twin[2](order[place]), twin[0])
                add_rows(part(order[place], 0, rows), twin[2](order[place]), rows)

    def hand(*places):
        if twin is not None:
            for place in places:
                which = order[place]
                line.send(
                    12 + place, lambda w=which: twin[1](w), lambda w=which: twin[2](w), twin[0]
                )

    hand(0, 1, 2, 3)
    yield
    join(0)
    send("Y0", pair_far, half, across)
    send("M0", pair_far, 0, behind)
    send("P0", pair_far, quarter, ahead)
    join(1)
    send("M1", far, 0, behind)
    join(2)
    send("Y1", pair_back, half, across)
    join(3)
    send("Y2", pair_front, half, across)
    yield
    hand(4, 5, 6, 7)
    yield
    add("M0", pair_back, 0, behind)
    send("M2", pair_back, 0, behind)
    add("P0", pair_front, quarter, ahead)
    send("P2", pair_front, 0, ahead)
    add("Y0", far, half, across)
    send("P1", far, half, ahead)
    yield
    join(4, 5, 6, 7)
    add("M1", back, 0, behind)
    add("Y1", back, half, across)
    send("M3", back, 0, behind)
    add("M2", pair, 0, behind)
    add("P2", pair, 0, ahead)
    send("Y3", pair, 0, across)
    add("P1", front, half, ahead)
    add("Y2", front, half, across)
    send("P3", front, 0, ahead)
    yield
    for name, device in (("M3", behind), ("P3", ahead), ("Y3", across)):
        line.take(offsets[name][2], landing(name), device)
    step = 16

    def body(index, carry):
        low = pl.multiple_of(index * step, step)
        total = part(mine, low, step)[...].astype(f32)
        for name in ("M3", "P3", "Y3"):
            total = total + stage[pl.ds(offsets[name][0] + low, step)].astype(f32)
        if store is None:
            result[pl.ds(low, step)] = total.astype(result.dtype)
        else:
            store(low, step, total)
        return carry

    lax.fori_loop(0, rows // step, body, 0)
    line.finish()


def sems(count):
    return [pltpu.SemaphoreType.DMA((count,)), pltpu.SemaphoreType.DMA((count,))]


ANY = pl.BlockSpec(memory_space=pl.ANY)
IN_VMEM = pl.BlockSpec(memory_space=pltpu.VMEM)


def params(collective_id):
    return pltpu.CompilerParams(
        collective_id=collective_id, has_side_effects=True, vmem_limit_bytes=VMEM_LIMIT
    )


def dot(a, b):
    return jnp.dot(a, b, preferred_element_type=f32)


def dot_nt(a, b):
    return lax.dot_general(a, b, (((1,), (1,)), ((), ())), preferred_element_type=f32)


def dot_tn(a, b):
    return lax.dot_general(a, b, (((0,), (0,)), ((), ())), preferred_element_type=f32)


def pick(index, values):
    chosen = values[-1]
    for at in range(len(values) - 2, -1, -1):
        chosen = jnp.where(index == at, values[at], chosen)
    return chosen


def moe_call(collective_id, sent, rows_first, grad_all, inner, outer):
    count, columns = sent.shape
    width = inner.shape[0]
    hidden_width = outer.shape[0]
    small = columns - width
    half = count // 2
    chips = GROUP // 2
    wide = 4
    rounds = GROUP // wide

    def kernel(
        sent_ref, first_ref, grad_ref, inner_ref, outer_ref,
        returned, out_terms, terms,
        rows_in, grads, hidden, back_gu, back, back_staged, back_stage, out_box, term_box,
        gs, gr, bs0, br0, bs1, br1, own_sem, load_sem, box_sem, term_sem,
    ):
        place = Place()
        axes, core, shard = place.tokens, place.core, place.shard
        gather_line = Line(gs, gr)

        def chip_of(which):
            return which[0] * RING + which[1]

        def blocks(which, other=False):
            return chip_of(which) * 2 + ((1 - core) if other else core)

        gather = gather_parts(
            axes, gather_line, sent_ref.at[pl.ds(half, half)],
            lambda which, low, n, other=False: rows_in.at[1, blocks(which, other), pl.ds(low, n)],
            half, own_sem, place.twin, twin_later=True,
        )

        def sum_of(chunk, send_sem, recv_sem):
            return sum_parts(
                axes, Line(send_sem, recv_sem),
                lambda which, low, n: back.at[chunk, blocks(which), pl.ds(low, n)],
                back_stage.at[chunk], half, returned.at[pl.ds(chunk * half, half)],
                (place.twin, lambda which: back.at[chunk, blocks(which, True)],
                 lambda which: back_staged.at[chunk, chip_of(which)]),
            )

        sums = [sum_of(0, bs0, br0), sum_of(1, bs1, br1)]

        def loads(t):
            at = pl.ds(t * wide, wide)
            return [
                pltpu.make_async_copy(first_ref.at[at], rows_in.at[0, at], load_sem.at[t, 0]),
                pltpu.make_async_copy(
                    grad_ref.at[at, pl.ds(0, half)], grads.at[0, at], load_sem.at[t, 1]
                ),
            ]

        second_grads = pltpu.make_async_copy(
            grad_ref.at[:, pl.ds(half, half)], grads.at[1], load_sem.at[rounds, 0]
        )

        def box_copy(chunk, first, slot):
            return pltpu.make_async_copy(
                out_box.at[slot],
                out_terms.at[pl.ds(first, wide), pl.ds(chunk * half, half)],
                box_sem.at[slot],
            )

        rows_count = wide * half
        lanes = lane_of((rows_count, small))
        is_high, is_rest = lanes == shard, lanes == shard + GROUP

        def tile(chunk, first, slot, wait_first):
            at = pl.ds(first, wide)
            row_block = rows_in[chunk, at].reshape(rows_count, columns)
            gate = jnp.sum(
                jnp.where(is_high | is_rest, row_block[:, width:].astype(f32), 0.0),
                axis=1, keepdims=True,
            )
            gate_up = dot(row_block[:, :width], inner_ref[...])
            gate_part, up_part = gate_up[:, :hidden_width], gate_up[:, hidden_width:]
            sigmoid = 1.0 / (1.0 + jnp.exp(-gate_part))
            active = gate_part * sigmoid
            product = active * up_part
            hidden_low = product.astype(bf16)
            hidden[chunk, at] = hidden_low.reshape(wide, half, hidden_width)
            out_rows = (gate * dot(hidden_low, outer_ref[...])).astype(bf16)

            @pl.when(wait_first)
            def _():
                box_copy(chunk, first, slot).wait()

            out_box[slot] = out_rows.reshape(wide, half, width)
            box_copy(chunk, first, slot).start()
            grad = grads[chunk, at].reshape(rows_count, width)
            grad_hidden = dot_nt(grad, outer_ref[...])
            grad_gate = jnp.sum(grad_hidden * product, axis=1, keepdims=True)
            grad_hidden = grad_hidden * gate
            grad_gate_up = jnp.concatenate(
                [
                    grad_hidden * up_part * sigmoid * (1.0 + gate_part * (1.0 - sigmoid)),
                    grad_hidden * active,
                ],
                axis=1,
            ).astype(bf16)
            back_gu[chunk, at] = grad_gate_up.reshape(wide, half, 2 * hidden_width)
            grads[chunk, at] = (gate * grad.astype(f32)).astype(bf16).reshape(wide, half, width)
            grad_rows = dot_nt(grad_gate_up, inner_ref[...]).astype(bf16)
            back[chunk, at, :, pl.ds(0, width)] = grad_rows.reshape(wide, half, width)
            high = grad_gate.astype(bf16).astype(f32)
            tail = jnp.where(is_high, high, jnp.where(is_rest, grad_gate - high, 0.0))
            back[chunk, at, :, pl.ds(width, small)] = tail.astype(bf16).reshape(wide, half, small)

        for t in range(rounds):
            for load in loads(t):
                load.start()
        second_grads.start()
        greet(axes.neighbours() + [place.twin])
        next(gather)

        def first_tiles(t, carry):
            hooks(t, ((2, lambda: next(gather)),))
            for load in loads(t):
                load.wait()
            tile(0, t * wide, lax.rem(t, 2), t >= 2)
            return carry

        lax.fori_loop(0, rounds, first_tiles, 0)
        next(sums[0])
        next(gather)
        second_grads.wait()
        near, beyond = lax.div(axes.spot, 2), 1 - lax.div(axes.spot, 2)
        chips_per_round = wide // 2
        firsts = [
            (side * RING + part * chips_per_round) * 2
            for side, part in (
                (axes.side, beyond), (1 - axes.side, near), (1 - axes.side, beyond), (axes.side, near),
            )
        ]
        arrivals = gather_order(axes)

        def arrived(*numbers):
            for number in numbers:
                gather_line.take(
                    12 + number, lambda: rows_in.at[1, blocks(arrivals[number], True)], place.twin
                )

        def second_tiles(t, carry):
            hooks(
                t,
                (
                    (0, lambda: arrived(0, 1, 2, 4)),
                    (1, lambda: (next(sums[0]), next(sums[0]), arrived(3, 5, 6))[2]),
                    (2, lambda: (next(gather), arrived(7))[1]),
                    (3, lambda: (next(sums[1]), next(sums[0]))[0]),
                ),
            )
            tile(1, pick(t, firsts), lax.rem(t, 2), t >= 0)
            return carry

        lax.fori_loop(0, rounds, second_tiles, 0)
        next(sums[1])
        next(sums[1])

        def term_copy(low, slot):
            return pltpu.make_async_copy(
                term_box.at[slot], terms.at[pl.ds(low, 256)], term_sem.at[slot]
            )

        every = 2 * GROUP * half

        def keep(index, low, value):
            slot = lax.rem(index, 2)

            @pl.when(index >= 2)
            def _():
                term_copy(low, slot).wait()

            term_box[slot] = value.astype(bf16)
            term_copy(low, slot).start()

        downs = hidden_width // 256

        def down_terms(index, carry):
            at = chunk_256(index)
            value = dot_tn(hidden[:, :, :, at].reshape(every, 256), grads[...].reshape(every, width))
            keep(index, pl.multiple_of(width + index * 256, 256), value)
            return carry

        lax.fori_loop(0, downs, down_terms, 0)

        def inner_terms(index, carry):
            hooks(
                index,
                (
                    (0, lambda: next(sums[0])),
                    (1, lambda: next(sums[1])),
                ),
            )
            at = chunk_256(index)
            value = dot_tn(
                rows_in[:, :, :, at].reshape(every, 256),
                back_gu[...].reshape(every, 2 * hidden_width),
            )
            keep(index + downs, pl.multiple_of(index * 256, 256), value)
            return carry

        lax.fori_loop(0, width // 256, inner_terms, 0)
        drained(sums[0])
        drained(sums[1])
        drained(gather)
        for slot in range(2):
            box_copy(1, 0, slot).wait()
            term_copy(0, slot).wait()

    term_rows = width + hidden_width
    return pl.pallas_call(
        kernel,
        out_shape=[
            jax.ShapeDtypeStruct((count, columns), f32),
            jax.ShapeDtypeStruct((GROUP, count, width), bf16),
            jax.ShapeDtypeStruct((term_rows, width), bf16),
        ],
        in_specs=[ANY, ANY, ANY, IN_VMEM, IN_VMEM],
        out_specs=[IN_VMEM, ANY, ANY],
        scratch_shapes=[
            pltpu.VMEM((2, GROUP, half, columns), bf16),
            pltpu.VMEM((2, GROUP, half, width), bf16),
            pltpu.VMEM((2, GROUP, half, hidden_width), bf16),
            pltpu.VMEM((2, GROUP, half, 2 * hidden_width), bf16),
            pltpu.VMEM((2, GROUP, half, columns), bf16),
            pltpu.VMEM((2, chips, half, columns), bf16),
            pltpu.VMEM((2, stage_rows(half), columns), bf16),
            pltpu.VMEM((2, wide, half, width), bf16),
            pltpu.VMEM((2, 256, width), bf16),
        ]
        + sems(GATHER_SEMS)
        + sems(SUM_SEMS) * 2
        + [
            pltpu.SemaphoreType.DMA,
            pltpu.SemaphoreType.DMA((rounds + 1, 2)),
            pltpu.SemaphoreType.DMA((2,)),
            pltpu.SemaphoreType.DMA((2,)),
        ],
        compiler_params=params(collective_id),
    )(sent, rows_first, grad_all, inner, outer)


WIDTH = 1024
QUERY = HEADS * HEAD_DIM
KEY = KV_HEADS * HEAD_DIM
EXPERTS = 16
SMALL = 128
LANES = 128
AT_K = QUERY
AT_V = AT_K + KEY
AT_S = AT_V + KEY
AT_O = AT_S + SMALL
PACKED = AT_O + WIDTH
ROWS_OWN = WIDTH // GROUP
KGAIN_OWN = KEY // GROUP
HEAD_PAIRS = KV_HEADS // 2
REST = 2 * KEY + SMALL
DENSE = QUERY + WIDTH + 2 * KEY


def drained(part):
    for _ in part:
        pass


def hooks(index, steps):
    for at, step in steps:
        pl.when(index == at)(step)


def chunk_256(index):
    return pl.ds(pl.multiple_of(index * 256, 256), 256)


def root_mean(values):
    return lax.rsqrt(jnp.mean(values * values, axis=1, keepdims=True) + norm_eps)


def lane_of(shape):
    return lax.broadcasted_iota(jnp.int32, shape, 1)


def turned(values, cosine, sine):
    first = (lane_of(values.shape) & (HEAD_DIM - 1)) < HEAD_DIM // 2
    swapped = jnp.where(
        first, pltpu.roll(values, LANES - HEAD_DIM // 2, 1), pltpu.roll(values, HEAD_DIM // 2, 1)
    )
    return values * cosine + swapped * sine


def gain_rows(small):
    rows = jnp.transpose(small.astype(f32))
    short = small.reshape(GROUP, ROWS_OWN, SMALL)[:, :KGAIN_OWN].reshape(KEY, SMALL)
    gain_k = jnp.transpose(short.astype(f32))[EXPERTS + 3 : EXPERTS + 4]
    return rows[EXPERTS : EXPERTS + 1], rows[EXPERTS + 1 : EXPERTS + 2], rows[EXPERTS + 2 : EXPERTS + 3], gain_k


def long_column(columns):
    cut = columns.reshape(GROUP, KGAIN_OWN, SMALL)
    return jnp.concatenate([cut, jnp.zeros_like(cut)], axis=1).reshape(WIDTH, SMALL)


def four_heads(chunk_a, chunk_b):
    low = lane_of(chunk_a.shape) < HEAD_DIM
    zero = jnp.zeros_like(chunk_a)
    return jnp.concatenate(
        [
            jnp.where(low, chunk_a, zero),
            jnp.where(low, pltpu.roll(chunk_a, HEAD_DIM, 1), zero),
            jnp.where(low, zero, pltpu.roll(chunk_b, HEAD_DIM, 1)),
            jnp.where(low, zero, chunk_b),
        ],
        axis=0,
    )


def two_chunks(blocks):
    rows = blocks.shape[0] // 4
    one, two, three, four = (blocks[n * rows : (n + 1) * rows] for n in range(4))
    low = lane_of(one.shape) < HEAD_DIM
    return (
        jnp.where(low, one, pltpu.roll(two, HEAD_DIM, 1)),
        jnp.where(low, pltpu.roll(three, HEAD_DIM, 1), four),
    )


def chunk_at(index, base=0):
    return pl.ds(pl.multiple_of(base + index * LANES, LANES), LANES)


def front_call(collective_id, tokens, cotangent, weights_own, gains, router, cosine, sine, routes, starts):
    count, width = tokens.shape
    seqs = starts.shape[0]
    positions = count // seqs
    length = REPS * positions
    score_scale = HEAD_DIM ** (-0.5)
    sent_width = width + SMALL

    def kernel(
        starts_ref, tokens_ref, grad_ref, query_w, key_w, value_w, output_w,
        gain_a_ref, gain_q_ref, gain_f_ref, gain_k_ref, router_ref, cos_ref, sin_ref, routes_ref,
        dense_out, grad_all, pairs_out, soft_out, rows_first,
        attn_in, query_raw, key_raw, query_low, mixed, middle, sent, gates_out,
        packed, small_box, dense, pairs, pair_own, soft_box, bias_box,
        ws0, wr0, ws1, wr1, ws2, wr2, gs0, gr0, gs1, gr1, ks0, kr0, ks1, kr1, rs, rr, own_sem, out_sem, soft_sem, pack_sem,
    ):
        place = Place()
        core = place.core
        packing = [
            pltpu.make_async_copy(
                source, packed.at[:, pl.ds(low, source.shape[1])], pack_sem.at[index]
            )
            for index, (source, low) in enumerate(
                ((key_w, AT_K), (value_w, AT_V), (query_w, 0), (output_w, AT_O))
            )
        ]
        for copy in packing:
            copy.start()
        small_box[...] = jnp.zeros_like(small_box)
        small_box[pl.ds(0, EXPERTS), pl.ds(0, ROWS_OWN)] = router_ref[...].astype(f32)
        for at, ref in enumerate((gain_a_ref, gain_q_ref, gain_f_ref, gain_k_ref)):
            size = ref.shape[0]
            small_box[pl.ds(EXPERTS + at, 1), pl.ds(0, size)] = (
                ref[...].astype(f32).reshape(1, size)
            )
        packed[:, pl.ds(AT_S, SMALL)] = jnp.transpose(small_box[...])[:ROWS_OWN].astype(bf16)

        def token_block(index, low, size):
            def block(which, row, n, other=False):
                at = (which[0] * RING + which[1]) * 2 + ((1 - core) if other else core)
                return dense.at[at, pl.ds(row, n), pl.ds(low, size)]

            return block

        def weight_gather(index, low, size, send_sem, recv_sem):
            return gather_parts(
                place.tokens, Line(send_sem, recv_sem), packed.at[:, pl.ds(low, size)],
                token_block(index, low, size), ROWS_OWN, own_sem.at[index], place.twin,
            )

        def rows_of(target):
            def block(which, row, n, other=False):
                at = (which[0] * RING + which[1]) * 2 + ((1 - core) if other else core)
                return target.at[at, pl.ds(row, n)]

            return block

        def pair_gather(seq, send_sem, recv_sem):
            def block(which, row, n, other=False):
                return pairs.at[seq, which[0] * RING + which[1], pl.ds(row, n)]

            return gather_parts(
                place.copies, Line(send_sem, recv_sem),
                pair_own.at[pl.ds(seq * positions, positions)], block, positions, own_sem.at[3 + seq],
            )

        def soft_copy(seq, index, slot):
            return pltpu.make_async_copy(
                soft_box.at[slot], soft_out.at[seq, index], soft_sem.at[slot]
            )

        rest_gather = weight_gather(0, AT_K, REST, ws0, wr0)
        query_gather = weight_gather(1, 0, QUERY, ws1, wr1)
        output_gather = weight_gather(2, AT_O, WIDTH, ws2, wr2)
        def grad_gather(seq, send_sem, recv_sem):
            base = seq * positions

            def block(which, row, n, other=False):
                at = (which[0] * RING + which[1]) * 2 + ((1 - core) if other else core)
                return grad_all.at[at, pl.ds(base + row, n)]

            return gather_parts(
                place.tokens, Line(send_sem, recv_sem), grad_ref.at[pl.ds(base, positions)], block,
                positions, own_sem.at[5 + seq], place.twin,
            )

        grads = [grad_gather(0, gs0, gr0), grad_gather(1, gs1, gr1)]
        first_rows = gather_parts(
            place.tokens, Line(rs, rr), sent.at[pl.ds(0, positions)], rows_of(rows_first), positions,
            own_sem.at[7], place.twin,
        )
        pair_gathers = [pair_gather(0, ks0, kr0), pair_gather(1, ks1, kr1)]

        greet(place.tokens.neighbours() + place.copies.neighbours() + [place.twin])
        for copy in packing:
            copy.wait()
        next(rest_gather)
        inputs = tokens_ref[...].astype(f32)
        middle[...] = inputs * root_mean(inputs)
        next(rest_gather)
        next(query_gather)
        query_at = place.rep * positions + lax.broadcasted_iota(jnp.int32, (positions, 1), 0)
        key_at = lax.broadcasted_iota(jnp.int32, (1, length), 1)
        for seq in range(seqs):
            allowed = key_at <= query_at
            for piece in range(starts_ref.shape[1]):
                start = starts_ref[seq, piece]
                query_inside = (query_at >= start) & (query_at < start + PIC)
                key_inside = (key_at >= start) & (key_at < start + PIC)
                allowed = allowed | (query_inside & key_inside)
            bias_box[seq] = jnp.where(allowed, 0.0, masked_score)
        next(rest_gather)
        next(query_gather)
        next(output_gather)
        drained(rest_gather)
        next(query_gather)
        next(output_gather)

        def weights(low, size):
            return dense[:, :, pl.ds(low, size)].reshape(width, size)

        small = weights(AT_S, SMALL)
        gain_a, gain_q, gain_f, gain_k = gain_rows(small)
        rows = (middle[...] * gain_a).astype(bf16)
        attn_in[...] = rows
        cos2 = jnp.concatenate([cos_ref[...]] * seqs, axis=0)
        sin2 = jnp.concatenate([sin_ref[...]] * seqs, axis=0)
        raw = dot(rows, weights(AT_K, KEY))
        key_raw[...] = raw
        scaled = raw * root_mean(raw) * gain_k
        for chunk in range(KEY // LANES):
            at = slice(chunk * LANES, (chunk + 1) * LANES)
            pair_own[:, at] = turned(scaled[:, at], cos2, sin2).astype(bf16)
        pair_own[:, KEY:] = dot(rows, weights(AT_V, KEY)).astype(bf16)
        next(pair_gathers[0])
        drained(query_gather)
        next(output_gather)
        next(grads[0])
        raw = dot(rows, weights(0, QUERY))
        query_raw[...] = raw
        scaled = raw * root_mean(raw) * gain_q
        for chunk in range(QUERY // LANES):
            at = slice(chunk * LANES, (chunk + 1) * LANES)
            query_low[:, at] = turned(scaled[:, at], cos2, sin2).astype(bf16)
        next(pair_gathers[0])
        next(pair_gathers[1])
        drained(output_gather)
        dense_copy = pltpu.make_async_copy(dense, dense_out, out_sem.at[0])
        dense_copy.start()
        next(grads[0])
        next(grads[1])
        next(pair_gathers[0])
        next(pair_gathers[1])
        next(grads[0])
        drained(pair_gathers[0])
        next(grads[1])

        def attend(seq, index, slot, wait_first):
            rows_at = pl.ds(seq * positions, positions)
            queries = four_heads(
                query_low[rows_at, chunk_at(2 * index)].astype(f32),
                query_low[rows_at, chunk_at(2 * index + 1)].astype(f32),
            )
            queries = (queries * score_scale).astype(bf16)
            keys = pairs[seq, :, :, chunk_at(index)].reshape(length, LANES)
            scores = dot_nt(queries, keys).reshape(4, positions, length) + bias_box[seq][None]
            scores = scores.reshape(4 * positions, length)
            raised = jnp.exp(scores - jnp.max(scores, axis=1, keepdims=True))
            soft = (raised * (1.0 / jnp.sum(raised, axis=1, keepdims=True))).astype(bf16)

            @pl.when(wait_first)
            def _():
                soft_copy(seq, index, slot).wait()

            soft_box[slot] = soft
            soft_copy(seq, index, slot).start()
            values = pairs[seq, :, :, chunk_at(index, KEY)].reshape(length, LANES)
            chunk_a, chunk_b = two_chunks(dot(soft, values))
            mixed[rows_at, chunk_at(2 * index)] = chunk_a.astype(bf16)
            mixed[rows_at, chunk_at(2 * index + 1)] = chunk_b.astype(bf16)

        def features(seq):
            at = pl.ds(seq * positions, positions)
            total = tokens_ref[at].astype(f32) + dot(mixed[at], weights(AT_O, WIDTH))
            middle[at] = total
            ffn_in = (total * root_mean(total) * gain_f).astype(bf16)
            sent[at, pl.ds(0, width)] = ffn_in
            lanes = lane_of((positions, SMALL))
            named = jnp.transpose(routes_ref[seq].astype(f32)).astype(jnp.int32)
            chosen = lanes == named[:, :1]
            for choice in range(1, named.shape[1]):
                chosen = chosen | (lanes == named[:, choice : choice + 1])
            logits = jnp.where(chosen, dot(ffn_in, small), masked_score)
            raised = jnp.exp(logits - jnp.max(logits, axis=1, keepdims=True))
            gates = raised * (1.0 / jnp.sum(raised, axis=1, keepdims=True))
            gates = jnp.where(chosen, gates, 0.0)
            gates_out[at] = gates
            high = gates.astype(bf16).astype(f32)
            tail = high + pltpu.roll(gates - high, EXPERTS, 1)
            sent[at, pl.ds(width, SMALL)] = tail.astype(bf16)

        def first_heads(index, carry):
            hooks(
                index,
                (
                    (1, lambda: next(grads[0])),
                    (2, lambda: next(pair_gathers[1])),
                    (3, lambda: next(grads[1])),
                ),
            )
            attend(0, index, lax.rem(index, 2), index >= 2)
            return carry

        lax.fori_loop(0, HEAD_PAIRS, first_heads, 0)
        features(0)
        next(first_rows)
        drained(pair_gathers[1])
        pairs_copy = pltpu.make_async_copy(pairs, pairs_out, out_sem.at[1])
        pairs_copy.start()

        def second_heads(index, carry):
            hooks(
                index,
                (
                    (1, lambda: next(grads[1])),
                    (3, lambda: next(first_rows)),
                ),
            )
            attend(1, index, lax.rem(index, 2), index >= 0)
            return carry

        lax.fori_loop(0, HEAD_PAIRS, second_heads, 0)
        features(1)
        next(first_rows)
        drained(grads[0])
        drained(grads[1])
        drained(first_rows)
        dense_copy.wait()
        pairs_copy.wait()
        for slot in range(2):
            soft_copy(1, 0, slot).wait()

    return pl.pallas_call(
        kernel,
        out_shape=[
            jax.ShapeDtypeStruct((GROUP, ROWS_OWN, PACKED), bf16),
            jax.ShapeDtypeStruct((GROUP, count, width), bf16),
            jax.ShapeDtypeStruct((seqs, REPS, positions, 2 * KEY), bf16),
            jax.ShapeDtypeStruct((seqs, HEAD_PAIRS, 4 * positions, length), bf16),
            jax.ShapeDtypeStruct((GROUP, positions, sent_width), bf16),
            jax.ShapeDtypeStruct((count, width), bf16),
            jax.ShapeDtypeStruct((count, QUERY), f32),
            jax.ShapeDtypeStruct((count, KEY), f32),
            jax.ShapeDtypeStruct((count, QUERY), bf16),
            jax.ShapeDtypeStruct((count, QUERY), bf16),
            jax.ShapeDtypeStruct((count, width), f32),
            jax.ShapeDtypeStruct((count, width + SMALL), bf16),
            jax.ShapeDtypeStruct((count, SMALL), f32),
        ],
        in_specs=[pl.BlockSpec(memory_space=pltpu.SMEM), IN_VMEM] + [ANY] * 5 + [IN_VMEM] * 8,
        out_specs=[ANY] * 5 + [IN_VMEM] * 8,
        scratch_shapes=[
            pltpu.VMEM((ROWS_OWN, PACKED), bf16),
            pltpu.VMEM((SMALL, LANES), f32),
            pltpu.VMEM((GROUP, ROWS_OWN, PACKED), bf16),
            pltpu.VMEM((seqs, REPS, positions, 2 * KEY), bf16),
            pltpu.VMEM((count, 2 * KEY), bf16),
            pltpu.VMEM((2, 4 * positions, length), bf16),
            pltpu.VMEM((seqs, positions, length), f32),
        ]
        + sems(GATHER_SEMS) * 8
        + [
            pltpu.SemaphoreType.DMA((8,)),
            pltpu.SemaphoreType.DMA((2,)),
            pltpu.SemaphoreType.DMA((2,)),
            pltpu.SemaphoreType.DMA((4,)),
        ],
        compiler_params=params(collective_id),
    )(starts, tokens, cotangent, *weights_own, *gains, router, cosine, sine, routes)


def key_chunk(index, base=0):
    low = lax.div(index, 2) * KEY + lax.rem(index, 2) * LANES + base
    return pl.ds(pl.multiple_of(low, LANES), LANES)


def norm_back(values, gain, grad):
    scale = root_mean(values)
    weighted = grad * gain
    mean = jnp.mean(values * weighted, axis=1, keepdims=True)
    inner = weighted * scale - values * (scale * scale * scale * mean)
    return inner, jnp.sum(grad * values * scale, axis=0, keepdims=True)


def back_call(
    collective_id, returned, gates, middle, sent, dense, cotangent, tokens, attn_in, query_raw, key_raw,
    query_low, mixed, pairs, soft, out_terms, expert_terms, cosine, sine,
):
    count, width = tokens.shape
    seqs, _, positions, _ = pairs.shape
    length = REPS * positions
    expert_rows = expert_terms.shape[0] // REPS
    side_rows = RING * expert_rows
    score_scale = HEAD_DIM ** (-0.5)
    chips = GROUP // 2

    def kernel(
        returned_ref, gates_ref, middle_ref, sent_ref, dense_ref, grad_ref, tokens_ref, attn_ref,
        query_raw_ref, key_raw_ref, query_ref, mixed_ref, pairs_ref, soft_ref, out_ref, expert_ref,
        cos_ref, sin_ref,
        block_out, tokens_grad, small_out, dense_out, expert_all,
        weight_box, weight_rest, wide_terms, rest_terms, dense_own,
        wide_staged, rest_staged, wide_stage, rest_stage,
        out_held, out_staged, out_stage, small_terms, small_staged, small_stage, small_own,
        expert_stage, expert_own,
        soft_box, key_box, value_box, pair_terms, pair_stage, pair_grads,
        grad_mixed, grad_query, grad_middle, grad_attn, grad_attn_in, gain_box,
        wide_got, rest_got, small_got, wide_total_box, rest_total_box,
        out_s, out_r, exp_s, exp_r, small_s, small_r, kv0_s, kv0_r, kva_s, kva_r, kvb_s, kvb_r, wide_s, wide_r, rest_s, rest_r,
        ge_s, ge_r, gwide_s, gwide_r, grest_s, grest_r, gsmall_s, gsmall_r,
        load_sem, held_sem, box_sem, own_sem, total_sem,
    ):
        place = Place()
        core = place.core
        token_axes, copy_axes = place.tokens, place.copies

        def chip_of(which):
            return which[0] * RING + which[1]

        def blocks(which, other=False):
            return chip_of(which) * 2 + ((1 - core) if other else core)

        def out_store(low, step, value):
            at = pl.ds(low, step)
            block_out[at] = (middle_ref[at] + value).astype(bf16)

        out_sum = sum_parts(
            token_axes, Line(out_s, out_r),
            lambda which, low, n: out_held.at[chip_of(which), pl.ds(low, n)],
            out_stage, count, None,
            (place.twin, lambda which: out_ref.at[blocks(which, True)],
             lambda which: out_staged.at[chip_of(which)]),
            store=out_store,
        )
        def expert_part(which, low, n):
            columns = pl.ds(pl.multiple_of(which[0] * width, width), width)
            return wide_terms.at[pl.ds(which[1] * expert_rows + low, n), columns]

        expert_sum = sum_parts(
            copy_axes, Line(exp_s, exp_r), expert_part, expert_stage, expert_rows, expert_own
        )

        def pair_sum(seq, low, size, index, send_sem, recv_sem):
            columns = pl.ds(low, size)
            return sum_parts(
                copy_axes, Line(send_sem, recv_sem),
                lambda which, row, n: pair_terms.at[seq, chip_of(which), pl.ds(row, n), columns],
                pair_stage.at[index, :, columns], positions,
                pair_grads.at[pl.ds(seq * positions, positions), columns],
            )

        first_pairs = pair_sum(0, 0, 2 * KEY, 0, kv0_s, kv0_r)
        second_pairs = [
            pair_sum(1, 0, KEY, 1, kva_s, kva_r), pair_sum(1, KEY, KEY, 1, kvb_s, kvb_r)
        ]

        def rows_of_block(terms, index, low, n):
            return terms.at[pl.ds(index * ROWS_OWN + low, n)]

        def dense_sum(terms, staged, stage, own, send_sem, recv_sem):
            return sum_parts(
                token_axes, Line(send_sem, recv_sem),
                lambda which, row, n: rows_of_block(terms, blocks(which), row, n),
                stage, ROWS_OWN, own,
                (place.twin, lambda which: rows_of_block(terms, blocks(which, True), 0, ROWS_OWN),
                 lambda which: staged.at[chip_of(which)]),
            )

        wide_sum = dense_sum(
            wide_terms, wide_staged, wide_stage, dense_own.at[:, pl.ds(0, QUERY + width)], wide_s, wide_r
        )
        rest_sum = dense_sum(
            rest_terms, rest_staged, rest_stage, dense_own.at[:, pl.ds(QUERY + width, 2 * KEY)],
            rest_s, rest_r,
        )
        small_sum = dense_sum(small_terms, small_staged, small_stage, small_own, small_s, small_r)

        def dense_total(index, low, size, got, total, send_sem, recv_sem):
            share = size // REPS

            def columns(rep):
                return pl.ds(pl.multiple_of(low + rep * share, LANES), share)

            return total_parts(
                place, Line(send_sem, recv_sem), lambda rep: dense_own.at[:, columns(rep)], got, total,
                lambda rep: dense_out.at[:, columns(rep)], total_sem.at[index],
            )

        wide_total = dense_total(0, 0, QUERY + width, wide_got, wide_total_box, gwide_s, gwide_r)
        rest_total = dense_total(
            1, QUERY + width, 2 * KEY, rest_got, rest_total_box, grest_s, grest_r
        )
        small_total = spread_parts(place, Line(gsmall_s, gsmall_r), small_own, small_got, small_out)
        expert_gather = gather_parts(
            copy_axes, Line(ge_s, ge_r), expert_own,
            lambda which, row, n, other=False: expert_all.at[chip_of(which), pl.ds(row, n)],
            expert_rows, own_sem,
        )

        def begin(part):
            for _ in range(3):
                next(part)

        def weight_load(low, index):
            return pltpu.make_async_copy(
                dense_ref.at[:, :, pl.ds(low, width)], weight_box, load_sem.at[index]
            )

        rest_load = pltpu.make_async_copy(
            dense_ref.at[:, :, pl.ds(AT_K, REST)], weight_rest, load_sem.at[1]
        )
        expert_loads = [
            pltpu.make_async_copy(
                expert_ref.at[pl.ds(side * side_rows, side_rows)],
                wide_terms.at[pl.ds(0, side_rows), pl.ds(side * width, width)],
                load_sem.at[(2, 4)[side]],
            )
            for side in range(2)
        ]
        held_loads = [
            pltpu.make_async_copy(
                out_ref.at[2 * chip + core], out_held.at[chip], held_sem.at[chip]
            )
            for chip in range(chips)
        ]

        def box_loads(number, slot):
            seq, index = lax.div(number, HEAD_PAIRS), lax.rem(number, HEAD_PAIRS)
            return [
                pltpu.make_async_copy(
                    soft_ref.at[seq, index], soft_box.at[slot], box_sem.at[slot, 0]
                ),
                pltpu.make_async_copy(
                    pairs_ref.at[seq, :, :, chunk_at(index)], key_box.at[slot], box_sem.at[slot, 1]
                ),
                pltpu.make_async_copy(
                    pairs_ref.at[seq, :, :, chunk_at(index, KEY)],
                    value_box.at[slot],
                    box_sem.at[slot, 2],
                ),
            ]

        for load in expert_loads:
            load.start()
        rest_load.start()
        weight_load(AT_O, 0).start()
        for load in held_loads + box_loads(0, 0):
            load.start()
        greet(
            token_axes.neighbours()
            + [place.twin]
            + [(place.shard, other) for other in place.others[1:]]
        )
        next(out_sum)
        for load in expert_loads:
            load.wait()
        begin(expert_sum)
        rest_load.wait()

        small = weight_rest[:, :, pl.ds(2 * KEY, SMALL)].reshape(width, SMALL)
        gain_a, gain_q, gain_f, gain_k = gain_rows(small)
        gates = gates_ref[...]
        tail = returned_ref[:, pl.ds(width, SMALL)].astype(f32)
        grad_gates = tail + pltpu.roll(tail, SMALL - EXPERTS, 1)
        grad_logits = gates * (grad_gates - jnp.sum(gates * grad_gates, axis=1, keepdims=True))
        grad_logits = grad_logits.astype(bf16)
        grad_ffn = returned_ref[:, pl.ds(0, width)].astype(f32) + dot_nt(grad_logits, small)
        inner, gain_f_terms = norm_back(middle_ref[...], gain_f, grad_ffn)
        inner = grad_ref[...].astype(f32) + inner
        grad_middle[...] = inner
        grad_attn[...] = inner.astype(bf16)
        gain_box[...] = jnp.zeros_like(gain_box)
        gain_box[pl.ds(EXPERTS + 2, 1)] = gain_f_terms
        weight_load(AT_O, 0).wait()
        grad_mixed[...] = dot_nt(
            grad_attn[...], weight_box[...].reshape(QUERY, width)
        ).astype(bf16)
        weight_load(0, 3).start()

        def attend_back(seq, index):
            number = seq * HEAD_PAIRS + index
            slot = lax.rem(number, 2)
            for load in box_loads(number, slot):
                load.wait()

            @pl.when(number + 1 < seqs * HEAD_PAIRS)
            def _():
                for load in box_loads(number + 1, 1 - slot):
                    load.start()

            rows_at = pl.ds(seq * positions, positions)
            first, second = chunk_at(2 * index), chunk_at(2 * index + 1)
            queries = four_heads(
                query_ref[rows_at, first].astype(f32), query_ref[rows_at, second].astype(f32)
            )
            queries = (queries * score_scale).astype(bf16)
            grads = four_heads(
                grad_mixed[rows_at, first].astype(f32), grad_mixed[rows_at, second].astype(f32)
            ).astype(bf16)
            keys = key_box[slot].reshape(length, LANES)
            values = value_box[slot].reshape(length, LANES)
            soft_low = soft_box[slot]
            value_terms = dot_tn(soft_low, grads)
            pair_terms[seq, :, :, key_chunk(index, KEY // 2)] = value_terms.astype(bf16).reshape(
                REPS, positions, LANES
            )
            soft_full = soft_low.astype(f32)
            grad_soft = dot_nt(grads, values)
            weighted = soft_full * grad_soft
            grad_scores = (
                weighted - soft_full * jnp.sum(weighted, axis=1, keepdims=True)
            ).astype(bf16)
            key_terms = dot_tn(grad_scores, queries)
            pair_terms[seq, :, :, key_chunk(index)] = key_terms.astype(bf16).reshape(
                REPS, positions, LANES
            )
            chunk_a, chunk_b = two_chunks(dot(grad_scores, keys) * score_scale)
            grad_query[rows_at, first] = chunk_a.astype(bf16)
            grad_query[rows_at, second] = chunk_b.astype(bf16)

        def out_ready():
            for load in held_loads:
                load.wait()
            next(out_sum)
            next(out_sum)

        def first_heads(index, carry):
            hooks(index, ((2, lambda: next(expert_sum)), (3, out_ready)))
            attend_back(0, index)
            return carry

        lax.fori_loop(0, HEAD_PAIRS, first_heads, 0)
        begin(first_pairs)

        def second_heads(index, carry):
            hooks(
                index,
                (
                    (2, lambda: begin(second_pairs[0])),
                    (3, lambda: (next(out_sum), next(expert_sum))[0]),
                ),
            )
            attend_back(1, index)
            return carry

        lax.fori_loop(0, HEAD_PAIRS, second_heads, 0)
        begin(second_pairs[1])
        next(second_pairs[0])
        router_terms = dot_tn(sent_ref[:, pl.ds(0, width)], grad_logits)

        cos2 = jnp.concatenate([cos_ref[...]] * seqs, axis=0)
        sin2 = -jnp.concatenate([sin_ref[...]] * seqs, axis=0)

        def turned_back(values):
            return jnp.concatenate(
                [
                    turned(values[:, low : low + LANES], cos2, sin2)
                    for low in range(0, values.shape[1], LANES)
                ],
                axis=1,
            )

        grad, gain_q_terms = norm_back(
            query_raw_ref[...], gain_q, turned_back(grad_query[...].astype(f32))
        )
        gain_box[pl.ds(EXPERTS + 1, 1)] = gain_q_terms
        grad_query_low = grad.astype(bf16)
        weight_load(0, 3).wait()
        grad_attn_in[...] = dot_nt(grad_query_low, weight_box[...].reshape(width, QUERY))

        next(first_pairs)
        next(second_pairs[1])
        next(first_pairs)
        next(second_pairs[0])

        drained(expert_sum)

        def q_rows(index, carry):
            at = chunk_256(index)
            wide_terms[at, pl.ds(0, QUERY)] = dot_tn(attn_ref[:, at], grad_query_low).astype(bf16)
            wide_terms[at, pl.ds(QUERY, width)] = dot_tn(mixed_ref[:, at], grad_attn[...]).astype(bf16)
            return carry

        lax.fori_loop(0, width // 256, q_rows, 0)
        next(wide_sum)
        next(second_pairs[1])
        next(out_sum)
        next(wide_sum)
        next(wide_sum)
        drained(first_pairs)
        drained(second_pairs[0])
        drained(second_pairs[1])
        next(expert_gather)

        grads = pair_grads[...]
        half = KEY // 2
        key_grads = jnp.concatenate([grads[:, :half], grads[:, KEY : KEY + half]], axis=1)
        value_grads = jnp.concatenate([grads[:, half:KEY], grads[:, KEY + half :]], axis=1)
        grad, gain_k_terms = norm_back(
            key_raw_ref[...], gain_k, turned_back(key_grads.astype(bf16).astype(f32))
        )
        grad_pairs = jnp.concatenate([grad.astype(bf16), value_grads.astype(bf16)], axis=1)

        def rest_rows(index, carry):
            at = chunk_256(index)
            rest_terms[at] = dot_tn(attn_ref[:, at], grad_pairs).astype(bf16)
            return carry

        lax.fori_loop(0, width // 256, rest_rows, 0)
        next(rest_sum)
        grad = grad_attn_in[...] + dot_nt(
            grad_pairs, weight_rest[:, :, pl.ds(0, 2 * KEY)].reshape(width, 2 * KEY)
        )
        next(rest_sum)
        next(rest_sum)
        values = tokens_ref[...].astype(f32)
        inner, gain_a_terms = norm_back(values, gain_a, grad)
        gain_box[pl.ds(EXPERTS, 1)] = gain_a_terms
        lanes = lane_of((KEY, SMALL))
        gain_k_column = jnp.where(
            lanes == EXPERTS + 3,
            jnp.transpose(jnp.broadcast_to(gain_k_terms, (SMALL, KEY))),
            0.0,
        )
        small_terms[...] = (
            router_terms + jnp.transpose(gain_box[...]) + long_column(gain_k_column)
        ).astype(bf16)
        next(small_sum)
        tokens_grad[...] = (grad_middle[...] + inner).astype(bf16)
        next(small_sum)
        next(small_sum)
        next(wide_sum)
        next(rest_sum)
        next(expert_gather)
        next(small_sum)
        next(wide_sum)
        next(small_sum)
        next(rest_sum)
        drained(out_sum)
        drained(wide_sum)
        next(wide_total)
        drained(small_sum)
        next(small_total)
        next(expert_gather)
        drained(rest_sum)
        next(rest_total)
        next(wide_total)
        next(expert_gather)
        drained(small_total)
        next(rest_total)
        drained(expert_gather)
        drained(wide_total)
        drained(rest_total)

    block = pltpu.VMEM((GROUP, ROWS_OWN, width), bf16)
    scratch = [
        block,
        pltpu.VMEM((GROUP, ROWS_OWN, REST), bf16),
        pltpu.VMEM((width, QUERY + width), bf16),
        pltpu.VMEM((width, 2 * KEY), bf16),
        pltpu.VMEM((ROWS_OWN, DENSE), bf16),
        pltpu.VMEM((chips, ROWS_OWN, QUERY + width), bf16),
        pltpu.VMEM((chips, ROWS_OWN, 2 * KEY), bf16),
        pltpu.VMEM((stage_rows(ROWS_OWN), QUERY + width), bf16),
        pltpu.VMEM((stage_rows(ROWS_OWN), 2 * KEY), bf16),
        pltpu.VMEM((chips, count, width), bf16),
        pltpu.VMEM((chips, count, width), bf16),
        pltpu.VMEM((stage_rows(count), width), bf16),
        pltpu.VMEM((width, SMALL), bf16),
        pltpu.VMEM((chips, ROWS_OWN, SMALL), bf16),
        pltpu.VMEM((stage_rows(ROWS_OWN), SMALL), bf16),
        pltpu.VMEM((ROWS_OWN, SMALL), bf16),
        pltpu.VMEM((stage_rows(expert_rows), width), bf16),
        pltpu.VMEM((expert_rows, width), bf16),
        pltpu.VMEM((2, 4 * positions, length), bf16),
        pltpu.VMEM((2, REPS, positions, LANES), bf16),
        pltpu.VMEM((2, REPS, positions, LANES), bf16),
        pltpu.VMEM((seqs, REPS, positions, 2 * KEY), bf16),
        pltpu.VMEM((seqs, stage_rows(positions), 2 * KEY), bf16),
        pltpu.VMEM((count, 2 * KEY), f32),
        pltpu.VMEM((count, QUERY), bf16),
        pltpu.VMEM((count, QUERY), bf16),
        pltpu.VMEM((count, width), f32),
        pltpu.VMEM((count, width), bf16),
        pltpu.VMEM((count, width), f32),
        pltpu.VMEM((SMALL, width), f32),
    ]
    wide_share, rest_share = (QUERY + width) // REPS, 2 * KEY // REPS
    scratch += [
        pltpu.VMEM((REPS, ROWS_OWN, wide_share), bf16),
        pltpu.VMEM((REPS, ROWS_OWN, rest_share), bf16),
        pltpu.VMEM((REPS, ROWS_OWN, SMALL), bf16),
        pltpu.VMEM((ROWS_OWN, wide_share), bf16),
        pltpu.VMEM((ROWS_OWN, rest_share), bf16),
    ]
    return pl.pallas_call(
        kernel,
        out_shape=[
            jax.ShapeDtypeStruct((count, width), bf16),
            jax.ShapeDtypeStruct((count, width), bf16),
            jax.ShapeDtypeStruct((ROWS_OWN, SMALL), f32),
            jax.ShapeDtypeStruct((ROWS_OWN, DENSE), bf16),
            jax.ShapeDtypeStruct((REPS, expert_rows, width), bf16),
        ],
        in_specs=[IN_VMEM] * 4 + [ANY] + [IN_VMEM] * 7 + [ANY] * 4 + [IN_VMEM] * 2,
        out_specs=[IN_VMEM, IN_VMEM, IN_VMEM, ANY, ANY],
        scratch_shapes=scratch
        + sems(SUM_SEMS) * 8
        + sems(GATHER_SEMS)
        + sems(TOTAL_SEMS) * 3
        + [
            pltpu.SemaphoreType.DMA((5,)),
            pltpu.SemaphoreType.DMA((chips,)),
            pltpu.SemaphoreType.DMA((2, 3)),
            pltpu.SemaphoreType.DMA,
            pltpu.SemaphoreType.DMA((2,)),
        ],
        compiler_params=params(collective_id),
    )(
        returned, gates, middle, sent, dense, cotangent, tokens, attn_in, query_raw, key_raw,
        query_low, mixed, pairs, soft, out_terms, expert_terms, cosine, sine,
    )


def finish_call(block_out, tokens_grad, small_sum, dense_own, expert_all, inner_rows):
    total_rows, width = expert_all.shape
    step = 256
    inner_steps, steps = inner_rows // step, total_rows // step

    def kernel(
        block_ref, tokens_ref, small_ref, dense_ref, expert_ref,
        block, tokens, inner, outer, query, key, value, output, router, gain_a, gain_q, gain_f, gain_k,
        low_box, full_box, load_sem, store_sem, row_sem,
    ):
        moves = [
            pltpu.make_async_copy(block_ref, block, row_sem.at[0]),
            pltpu.make_async_copy(tokens_ref, tokens, row_sem.at[1]),
        ]
        loads, stores = [], []
        for at in range(steps):
            loads.append(
                pltpu.make_async_copy(
                    expert_ref.at[pl.ds(at * step, step)], low_box.at[at], load_sem.at[at]
                )
            )
            if at < inner_steps:
                target = inner.at[pl.ds(at * step, step)]
            else:
                target = outer.at[pl.ds((at - inner_steps) * step, step)]
            stores.append(pltpu.make_async_copy(full_box.at[at], target, store_sem.at[at]))
        for copy in loads + moves:
            copy.start()
        for at in range(steps):
            loads[at].wait()
            full_box[at] = low_box[at].astype(f32)
            stores[at].start()
        at_k = QUERY + WIDTH
        for low, target in ((0, query), (at_k, key), (at_k + KEY, value), (QUERY, output)):
            target[...] = dense_ref[:, pl.ds(low, target.shape[1])].astype(f32)
        turned_small = jnp.transpose(small_ref[...])
        router[...] = turned_small[:EXPERTS, :ROWS_OWN]
        for index, target in enumerate((gain_a, gain_q, gain_f, gain_k)):
            size = target.shape[0]
            target[...] = turned_small[EXPERTS + index, :size].reshape(size)
        for copy in stores + moves:
            copy.wait()

    shapes = [(ROWS_OWN, QUERY), (ROWS_OWN, KEY), (ROWS_OWN, KEY), (ROWS_OWN, WIDTH)]
    shapes += [(EXPERTS, ROWS_OWN), (ROWS_OWN,), (ROWS_OWN,), (ROWS_OWN,), (KGAIN_OWN,)]
    return pl.pallas_call(
        kernel,
        out_shape=[
            jax.ShapeDtypeStruct(block_out.shape, bf16),
            jax.ShapeDtypeStruct(tokens_grad.shape, bf16),
            jax.ShapeDtypeStruct((inner_rows, width), f32),
            jax.ShapeDtypeStruct((total_rows - inner_rows, width), f32),
        ]
        + [jax.ShapeDtypeStruct(shape, f32) for shape in shapes],
        in_specs=[ANY, ANY, IN_VMEM, IN_VMEM, ANY],
        out_specs=[ANY] * 4 + [IN_VMEM] * len(shapes),
        scratch_shapes=[
            pltpu.VMEM((steps, step, width), bf16),
            pltpu.VMEM((steps, step, width), f32),
            pltpu.SemaphoreType.DMA((steps,)),
            pltpu.SemaphoreType.DMA((steps,)),
            pltpu.SemaphoreType.DMA((2,)),
        ],
        compiler_params=pltpu.CompilerParams(vmem_limit_bytes=VMEM_LIMIT),
    )(block_out, tokens_grad, small_sum, dense_own, expert_all)


def rotary_tables(positions):
    lane = jnp.arange(LANES, dtype=jnp.int32)
    half = HEAD_DIM // 2
    exponent = (lane % half).astype(f32) * (2.0 / HEAD_DIM)
    frequency = rope_base ** (-exponent)
    angles = positions.astype(f32)[:, None] * frequency[None, :]
    sign = jnp.where(lane % HEAD_DIM < half, -1.0, 1.0).astype(f32)
    return jnp.cos(angles), jnp.sin(angles) * sign[None, :]


def shards(
    tokens,
    cotangent,
    routes,
    picture_starts,
    attn_gain,
    query_weight,
    key_weight,
    value_weight,
    query_gain,
    key_gain,
    output_weight,
    ffn_gain,
    router_weight,
    expert_in,
    expert_down,
):
    seqs, positions, width = tokens.shape
    count = seqs * positions
    query_pos = lax.axis_index("rep") * positions + jnp.arange(positions, dtype=jnp.int32)
    cosine, sine = rotary_tables(query_pos)
    rows = tokens.reshape(count, width)
    grad_rows = cotangent.reshape(count, width)
    (
        dense, grad_all, pairs, soft, rows_first,
        attn_in, query_raw, key_raw, query_low, mixed, middle, sent, gates,
    ) = front_call(
        1, rows, grad_rows, (query_weight, key_weight, value_weight, output_weight),
        (attn_gain, query_gain, ffn_gain, key_gain), router_weight.T,
        cosine, sine, jnp.transpose(routes, (0, 2, 1)), picture_starts,
    )
    returned, out_terms, expert_terms = moe_call(
        2, sent, rows_first, grad_all, expert_in[0], expert_down[0]
    )
    block_out, tokens_grad, small_sum, dense_out, expert_all = back_call(
        3, returned, gates, middle, sent, dense, grad_rows, rows, attn_in,
        query_raw, key_raw, query_low, mixed, pairs, soft, out_terms, expert_terms, cosine, sine,
    )
    (
        block_out, tokens_grad, inner, outer, query, key, value, output, router, gain_a, gain_q, gain_f, gain_k,
    ) = finish_call(
        block_out, tokens_grad, small_sum, dense_out, expert_all.reshape(-1, width), expert_in.shape[1]
    )
    return (
        block_out.reshape(tokens.shape),
        tokens_grad.reshape(tokens.shape),
        gain_a,
        query,
        key,
        value,
        gain_q,
        gain_k,
        output,
        gain_f,
        router.T,
        inner[None],
        outer[None],
    )


def solution(mesh):
    by_tokens = P("shard", "rep", None)
    rows, line, block = P("shard", None), P("shard"), P("shard", None, None)
    in_specs = (
        by_tokens, by_tokens, by_tokens, rows, line, rows, rows, rows, line, line, rows, line, rows, block, block,
    )
    out_specs = (
        by_tokens, by_tokens, line, rows, rows, rows, line, line, rows, line, rows, block, block,
    )
    return jax.shard_map(shards, mesh=mesh, in_specs=in_specs, out_specs=out_specs, check_vma=False)
```
